32 devices in a mesh: fsdp: 8 (over y, x, core), dp: 4 (over z).
Axes of the slice: x: 2, y: 2, z: 4, core: 2. Of those that a mesh axis runs over, the one named last changes fastest.
Arguments:
- hidden: bfloat16 [32, 1024, 768], P(('fsdp', 'dp')), may hold values from -6 to 6
- segment_ids: int32 [32, 1024], P(('fsdp', 'dp')), may hold values from 0 to 19, never falling along the last dimension, each value on 1 to 64 neighbouring positions
- memory: bfloat16 [32, 20, 10, 768], P(('fsdp', 'dp')), may hold values from -6 to 6
- memory_row: int32 [32, 20], P(('fsdp', 'dp')), may hold values from 0 to 19, each once within a row
- buckets: int32 [2047], replicated, may hold values from 0 to 31
- attn_gain: bfloat16 [768], P('fsdp'), may hold values from 0.25 to 1.75
- ffn_gain: bfloat16 [768], P('fsdp'), may hold values from 0.25 to 1.75
- rel_table: bfloat16 [384], P('fsdp'), may hold values from -3 to 3
- w_qkv: bfloat16 [768, 2304], P('fsdp'), may hold values from -0.21875 to 0.21875
- w_attn_out: bfloat16 [768, 768], P('fsdp'), may hold values from -1.25 to 1.25
- w_in: bfloat16 [768, 3072], P('fsdp'), may hold values from -0.21875 to 0.21875
- w_down: bfloat16 [3072, 768], P('fsdp'), may hold values from -0.109375 to 0.109375
- w_prefix: bfloat16 [768, 3072], P('fsdp'), may hold values from -0.21875 to 0.21875
- cotangent: bfloat16 [32, 1024, 768], P(('fsdp', 'dp')), may hold values from -6 to 6
Outputs:
- output: bfloat16 [32, 1024, 768], P(('fsdp', 'dp'))
- hidden_grad: float32 [32, 1024, 768], P(('fsdp', 'dp'))
- memory_grad: float32 [32, 20, 10, 768], P(('fsdp', 'dp'))
- attn_gain_grad: float32 [768], P('fsdp')
- ffn_gain_grad: float32 [768], P('fsdp')
- rel_table_grad: float32 [384], P('fsdp')
- w_qkv_grad: float32 [768, 2304], P('fsdp')
- w_attn_out_grad: float32 [768, 768], P('fsdp')
- w_in_grad: float32 [768, 3072], P('fsdp')
- w_down_grad: float32 [3072, 768], P('fsdp')
- w_prefix_grad: float32 [768, 3072], P('fsdp')
The draws below stay inside these ranges and needn't reach their ends.
Inputs may be any that keep to these rules, and one draw needn't show every extreme that they name: `segment_ids`: in each row the segment ids never fall; each of the 20 questions has 1 to 64 tokens, and some question of each row has exactly 64. Each row of memory_row is a permutation of the 20 memory slots.
All inputs are finite; a program needn't handle non-finite values.
Results may differ from the reference program's by a relative error of at most 0.015.
Values may be sent and summed in bfloat16 or wider, within the bound.
A program may use at most 384 MiB of HBM per device.

```python
import math
import jax
import jax.numpy as jnp
import numpy as np
from jax import lax

D = 768
H = 12
DH = 64
FF = 3072
NB = 32
LEN = 1024
QLEN = 64
QPR = 20
PAIRS = 10
ROWS = 32


def place_ends(array, rng, low, largest):
    longest = array.shape.index(max(array.shape))
    spots = []
    for shift in (0, 1):
        where = [jax.random.randint(jax.random.fold_in(rng, axis), (), 0, length) for axis, length in enumerate(array.shape)]
        where[longest] = (where[longest] + shift) % array.shape[longest]
        spots.append(tuple(where))
    return array.at[spots[0]].set(low).at[spots[1]].set(largest)


def strengthened(drawn, stream_key, source, target, shards_of, factor):
    def block_of(axis_at):
        return (jnp.arange(drawn.shape[axis_at]) // (drawn.shape[axis_at] // shards_of)).reshape((-1,) + (1,) * (drawn.ndim - 1 - axis_at))

    first = jax.random.permutation(stream_key, shards_of)[block_of(target)]
    other_side = (block_of(target) + shards_of // 2) % shards_of
    return jnp.where((block_of(source) == first) | (block_of(source) == other_side), factor * drawn, drawn)


def steps_of(own_key, shape, pieces, smallest, high):
    gain, own = 1.0, jax.random.fold_in(own_key, 6)
    for axis_at, blocks in pieces:
        draws = jnp.exp(jax.random.uniform(jax.random.fold_in(own, axis_at), (blocks,), jnp.float32, smallest / len(pieces), high / len(pieces)))
        gain = gain * jnp.repeat(draws, shape[axis_at] // blocks).reshape([-1 if axis == axis_at else 1 for axis in range(len(shape))])
    return gain


def split_up(amount, total, bound, slope):
    weights = [(1 << 20) // math.isqrt(grade ** slope) + 1 for grade in range(2, amount + 1)]
    surplus, counts = total - bound - (amount - 1), [1] * (amount - 1)
    while surplus > 0:
        movable = [i for i in range(amount - 1) if counts[i] < bound]
        mass, remaining = sum([weights[i] for i in movable]), surplus
        for i in movable:
            extra = min(bound - counts[i], max(1, remaining * weights[i] // mass), surplus)
            counts[i] = counts[i] + extra
            surplus = surplus - extra
    return np.array([bound] + counts)


def uneven(rng, count, total, reach, lean):
    if count == 2:
        one = jax.random.randint(rng, (), max(1, total - reach), min(reach, total - 1) + 1)
        return jnp.stack([one, total - one])
    lengths = jnp.asarray(split_up(count, total, reach, lean), jnp.int32)
    twos = (count - 1) // 2
    donor, taker = lengths[1:1 + 2 * twos:2], lengths[2:2 + 2 * twos:2]
    margin = jnp.minimum(donor - 1, reach - taker)
    moved = jax.random.randint(jax.random.fold_in(rng, 1), (twos,), 0, 1 << 20) % (margin + 1)
    lengths = lengths.at[1:1 + 2 * twos:2].set(donor - moved).at[2:2 + 2 * twos:2].set(taker + moved)
    return lengths[jax.random.permutation(jax.random.fold_in(rng, 2), count)]


def noise(stream_key, dims, scale, reach, shards=(), kind=jnp.bfloat16):
    entries = scale * jax.random.normal(stream_key, dims, jnp.float32)
    if shards:
        entries = entries * steps_of(stream_key, dims, shards, -0.22, 0.18)
    return jnp.clip(entries, -reach, reach).astype(kind)


def gaussian_with(stream_key, dims, spread, reach, shards, heavy, held_as=jnp.bfloat16):
    values = spread * jax.random.normal(stream_key, dims, jnp.float32)
    if shards:
        values = values * steps_of(stream_key, dims, shards, -0.22, 0.18)
    return jnp.clip(strengthened(values, jax.random.fold_in(stream_key, 3), *heavy), -reach, reach).astype(held_as)


def setup_inputs(seed: int = 0) -> dict:
    seeds = jax.random.split(jax.random.key(seed), 15)
    hidden = gaussian_with(seeds[0], (ROWS, LEN, D), 1.0, 6.0, ((0, 32),), (0, 2, 32, 2.75))
    segment_ids = jax.vmap(lambda own: jnp.searchsorted(jnp.cumsum(uneven(own, QPR, LEN, QLEN, 1)), jnp.arange(LEN), side="right"))(jax.random.split(seeds[1], ROWS)).reshape((ROWS, LEN)).astype(jnp.int32)
    memory = gaussian_with(seeds[2], (ROWS, QPR, PAIRS, D), 1.0, 6.0, ((0, 32),), (0, 3, 32, 2.75))
    memory_row = jax.vmap(lambda own: jax.random.permutation(own, QPR))(jax.random.split(seeds[3], ROWS)).reshape((ROWS, QPR)).astype(jnp.int32)
    buckets = place_ends(jax.random.randint(seeds[4], (2 * LEN - 1,), 0, NB), jax.random.fold_in(seeds[4], 1), 0, NB - 1).astype(jnp.int32)
    attn_gain = jnp.clip(1.0 + 0.15 * jax.random.normal(seeds[5], (D,), jnp.float32), 0.25, 1.75).astype(jnp.bfloat16)
    ffn_gain = jnp.clip(1.0 + 0.15 * jax.random.normal(seeds[6], (D,), jnp.float32), 0.25, 1.75).astype(jnp.bfloat16)
    rel_table = noise(seeds[7], (NB * H,), 0.5, 3.0, ((0, 8),))
    w_qkv = noise(seeds[8], (D, 3 * D), D ** -0.5, 0.21875, ((0, 8),))
    w_attn_out = noise(seeds[9], (D, D), (D // 32) ** -0.5, 1.25, ((0, 8),))
    w_in = noise(seeds[10], (D, FF), D ** -0.5, 0.21875, ((0, 8),))
    w_down = noise(seeds[11], (FF, D), FF ** -0.5, 0.109375, ((0, 8),))
    w_prefix = noise(seeds[12], (D, 4 * D), D ** -0.5, 0.21875, ((0, 8),))
    cotangent = noise(seeds[13], (ROWS, LEN, D), 1.0, 6.0, ((0, 32),))
    return {"hidden": hidden, "segment_ids": segment_ids, "memory": memory, "memory_row": memory_row, "buckets": buckets, "attn_gain": attn_gain, "ffn_gain": ffn_gain, "rel_table": rel_table, "w_qkv": w_qkv, "w_attn_out": w_attn_out, "w_in": w_in, "w_down": w_down, "w_prefix": w_prefix, "cotangent": cotangent}


epsilon = 1e-06
masked_out = -1e+30
highest = lax.Precision.HIGHEST

@jax.custom_vjp
def low(v):
    return lax.optimization_barrier(v.astype(jnp.bfloat16)).astype(jnp.float32)

@jax.custom_vjp
def low_back(v):
    return v

def low_keep(v):
    return (low(v), None)

def low_pass(kept, grad):
    return (grad,)

def back_keep(v):
    return (v, None)

def back_low(kept, grad):
    return (low(grad),)
low.defvjp(low_keep, low_pass)
low_back.defvjp(back_keep, back_low)

def rms_scale(values, norm_gain):
    return values * lax.rsqrt(lax.optimization_barrier(jnp.mean(values * values, axis=-1, keepdims=True)) + epsilon) * norm_gain

def position_bias(relative, first_row, block_rows, sequence_length, slot_count):
    query_pos = first_row + jnp.arange(block_rows, dtype=jnp.int32)
    offsets = query_pos[:, None] - jnp.arange(sequence_length, dtype=jnp.int32)[None, :] + (sequence_length - 1)
    per_token_bias = jnp.transpose(jnp.take(relative, offsets, axis=0), (2, 0, 1))
    return jnp.pad(per_token_bias, ((0, 0), (0, 0), (0, slot_count)))

def row_forward(tokens, segments, stored, chosen, buckets, params):
    attn_gain, ffn_gain, rel_table, w_qkv, w_attn_out, w_in, w_down, w_prefix = params
    sequence_length = tokens.shape[0]
    slot_count = QPR * PAIRS * 2
    normed = low(rms_scale(tokens, attn_gain))
    projected = low_back(low(jnp.dot(normed, w_qkv, precision=highest)))
    picker = (chosen[:, None] == jnp.arange(QPR, dtype=jnp.int32)[None, :]).astype(jnp.float32)
    picked = jnp.einsum('qs,spd->qpd', picker, stored, precision=highest)
    prefix = low_back(low(jnp.einsum('qpd,de->qpe', picked, w_prefix, precision=highest)))
    queries = projected[:, :D].reshape(sequence_length, H, DH)
    all_keys = jnp.concatenate([projected[:, D:2 * D].reshape(sequence_length, H, DH), prefix[:, :, :2 * D].reshape(slot_count, H, DH)], axis=0)
    all_values = jnp.concatenate([projected[:, 2 * D:].reshape(sequence_length, H, DH), prefix[:, :, 2 * D:].reshape(slot_count, H, DH)], axis=0)
    bucket_hot = (buckets[:, None] == jnp.arange(NB, dtype=jnp.int32)[None, :]).astype(jnp.float32)
    relative = jnp.dot(bucket_hot, rel_table.reshape(NB, H), precision=highest)
    key_segments = jnp.concatenate([segments, jnp.arange(slot_count, dtype=jnp.int32) // (PAIRS * 2)])
    block_rows = min(512, sequence_length)
    score_scale = DH ** (-0.5)

    def one_block(first_row):
        block_queries = lax.dynamic_slice_in_dim(queries, first_row, block_rows, 0)
        block_segments = lax.dynamic_slice_in_dim(segments, first_row, block_rows, 0)
        scores = jnp.einsum('qhd,khd->hqk', block_queries, all_keys, precision=highest)
        logits = low_back(scores * score_scale + position_bias(relative, first_row, block_rows, sequence_length, slot_count))
        allowed = block_segments[:, None] == key_segments[None, :]
        logits = jnp.where(allowed[None], logits, masked_out)
        row_peak = lax.optimization_barrier(jnp.max(logits, axis=-1, keepdims=True))
        exponent = jnp.exp(logits - row_peak)
        soft = low(exponent / lax.optimization_barrier(jnp.sum(exponent, axis=-1, keepdims=True)))
        return jnp.einsum('hqk,khd->qhd', soft, all_values, precision=highest)
    starts = jnp.arange(sequence_length // block_rows, dtype=jnp.int32) * block_rows
    blended = lax.map(jax.checkpoint(one_block), starts)
    attended = low_back(low(blended.reshape(sequence_length, D)))
    after_attn = tokens + low_back(jnp.dot(attended, w_attn_out, precision=highest))
    normed_ffn = low(rms_scale(after_attn, ffn_gain))
    hidden_pre = low_back(jnp.dot(normed_ffn, w_in, precision=highest))
    activation = low(jax.nn.gelu(hidden_pre))
    return after_attn + low_back(jnp.dot(activation, w_down, precision=highest))

def reference(hidden, segment_ids, memory, memory_row, buckets, attn_gain, ffn_gain, rel_table, w_qkv, w_attn_out, w_in, w_down, w_prefix, cotangent):
    weights = tuple((tensor.astype(jnp.float32) for tensor in (attn_gain, ffn_gain, rel_table, w_qkv, w_attn_out, w_in, w_down, w_prefix)))

    def one_row(totals, row_inputs):
        row_tokens, row_segments, row_memory, row_chosen, row_grad = row_inputs

        def forward(tokens, stored, params):
            return row_forward(tokens, row_segments, stored, row_chosen, buckets, params)
        result, pullback = jax.vjp(forward, row_tokens.astype(jnp.float32), row_memory.astype(jnp.float32), weights)
        tokens_grad, stored_grad, weight_grads = pullback(row_grad.astype(jnp.float32))
        totals = jax.tree.map(lambda earlier, later: earlier + later, totals, weight_grads)
        return (totals, (result.astype(jnp.bfloat16), tokens_grad, stored_grad))
    initial = jax.tree.map(jnp.zeros_like, weights)
    totals, (output, hidden_grad, memory_grad) = lax.scan(one_row, initial, (hidden, segment_ids, memory, memory_row, cotangent))
    return (output, hidden_grad, memory_grad, totals[0], totals[1], totals[2], totals[3], totals[4], totals[5], totals[6], totals[7])
```

```python
import functools
import jax
import jax.numpy as jnp
from jax import lax
from jax.experimental import pallas as pl
from jax.experimental.pallas import tpu as pltpu

H = 12
DH = 64
NB = 32
QLEN = 64
QPR = 20
PAIRS = 10

WIN = 80
SLOT = 16
KEYS = 128
GROUP = 4
GW = GROUP * DH
masked_out = -1e30
f32 = jnp.float32
bf16 = jnp.bfloat16
NT = (((1,), (1,)), ((), ()))
TN = (((0,), (0,)), ((), ()))


def mm(a, b, dims=(((1,), (0,)), ((), ()))):
    return lax.dot_general(a, b, dims, preferred_element_type=f32)


def bucket_hot(idx_ref):
    return (lax.broadcasted_iota(jnp.int32, (NB, KEYS), 0) == idx_ref[...]).astype(f32)


def fill_bias(table_ref, idx_ref, bias):
    hot = bucket_hot(idx_ref).astype(bf16)
    lines = mm(table_ref[...], hot)
    lane = lax.broadcasted_iota(jnp.int32, (WIN, KEYS), 1)
    for h in range(H):
        wide = jnp.broadcast_to(lines[h : h + 1, :], (WIN, KEYS))
        rolled = pltpu.roll(wide, 0, 1, stride=1, stride_axis=0)
        bias[h * WIN : (h + 1) * WIN, :] = jnp.where(lane < WIN, rolled, 0.0)


def stack_heads(block):
    lane = lax.broadcasted_iota(jnp.int32, block.shape, 1) // DH
    zero = jnp.zeros_like(block)
    return jnp.concatenate([jnp.where(lane == h, block, zero) for h in range(GROUP)], axis=0)


def merge_heads(stacked):
    lane = lax.broadcasted_iota(jnp.int32, (WIN, GW), 1) // DH
    out = stacked[:WIN]
    for h in range(1, GROUP):
        out = jnp.where(lane == h, stacked[h * WIN : (h + 1) * WIN], out)
    return out


def key_tile(tokens, low, high):
    rest = jnp.zeros((KEYS - WIN - 2 * SLOT, tokens.shape[1]), tokens.dtype)
    return jnp.concatenate([tokens, low, high, rest], axis=0)


def key_cost(begin, end):
    lane = lax.broadcasted_iota(jnp.int32, (1, KEYS), 1)
    token = (lane >= begin) & (lane < end)
    first = (lane >= WIN) & (lane < WIN + PAIRS)
    second = (lane >= WIN + SLOT) & (lane < WIN + SLOT + PAIRS)
    return jnp.where(token | first | second, 0.0, masked_out).astype(f32)


def soft_rows(stack, keys, bias_block, cost):
    logits = mm(stack, keys, NT) + (bias_block + cost)
    peak = jnp.max(logits, axis=1, keepdims=True)
    raw = jnp.exp(logits - peak)
    return raw * (1.0 / jnp.sum(raw, axis=1, keepdims=True))


def window(start_ref, q):
    start = start_ref[q]
    base = pl.multiple_of((start // 16) * 16, 16)
    base = jnp.minimum(base, start_ref[QPR] - WIN)
    base = pl.multiple_of(base, 16)
    return base, start - base, start_ref[q + 1] - base


def forward_kernel(start_ref, proj_ref, prefix_ref, table_ref, idx_ref, out_ref, bias):
    width = out_ref.shape[1]
    fill_bias(table_ref, idx_ref, bias)

    def body(q, carry):
        base, begin, end = window(start_ref, q)
        cost = key_cost(begin, end)
        row = lax.broadcasted_iota(jnp.int32, (WIN, GW), 0)
        mine = (row >= begin) & (row < end)
        rows = pl.ds(base, WIN)
        for g in range(width // GW):
            at = g * GW
            stack = stack_heads(proj_ref[rows, at : at + GW] * bf16(DH**-0.5))
            keys = key_tile(
                proj_ref[rows, width + at : width + at + GW],
                prefix_ref[q, :, at : at + GW],
                prefix_ref[q, :, width + at : width + at + GW],
            )
            values = key_tile(
                proj_ref[rows, 2 * width + at : 2 * width + at + GW],
                prefix_ref[q, :, 2 * width + at : 2 * width + at + GW],
                prefix_ref[q, :, 3 * width + at : 3 * width + at + GW],
            )
            soft = soft_rows(stack, keys, bias[g * GROUP * WIN : (g + 1) * GROUP * WIN, :], cost)
            blended = merge_heads(mm(soft.astype(bf16), values)).astype(bf16)
            out_ref[rows, at : at + GW] = jnp.where(mine, blended, out_ref[rows, at : at + GW])
        return carry

    lax.fori_loop(0, QPR, body, 0)


def backward_kernel(
    start_ref, proj_ref, prefix_ref, grad_ref, table_ref, idx_ref,
    token_ref, slot_ref, table_grad_ref, bias, bias_grad,
):
    width = grad_ref.shape[1]
    fill_bias(table_ref, idx_ref, bias)
    bias_grad[...] = jnp.zeros_like(bias_grad)

    def body(q, carry):
        base, begin, end = window(start_ref, q)
        cost = key_cost(begin, end)
        row = lax.broadcasted_iota(jnp.int32, (WIN, GW), 0)
        mine = (row >= begin) & (row < end)
        rows = pl.ds(base, WIN)
        for g in range(width // GW):
            at = g * GW
            heads = slice(g * GROUP * WIN, (g + 1) * GROUP * WIN)
            stack = stack_heads(proj_ref[rows, at : at + GW] * bf16(DH**-0.5))
            keys = key_tile(
                proj_ref[rows, width + at : width + at + GW],
                prefix_ref[q, :, at : at + GW],
                prefix_ref[q, :, width + at : width + at + GW],
            )
            values = key_tile(
                proj_ref[rows, 2 * width + at : 2 * width + at + GW],
                prefix_ref[q, :, 2 * width + at : 2 * width + at + GW],
                prefix_ref[q, :, 3 * width + at : 3 * width + at + GW],
            )
            grad = grad_ref[rows, at : at + GW]
            grads = stack_heads(jnp.where(mine, grad, jnp.zeros_like(grad)))
            soft = soft_rows(stack, keys, bias[heads, :], cost)
            prob_grad = mm(grads, values, NT)
            weighted = soft * prob_grad
            logit_grad = weighted - soft * jnp.sum(weighted, axis=1, keepdims=True)
            low = logit_grad.astype(bf16)
            bias_grad[heads, :] += low.astype(f32)
            query_grad = (merge_heads(mm(low, keys)) * DH**-0.5).astype(bf16)
            key_grad = mm(low, stack, TN).astype(bf16)
            value_grad = mm(soft.astype(bf16), grads, TN).astype(bf16)
            for part, fresh in ((0, query_grad), (1, key_grad[:WIN]), (2, value_grad[:WIN])):
                cols = slice(part * width + at, part * width + at + GW)
                token_ref[rows, cols] = jnp.where(mine, fresh, token_ref[rows, cols])
            for part, fresh in ((0, key_grad), (2, value_grad)):
                for s in range(2):
                    cols = slice((part + s) * width + at, (part + s) * width + at + GW)
                    slot_ref[q, :, cols] = fresh[WIN + s * SLOT : WIN + (s + 1) * SLOT]
        return carry

    lax.fori_loop(0, QPR, body, 0)
    lane = lax.broadcasted_iota(jnp.int32, (H, KEYS), 1)
    sums = jnp.zeros((H, KEYS), f32)
    for i in range(WIN):
        line = jnp.where(lane < WIN, bias_grad[pl.ds(i, H, stride=WIN), :], 0.0)
        sums += line if i == 0 else pltpu.roll(line, KEYS - i, 1)
    sums = jnp.concatenate([sums, jnp.zeros((16 - H, KEYS), f32)], axis=0)
    table_grad_ref[...] = lax.dot_general(
        bucket_hot(idx_ref), sums, NT, precision=lax.Precision.HIGHEST, preferred_element_type=f32
    )


SMEM = pl.BlockSpec(memory_space=pltpu.SMEM)
VMEM = pl.BlockSpec(memory_space=pltpu.VMEM)


def attend(starts, projected, prefix, table, idx):
    length = projected.shape[0]
    width = projected.shape[1] // 3
    return pl.pallas_call(
        forward_kernel,
        out_shape=jax.ShapeDtypeStruct((length, width), bf16),
        in_specs=[SMEM, VMEM, VMEM, VMEM, VMEM],
        out_specs=VMEM,
        scratch_shapes=[pltpu.VMEM((H * WIN, KEYS), f32)],
        compiler_params=pltpu.CompilerParams(vmem_limit_bytes=40 << 20),
        name="attend",
    )(starts, projected, prefix, table, idx)


def attend_back(starts, projected, prefix, grad, table, idx):
    length = projected.shape[0]
    return pl.pallas_call(
        backward_kernel,
        out_shape=(
            jax.ShapeDtypeStruct(projected.shape, bf16),
            jax.ShapeDtypeStruct(prefix.shape, bf16),
            jax.ShapeDtypeStruct((NB, 16), f32),
        ),
        in_specs=[SMEM, VMEM, VMEM, VMEM, VMEM, VMEM],
        out_specs=(VMEM, VMEM, VMEM),
        scratch_shapes=[pltpu.VMEM((H * WIN, KEYS), f32), pltpu.VMEM((H * WIN, KEYS), f32)],
        compiler_params=pltpu.CompilerParams(vmem_limit_bytes=48 << 20),
        name="attend_back",
    )(starts, projected, prefix, grad, table, idx)


def row_starts(segments):
    length = segments.shape[0]
    ids = jnp.arange(QPR + 1, dtype=jnp.int32)
    return jnp.sum((segments[None, :] < ids[:, None]).astype(jnp.int32), axis=1)


def near_buckets(buckets, length):
    back = buckets[length - QLEN : length][::-1]
    ahead = buckets[length : length + QLEN - 1][::-1]
    return jnp.concatenate([back, buckets[length - 1 : length], ahead])[None, :]


from jax.sharding import PartitionSpec as P

epsilon = 1e-06


def rms_scale(values, norm_gain):
    return (
        values * lax.rsqrt(jnp.mean(values * values, axis=-1, keepdims=True) + epsilon) * norm_gain
    )


def prefix_kernel(row_ref, memory_ref, w_ref, picked_ref, prefix_ref):
    width = w_ref.shape[0]
    for q in range(QPR):
        picked_ref[q] = memory_ref[row_ref[q]]
    picked = picked_ref[...].reshape(QPR * SLOT, width)
    for at in range(0, w_ref.shape[1], width):
        part = mm(picked, w_ref[:, at : at + width]).astype(bf16)
        prefix_ref[:, :, at : at + width] = part.reshape(QPR, SLOT, width)


def make_prefix(chosen, memory, w_prefix):
    padded = jnp.pad(memory, ((0, 0), (0, SLOT - PAIRS), (0, 0)))
    return pl.pallas_call(
        prefix_kernel,
        out_shape=(
            jax.ShapeDtypeStruct(padded.shape, bf16),
            jax.ShapeDtypeStruct((QPR, SLOT, w_prefix.shape[1]), bf16),
        ),
        in_specs=[SMEM, VMEM, VMEM],
        out_specs=(VMEM, VMEM),
        compiler_params=pltpu.CompilerParams(vmem_limit_bytes=40 << 20),
        name="make_prefix",
    )(chosen, padded, w_prefix)


def memory_kernel(row_ref, slot_ref, w_ref, out_ref, held):
    width = w_ref.shape[0]
    slots = slot_ref[...].reshape(QPR * SLOT, w_ref.shape[1])
    held[...] = mm(slots, w_ref[...], NT).reshape(QPR, SLOT, width)
    for q in range(QPR):
        out_ref[row_ref[q]] = held[q, :PAIRS, :]


def memory_back(chosen, slot_grad, w_prefix):
    width = w_prefix.shape[0]
    return pl.pallas_call(
        memory_kernel,
        out_shape=jax.ShapeDtypeStruct((QPR, PAIRS, width), f32),
        in_specs=[SMEM, VMEM, VMEM],
        out_specs=VMEM,
        scratch_shapes=[pltpu.VMEM((QPR, SLOT, width), f32)],
        compiler_params=pltpu.CompilerParams(vmem_limit_bytes=40 << 20),
        name="memory_back",
    )(chosen, slot_grad, w_prefix)


def row_pass(hidden, segments, memory, chosen, buckets, cotangent, full):
    attn_gain, ffn_gain, rel_table, w_qkv, w_attn_out, w_in, w_down, w_prefix = full
    length, width = hidden.shape
    starts = row_starts(segments)
    idx = near_buckets(buckets, length)
    table = jnp.pad(rel_table.reshape(NB, H).T, ((0, 16 - H), (0, 0)))
    tokens = hidden.astype(f32)
    gain_one = attn_gain.astype(f32)
    gain_two = ffn_gain.astype(f32)

    normed = rms_scale(tokens, gain_one).astype(bf16)
    projected = mm(normed, w_qkv).astype(bf16)
    picked, prefix = make_prefix(chosen, memory, w_prefix)
    attended = attend(starts, projected, prefix, table, idx)
    after_attn = tokens + mm(attended, w_attn_out)
    normed_ffn = rms_scale(after_attn, gain_two).astype(bf16)
    hidden_pre = mm(normed_ffn, w_in)
    activation = jax.nn.gelu(hidden_pre).astype(bf16)
    output = (after_attn + mm(activation, w_down)).astype(bf16)

    grad_out = cotangent.astype(f32)
    down_grad = mm(activation, cotangent, TN)
    act_grad = mm(cotangent, w_down, NT)
    pre_grad = jax.vjp(jax.nn.gelu, hidden_pre)[1](act_grad)[0].astype(bf16)
    in_grad = mm(normed_ffn, pre_grad, TN)
    normed_ffn_grad = mm(pre_grad, w_in, NT)
    residual_part, ffn_gain_grad = jax.vjp(rms_scale, after_attn, gain_two)[1](normed_ffn_grad)
    after_grad = grad_out + residual_part
    attn_branch = after_grad.astype(bf16)
    attn_out_grad = mm(attended, attn_branch, TN)
    attended_grad = mm(attn_branch, w_attn_out, NT).astype(bf16)
    token_grad, slot_grad, table_grad = attend_back(
        starts, projected, prefix, attended_grad, table, idx
    )
    qkv_grad = mm(normed, token_grad, TN)
    normed_grad = mm(token_grad, w_qkv, NT)
    flat = (QPR * SLOT, -1)
    prefix_grad = mm(picked.reshape(flat), slot_grad.reshape(flat), TN)
    memory_grad = memory_back(chosen, slot_grad, w_prefix)
    norm_part, attn_gain_grad = jax.vjp(rms_scale, tokens, gain_one)[1](normed_grad)
    hidden_grad = after_grad + norm_part
    small = jnp.concatenate([attn_gain_grad, ffn_gain_grad, table_grad[:, :H].reshape(NB * H)])
    return output, hidden_grad, memory_grad, small, (qkv_grad, attn_out_grad, in_grad, down_grad, prefix_grad)


def local(
    hidden, segment_ids, memory, memory_row, buckets, attn_gain, ffn_gain, rel_table,
    w_qkv, w_attn_out, w_in, w_down, w_prefix, cotangent,
):
    sizes = (attn_gain.shape[0], ffn_gain.shape[0], rel_table.shape[0])
    small = lax.all_gather(jnp.concatenate([attn_gain, ffn_gain, rel_table]), "fsdp", axis=0)
    cuts = (0, sizes[0], sizes[0] + sizes[1], sum(sizes))
    full = tuple(small[:, cuts[i] : cuts[i + 1]].reshape(-1) for i in range(3)) + tuple(
        lax.all_gather(w, "fsdp", axis=0, tiled=True)
        for w in (w_qkv, w_attn_out, w_in, w_down, w_prefix)
    )
    outs = []
    total = None
    for r in range(hidden.shape[0]):
        *own, small_grad, grads = row_pass(
            hidden[r], segment_ids[r], memory[r], memory_row[r], buckets, cotangent[r], full
        )
        outs.append(own)
        fresh = (small_grad,) + grads
        total = fresh if total is None else jax.tree.map(jnp.add, total, fresh)
    output, hidden_grad, memory_grad = (jnp.stack(x) for x in zip(*outs))
    small_grad = lax.psum(total[0], ("fsdp", "dp"))
    me = lax.axis_index("fsdp")
    bases = (0, full[0].shape[0], full[0].shape[0] + full[1].shape[0])
    shares = [
        lax.dynamic_slice_in_dim(small_grad, base + me * size, size) for base, size in zip(bases, sizes)
    ]
    for gradient in total[1:]:
        share = lax.psum_scatter(
            gradient.astype(bf16), "fsdp", scatter_dimension=0, tiled=True
        )
        shares.append(lax.psum(share, "dp").astype(f32))
    return (output, hidden_grad, memory_grad) + tuple(shares)


def solution(mesh):
    rows = ("fsdp", "dp")
    placed = (
        P(rows, None, None), P(rows, None), P(rows, None, None, None), P(rows, None), P(),
        P("fsdp"), P("fsdp"), P("fsdp"),
        P("fsdp", None), P("fsdp", None), P("fsdp", None), P("fsdp", None), P("fsdp", None),
        P(rows, None, None),
    )
    return jax.shard_map(
        local,
        mesh=mesh,
        in_specs=placed,
        out_specs=(
            P(rows, None, None), P(rows, None, None), P(rows, None, None, None),
            P("fsdp"), P("fsdp"), P("fsdp"),
            P("fsdp", None), P("fsdp", None), P("fsdp", None), P("fsdp", None), P("fsdp", None),
        ),
        check_vma=False,
    )
```

```python
import functools
import jax
import jax.numpy as jnp
from jax import lax
from jax.experimental import pallas as pl
from jax.experimental.pallas import tpu as pltpu
from jax.sharding import PartitionSpec as P

H = 12
DH = 64
NB = 32
QLEN = 64
QPR = 20
PAIRS = 10

WIN = 80
SLOT = 16
KEYS = 128
GROUP = 4
GW = GROUP * DH
masked_out = -1e30
f32 = jnp.float32
bf16 = jnp.bfloat16
NT = (((1,), (1,)), ((), ()))
TN = (((0,), (0,)), ((), ()))


def mm(a, b, dims=(((1,), (0,)), ((), ()))):
    return lax.dot_general(a, b, dims, preferred_element_type=f32)


def bucket_hot(idx_ref):
    return (lax.broadcasted_iota(jnp.int32, (NB, KEYS), 0) == idx_ref[...]).astype(f32)


def fill_bias(table_ref, idx_ref, bias):
    hot = bucket_hot(idx_ref).astype(bf16)
    lines = mm(table_ref[...], hot)
    lane = lax.broadcasted_iota(jnp.int32, (WIN, KEYS), 1)
    for h in range(H):
        wide = jnp.broadcast_to(lines[h : h + 1, :], (WIN, KEYS))
        rolled = pltpu.roll(wide, 0, 1, stride=1, stride_axis=0)
        bias[h * WIN : (h + 1) * WIN, :] = jnp.where(lane < WIN, rolled, 0.0)


def stack_heads(block):
    lane = lax.broadcasted_iota(jnp.int32, block.shape, 1) // DH
    zero = jnp.zeros_like(block)
    return jnp.concatenate([jnp.where(lane == h, block, zero) for h in range(GROUP)], axis=0)


def merge_heads(stacked):
    lane = lax.broadcasted_iota(jnp.int32, (WIN, GW), 1) // DH
    out = stacked[:WIN]
    for h in range(1, GROUP):
        out = jnp.where(lane == h, stacked[h * WIN : (h + 1) * WIN], out)
    return out


def key_tile(tokens, low, high):
    rest = jnp.zeros((KEYS - WIN - 2 * SLOT, tokens.shape[1]), tokens.dtype)
    return jnp.concatenate([tokens, low, high, rest], axis=0)


def key_cost(begin, end):
    lane = lax.broadcasted_iota(jnp.int32, (1, KEYS), 1)
    token = (lane >= begin) & (lane < end)
    first = (lane >= WIN) & (lane < WIN + PAIRS)
    second = (lane >= WIN + SLOT) & (lane < WIN + SLOT + PAIRS)
    return jnp.where(token | first | second, 0.0, masked_out).astype(f32)


def soft_rows(stack, keys, bias_block, cost):
    logits = mm(stack, keys, NT) + (bias_block + cost)
    peak = jnp.max(logits, axis=1, keepdims=True)
    raw = jnp.exp(logits - peak)
    return raw * (1.0 / jnp.sum(raw, axis=1, keepdims=True))


def window(start_ref, q):
    start = start_ref[q]
    base = pl.multiple_of((start // 16) * 16, 16)
    base = jnp.minimum(base, start_ref[QPR] - WIN)
    base = pl.multiple_of(base, 16)
    return base, start - base, start_ref[q + 1] - base


def forward_kernel(start_ref, proj_ref, prefix_ref, table_ref, idx_ref, out_ref, bias):
    width = out_ref.shape[1]
    fill_bias(table_ref, idx_ref, bias)

    def body(q, carry):
        base, begin, end = window(start_ref, q)
        cost = key_cost(begin, end)
        row = lax.broadcasted_iota(jnp.int32, (WIN, GW), 0)
        mine = (row >= begin) & (row < end)
        rows = pl.ds(base, WIN)
        for g in range(width // GW):
            at = g * GW
            stack = stack_heads(proj_ref[rows, at : at + GW] * bf16(DH**-0.5))
            keys = key_tile(
                proj_ref[rows, width + at : width + at + GW],
                prefix_ref[q, :, at : at + GW],
                prefix_ref[q, :, width + at : width + at + GW],
            )
            values = key_tile(
                proj_ref[rows, 2 * width + at : 2 * width + at + GW],
                prefix_ref[q, :, 2 * width + at : 2 * width + at + GW],
                prefix_ref[q, :, 3 * width + at : 3 * width + at + GW],
            )
            soft = soft_rows(stack, keys, bias[g * GROUP * WIN : (g + 1) * GROUP * WIN, :], cost)
            blended = merge_heads(mm(soft.astype(bf16), values)).astype(bf16)
            out_ref[rows, at : at + GW] = jnp.where(mine, blended, out_ref[rows, at : at + GW])
        return carry

    lax.fori_loop(0, QPR, body, 0)


def backward_kernel(
    start_ref, proj_ref, prefix_ref, grad_ref, table_ref, idx_ref,
    token_ref, slot_ref, table_grad_ref, bias, bias_grad,
):
    width = grad_ref.shape[1]
    fill_bias(table_ref, idx_ref, bias)
    bias_grad[...] = jnp.zeros_like(bias_grad)

    def body(q, carry):
        base, begin, end = window(start_ref, q)
        cost = key_cost(begin, end)
        row = lax.broadcasted_iota(jnp.int32, (WIN, GW), 0)
        mine = (row >= begin) & (row < end)
        rows = pl.ds(base, WIN)
        for g in range(width // GW):
            at = g * GW
            heads = slice(g * GROUP * WIN, (g + 1) * GROUP * WIN)
            stack = stack_heads(proj_ref[rows, at : at + GW] * bf16(DH**-0.5))
            keys = key_tile(
                proj_ref[rows, width + at : width + at + GW],
                prefix_ref[q, :, at : at + GW],
                prefix_ref[q, :, width + at : width + at + GW],
            )
            values = key_tile(
                proj_ref[rows, 2 * width + at : 2 * width + at + GW],
                prefix_ref[q, :, 2 * width + at : 2 * width + at + GW],
                prefix_ref[q, :, 3 * width + at : 3 * width + at + GW],
            )
            grad = grad_ref[rows, at : at + GW]
            grads = stack_heads(jnp.where(mine, grad, jnp.zeros_like(grad)))
            soft = soft_rows(stack, keys, bias[heads, :], cost)
            prob_grad = mm(grads, values, NT)
            weighted = soft * prob_grad
            logit_grad = weighted - soft * jnp.sum(weighted, axis=1, keepdims=True)
            low = logit_grad.astype(bf16)
            bias_grad[heads, :] += low.astype(f32)
            query_grad = (merge_heads(mm(low, keys)) * DH**-0.5).astype(bf16)
            key_grad = mm(low, stack, TN).astype(bf16)
            value_grad = mm(soft.astype(bf16), grads, TN).astype(bf16)
            for part, fresh in ((0, query_grad), (1, key_grad[:WIN]), (2, value_grad[:WIN])):
                cols = slice(part * width + at, part * width + at + GW)
                token_ref[rows, cols] = jnp.where(mine, fresh, token_ref[rows, cols])
            for part, fresh in ((0, key_grad), (2, value_grad)):
                for s in range(2):
                    cols = slice((part + s) * width + at, (part + s) * width + at + GW)
                    slot_ref[q, :, cols] = fresh[WIN + s * SLOT : WIN + (s + 1) * SLOT]
        return carry

    lax.fori_loop(0, QPR, body, 0)
    lane = lax.broadcasted_iota(jnp.int32, (H, KEYS), 1)
    sums = jnp.zeros((H, KEYS), f32)
    for i in range(WIN):
        line = jnp.where(lane < WIN, bias_grad[pl.ds(i, H, stride=WIN), :], 0.0)
        sums += line if i == 0 else pltpu.roll(line, KEYS - i, 1)
    sums = jnp.concatenate([sums, jnp.zeros((16 - H, KEYS), f32)], axis=0)
    table_grad_ref[...] = lax.dot_general(
        bucket_hot(idx_ref), sums, NT, precision=lax.Precision.HIGHEST, preferred_element_type=f32
    )


SMEM = pl.BlockSpec(memory_space=pltpu.SMEM)
VMEM = pl.BlockSpec(memory_space=pltpu.VMEM)


def attend(starts, projected, prefix, table, idx):
    length = projected.shape[0]
    width = projected.shape[1] // 3
    return pl.pallas_call(
        forward_kernel,
        out_shape=jax.ShapeDtypeStruct((length, width), bf16),
        in_specs=[SMEM, VMEM, VMEM, VMEM, VMEM],
        out_specs=VMEM,
        scratch_shapes=[pltpu.VMEM((H * WIN, KEYS), f32)],
        compiler_params=pltpu.CompilerParams(vmem_limit_bytes=40 << 20),
        name="attend",
    )(starts, projected, prefix, table, idx)


def attend_back(starts, projected, prefix, grad, table, idx):
    length = projected.shape[0]
    return pl.pallas_call(
        backward_kernel,
        out_shape=(
            jax.ShapeDtypeStruct(projected.shape, bf16),
            jax.ShapeDtypeStruct(prefix.shape, bf16),
            jax.ShapeDtypeStruct((NB, 16), f32),
        ),
        in_specs=[SMEM, VMEM, VMEM, VMEM, VMEM, VMEM],
        out_specs=(VMEM, VMEM, VMEM),
        scratch_shapes=[pltpu.VMEM((H * WIN, KEYS), f32), pltpu.VMEM((H * WIN, KEYS), f32)],
        compiler_params=pltpu.CompilerParams(vmem_limit_bytes=48 << 20),
        name="attend_back",
    )(starts, projected, prefix, grad, table, idx)


def row_starts(segments):
    length = segments.shape[0]
    ids = jnp.arange(QPR + 1, dtype=jnp.int32)
    return jnp.sum((segments[None, :] < ids[:, None]).astype(jnp.int32), axis=1)


def near_buckets(buckets, length):
    back = buckets[length - QLEN : length][::-1]
    ahead = buckets[length : length + QLEN - 1][::-1]
    return jnp.concatenate([back, buckets[length - 1 : length], ahead])[None, :]


epsilon = 1e-06


class Place:
    def __init__(self):
        me = lax.axis_index("fsdp")
        self.me, self.c, self.x, self.y = me, me % 2, (me // 2) % 2, me // 4
        self.z = lax.axis_index("dp")

    def at(self, dy, dx, dc):
        return 4 * ((self.y + dy) % 2) + 2 * ((self.x + dx) % 2) + (self.c + dc) % 2


def greet(peers):
    barrier = pltpu.get_barrier_semaphore()
    for peer in peers:
        pl.semaphore_signal(barrier, inc=1, device_id=peer, device_id_type=MESH)
    pl.semaphore_wait(barrier, len(peers))


MESH = pl.DeviceIdType.MESH


class Gather:
    COPIES = 8

    def __init__(self, place, shard, full, send, recv, own_sem):
        self.p, self.shard, self.full = place, shard, full
        self.send, self.recv, self.own_sem = send, recv, own_sem
        self.rows = shard.shape[0]
        self.half = self.rows // 2

    def piece(self, dy, dx, dc, part=None):
        begin = self.p.at(dy, dx, dc) * self.rows
        size = self.rows
        if part is not None:
            begin, size = begin + part * self.half, self.half
        return self.full.at[pl.ds(pl.multiple_of(begin, 16), size), :]

    def copy(self, k, src, dst, dy, dx, dc):
        return pltpu.make_async_remote_copy(
            src_ref=src, dst_ref=dst, send_sem=self.send.at[k], recv_sem=self.recv.at[k],
            device_id={"fsdp": self.p.at(dy, dx, dc)}, device_id_type=MESH,
        )

    def own(self):
        return pltpu.make_async_copy(self.shard, self.piece(0, 0, 0), self.own_sem)

    def first(self):
        mine = self.piece(0, 0, 0)
        self.copy(0, self.shard, mine, 0, 1, 0).start()
        self.copy(1, self.shard, mine, 1, 0, 0).start()
        self.copy(2, self.shard, mine, 0, 0, 1).start()
        self.own().start()

    def await_piece(self, k, piece):
        self.copy(k, piece, piece, 0, 0, 1).wait_recv()

    def relay(self):
        from_x, from_y = self.piece(0, 1, 0), self.piece(1, 0, 0)
        self.await_piece(0, from_x)
        top = self.piece(0, 1, 0, 0)
        self.copy(3, top, top, 1, 0, 0).start()
        self.copy(4, from_x, from_x, 0, 0, 1).start()
        self.await_piece(1, from_y)
        low = self.piece(1, 0, 0, 1)
        self.copy(5, low, low, 0, 1, 0).start()
        self.copy(6, from_y, from_y, 0, 0, 1).start()

    def last(self):
        self.await_piece(3, self.piece(1, 1, 0, 0))
        self.await_piece(5, self.piece(1, 1, 0, 1))
        far = self.piece(1, 1, 0)
        self.copy(7, far, far, 0, 0, 1).start()

    def finish(self):
        self.own().wait()
        self.await_piece(2, self.piece(0, 0, 1))
        self.await_piece(4, self.piece(0, 1, 1))
        self.await_piece(6, self.piece(1, 0, 1))
        self.await_piece(7, self.piece(1, 1, 1))

    def drain(self):
        whole, part = self.piece(0, 0, 0), self.piece(0, 0, 0, 0)
        for k in range(self.COPIES):
            src = part if k in (3, 5) else whole
            self.copy(k, src, src, 0, 0, 1).wait_send()


def first_kernel(
    hidden_ref, small_ref, qkv_ref, prefix_ref,
    normed_ref, projected_ref, gains_ref, qkv_out, prefix_out,
    qkv_full, prefix_full, small_all, send, recv, small_send, small_recv, local_sem,
):
    place = Place()
    length, width = hidden_ref.shape
    others = [(dy, dx, dc) for dy in (0, 1) for dx in (0, 1) for dc in (0, 1)][1:]
    greet([{"fsdp": place.at(*o)} for o in others])
    one = Gather(place, qkv_ref, qkv_full, send.at[0], recv.at[0], local_sem.at[0])
    two = Gather(place, prefix_ref, prefix_full, send.at[1], recv.at[1], local_sem.at[1])
    row = lax.broadcasted_iota(jnp.int32, small_ref.shape, 0)
    small_all[0] = jnp.where(
        row < 2,
        pltpu.roll(small_ref[...], place.me * (width // 8), 1),
        pltpu.roll(small_ref[...], place.me * (NB * H // 8), 1),
    )

    def small_copy(k):
        return pltpu.make_async_remote_copy(
            src_ref=small_all.at[0], dst_ref=small_all.at[k + 1],
            send_sem=small_send.at[k], recv_sem=small_recv.at[k],
            device_id={"fsdp": place.at(*others[k])}, device_id_type=MESH,
        )

    for k in range(7):
        small_copy(k).start()
    one.first()
    two.first()
    for k in range(7):
        small_copy(k).wait_recv()
    gains_ref[...] = jnp.sum(small_all[...], axis=0)
    gain = gains_ref[0:1, :]

    tile = 256

    def norm(i, carry):
        rows = pl.ds(pl.multiple_of(i * tile, tile), tile)
        values = hidden_ref[rows, :].astype(f32)
        scale = lax.rsqrt(jnp.mean(values * values, axis=1, keepdims=True) + epsilon)
        normed_ref[rows, :] = (values * scale * gain).astype(bf16)
        return carry

    lax.fori_loop(0, length // tile, norm, 0)
    one.relay()
    two.relay()
    one.last()
    one.finish()
    keep_one = pltpu.make_async_copy(qkv_full, qkv_out, local_sem.at[0])
    keep_one.start()

    def project(i, carry):
        rows = pl.ds(pl.multiple_of(i * tile, tile), tile)
        block = normed_ref[rows, :]
        for at in range(0, 3 * width, width):
            projected_ref[rows, at : at + width] = mm(block, qkv_full[:, at : at + width]).astype(bf16)
        return carry

    lax.fori_loop(0, length // tile, project, 0)
    two.last()
    two.finish()
    keep_two = pltpu.make_async_copy(prefix_full, prefix_out, local_sem.at[1])
    keep_two.start()
    for k in range(7):
        small_copy(k).wait_send()
    one.drain()
    two.drain()
    keep_one.wait()
    keep_two.wait()


ANY = pl.BlockSpec(memory_space=pl.ANY)


def first_part(hidden, small, w_qkv, w_prefix):
    length, width = hidden.shape
    full_one = (8 * w_qkv.shape[0], w_qkv.shape[1])
    full_two = (8 * w_prefix.shape[0], w_prefix.shape[1])
    return pl.pallas_call(
        first_kernel,
        out_shape=(
            jax.ShapeDtypeStruct((length, width), bf16),
            jax.ShapeDtypeStruct((length, 3 * width), bf16),
            jax.ShapeDtypeStruct(small.shape, f32),
            jax.ShapeDtypeStruct(full_one, bf16),
            jax.ShapeDtypeStruct(full_two, bf16),
        ),
        in_specs=[VMEM, VMEM, ANY, ANY],
        out_specs=(VMEM, VMEM, VMEM, ANY, ANY),
        scratch_shapes=[
            pltpu.VMEM(full_one, bf16),
            pltpu.VMEM(full_two, bf16),
            pltpu.VMEM((8,) + small.shape, f32),
            pltpu.SemaphoreType.DMA((2, Gather.COPIES)),
            pltpu.SemaphoreType.DMA((2, Gather.COPIES)),
            pltpu.SemaphoreType.DMA((7,)),
            pltpu.SemaphoreType.DMA((7,)),
            pltpu.SemaphoreType.DMA((2,)),
        ],
        compiler_params=pltpu.CompilerParams(
            collective_id=0, has_side_effects=True, vmem_limit_bytes=48 << 20
        ),
        name="first_part",
    )(hidden, small, w_qkv, w_prefix)


def pack_small(attn_gain, ffn_gain, rel_table, width):
    lines = [jnp.pad(v.astype(f32), (0, width - v.shape[0])) for v in (attn_gain, ffn_gain, rel_table)]
    return jnp.concatenate([jnp.stack(lines), jnp.zeros((5, width), f32)])


def rms_scale(values, norm_gain):
    return (
        values * lax.rsqrt(jnp.mean(values * values, axis=-1, keepdims=True) + epsilon) * norm_gain
    )


def prefix_kernel(row_ref, memory_ref, w_ref, picked_ref, prefix_ref):
    width = w_ref.shape[0]
    for q in range(QPR):
        picked_ref[q] = memory_ref[row_ref[q]]
    picked = picked_ref[...].reshape(QPR * SLOT, width)
    for at in range(0, w_ref.shape[1], width):
        part = mm(picked, w_ref[:, at : at + width]).astype(bf16)
        prefix_ref[:, :, at : at + width] = part.reshape(QPR, SLOT, width)


def make_prefix(chosen, memory, w_prefix):
    padded = jnp.pad(memory, ((0, 0), (0, SLOT - PAIRS), (0, 0)))
    return pl.pallas_call(
        prefix_kernel,
        out_shape=(
            jax.ShapeDtypeStruct(padded.shape, bf16),
            jax.ShapeDtypeStruct((QPR, SLOT, w_prefix.shape[1]), bf16),
        ),
        in_specs=[SMEM, VMEM, VMEM],
        out_specs=(VMEM, VMEM),
        compiler_params=pltpu.CompilerParams(vmem_limit_bytes=40 << 20),
        name="make_prefix",
    )(chosen, padded, w_prefix)


def memory_kernel(row_ref, slot_ref, w_ref, out_ref, held):
    width = w_ref.shape[0]
    slots = slot_ref[...].reshape(QPR * SLOT, w_ref.shape[1])
    held[...] = mm(slots, w_ref[...], NT).reshape(QPR, SLOT, width)
    for q in range(QPR):
        out_ref[row_ref[q]] = held[q, :PAIRS, :]


def memory_back(chosen, slot_grad, w_prefix):
    width = w_prefix.shape[0]
    return pl.pallas_call(
        memory_kernel,
        out_shape=jax.ShapeDtypeStruct((QPR, PAIRS, width), f32),
        in_specs=[SMEM, VMEM, VMEM],
        out_specs=VMEM,
        scratch_shapes=[pltpu.VMEM((QPR, SLOT, width), f32)],
        compiler_params=pltpu.CompilerParams(vmem_limit_bytes=40 << 20),
        name="memory_back",
    )(chosen, slot_grad, w_prefix)


def row_pass(hidden, segments, memory, chosen, buckets, cotangent, full, made=None):
    attn_gain, ffn_gain, rel_table, w_qkv, w_attn_out, w_in, w_down, w_prefix = full
    length, width = hidden.shape
    starts = row_starts(segments)
    idx = near_buckets(buckets, length)
    table = jnp.pad(rel_table.reshape(NB, H).T, ((0, 16 - H), (0, 0)))
    tokens = hidden.astype(f32)
    gain_one = attn_gain.astype(f32)
    gain_two = ffn_gain.astype(f32)

    if made is None:
        normed = rms_scale(tokens, gain_one).astype(bf16)
        projected = mm(normed, w_qkv).astype(bf16)
    else:
        normed, projected = made
    picked, prefix = make_prefix(chosen, memory, w_prefix)
    attended = attend(starts, projected, prefix, table, idx)
    after_attn = tokens + mm(attended, w_attn_out)
    normed_ffn = rms_scale(after_attn, gain_two).astype(bf16)
    hidden_pre = mm(normed_ffn, w_in)
    activation = jax.nn.gelu(hidden_pre).astype(bf16)
    output = (after_attn + mm(activation, w_down)).astype(bf16)

    grad_out = cotangent.astype(f32)
    down_grad = mm(activation, cotangent, TN)
    act_grad = mm(cotangent, w_down, NT)
    pre_grad = jax.vjp(jax.nn.gelu, hidden_pre)[1](act_grad)[0].astype(bf16)
    in_grad = mm(normed_ffn, pre_grad, TN)
    normed_ffn_grad = mm(pre_grad, w_in, NT)
    residual_part, ffn_gain_grad = jax.vjp(rms_scale, after_attn, gain_two)[1](normed_ffn_grad)
    after_grad = grad_out + residual_part
    attn_branch = after_grad.astype(bf16)
    attn_out_grad = mm(attended, attn_branch, TN)
    attended_grad = mm(attn_branch, w_attn_out, NT).astype(bf16)
    token_grad, slot_grad, table_grad = attend_back(
        starts, projected, prefix, attended_grad, table, idx
    )
    qkv_grad = mm(normed, token_grad, TN)
    normed_grad = mm(token_grad, w_qkv, NT)
    flat = (QPR * SLOT, -1)
    prefix_grad = mm(picked.reshape(flat), slot_grad.reshape(flat), TN)
    memory_grad = memory_back(chosen, slot_grad, w_prefix)
    norm_part, attn_gain_grad = jax.vjp(rms_scale, tokens, gain_one)[1](normed_grad)
    hidden_grad = after_grad + norm_part
    small = jnp.concatenate([attn_gain_grad, ffn_gain_grad, table_grad[:, :H].reshape(NB * H)])
    return output, hidden_grad, memory_grad, small, (qkv_grad, attn_out_grad, in_grad, down_grad, prefix_grad)


def local(
    near, hidden, segment_ids, memory, memory_row, buckets, attn_gain, ffn_gain, rel_table,
    w_qkv, w_attn_out, w_in, w_down, w_prefix, cotangent,
):
    sizes = (attn_gain.shape[0], ffn_gain.shape[0], rel_table.shape[0])
    made = None
    if near:
        rest = [lax.all_gather(w, "fsdp", axis=0, tiled=True) for w in (w_attn_out, w_in, w_down)]
        normed, projected, gains, full_qkv, full_prefix = first_part(
            hidden[0], pack_small(attn_gain, ffn_gain, rel_table, hidden.shape[2]), w_qkv, w_prefix
        )
        made = (normed, projected)
        full = (gains[0].astype(bf16), gains[1].astype(bf16), gains[2, : NB * H].astype(bf16), full_qkv, *rest, full_prefix)
    else:
        small = lax.all_gather(jnp.concatenate([attn_gain, ffn_gain, rel_table]), "fsdp", axis=0)
        cuts = (0, sizes[0], sizes[0] + sizes[1], sum(sizes))
        full = tuple(small[:, cuts[i] : cuts[i + 1]].reshape(-1) for i in range(3)) + tuple(
            lax.all_gather(w, "fsdp", axis=0, tiled=True)
            for w in (w_qkv, w_attn_out, w_in, w_down, w_prefix)
        )
    outs = []
    total = None
    for r in range(hidden.shape[0]):
        *own, small_grad, grads = row_pass(
            hidden[r], segment_ids[r], memory[r], memory_row[r], buckets, cotangent[r], full, made
        )
        outs.append(own)
        fresh = (small_grad,) + grads
        total = fresh if total is None else jax.tree.map(jnp.add, total, fresh)
    output, hidden_grad, memory_grad = (jnp.stack(x) for x in zip(*outs))
    small_grad = lax.psum(total[0], ("fsdp", "dp"))
    me = lax.axis_index("fsdp")
    bases = (0, full[0].shape[0], full[0].shape[0] + full[1].shape[0])
    shares = [
        lax.dynamic_slice_in_dim(small_grad, base + me * size, size) for base, size in zip(bases, sizes)
    ]
    for gradient in total[1:]:
        share = lax.psum_scatter(
            gradient.astype(bf16), "fsdp", scatter_dimension=0, tiled=True
        )
        shares.append(lax.psum(share, "dp").astype(f32))
    return (output, hidden_grad, memory_grad) + tuple(shares)


def solution(mesh):
    rows = ("fsdp", "dp")
    placed = (
        P(rows, None, None), P(rows, None), P(rows, None, None, None), P(rows, None), P(),
        P("fsdp"), P("fsdp"), P("fsdp"),
        P("fsdp", None), P("fsdp", None), P("fsdp", None), P("fsdp", None), P("fsdp", None),
        P(rows, None, None),
    )
    near = mesh.shape["fsdp"] == 8 and mesh.shape["dp"] == 4
    return jax.shard_map(
        functools.partial(local, near),
        mesh=mesh,
        in_specs=placed,
        out_specs=(
            P(rows, None, None), P(rows, None, None), P(rows, None, None, None),
            P("fsdp"), P("fsdp"), P("fsdp"),
            P("fsdp", None), P("fsdp", None), P("fsdp", None), P("fsdp", None), P("fsdp", None),
        ),
        check_vma=False,
    )
```

```python
import functools
import jax
import jax.numpy as jnp
from jax import lax
from jax.experimental import pallas as pl
from jax.experimental.pallas import tpu as pltpu
from jax.sharding import PartitionSpec as P

H = 12
DH = 64
NB = 32
QLEN = 64
QPR = 20
D_MODEL = 768
PAIRS = 10

WIN = 80
SLOT = 16
KEYS = 128
GROUP = 4
GW = GROUP * DH
masked_out = -1e30
f32 = jnp.float32
bf16 = jnp.bfloat16
NT = (((1,), (1,)), ((), ()))
TN = (((0,), (0,)), ((), ()))


def mm(a, b, dims=(((1,), (0,)), ((), ()))):
    return lax.dot_general(a, b, dims, preferred_element_type=f32)


def bucket_hot(idx_ref):
    return (lax.broadcasted_iota(jnp.int32, (NB, KEYS), 0) == idx_ref[...]).astype(f32)


def fill_bias(table_ref, idx_ref, bias):
    hot = bucket_hot(idx_ref).astype(bf16)
    lines = mm(table_ref[...], hot)
    lane = lax.broadcasted_iota(jnp.int32, (WIN, KEYS), 1)
    for h in range(H):
        wide = jnp.broadcast_to(lines[h : h + 1, :], (WIN, KEYS))
        rolled = pltpu.roll(wide, 0, 1, stride=1, stride_axis=0)
        bias[h * WIN : (h + 1) * WIN, :] = jnp.where(lane < WIN, rolled, 0.0)


def stack_heads(block):
    lane = lax.broadcasted_iota(jnp.int32, (1, GW), 1)
    parts = []
    for h in range(GROUP):
        mask = jnp.where((lane >= h * DH) & (lane < (h + 1) * DH), 1.0, 0.0).astype(bf16)
        parts.append(block * mask)
    return jnp.concatenate(parts, axis=0)


def merge_heads(stacked):
    lane = lax.broadcasted_iota(jnp.int32, (WIN, GW), 1)
    out = stacked[:WIN]
    for h in range(1, GROUP):
        out = jnp.where(lane >= h * DH, stacked[h * WIN : (h + 1) * WIN], out)
    return out


def key_tile(tokens, low, high):
    rest = jnp.zeros((KEYS - WIN - 2 * SLOT, tokens.shape[1]), tokens.dtype)
    return jnp.concatenate([tokens, low, high, rest], axis=0)


def key_cost(begin, end):
    lane = lax.broadcasted_iota(jnp.int32, (1, KEYS), 1)
    token = (lane >= begin) & (lane < end)
    first = (lane >= WIN) & (lane < WIN + PAIRS)
    second = (lane >= WIN + SLOT) & (lane < WIN + SLOT + PAIRS)
    return jnp.where(token | first | second, 0.0, masked_out).astype(f32)


def soft_rows(stack, keys, bias_block, cost):
    logits = mm(stack, keys, NT) + (bias_block + cost)
    peak = jnp.max(logits, axis=1, keepdims=True)
    raw = jnp.exp(logits - peak)
    return raw * (1.0 / jnp.sum(raw, axis=1, keepdims=True))


def window(start_ref, q):
    start = start_ref[q]
    base = pl.multiple_of((start // 16) * 16, 16)
    base = jnp.minimum(base, start_ref[QPR] - WIN)
    base = pl.multiple_of(base, 16)
    return base, start - base, start_ref[q + 1] - base


def forward_kernel(start_ref, proj_ref, prefix_ref, table_ref, idx_ref, out_ref, bias):
    width = out_ref.shape[1]
    fill_bias(table_ref, idx_ref, bias)

    def body(q, carry):
        base, begin, end = window(start_ref, q)
        cost = key_cost(begin, end)
        row = lax.broadcasted_iota(jnp.int32, (WIN, GW), 0)
        mine = (row >= begin) & (row < end)
        rows = pl.ds(base, WIN)
        for g in range(width // GW):
            at = g * GW
            stack = stack_heads(proj_ref[rows, at : at + GW] * bf16(DH**-0.5))
            keys = key_tile(
                proj_ref[rows, width + at : width + at + GW],
                prefix_ref[q, :, at : at + GW],
                prefix_ref[q, :, width + at : width + at + GW],
            )
            values = key_tile(
                proj_ref[rows, 2 * width + at : 2 * width + at + GW],
                prefix_ref[q, :, 2 * width + at : 2 * width + at + GW],
                prefix_ref[q, :, 3 * width + at : 3 * width + at + GW],
            )
            soft = soft_rows(stack, keys, bias[g * GROUP * WIN : (g + 1) * GROUP * WIN, :], cost)
            blended = merge_heads(mm(soft.astype(bf16), values)).astype(bf16)
            out_ref[rows, at : at + GW] = jnp.where(mine, blended, out_ref[rows, at : at + GW])
        return carry

    lax.fori_loop(0, QPR, body, 0)


def backward_kernel(
    start_ref, proj_ref, prefix_ref, grad_ref, table_ref, idx_ref,
    token_ref, slot_ref, table_grad_ref, bias, bias_grad,
):
    width = grad_ref.shape[1]
    fill_bias(table_ref, idx_ref, bias)
    bias_grad[...] = jnp.zeros_like(bias_grad)

    def body(q, carry):
        base, begin, end = window(start_ref, q)
        cost = key_cost(begin, end)
        row = lax.broadcasted_iota(jnp.int32, (WIN, GW), 0)
        mine = (row >= begin) & (row < end)
        rows = pl.ds(base, WIN)
        for g in range(width // GW):
            at = g * GW
            heads = slice(g * GROUP * WIN, (g + 1) * GROUP * WIN)
            stack = stack_heads(proj_ref[rows, at : at + GW] * bf16(DH**-0.5))
            keys = key_tile(
                proj_ref[rows, width + at : width + at + GW],
                prefix_ref[q, :, at : at + GW],
                prefix_ref[q, :, width + at : width + at + GW],
            )
            values = key_tile(
                proj_ref[rows, 2 * width + at : 2 * width + at + GW],
                prefix_ref[q, :, 2 * width + at : 2 * width + at + GW],
                prefix_ref[q, :, 3 * width + at : 3 * width + at + GW],
            )
            grad = grad_ref[rows, at : at + GW]
            grads = stack_heads(jnp.where(mine, grad, jnp.zeros_like(grad)))
            soft = soft_rows(stack, keys, bias[heads, :], cost)
            prob_grad = mm(grads, values, NT)
            weighted = soft * prob_grad
            logit_grad = weighted - soft * jnp.sum(weighted, axis=1, keepdims=True)
            low = logit_grad.astype(bf16)
            bias_grad[heads, :] += low.astype(f32)
            query_grad = (merge_heads(mm(low, keys)) * DH**-0.5).astype(bf16)
            key_grad = mm(low, stack, TN).astype(bf16)
            value_grad = mm(soft.astype(bf16), grads, TN).astype(bf16)
            for part, fresh in ((0, query_grad), (1, key_grad[:WIN]), (2, value_grad[:WIN])):
                cols = slice(part * width + at, part * width + at + GW)
                token_ref[rows, cols] = jnp.where(mine, fresh, token_ref[rows, cols])
            for part, fresh in ((0, key_grad), (2, value_grad)):
                for s in range(2):
                    cols = slice((part + s) * width + at, (part + s) * width + at + GW)
                    slot_ref[q, :, cols] = fresh[WIN + s * SLOT : WIN + (s + 1) * SLOT]
        return carry

    lax.fori_loop(0, QPR, body, 0)
    lane = lax.broadcasted_iota(jnp.int32, (H, KEYS), 1)
    sums = jnp.zeros((H, KEYS), f32)
    for i in range(WIN):
        line = jnp.where(lane < WIN, bias_grad[pl.ds(i, H, stride=WIN), :], 0.0)
        sums += line if i == 0 else pltpu.roll(line, KEYS - i, 1)
    sums = jnp.concatenate([sums, jnp.zeros((16 - H, KEYS), f32)], axis=0)
    table_grad_ref[...] = lax.dot_general(
        bucket_hot(idx_ref), sums, NT, precision=lax.Precision.HIGHEST, preferred_element_type=f32
    )


SMEM = pl.BlockSpec(memory_space=pltpu.SMEM)
VMEM = pl.BlockSpec(memory_space=pltpu.VMEM)


def attend(starts, projected, prefix, table, idx):
    length = projected.shape[0]
    width = projected.shape[1] // 3
    return pl.pallas_call(
        forward_kernel,
        out_shape=jax.ShapeDtypeStruct((length, width), bf16),
        in_specs=[SMEM, VMEM, VMEM, VMEM, VMEM],
        out_specs=VMEM,
        scratch_shapes=[pltpu.VMEM((H * WIN, KEYS), f32)],
        compiler_params=pltpu.CompilerParams(vmem_limit_bytes=40 << 20),
        name="attend",
    )(starts, projected, prefix, table, idx)


def attend_back(starts, projected, prefix, grad, table, idx):
    length = projected.shape[0]
    return pl.pallas_call(
        backward_kernel,
        out_shape=(
            jax.ShapeDtypeStruct(projected.shape, bf16),
            jax.ShapeDtypeStruct(prefix.shape, bf16),
            jax.ShapeDtypeStruct((NB, 16), f32),
        ),
        in_specs=[SMEM, VMEM, VMEM, VMEM, VMEM, VMEM],
        out_specs=(VMEM, VMEM, VMEM),
        scratch_shapes=[pltpu.VMEM((H * WIN, KEYS), f32), pltpu.VMEM((H * WIN, KEYS), f32)],
        compiler_params=pltpu.CompilerParams(vmem_limit_bytes=48 << 20),
        name="attend_back",
    )(starts, projected, prefix, grad, table, idx)


def row_starts(segments):
    length = segments.shape[0]
    ids = jnp.arange(QPR + 1, dtype=jnp.int32)
    return jnp.sum((segments[None, :] < ids[:, None]).astype(jnp.int32), axis=1)


def near_buckets(buckets, length):
    back = buckets[length - QLEN : length][::-1]
    ahead = buckets[length : length + QLEN - 1][::-1]
    return jnp.concatenate([back, buckets[length - 1 : length], ahead])[None, :]


epsilon = 1e-06


MESH = pl.DeviceIdType.MESH
ANY = pl.BlockSpec(memory_space=pl.ANY)


class Place:
    def __init__(self):
        me = lax.axis_index("fsdp")
        self.me, self.c, self.x, self.y = me, me % 2, (me // 2) % 2, me // 4
        self.z = lax.axis_index("dp")

    def at(self, dy, dx, dc):
        return 4 * ((self.y + dy) % 2) + 2 * ((self.x + dx) % 2) + (self.c + dc) % 2


OTHERS = [(dy, dx, dc) for dy in (0, 1) for dx in (0, 1) for dc in (0, 1)][1:]


def greet(peers):
    barrier = pltpu.get_barrier_semaphore()
    for peer in peers:
        pl.semaphore_signal(barrier, inc=1, device_id=peer, device_id_type=MESH)
    pl.semaphore_wait(barrier, len(peers))


class Gather:
    COPIES = 8

    def __init__(self, place, shard, full, down, k, send, recv, own_sem):
        self.p, self.shard, self.full, self.down = place, shard, full, down
        self.send, self.recv, self.own_sem = send.at[k], recv.at[k], own_sem.at[k]
        self.rows = shard.shape[0]
        self.half = self.rows // 2

    def piece(self, dy, dx, dc, part=None):
        f = self.p.at(dy, dx, dc)
        begin = (f % 2) * self.rows if self.down else f * self.rows
        size = self.rows
        if part is not None:
            begin, size = begin + part * self.half, self.half
        rows = pl.ds(pl.multiple_of(begin, 16), size)
        return self.full.at[f // 2, rows, :] if self.down else self.full.at[:, rows, :]

    def copy(self, k, src, dst, dy, dx, dc):
        return pltpu.make_async_remote_copy(
            src_ref=src, dst_ref=dst, send_sem=self.send.at[k], recv_sem=self.recv.at[k],
            device_id={"fsdp": self.p.at(dy, dx, dc)}, device_id_type=MESH,
        )

    def own(self):
        if self.down:
            return [pltpu.make_async_copy(self.shard, self.piece(0, 0, 0), self.own_sem.at[0])]
        rows = pl.ds(pl.multiple_of(self.p.me * self.rows, 16), self.rows)
        width = self.full.shape[2]
        return [
            pltpu.make_async_copy(
                self.shard.at[:, s * width : (s + 1) * width], self.full.at[s, rows, :], self.own_sem.at[s]
            )
            for s in range(self.full.shape[0])
        ]

    def load(self):
        for copy in self.own():
            copy.start()

    def first(self):
        for copy in self.own():
            copy.wait()
        mine = self.piece(0, 0, 0)
        self.copy(0, mine, mine, 0, 1, 0).start()
        self.copy(1, mine, mine, 1, 0, 0).start()
        self.copy(2, mine, mine, 0, 0, 1).start()

    def landed(self, k, piece):
        self.copy(k, piece, piece, 0, 0, 1).wait_recv()

    def relay(self):
        from_x, from_y = self.piece(0, 1, 0), self.piece(1, 0, 0)
        self.landed(0, from_x)
        top = self.piece(0, 1, 0, 0)
        self.copy(3, top, top, 1, 0, 0).start()
        self.copy(4, from_x, from_x, 0, 0, 1).start()
        self.landed(1, from_y)
        low = self.piece(1, 0, 0, 1)
        self.copy(5, low, low, 0, 1, 0).start()
        self.copy(6, from_y, from_y, 0, 0, 1).start()

    def last(self):
        self.landed(3, self.piece(1, 1, 0, 0))
        self.landed(5, self.piece(1, 1, 0, 1))
        far = self.piece(1, 1, 0)
        self.copy(7, far, far, 0, 0, 1).start()

    def finish(self):
        self.landed(2, self.piece(0, 0, 1))
        self.landed(4, self.piece(0, 1, 1))
        self.landed(6, self.piece(1, 0, 1))
        self.landed(7, self.piece(1, 1, 1))

    def drain(self):
        whole, part = self.piece(0, 0, 0), self.piece(0, 0, 0, 0)
        for k in range(self.COPIES):
            src = part if k in (3, 5) else whole
            self.copy(k, src, src, 0, 0, 1).wait_send()


class Scatter:
    COPIES = 7

    def __init__(self, place, side, bufs, u, send, recv):
        self.p, self.side = place, side
        self.rc, self.rd, self.re, self.rx, self.ry = (b.at[u] for b in bufs)
        self.send, self.recv = send.at[u], recv.at[u]
        self.half = self.rd.shape[0]

    def mine(self, dy, dx):
        return self.side(self.p.c).at[2 * ((self.p.y + dy) % 2) + (self.p.x + dx) % 2]

    def copy(self, k, src, dst, dy, dx, dc):
        return pltpu.make_async_remote_copy(
            src_ref=src, dst_ref=dst, send_sem=self.send.at[k], recv_sem=self.recv.at[k],
            device_id={"fsdp": self.p.at(dy, dx, dc)}, device_id_type=MESH,
        )

    def part(self, k):
        low, high = pl.ds(0, self.half), pl.ds(self.half, self.half)
        if k == 0:
            return self.copy(0, self.side(1 - self.p.c), self.rc, 0, 0, 1)
        if k == 1:
            return self.copy(1, self.mine(1, 1).at[low], self.rd, 0, 1, 0)
        if k == 2:
            return self.copy(2, self.mine(1, 1).at[high], self.re, 1, 0, 0)
        if k == 3:
            return self.copy(3, self.mine(0, 1).at[low], self.rx.at[low], 0, 1, 0)
        if k == 4:
            return self.copy(4, self.mine(1, 0).at[high], self.ry.at[high], 1, 0, 0)
        if k == 5:
            return self.copy(5, self.mine(0, 1).at[high], self.rx.at[high], 0, 1, 0)
        return self.copy(6, self.mine(1, 0).at[low], self.ry.at[low], 1, 0, 0)

    def core(self):
        self.part(0).start()

    def fold(self):
        self.part(0).wait_recv()
        own = self.side(self.p.c)
        own[...] = (own[...].astype(f32) + self.rc[...].astype(f32)).astype(bf16)
        for k in (1, 2, 3, 4):
            self.part(k).start()

    def relay(self):
        low, high = pl.ds(0, self.half), pl.ds(self.half, self.half)
        nx, ny = self.mine(0, 1).at[high], self.mine(1, 0).at[low]
        self.part(1).wait_recv()
        ny[...] = (ny[...].astype(f32) + self.rd[...].astype(f32)).astype(bf16)
        self.part(6).start()
        self.part(2).wait_recv()
        nx[...] = (nx[...].astype(f32) + self.re[...].astype(f32)).astype(bf16)
        self.part(5).start()

    def total(self):
        for k in (3, 4, 5, 6):
            self.part(k).wait_recv()
        return self.mine(0, 0)[...].astype(f32) + (self.rx[...].astype(f32) + self.ry[...].astype(f32))

    def drain(self):
        for k in range(self.COPIES):
            self.part(k).wait_send()


def loop(n, body, unroll=1):
    def step(i, carry):
        body(i)
        return carry

    lax.fori_loop(0, n, step, 0, unroll=unroll)


GELU_A = 0.7978845608028654
GELU_B = 0.044715


def gelu_pair(v):
    square = v * v
    t = jnp.tanh(v * (GELU_A + (GELU_A * GELU_B) * square))
    half = 0.5 + 0.5 * t
    slope = half + (0.5 * v) * (1.0 - t * t) * (GELU_A + (3.0 * GELU_A * GELU_B) * square)
    return v * half, slope


TILE = 256
BLOCK = 16
OVERLAP = 6


def rows_of(i):
    return pl.ds(pl.multiple_of(i * TILE, TILE), TILE)


def table_bias(gains, idx_ref, select_ref, bias):
    wide = jnp.where(select_ref[...] > 0, jnp.broadcast_to(gains[2:3, : NB * H], (16, NB * H)), 0.0)
    lines = mm(wide.astype(bf16), entry_hot(idx_ref))
    lane = lax.broadcasted_iota(jnp.int32, (WIN, KEYS), 1)
    for h in range(H):
        rolled = pltpu.roll(jnp.broadcast_to(lines[h : h + 1, :], (WIN, KEYS)), 0, 1, stride=1, stride_axis=0)
        bias[h * WIN : (h + 1) * WIN, :] = jnp.where(lane < WIN, rolled, 0.0)


def entry_hot(idx_ref):
    off = lax.broadcasted_iota(jnp.int32, (NB * H, KEYS), 0) - H * idx_ref[...]
    return jnp.where((off >= 0) & (off < H), 1.0, 0.0).astype(bf16)


def question(window_ref, q):
    return window_ref[3 * q] * BLOCK, window_ref[3 * q + 1], window_ref[3 * q + 2]


def attend_one(q, window_ref, proj, prefix, bias, pad):
    base, begin, end = question(window_ref, q)
    cost = key_cost(begin, end)
    rows = pl.ds(base, WIN)
    width = proj.shape[2]
    for g in range(width // GW):
        cols = slice(g * GW, (g + 1) * GW)
        stack = stack_heads(proj[0, rows, cols] * bf16(DH**-0.5))
        keys = key_tile(proj[1, rows, cols], prefix[0, q, :, cols], prefix[1, q, :, cols])
        values = key_tile(proj[2, rows, cols], prefix[2, q, :, cols], prefix[3, q, :, cols])
        soft = soft_rows(stack, keys, bias[g * GROUP * WIN : (g + 1) * GROUP * WIN, :], cost)
        pad[q, :, cols] = merge_heads(mm(soft.astype(bf16), values)).astype(bf16)


def unpad(b, piece_ref, pads, outs):
    row = lax.broadcasted_iota(jnp.int32, (BLOCK, 1), 0)
    sums = [jnp.zeros((BLOCK, pad.shape[-1]), bf16) for pad in pads]
    for k in range(OVERLAP):
        at = 4 * (OVERLAP * b + k)
        q, off = piece_ref[at], piece_ref[at + 1] * BLOCK
        mine = (row >= piece_ref[at + 2]) & (row < piece_ref[at + 3])
        for s, pad in enumerate(pads):
            sums[s] = jnp.where(mine, pad[q, pl.ds(off, BLOCK), :], sums[s])
    for total, out in zip(sums, outs):
        out[pl.ds(pl.multiple_of(b * BLOCK, BLOCK), BLOCK), :] = total


def layout_tables(segments):
    length = segments.shape[0]
    starts = row_starts(segments)
    low, high = starts[:-1], starts[1:]
    base = jnp.minimum(low // BLOCK, (length - WIN) // BLOCK)
    windows = jnp.stack([base, low - BLOCK * base, high - BLOCK * base], axis=1).reshape(-1)
    at = jnp.arange(length // BLOCK, dtype=jnp.int32)[:, None] * BLOCK
    ids = jnp.arange(QPR, dtype=jnp.int32)
    q = jnp.sum((high[None, :] <= at).astype(jnp.int32), axis=1, keepdims=True)
    q = jnp.minimum(q + jnp.arange(OVERLAP, dtype=jnp.int32)[None, :], QPR - 1)
    hot = (q[:, :, None] == ids).astype(jnp.int32)
    pick = lambda v: jnp.sum(hot * v, axis=2)
    begin, end = jnp.clip(pick(low) - at, 0, BLOCK), jnp.clip(pick(high) - at, 0, BLOCK)
    off = jnp.clip(at // BLOCK - pick(base), 0, (WIN - BLOCK) // BLOCK)
    return windows, jnp.stack([q, off, begin, end], axis=2).reshape(-1)


def forward_part_kernel(
    window_ref, piece_ref, chosen_ref, memory_ref, small_ref, idx_ref, select_ref,
    hidden_hbm, cot_hbm, qkv_w, prefix_w, out_w, in_w, down_w,
    output_hbm, normed_hbm, proj_hbm, prefix_hbm, picked_hbm, gains_ref, gain_grad_ref,
    attended_grad_hbm, after_grad_hbm, qkv_hbm, prefix_w_hbm, in_grad_hbm, out_grad_hbm, sums_ref,
    w_qkv, w_prefix, w_out, w_in, w_down, hidden, cot, normed, act, slope, prefix, picked, pad, attended,
    after, down_grads, attended_grad, bias, small_all,
    rc, rd, re, rx, ry, send, recv, g_send, g_recv, own_sem, small_send, small_recv, io_sem,
):
    place = Place()
    length, width = hidden.shape
    steps = length // TILE
    chunks = w_in.shape[0]
    proj = slope
    weights = ((qkv_w, w_qkv), (prefix_w, w_prefix), (out_w, w_out), (in_w, w_in), (down_w, w_down))
    g_qkv, g_prefix, g_out, g_in, g_down = (
        Gather(place, shard, full, k == 4, k, g_send, g_recv, own_sem) for k, (shard, full) in enumerate(weights)
    )

    def io(k, src, dst):
        return pltpu.make_async_copy(src, dst, io_sem.at[k])

    load_hidden, load_cot = io(0, hidden_hbm, hidden), io(1, cot_hbm, cot)
    for g in (g_qkv, g_prefix, g_out, g_in, g_down):
        g.load()
    load_hidden.start()
    load_cot.start()
    row = lax.broadcasted_iota(jnp.int32, small_ref.shape, 0)
    small_all[0] = jnp.where(
        row < 2,
        pltpu.roll(small_ref[...], place.me * (width // 8), 1),
        pltpu.roll(small_ref[...], place.me * (NB * H // 8), 1),
    )
    greet([{"fsdp": place.at(*o)} for o in OTHERS])

    def small_copy(k):
        return pltpu.make_async_remote_copy(
            src_ref=small_all.at[0], dst_ref=small_all.at[k + 1],
            send_sem=small_send.at[k], recv_sem=small_recv.at[k],
            device_id={"fsdp": place.at(*OTHERS[k])}, device_id_type=MESH,
        )

    for k in range(7):
        small_copy(k).start()
    g_qkv.first()
    g_prefix.first()
    load_hidden.wait()
    for q in range(QPR):
        picked[q] = memory_ref[chosen_ref[q]]
    keep_picked = io(2, picked, picked_hbm)
    keep_picked.start()
    for k in range(7):
        small_copy(k).wait_recv()
    gains_ref[...] = jnp.sum(small_all[...], axis=0)
    gain_one, gain_two = gains_ref[0:1, :], gains_ref[1:2, :]

    def norm(i):
        rows = rows_of(i)
        values = hidden[rows, :].astype(f32)
        scale = lax.rsqrt(jnp.mean(values * values, axis=1, keepdims=True) + epsilon)
        normed[rows, :] = (values * scale * gain_one).astype(bf16)

    loop(steps, norm)
    keep_normed = io(3, normed, normed_hbm)
    keep_normed.start()
    table_bias(gains_ref, idx_ref, select_ref, bias)
    g_qkv.relay()
    g_out.first()
    g_in.first()
    g_prefix.relay()
    g_down.first()
    g_qkv.last()
    g_qkv.finish()
    keep_qkv = io(4, w_qkv, qkv_hbm)
    keep_qkv.start()

    def project(step):
        s, rows = step // steps, rows_of(step % steps)
        proj[s, rows, :] = mm(normed[rows, :], w_qkv[s]).astype(bf16)

    loop(3 * steps, project)
    keep_proj = io(5, proj.at[0:3], proj_hbm)
    keep_proj.start()
    g_prefix.last()
    g_prefix.finish()
    keep_prefix_w = io(6, w_prefix, prefix_w_hbm)
    keep_prefix_w.start()

    def make_prefix_slot(s):
        part = mm(picked[...].reshape(QPR * SLOT, width), w_prefix[s])
        prefix[s] = part.astype(bf16).reshape(QPR, SLOT, width)

    loop(4, make_prefix_slot)
    keep_prefix = io(7, prefix, prefix_hbm)
    keep_prefix.start()
    g_out.relay()
    g_in.relay()

    def attend_step(q):
        attend_one(q, window_ref, proj, prefix, bias, pad)

    loop(QPR // 2, attend_step)
    g_out.last()
    g_in.last()
    g_down.relay()
    loop(QPR // 2, lambda q: attend_step(q + QPR // 2))
    loop(length // BLOCK, lambda b: unpad(b, piece_ref, (pad,), (attended,)))
    g_out.finish()
    keep_normed.wait()

    def attn_out(i):
        rows = rows_of(i)
        values = hidden[rows, :].astype(f32) + mm(attended[rows, :], w_out[0])
        after[rows, :] = values
        scale = lax.rsqrt(jnp.mean(values * values, axis=1, keepdims=True) + epsilon)
        normed[rows, :] = (values * scale * gain_two).astype(bf16)

    loop(steps, attn_out)
    g_in.finish()
    g_down.last()
    keep_proj.wait()

    def hidden_chunk(step):
        j, rows = step // steps, rows_of(step % steps)
        act_part, slope_part = gelu_pair(mm(normed[rows, :], w_in[j]))
        act[j, rows, :] = act_part.astype(bf16)
        slope[j, rows, :] = slope_part.astype(bf16)

    loop(chunks * steps, hidden_chunk)
    load_cot.wait()

    def down_chunk(step):
        j, c = step // 2, step % 2
        cols = pl.ds(pl.multiple_of(c * (width // 2), 128), width // 2)
        part = mm(act[j, :, cols], cot[...], TN)
        down_grads[j, c] = part.astype(bf16).reshape(4, width // 8, width)

    loop(chunks * 2, down_chunk)
    bufs = (rc, rd, re, rx, ry)
    units = [Scatter(place, lambda c, u=u: down_grads.at[:, c, u], bufs, u, send, recv) for u in range(4)]
    for u in units:
        u.core()
    g_down.finish()

    def slope_chunk(step):
        j, rows = step // steps, rows_of(step % steps)
        act_grad = mm(cot[rows, :], w_down[j], NT)
        slope[j, rows, :] = (act_grad * slope[j, rows, :].astype(f32)).astype(bf16)

    loop(chunks * steps, slope_chunk)
    for u in units:
        u.fold()
    keep_prefix_w.wait()
    keep_qkv.wait()
    g_qkv.drain()
    g_prefix.drain()
    in_grad, out_grad = w_prefix, w_qkv

    def in_chunk(step):
        j, c = step // 2, step % 2
        cols = pl.ds(pl.multiple_of(c * (width // 2), 128), width // 2)
        in_grad[j, cols, :] = mm(normed[:, cols], slope[j], TN).astype(bf16)

    loop(chunks * 2, in_chunk)
    keep_in = io(8, in_grad, in_grad_hbm)
    keep_in.start()
    for u in units:
        u.relay()

    def out_rows(i):
        rows = rows_of(i)
        total = after[rows, :]
        for j in range(chunks):
            total += mm(act[j, rows, :], w_down[j])
        hidden[rows, :] = total.astype(bf16)

    loop(steps, out_rows)
    keep_output = io(9, hidden, output_hbm)
    keep_output.start()
    gain_grad_ref[...] = jnp.zeros_like(gain_grad_ref)

    def back_rows(i):
        rows = rows_of(i)
        grad = mm(slope[0, rows, :], w_in[0], NT)
        for j in range(1, chunks):
            grad += mm(slope[j, rows, :], w_in[j], NT)
        values = after[rows, :]
        scale = lax.rsqrt(jnp.mean(values * values, axis=1, keepdims=True) + epsilon)
        unit = values * scale
        gain_grad_ref[0:1, :] += jnp.sum(grad * unit, axis=0, keepdims=True)
        pulled = grad * gain_two
        mixed = pulled - unit * jnp.mean(pulled * unit, axis=1, keepdims=True)
        result = cot[rows, :].astype(f32) + scale * mixed
        after[rows, :] = result
        low = result.astype(bf16)
        normed[rows, :] = low
        attended_grad[rows, :] = mm(low, w_out[0], NT).astype(bf16)

    loop(steps, back_rows)
    keep_after = io(10, after, after_grad_hbm)
    keep_after.start()
    keep_attended = io(11, attended_grad, attended_grad_hbm)
    keep_attended.start()
    for c in range(2):
        cols = slice(c * (width // 2), (c + 1) * (width // 2))
        out_grad[0, cols, :] = mm(attended[:, cols], normed[...], TN).astype(bf16)
    keep_out = io(12, out_grad.at[0], out_grad_hbm)
    keep_out.start()
    for k, u in enumerate(units):
        sums_ref[k] = u.total().astype(bf16)
    for k in range(7):
        small_copy(k).wait_send()
    for g in (g_out, g_in, g_down):
        g.drain()
    for u in units:
        u.drain()
    for copy in (
        keep_picked, keep_prefix, keep_in, keep_output, keep_after, keep_attended, keep_out
    ):
        copy.wait()


def forward_part(windows, pieces, chosen, memory, small, idx, select, hidden, cot, w_qkv, w_prefix, w_out, w_in, w_down):
    length, width = hidden.shape
    chunks = w_in.shape[1] // width
    eighth = width // 8
    units = w_down.shape[0] // eighth
    sds = jax.ShapeDtypeStruct
    return pl.pallas_call(
        forward_part_kernel,
        out_shape=(
            sds((length, width), bf16),
            sds((length, width), bf16),
            sds((3, length, width), bf16),
            sds((4, QPR, SLOT, width), bf16),
            sds((QPR, SLOT, width), bf16),
            sds(small.shape, f32),
            sds((8, width), f32),
            sds((length, width), bf16),
            sds((length, width), f32),
            sds((3, width, width), bf16),
            sds((4, width, width), bf16),
            sds((chunks, width, width), bf16),
            sds((width, width), bf16),
            sds((units, eighth, width), bf16),
        ),
        in_specs=[SMEM] * 3 + [VMEM] * 4 + [ANY] * 7,
        out_specs=(ANY,) * 5 + (VMEM,) * 2 + (ANY,) * 6 + (VMEM,),
        scratch_shapes=[
            pltpu.VMEM((3, width, width), bf16),
            pltpu.VMEM((4, width, width), bf16),
            pltpu.VMEM((1, width, width), bf16),
            pltpu.VMEM((chunks, width, width), bf16),
            pltpu.VMEM((chunks, width, width), bf16),
            pltpu.VMEM((length, width), bf16),
            pltpu.VMEM((length, width), bf16),
            pltpu.VMEM((length, width), bf16),
            pltpu.VMEM((chunks, length, width), bf16),
            pltpu.VMEM((chunks, length, width), bf16),
            pltpu.VMEM((4, QPR, SLOT, width), bf16),
            pltpu.VMEM((QPR, SLOT, width), bf16),
            pltpu.VMEM((QPR, WIN, width), bf16),
            pltpu.VMEM((length, width), bf16),
            pltpu.VMEM((length, width), f32),
            pltpu.VMEM((4, 2, units, eighth, width), bf16),
            pltpu.VMEM((length, width), bf16),
            pltpu.VMEM((H * WIN, KEYS), f32),
            pltpu.VMEM((8,) + small.shape, f32),
            pltpu.VMEM((units, 4, eighth, width), bf16),
            pltpu.VMEM((units, eighth // 2, width), bf16),
            pltpu.VMEM((units, eighth // 2, width), bf16),
            pltpu.VMEM((units, eighth, width), bf16),
            pltpu.VMEM((units, eighth, width), bf16),
            pltpu.SemaphoreType.DMA((units, Scatter.COPIES)),
            pltpu.SemaphoreType.DMA((units, Scatter.COPIES)),
            pltpu.SemaphoreType.DMA((5, Gather.COPIES)),
            pltpu.SemaphoreType.DMA((5, Gather.COPIES)),
            pltpu.SemaphoreType.DMA((5, 4)),
            pltpu.SemaphoreType.DMA((7,)),
            pltpu.SemaphoreType.DMA((7,)),
            pltpu.SemaphoreType.DMA((13,)),
        ],
        compiler_params=pltpu.CompilerParams(
            collective_id=0, has_side_effects=True, vmem_limit_bytes=62 << 20
        ),
        name="forward_part",
    )(windows, pieces, chosen, memory, small, idx, select, hidden, cot, w_qkv, w_prefix, w_out, w_in, w_down)


def head_select():
    entry = jnp.arange(NB * H, dtype=jnp.int32)[None, :]
    head = jnp.arange(16, dtype=jnp.int32)[:, None]
    return (entry % H == head).astype(f32)


def pack_small(attn_gain, ffn_gain, rel_table, width):
    lines = [jnp.pad(v.astype(f32), (0, width - v.shape[0])) for v in (attn_gain, ffn_gain, rel_table)]
    return jnp.concatenate([jnp.stack(lines), jnp.zeros((5, width), f32)])


def rms_scale(values, norm_gain):
    return (
        values * lax.rsqrt(jnp.mean(values * values, axis=-1, keepdims=True) + epsilon) * norm_gain
    )


def prefix_kernel(row_ref, memory_ref, w_ref, picked_ref, prefix_ref):
    width = w_ref.shape[0]
    for q in range(QPR):
        picked_ref[q] = memory_ref[row_ref[q]]
    picked = picked_ref[...].reshape(QPR * SLOT, width)
    for at in range(0, w_ref.shape[1], width):
        part = mm(picked, w_ref[:, at : at + width]).astype(bf16)
        prefix_ref[:, :, at : at + width] = part.reshape(QPR, SLOT, width)


def make_prefix(chosen, memory, w_prefix):
    padded = jnp.pad(memory, ((0, 0), (0, SLOT - PAIRS), (0, 0)))
    return pl.pallas_call(
        prefix_kernel,
        out_shape=(
            jax.ShapeDtypeStruct(padded.shape, bf16),
            jax.ShapeDtypeStruct((QPR, SLOT, w_prefix.shape[1]), bf16),
        ),
        in_specs=[SMEM, VMEM, VMEM],
        out_specs=(VMEM, VMEM),
        compiler_params=pltpu.CompilerParams(vmem_limit_bytes=40 << 20),
        name="make_prefix",
    )(chosen, padded, w_prefix)


def memory_kernel(row_ref, slot_ref, w_ref, out_ref, held):
    width = w_ref.shape[0]
    slots = slot_ref[...].reshape(QPR * SLOT, w_ref.shape[1])
    held[...] = mm(slots, w_ref[...], NT).reshape(QPR, SLOT, width)
    for q in range(QPR):
        out_ref[row_ref[q]] = held[q, :PAIRS, :]


def memory_back(chosen, slot_grad, w_prefix):
    width = w_prefix.shape[0]
    return pl.pallas_call(
        memory_kernel,
        out_shape=jax.ShapeDtypeStruct((QPR, PAIRS, width), f32),
        in_specs=[SMEM, VMEM, VMEM],
        out_specs=VMEM,
        scratch_shapes=[pltpu.VMEM((QPR, SLOT, width), f32)],
        compiler_params=pltpu.CompilerParams(vmem_limit_bytes=40 << 20),
        name="memory_back",
    )(chosen, slot_grad, w_prefix)


def plain_row_pass(hidden, segments, memory, chosen, buckets, cotangent, full):
    attn_gain, ffn_gain, rel_table, w_qkv, w_attn_out, w_in, w_down, w_prefix = full
    length, width = hidden.shape
    starts = row_starts(segments)
    idx = near_buckets(buckets, length)
    table = jnp.pad(rel_table.reshape(NB, H).T, ((0, 16 - H), (0, 0)))
    tokens = hidden.astype(f32)
    gain_one = attn_gain.astype(f32)
    gain_two = ffn_gain.astype(f32)

    normed = rms_scale(tokens, gain_one).astype(bf16)
    projected = mm(normed, w_qkv).astype(bf16)
    picked, prefix = make_prefix(chosen, memory, w_prefix)
    attended = attend(starts, projected, prefix, table, idx)
    after_attn = tokens + mm(attended, w_attn_out)
    normed_ffn = rms_scale(after_attn, gain_two).astype(bf16)
    hidden_pre = mm(normed_ffn, w_in)
    activation = jax.nn.gelu(hidden_pre).astype(bf16)
    output = (after_attn + mm(activation, w_down)).astype(bf16)

    grad_out = cotangent.astype(f32)
    down_grad = mm(activation, cotangent, TN)
    act_grad = mm(cotangent, w_down, NT)
    pre_grad = jax.vjp(jax.nn.gelu, hidden_pre)[1](act_grad)[0].astype(bf16)
    in_grad = mm(normed_ffn, pre_grad, TN)
    normed_ffn_grad = mm(pre_grad, w_in, NT)
    residual_part, ffn_gain_grad = jax.vjp(rms_scale, after_attn, gain_two)[1](normed_ffn_grad)
    after_grad = grad_out + residual_part
    attn_branch = after_grad.astype(bf16)
    attn_out_grad = mm(attended, attn_branch, TN)
    attended_grad = mm(attn_branch, w_attn_out, NT).astype(bf16)
    token_grad, slot_grad, table_grad = attend_back(
        starts, projected, prefix, attended_grad, table, idx
    )
    qkv_grad = mm(normed, token_grad, TN)
    normed_grad = mm(token_grad, w_qkv, NT)
    flat = (QPR * SLOT, -1)
    prefix_grad = mm(picked.reshape(flat), slot_grad.reshape(flat), TN)
    memory_grad = memory_back(chosen, slot_grad, w_prefix)
    norm_part, attn_gain_grad = jax.vjp(rms_scale, tokens, gain_one)[1](normed_grad)
    hidden_grad = after_grad + norm_part
    small = jnp.concatenate([attn_gain_grad, ffn_gain_grad, table_grad[:, :H].reshape(NB * H)])
    return output, hidden_grad, memory_grad, small, (qkv_grad, attn_out_grad, in_grad, down_grad, prefix_grad)


def near_row_pass(hidden, segments, memory, chosen, buckets, cotangent, shards):
    attn_gain, ffn_gain, rel_table, w_qkv, w_attn_out, w_in, w_down, w_prefix = shards
    length, width = hidden.shape
    starts = row_starts(segments)
    idx = near_buckets(buckets, length)
    padded = jnp.pad(memory, ((0, 0), (0, SLOT - PAIRS), (0, 0)))
    (
        output, normed, proj, prefix, picked, gains, ffn_gain_grad, attended_grad, after_grad,
        full_qkv, full_prefix, in_grad, attn_out_grad, down_share,
    ) = forward_part(
        *layout_tables(segments), chosen, padded,
        pack_small(attn_gain, ffn_gain, rel_table, width), idx, head_select(),
        hidden, cotangent, w_qkv, w_prefix, w_attn_out, w_in, w_down,
    )
    side = lambda slots: jnp.transpose(slots, (1, 0, 2)).reshape(width, -1)
    w_qkv, w_prefix, in_grad = side(full_qkv), side(full_prefix), side(in_grad)
    table = jnp.pad(gains[2, : NB * H].astype(bf16).reshape(NB, H).T, ((0, 16 - H), (0, 0)))
    projected = jnp.transpose(proj, (1, 0, 2)).reshape(length, 3 * width)
    prefix = jnp.transpose(prefix, (1, 2, 0, 3)).reshape(QPR, SLOT, 4 * width)
    token_grad, slot_grad, table_grad = attend_back(
        starts, projected, prefix, attended_grad, table, idx
    )
    qkv_grad = mm(normed, token_grad, TN)
    normed_grad = mm(token_grad, w_qkv, NT)
    flat = (QPR * SLOT, -1)
    prefix_grad = mm(picked.reshape(flat), slot_grad.reshape(flat), TN)
    memory_grad = memory_back(chosen, slot_grad, w_prefix)
    norm_part, attn_gain_grad = jax.vjp(rms_scale, hidden.astype(f32), gains[0])[1](normed_grad)
    hidden_grad = after_grad + norm_part
    small = jnp.concatenate([attn_gain_grad, ffn_gain_grad[0], table_grad[:, :H].reshape(NB * H)])
    shares = [
        None if gradient is None
        else lax.psum_scatter(gradient.astype(bf16), "fsdp", scatter_dimension=0, tiled=True)
        for gradient in (qkv_grad, attn_out_grad, in_grad, None, prefix_grad)
    ]
    shares[3] = down_share.reshape(-1, width)
    return output, hidden_grad, memory_grad, small, shares


def near_local(
    hidden, segment_ids, memory, memory_row, buckets, attn_gain, ffn_gain, rel_table,
    w_qkv, w_attn_out, w_in, w_down, w_prefix, cotangent,
):
    sizes = (attn_gain.shape[0], ffn_gain.shape[0], rel_table.shape[0])
    shards = (attn_gain, ffn_gain, rel_table, w_qkv, w_attn_out, w_in, w_down, w_prefix)
    *own, small_grad, shares = near_row_pass(
        hidden[0], segment_ids[0], memory[0], memory_row[0], buckets, cotangent[0], shards
    )
    small_grad = lax.psum(small_grad, ("fsdp", "dp"))
    me = lax.axis_index("fsdp")
    bases = (0, 8 * sizes[0], 8 * (sizes[0] + sizes[1]))
    small_shares = [
        lax.dynamic_slice_in_dim(small_grad, base + me * size, size) for base, size in zip(bases, sizes)
    ]
    shares = [lax.psum(share, "dp").astype(f32) for share in shares]
    return tuple(x[None] for x in own) + tuple(small_shares) + tuple(shares)


def plain_local(
    hidden, segment_ids, memory, memory_row, buckets, attn_gain, ffn_gain, rel_table,
    w_qkv, w_attn_out, w_in, w_down, w_prefix, cotangent,
):
    sizes = (attn_gain.shape[0], ffn_gain.shape[0], rel_table.shape[0])
    small = lax.all_gather(jnp.concatenate([attn_gain, ffn_gain, rel_table]), "fsdp", axis=0)
    cuts = (0, sizes[0], sizes[0] + sizes[1], sum(sizes))
    full = tuple(small[:, cuts[i] : cuts[i + 1]].reshape(-1) for i in range(3)) + tuple(
        lax.all_gather(w, "fsdp", axis=0, tiled=True)
        for w in (w_qkv, w_attn_out, w_in, w_down, w_prefix)
    )
    outs = []
    total = None
    for r in range(hidden.shape[0]):
        *own, small_grad, grads = plain_row_pass(
            hidden[r], segment_ids[r], memory[r], memory_row[r], buckets, cotangent[r], full
        )
        outs.append(own)
        fresh = (small_grad,) + grads
        total = fresh if total is None else jax.tree.map(jnp.add, total, fresh)
    output, hidden_grad, memory_grad = (jnp.stack(x) for x in zip(*outs))
    small_grad = lax.psum(total[0], ("fsdp", "dp"))
    me = lax.axis_index("fsdp")
    bases = (0, full[0].shape[0], full[0].shape[0] + full[1].shape[0])
    shares = [
        lax.dynamic_slice_in_dim(small_grad, base + me * size, size) for base, size in zip(bases, sizes)
    ]
    for gradient in total[1:]:
        share = lax.psum_scatter(
            gradient.astype(bf16), "fsdp", scatter_dimension=0, tiled=True
        )
        shares.append(lax.psum(share, "dp").astype(f32))
    return (output, hidden_grad, memory_grad) + tuple(shares)


def solution(mesh):
    rows = ("fsdp", "dp")
    placed = (
        P(rows, None, None), P(rows, None), P(rows, None, None, None), P(rows, None), P(),
        P("fsdp"), P("fsdp"), P("fsdp"),
        P("fsdp", None), P("fsdp", None), P("fsdp", None), P("fsdp", None), P("fsdp", None),
        P(rows, None, None),
    )
    near = mesh.shape["fsdp"] == 8 and mesh.shape["dp"] == 4
    return jax.shard_map(
        near_local if near else plain_local,
        mesh=mesh,
        in_specs=placed,
        out_specs=(
            P(rows, None, None), P(rows, None, None), P(rows, None, None, None),
            P("fsdp"), P("fsdp"), P("fsdp"),
            P("fsdp", None), P("fsdp", None), P("fsdp", None), P("fsdp", None), P("fsdp", None),
        ),
        check_vma=False,
    )
```

```python
import functools
import jax
import jax.numpy as jnp
from jax import lax
from jax.experimental import pallas as pl
from jax.experimental.pallas import tpu as pltpu
from jax.sharding import PartitionSpec as P

H = 12
DH = 64
NB = 32
QLEN = 64
QPR = 20
D_MODEL = 768
PAIRS = 10

WIN = 80
SLOT = 16
KEYS = 128
GROUP = 4
GW = GROUP * DH
masked_out = -1e30
f32 = jnp.float32
bf16 = jnp.bfloat16
NT = (((1,), (1,)), ((), ()))
TN = (((0,), (0,)), ((), ()))


def mm(a, b, dims=(((1,), (0,)), ((), ()))):
    return lax.dot_general(a, b, dims, preferred_element_type=f32)


def bucket_hot(idx_ref):
    return (lax.broadcasted_iota(jnp.int32, (NB, KEYS), 0) == idx_ref[...]).astype(f32)


def fill_bias(table_ref, idx_ref, bias):
    hot = bucket_hot(idx_ref).astype(bf16)
    lines = mm(table_ref[...], hot)
    lane = lax.broadcasted_iota(jnp.int32, (WIN, KEYS), 1)
    for h in range(H):
        wide = jnp.broadcast_to(lines[h : h + 1, :], (WIN, KEYS))
        rolled = pltpu.roll(wide, 0, 1, stride=1, stride_axis=0)
        bias[h * WIN : (h + 1) * WIN, :] = jnp.where(lane < WIN, rolled, 0.0)


def stack_heads(block):
    lane = lax.broadcasted_iota(jnp.int32, (1, GW), 1)
    parts = []
    for h in range(GROUP):
        mask = jnp.where((lane >= h * DH) & (lane < (h + 1) * DH), 1.0, 0.0).astype(bf16)
        parts.append(block * mask)
    return jnp.concatenate(parts, axis=0)


def merge_heads(stacked):
    lane = lax.broadcasted_iota(jnp.int32, (WIN, GW), 1)
    out = stacked[:WIN]
    for h in range(1, GROUP):
        out = jnp.where(lane >= h * DH, stacked[h * WIN : (h + 1) * WIN], out)
    return out


def key_tile(tokens, low, high):
    rest = jnp.zeros((KEYS - WIN - 2 * SLOT, tokens.shape[1]), tokens.dtype)
    return jnp.concatenate([tokens, low, high, rest], axis=0)


def key_cost(begin, end):
    lane = lax.broadcasted_iota(jnp.int32, (1, KEYS), 1)
    token = (lane >= begin) & (lane < end)
    first = (lane >= WIN) & (lane < WIN + PAIRS)
    second = (lane >= WIN + SLOT) & (lane < WIN + SLOT + PAIRS)
    return jnp.where(token | first | second, 0.0, masked_out).astype(f32)


def soft_rows(stack, keys, bias_block, cost):
    logits = mm(stack, keys, NT) + (bias_block + cost)
    peak = jnp.max(logits, axis=1, keepdims=True)
    raw = jnp.exp(logits - peak)
    return raw * (1.0 / jnp.sum(raw, axis=1, keepdims=True))


def window(start_ref, q):
    start = start_ref[q]
    base = pl.multiple_of((start // 16) * 16, 16)
    base = jnp.minimum(base, start_ref[QPR] - WIN)
    base = pl.multiple_of(base, 16)
    return base, start - base, start_ref[q + 1] - base


def forward_kernel(start_ref, proj_ref, prefix_ref, table_ref, idx_ref, out_ref, bias):
    width = out_ref.shape[1]
    fill_bias(table_ref, idx_ref, bias)

    def body(q, carry):
        base, begin, end = window(start_ref, q)
        cost = key_cost(begin, end)
        row = lax.broadcasted_iota(jnp.int32, (WIN, GW), 0)
        mine = (row >= begin) & (row < end)
        rows = pl.ds(base, WIN)
        for g in range(width // GW):
            at = g * GW
            stack = stack_heads(proj_ref[rows, at : at + GW] * bf16(DH**-0.5))
            keys = key_tile(
                proj_ref[rows, width + at : width + at + GW],
                prefix_ref[q, :, at : at + GW],
                prefix_ref[q, :, width + at : width + at + GW],
            )
            values = key_tile(
                proj_ref[rows, 2 * width + at : 2 * width + at + GW],
                prefix_ref[q, :, 2 * width + at : 2 * width + at + GW],
                prefix_ref[q, :, 3 * width + at : 3 * width + at + GW],
            )
            soft = soft_rows(stack, keys, bias[g * GROUP * WIN : (g + 1) * GROUP * WIN, :], cost)
            blended = merge_heads(mm(soft.astype(bf16), values)).astype(bf16)
            out_ref[rows, at : at + GW] = jnp.where(mine, blended, out_ref[rows, at : at + GW])
        return carry

    lax.fori_loop(0, QPR, body, 0)


def backward_kernel(
    start_ref, proj_ref, prefix_ref, grad_ref, table_ref, idx_ref,
    token_ref, slot_ref, table_grad_ref, bias, bias_grad,
):
    width = grad_ref.shape[1]
    fill_bias(table_ref, idx_ref, bias)
    bias_grad[...] = jnp.zeros_like(bias_grad)

    def body(q, carry):
        base, begin, end = window(start_ref, q)
        cost = key_cost(begin, end)
        row = lax.broadcasted_iota(jnp.int32, (WIN, GW), 0)
        mine = (row >= begin) & (row < end)
        rows = pl.ds(base, WIN)
        for g in range(width // GW):
            at = g * GW
            heads = slice(g * GROUP * WIN, (g + 1) * GROUP * WIN)
            stack = stack_heads(proj_ref[rows, at : at + GW] * bf16(DH**-0.5))
            keys = key_tile(
                proj_ref[rows, width + at : width + at + GW],
                prefix_ref[q, :, at : at + GW],
                prefix_ref[q, :, width + at : width + at + GW],
            )
            values = key_tile(
                proj_ref[rows, 2 * width + at : 2 * width + at + GW],
                prefix_ref[q, :, 2 * width + at : 2 * width + at + GW],
                prefix_ref[q, :, 3 * width + at : 3 * width + at + GW],
            )
            grad = grad_ref[rows, at : at + GW]
            grads = stack_heads(jnp.where(mine, grad, jnp.zeros_like(grad)))
            soft = soft_rows(stack, keys, bias[heads, :], cost)
            prob_grad = mm(grads, values, NT)
            weighted = soft * prob_grad
            logit_grad = weighted - soft * jnp.sum(weighted, axis=1, keepdims=True)
            low = logit_grad.astype(bf16)
            bias_grad[heads, :] += low.astype(f32)
            query_grad = (merge_heads(mm(low, keys)) * DH**-0.5).astype(bf16)
            key_grad = mm(low, stack, TN).astype(bf16)
            value_grad = mm(soft.astype(bf16), grads, TN).astype(bf16)
            for part, fresh in ((0, query_grad), (1, key_grad[:WIN]), (2, value_grad[:WIN])):
                cols = slice(part * width + at, part * width + at + GW)
                token_ref[rows, cols] = jnp.where(mine, fresh, token_ref[rows, cols])
            for part, fresh in ((0, key_grad), (2, value_grad)):
                for s in range(2):
                    cols = slice((part + s) * width + at, (part + s) * width + at + GW)
                    slot_ref[q, :, cols] = fresh[WIN + s * SLOT : WIN + (s + 1) * SLOT]
        return carry

    lax.fori_loop(0, QPR, body, 0)
    lane = lax.broadcasted_iota(jnp.int32, (H, KEYS), 1)
    sums = jnp.zeros((H, KEYS), f32)
    for i in range(WIN):
        line = jnp.where(lane < WIN, bias_grad[pl.ds(i, H, stride=WIN), :], 0.0)
        sums += line if i == 0 else pltpu.roll(line, KEYS - i, 1)
    sums = jnp.concatenate([sums, jnp.zeros((16 - H, KEYS), f32)], axis=0)
    table_grad_ref[...] = lax.dot_general(
        bucket_hot(idx_ref), sums, NT, precision=lax.Precision.HIGHEST, preferred_element_type=f32
    )


SMEM = pl.BlockSpec(memory_space=pltpu.SMEM)
VMEM = pl.BlockSpec(memory_space=pltpu.VMEM)


def attend(starts, projected, prefix, table, idx):
    length = projected.shape[0]
    width = projected.shape[1] // 3
    return pl.pallas_call(
        forward_kernel,
        out_shape=jax.ShapeDtypeStruct((length, width), bf16),
        in_specs=[SMEM, VMEM, VMEM, VMEM, VMEM],
        out_specs=VMEM,
        scratch_shapes=[pltpu.VMEM((H * WIN, KEYS), f32)],
        compiler_params=pltpu.CompilerParams(vmem_limit_bytes=40 << 20),
        name="attend",
    )(starts, projected, prefix, table, idx)


def attend_back(starts, projected, prefix, grad, table, idx):
    length = projected.shape[0]
    return pl.pallas_call(
        backward_kernel,
        out_shape=(
            jax.ShapeDtypeStruct(projected.shape, bf16),
            jax.ShapeDtypeStruct(prefix.shape, bf16),
            jax.ShapeDtypeStruct((NB, 16), f32),
        ),
        in_specs=[SMEM, VMEM, VMEM, VMEM, VMEM, VMEM],
        out_specs=(VMEM, VMEM, VMEM),
        scratch_shapes=[pltpu.VMEM((H * WIN, KEYS), f32), pltpu.VMEM((H * WIN, KEYS), f32)],
        compiler_params=pltpu.CompilerParams(vmem_limit_bytes=48 << 20),
        name="attend_back",
    )(starts, projected, prefix, grad, table, idx)


def row_starts(segments):
    length = segments.shape[0]
    ids = jnp.arange(QPR + 1, dtype=jnp.int32)
    return jnp.sum((segments[None, :] < ids[:, None]).astype(jnp.int32), axis=1)


def near_buckets(buckets, length):
    back = buckets[length - QLEN : length][::-1]
    ahead = buckets[length : length + QLEN - 1][::-1]
    return jnp.concatenate([back, buckets[length - 1 : length], ahead])[None, :]


epsilon = 1e-06


MESH = pl.DeviceIdType.MESH
ANY = pl.BlockSpec(memory_space=pl.ANY)


class Place:
    def __init__(self):
        me = lax.axis_index("fsdp")
        self.me, self.c, self.x, self.y = me, me % 2, (me // 2) % 2, me // 4
        self.z = lax.axis_index("dp")

    def at(self, dy, dx, dc):
        return 4 * ((self.y + dy) % 2) + 2 * ((self.x + dx) % 2) + (self.c + dc) % 2


OTHERS = [(dy, dx, dc) for dy in (0, 1) for dx in (0, 1) for dc in (0, 1)][1:]


def greet(peers):
    barrier = pltpu.get_barrier_semaphore()
    for peer in peers:
        pl.semaphore_signal(barrier, inc=1, device_id=peer, device_id_type=MESH)
    pl.semaphore_wait(barrier, len(peers))


class Gather:
    COPIES = 8

    def __init__(self, place, shard, full, down, k, send, recv, own_sem):
        self.p, self.shard, self.full, self.down = place, shard, full, down
        self.send, self.recv, self.own_sem = send.at[k], recv.at[k], own_sem.at[k]
        self.rows = shard.shape[0]
        self.half = self.rows // 2

    def piece(self, dy, dx, dc, part=None):
        f = self.p.at(dy, dx, dc)
        begin = (f % 2) * self.rows if self.down else f * self.rows
        size = self.rows
        if part is not None:
            begin, size = begin + part * self.half, self.half
        rows = pl.ds(pl.multiple_of(begin, 16), size)
        return self.full.at[f // 2, rows, :] if self.down else self.full.at[:, rows, :]

    def copy(self, k, src, dst, dy, dx, dc):
        return pltpu.make_async_remote_copy(
            src_ref=src, dst_ref=dst, send_sem=self.send.at[k], recv_sem=self.recv.at[k],
            device_id={"fsdp": self.p.at(dy, dx, dc)}, device_id_type=MESH,
        )

    def own(self):
        if self.down:
            return [pltpu.make_async_copy(self.shard, self.piece(0, 0, 0), self.own_sem.at[0])]
        rows = pl.ds(pl.multiple_of(self.p.me * self.rows, 16), self.rows)
        width = self.full.shape[2]
        return [
            pltpu.make_async_copy(
                self.shard.at[:, s * width : (s + 1) * width], self.full.at[s, rows, :], self.own_sem.at[s]
            )
            for s in range(self.full.shape[0])
        ]

    def load(self):
        for copy in self.own():
            copy.start()

    def first(self):
        for copy in self.own():
            copy.wait()
        mine = self.piece(0, 0, 0)
        self.copy(0, mine, mine, 0, 1, 0).start()
        self.copy(1, mine, mine, 1, 0, 0).start()
        self.copy(2, mine, mine, 0, 0, 1).start()

    def landed(self, k, piece):
        self.copy(k, piece, piece, 0, 0, 1).wait_recv()

    def relay(self):
        from_x, from_y = self.piece(0, 1, 0), self.piece(1, 0, 0)
        self.landed(0, from_x)
        top = self.piece(0, 1, 0, 0)
        self.copy(3, top, top, 1, 0, 0).start()
        self.copy(4, from_x, from_x, 0, 0, 1).start()
        self.landed(1, from_y)
        low = self.piece(1, 0, 0, 1)
        self.copy(5, low, low, 0, 1, 0).start()
        self.copy(6, from_y, from_y, 0, 0, 1).start()

    def last(self):
        self.landed(3, self.piece(1, 1, 0, 0))
        self.landed(5, self.piece(1, 1, 0, 1))
        far = self.piece(1, 1, 0)
        self.copy(7, far, far, 0, 0, 1).start()

    def finish(self):
        self.landed(2, self.piece(0, 0, 1))
        self.landed(4, self.piece(0, 1, 1))
        self.landed(6, self.piece(1, 0, 1))
        self.landed(7, self.piece(1, 1, 1))

    def drain(self):
        whole, part = self.piece(0, 0, 0), self.piece(0, 0, 0, 0)
        for k in range(self.COPIES):
            src = part if k in (3, 5) else whole
            self.copy(k, src, src, 0, 0, 1).wait_send()


class Scatter:
    COPIES = 7

    def __init__(self, place, other, own, bufs, u, send, recv):
        self.p, self.other, self.own = place, other, own
        self.rc, self.rd, self.re, self.rx, self.ry = (b.at[u] for b in bufs)
        self.send, self.recv = send, recv
        self.half = self.rd.shape[0]

    def mine(self, dy, dx):
        return self.own.at[2 * ((self.p.y + dy) % 2) + (self.p.x + dx) % 2]

    def copy(self, k, src, dst, dy, dx, dc):
        return pltpu.make_async_remote_copy(
            src_ref=src, dst_ref=dst, send_sem=self.send.at[k], recv_sem=self.recv.at[k],
            device_id={"fsdp": self.p.at(dy, dx, dc)}, device_id_type=MESH,
        )

    def part(self, k):
        low, high = pl.ds(0, self.half), pl.ds(self.half, self.half)
        if k == 0:
            return self.copy(0, self.other, self.rc, 0, 0, 1)
        if k == 1:
            return self.copy(1, self.mine(1, 1).at[low], self.rd, 0, 1, 0)
        if k == 2:
            return self.copy(2, self.mine(1, 1).at[high], self.re, 1, 0, 0)
        if k == 3:
            return self.copy(3, self.mine(0, 1).at[low], self.rx.at[low], 0, 1, 0)
        if k == 4:
            return self.copy(4, self.mine(1, 0).at[high], self.ry.at[high], 1, 0, 0)
        if k == 5:
            return self.copy(5, self.mine(0, 1).at[high], self.rx.at[high], 0, 1, 0)
        return self.copy(6, self.mine(1, 0).at[low], self.ry.at[low], 1, 0, 0)

    def core(self):
        self.part(0).start()

    def fold(self):
        self.part(0).wait_recv()
        self.own[...] = (self.own[...].astype(f32) + self.rc[...].astype(f32)).astype(bf16)
        for k in (1, 2, 3, 4):
            self.part(k).start()

    def relay(self):
        low, high = pl.ds(0, self.half), pl.ds(self.half, self.half)
        nx, ny = self.mine(0, 1).at[high], self.mine(1, 0).at[low]
        self.part(1).wait_recv()
        ny[...] = (ny[...].astype(f32) + self.rd[...].astype(f32)).astype(bf16)
        self.part(6).start()
        self.part(2).wait_recv()
        nx[...] = (nx[...].astype(f32) + self.re[...].astype(f32)).astype(bf16)
        self.part(5).start()

    def total(self):
        for k in (3, 4, 5, 6):
            self.part(k).wait_recv()
        return self.mine(0, 0)[...].astype(f32) + (self.rx[...].astype(f32) + self.ry[...].astype(f32))

    def settle(self):
        total = self.total().astype(bf16)
        self.mine(0, 0)[...] = total

    def drain(self):
        for k in range(self.COPIES):
            self.part(k).wait_send()


def loop(n, body, unroll=1):
    def step(i, carry):
        body(i)
        return carry

    lax.fori_loop(0, n, step, 0, unroll=unroll)


GELU_A = 0.7978845608028654
GELU_B = 0.044715


def gelu_pair(v):
    square = v * v
    t = jnp.tanh(v * (GELU_A + (GELU_A * GELU_B) * square))
    half = 0.5 + 0.5 * t
    slope = half + (0.5 * v) * (1.0 - t * t) * (GELU_A + (3.0 * GELU_A * GELU_B) * square)
    return v * half, slope


TILE = 256
BLOCK = 16
OVERLAP = 6


def rows_of(i):
    return pl.ds(pl.multiple_of(i * TILE, TILE), TILE)


def table_bias(gains, idx_ref, select_ref, bias):
    wide = jnp.where(select_ref[...] > 0, jnp.broadcast_to(gains[2:3, : NB * H], (16, NB * H)), 0.0)
    lines = mm(wide.astype(bf16), entry_hot(idx_ref))
    lane = lax.broadcasted_iota(jnp.int32, (WIN, KEYS), 1)
    for h in range(H):
        rolled = pltpu.roll(jnp.broadcast_to(lines[h : h + 1, :], (WIN, KEYS)), 0, 1, stride=1, stride_axis=0)
        bias[h * WIN : (h + 1) * WIN, :] = jnp.where(lane < WIN, rolled, 0.0)


def entry_hot(idx_ref):
    off = lax.broadcasted_iota(jnp.int32, (NB * H, KEYS), 0) - H * idx_ref[...]
    return jnp.where((off >= 0) & (off < H), 1.0, 0.0).astype(bf16)


def question(window_ref, q):
    return window_ref[3 * q] * BLOCK, window_ref[3 * q + 1], window_ref[3 * q + 2]


def attend_one(q, window_ref, proj, prefix, bias, pad):
    base, begin, end = question(window_ref, q)
    cost = key_cost(begin, end)
    rows = pl.ds(base, WIN)
    width = proj.shape[2]
    for g in range(width // GW):
        cols = slice(g * GW, (g + 1) * GW)
        stack = stack_heads(proj[0, rows, cols] * bf16(DH**-0.5))
        keys = key_tile(proj[1, rows, cols], prefix[0, q, :, cols], prefix[1, q, :, cols])
        values = key_tile(proj[2, rows, cols], prefix[2, q, :, cols], prefix[3, q, :, cols])
        soft = soft_rows(stack, keys, bias[g * GROUP * WIN : (g + 1) * GROUP * WIN, :], cost)
        pad[q, :, cols] = merge_heads(mm(soft.astype(bf16), values)).astype(bf16)


def unpad(b, piece_ref, pads, outs):
    row = lax.broadcasted_iota(jnp.int32, (BLOCK, 1), 0)
    sums = [jnp.zeros((BLOCK, pad.shape[-1]), bf16) for pad in pads]
    for k in range(OVERLAP):
        at = 4 * (OVERLAP * b + k)
        q, off = piece_ref[at], piece_ref[at + 1] * BLOCK
        mine = (row >= piece_ref[at + 2]) & (row < piece_ref[at + 3])
        for s, pad in enumerate(pads):
            sums[s] = jnp.where(mine, pad[q, pl.ds(off, BLOCK), :], sums[s])
    for total, out in zip(sums, outs):
        out[pl.ds(pl.multiple_of(b * BLOCK, BLOCK), BLOCK), :] = total


def layout_tables(segments):
    length = segments.shape[0]
    starts = row_starts(segments)
    low, high = starts[:-1], starts[1:]
    base = jnp.minimum(low // BLOCK, (length - WIN) // BLOCK)
    windows = jnp.stack([base, low - BLOCK * base, high - BLOCK * base], axis=1).reshape(-1)
    at = jnp.arange(length // BLOCK, dtype=jnp.int32)[:, None] * BLOCK
    ids = jnp.arange(QPR, dtype=jnp.int32)
    q = jnp.sum((high[None, :] <= at).astype(jnp.int32), axis=1, keepdims=True)
    q = jnp.minimum(q + jnp.arange(OVERLAP, dtype=jnp.int32)[None, :], QPR - 1)
    hot = (q[:, :, None] == ids).astype(jnp.int32)
    pick = lambda v: jnp.sum(hot * v, axis=2)
    begin, end = jnp.clip(pick(low) - at, 0, BLOCK), jnp.clip(pick(high) - at, 0, BLOCK)
    off = jnp.clip(at // BLOCK - pick(base), 0, (WIN - BLOCK) // BLOCK)
    return windows, jnp.stack([q, off, begin, end], axis=2).reshape(-1)


def forward_part_kernel(
    window_ref, piece_ref, chosen_ref, memory_ref, small_ref, idx_ref, select_ref,
    hidden_hbm, cot_hbm, qkv_w, prefix_w, out_w, in_w, down_w,
    output_hbm, normed_hbm, proj_hbm, prefix_hbm, picked_hbm, gains_ref, gain_grad_ref,
    attended_grad_hbm, after_grad_hbm, qkv_hbm, prefix_w_hbm, in_grad_hbm, out_grad_hbm, sums_ref,
    w_qkv, w_prefix, w_out, w_in, w_down, hidden, cot, normed, act, slope, prefix, picked, pad, attended,
    after, down_grads, attended_grad, bias, small_all,
    rc, rd, re, rx, ry, send, recv, g_send, g_recv, own_sem, small_send, small_recv, io_sem,
):
    place = Place()
    length, width = hidden.shape
    steps = length // TILE
    chunks = w_in.shape[0]
    proj = slope
    weights = ((qkv_w, w_qkv), (prefix_w, w_prefix), (out_w, w_out), (in_w, w_in), (down_w, w_down))
    g_qkv, g_prefix, g_out, g_in, g_down = (
        Gather(place, shard, full, k == 4, k, g_send, g_recv, own_sem) for k, (shard, full) in enumerate(weights)
    )

    def io(k, src, dst):
        return pltpu.make_async_copy(src, dst, io_sem.at[k])

    load_hidden, load_cot = io(0, hidden_hbm, hidden), io(1, cot_hbm, cot)
    for g in (g_qkv, g_prefix, g_out, g_in, g_down):
        g.load()
    load_hidden.start()
    load_cot.start()
    row = lax.broadcasted_iota(jnp.int32, small_ref.shape, 0)
    small_all[0] = jnp.where(
        row < 2,
        pltpu.roll(small_ref[...], place.me * (width // 8), 1),
        pltpu.roll(small_ref[...], place.me * (NB * H // 8), 1),
    )
    greet([{"fsdp": place.at(*o)} for o in OTHERS])

    def small_copy(k):
        return pltpu.make_async_remote_copy(
            src_ref=small_all.at[0], dst_ref=small_all.at[k + 1],
            send_sem=small_send.at[k], recv_sem=small_recv.at[k],
            device_id={"fsdp": place.at(*OTHERS[k])}, device_id_type=MESH,
        )

    for k in range(7):
        small_copy(k).start()
    g_qkv.first()
    g_prefix.first()
    load_hidden.wait()
    for q in range(QPR):
        picked[q] = memory_ref[chosen_ref[q]]
    keep_picked = io(2, picked, picked_hbm)
    keep_picked.start()
    for k in range(7):
        small_copy(k).wait_recv()
    gains_ref[...] = jnp.sum(small_all[...], axis=0)
    gain_one, gain_two = gains_ref[0:1, :], gains_ref[1:2, :]

    def norm(i):
        rows = rows_of(i)
        values = hidden[rows, :].astype(f32)
        scale = lax.rsqrt(jnp.mean(values * values, axis=1, keepdims=True) + epsilon)
        normed[rows, :] = (values * scale * gain_one).astype(bf16)

    loop(steps, norm)
    keep_normed = io(3, normed, normed_hbm)
    keep_normed.start()
    table_bias(gains_ref, idx_ref, select_ref, bias)
    g_qkv.relay()
    g_out.first()
    g_in.first()
    g_prefix.relay()
    g_down.first()
    g_qkv.last()
    g_qkv.finish()
    keep_qkv = io(4, w_qkv, qkv_hbm)
    keep_qkv.start()

    def project(step):
        s, rows = step // steps, rows_of(step % steps)
        proj[s, rows, :] = mm(normed[rows, :], w_qkv[s]).astype(bf16)

    loop(3 * steps, project)
    keep_proj = io(5, proj.at[0:3], proj_hbm)
    keep_proj.start()
    g_prefix.last()
    g_prefix.finish()
    keep_prefix_w = io(6, w_prefix, prefix_w_hbm)
    keep_prefix_w.start()

    def make_prefix_slot(s):
        part = mm(picked[...].reshape(QPR * SLOT, width), w_prefix[s])
        prefix[s] = part.astype(bf16).reshape(QPR, SLOT, width)

    loop(4, make_prefix_slot)
    keep_prefix = io(7, prefix, prefix_hbm)
    keep_prefix.start()
    g_out.relay()
    g_in.relay()

    def attend_step(q):
        attend_one(q, window_ref, proj, prefix, bias, pad)

    loop(QPR // 2, attend_step)
    g_out.last()
    g_in.last()
    g_down.relay()
    loop(QPR // 2, lambda q: attend_step(q + QPR // 2))
    loop(length // BLOCK, lambda b: unpad(b, piece_ref, (pad,), (attended,)))
    g_out.finish()
    keep_normed.wait()

    def attn_out(i):
        rows = rows_of(i)
        values = hidden[rows, :].astype(f32) + mm(attended[rows, :], w_out[0])
        after[rows, :] = values
        scale = lax.rsqrt(jnp.mean(values * values, axis=1, keepdims=True) + epsilon)
        normed[rows, :] = (values * scale * gain_two).astype(bf16)

    loop(steps, attn_out)
    g_in.finish()
    g_down.last()
    keep_proj.wait()

    def hidden_chunk(step):
        j, rows = step // steps, rows_of(step % steps)
        act_part, slope_part = gelu_pair(mm(normed[rows, :], w_in[j]))
        act[j, rows, :] = act_part.astype(bf16)
        slope[j, rows, :] = slope_part.astype(bf16)

    loop(chunks * steps, hidden_chunk)
    load_cot.wait()

    def down_chunk(step):
        j, c = step // 2, step % 2
        cols = pl.ds(pl.multiple_of(c * (width // 2), 128), width // 2)
        part = mm(act[j, :, cols], cot[...], TN)
        down_grads[j, c] = part.astype(bf16).reshape(4, width // 8, width)

    loop(chunks * 2, down_chunk)
    bufs = (rc, rd, re, rx, ry)
    units = [
        Scatter(
            place, down_grads.at[:, 1 - place.c, u], down_grads.at[:, place.c, u], bufs, u, send.at[u], recv.at[u]
        )
        for u in range(4)
    ]
    for u in units:
        u.core()
    g_down.finish()

    def slope_chunk(step):
        j, rows = step // steps, rows_of(step % steps)
        act_grad = mm(cot[rows, :], w_down[j], NT)
        slope[j, rows, :] = (act_grad * slope[j, rows, :].astype(f32)).astype(bf16)

    loop(chunks * steps, slope_chunk)
    for u in units:
        u.fold()
    keep_prefix_w.wait()
    keep_qkv.wait()
    g_qkv.drain()
    g_prefix.drain()
    in_grad, out_grad = w_prefix, w_qkv

    def in_chunk(step):
        j, c = step // 2, step % 2
        cols = pl.ds(pl.multiple_of(c * (width // 2), 128), width // 2)
        in_grad[j, cols, :] = mm(normed[:, cols], slope[j], TN).astype(bf16)

    loop(chunks * 2, in_chunk)
    keep_in = io(8, in_grad, in_grad_hbm)
    keep_in.start()
    for u in units:
        u.relay()

    def out_rows(i):
        rows = rows_of(i)
        total = after[rows, :]
        for j in range(chunks):
            total += mm(act[j, rows, :], w_down[j])
        hidden[rows, :] = total.astype(bf16)

    loop(steps, out_rows)
    keep_output = io(9, hidden, output_hbm)
    keep_output.start()
    gain_grad_ref[...] = jnp.zeros_like(gain_grad_ref)

    def back_rows(i):
        rows = rows_of(i)
        grad = mm(slope[0, rows, :], w_in[0], NT)
        for j in range(1, chunks):
            grad += mm(slope[j, rows, :], w_in[j], NT)
        values = after[rows, :]
        scale = lax.rsqrt(jnp.mean(values * values, axis=1, keepdims=True) + epsilon)
        unit = values * scale
        gain_grad_ref[0:1, :] += jnp.sum(grad * unit, axis=0, keepdims=True)
        pulled = grad * gain_two
        mixed = pulled - unit * jnp.mean(pulled * unit, axis=1, keepdims=True)
        result = cot[rows, :].astype(f32) + scale * mixed
        after[rows, :] = result
        low = result.astype(bf16)
        normed[rows, :] = low
        attended_grad[rows, :] = mm(low, w_out[0], NT).astype(bf16)

    loop(steps, back_rows)
    keep_after = io(10, after, after_grad_hbm)
    keep_after.start()
    keep_attended = io(11, attended_grad, attended_grad_hbm)
    keep_attended.start()
    for c in range(2):
        cols = slice(c * (width // 2), (c + 1) * (width // 2))
        out_grad[0, cols, :] = mm(attended[:, cols], normed[...], TN).astype(bf16)
    keep_out = io(12, out_grad.at[0], out_grad_hbm)
    keep_out.start()
    for k, u in enumerate(units):
        sums_ref[k] = u.total().astype(bf16)
    for k in range(7):
        small_copy(k).wait_send()
    for g in (g_out, g_in, g_down):
        g.drain()
    for u in units:
        u.drain()
    for copy in (
        keep_picked, keep_prefix, keep_in, keep_output, keep_after, keep_attended, keep_out
    ):
        copy.wait()


def forward_part(windows, pieces, chosen, memory, small, idx, select, hidden, cot, w_qkv, w_prefix, w_out, w_in, w_down):
    length, width = hidden.shape
    chunks = w_in.shape[1] // width
    eighth = width // 8
    units = w_down.shape[0] // eighth
    sds = jax.ShapeDtypeStruct
    return pl.pallas_call(
        forward_part_kernel,
        out_shape=(
            sds((length, width), bf16),
            sds((length, width), bf16),
            sds((3, length, width), bf16),
            sds((4, QPR, SLOT, width), bf16),
            sds((QPR, SLOT, width), bf16),
            sds(small.shape, f32),
            sds((8, width), f32),
            sds((length, width), bf16),
            sds((length, width), f32),
            sds((3, width, width), bf16),
            sds((4, width, width), bf16),
            sds((chunks, width, width), bf16),
            sds((width, width), bf16),
            sds((units, eighth, width), bf16),
        ),
        in_specs=[SMEM] * 3 + [VMEM] * 4 + [ANY] * 7,
        out_specs=(ANY,) * 5 + (VMEM,) * 2 + (ANY,) * 6 + (VMEM,),
        scratch_shapes=[
            pltpu.VMEM((3, width, width), bf16),
            pltpu.VMEM((4, width, width), bf16),
            pltpu.VMEM((1, width, width), bf16),
            pltpu.VMEM((chunks, width, width), bf16),
            pltpu.VMEM((chunks, width, width), bf16),
            pltpu.VMEM((length, width), bf16),
            pltpu.VMEM((length, width), bf16),
            pltpu.VMEM((length, width), bf16),
            pltpu.VMEM((chunks, length, width), bf16),
            pltpu.VMEM((chunks, length, width), bf16),
            pltpu.VMEM((4, QPR, SLOT, width), bf16),
            pltpu.VMEM((QPR, SLOT, width), bf16),
            pltpu.VMEM((QPR, WIN, width), bf16),
            pltpu.VMEM((length, width), bf16),
            pltpu.VMEM((length, width), f32),
            pltpu.VMEM((4, 2, units, eighth, width), bf16),
            pltpu.VMEM((length, width), bf16),
            pltpu.VMEM((H * WIN, KEYS), f32),
            pltpu.VMEM((8,) + small.shape, f32),
            pltpu.VMEM((units, 4, eighth, width), bf16),
            pltpu.VMEM((units, eighth // 2, width), bf16),
            pltpu.VMEM((units, eighth // 2, width), bf16),
            pltpu.VMEM((units, eighth, width), bf16),
            pltpu.VMEM((units, eighth, width), bf16),
            pltpu.SemaphoreType.DMA((units, Scatter.COPIES)),
            pltpu.SemaphoreType.DMA((units, Scatter.COPIES)),
            pltpu.SemaphoreType.DMA((5, Gather.COPIES)),
            pltpu.SemaphoreType.DMA((5, Gather.COPIES)),
            pltpu.SemaphoreType.DMA((5, 4)),
            pltpu.SemaphoreType.DMA((7,)),
            pltpu.SemaphoreType.DMA((7,)),
            pltpu.SemaphoreType.DMA((13,)),
        ],
        compiler_params=pltpu.CompilerParams(
            collective_id=0, has_side_effects=True, vmem_limit_bytes=62 << 20
        ),
        name="forward_part",
    )(windows, pieces, chosen, memory, small, idx, select, hidden, cot, w_qkv, w_prefix, w_out, w_in, w_down)


def head_select():
    entry = jnp.arange(NB * H, dtype=jnp.int32)[None, :]
    head = jnp.arange(16, dtype=jnp.int32)[:, None]
    return (entry % H == head).astype(f32)


def pack_small(attn_gain, ffn_gain, rel_table, width):
    lines = [jnp.pad(v.astype(f32), (0, width - v.shape[0])) for v in (attn_gain, ffn_gain, rel_table)]
    return jnp.concatenate([jnp.stack(lines), jnp.zeros((5, width), f32)])


class Line:
    def __init__(self, place, own, below, above, up, down, k, send, recv):
        self.z, self.own, self.below, self.above, self.up, self.down = place.z, own, below, above, up, down
        self.send, self.recv = send.at[k], recv.at[k]

    def rise(self, src):
        return pltpu.make_async_remote_copy(
            src_ref=src, dst_ref=self.below, send_sem=self.send.at[0], recv_sem=self.recv.at[0],
            device_id={"dp": self.z + 1}, device_id_type=MESH,
        )

    def sink(self, src):
        return pltpu.make_async_remote_copy(
            src_ref=src, dst_ref=self.above, send_sem=self.send.at[1], recv_sem=self.recv.at[1],
            device_id={"dp": self.z - 1}, device_id_type=MESH,
        )

    def start(self):
        @pl.when(self.z == 0)
        def _():
            self.below[...] = jnp.zeros_like(self.below)
            self.rise(self.own).start()

        @pl.when(self.z == 3)
        def _():
            self.above[...] = jnp.zeros_like(self.above)
            self.sink(self.own).start()

    def pass_up(self):
        self.rise(self.own).wait_recv()
        self.up[...] = (self.below[...].astype(f32) + self.own[...].astype(f32)).astype(self.up.dtype)
        self.rise(self.up).start()

    def pass_down(self):
        self.sink(self.own).wait_recv()
        self.down[...] = (self.above[...].astype(f32) + self.own[...].astype(f32)).astype(self.down.dtype)
        self.sink(self.down).start()

    def near(self):
        pl.when(self.z == 1)(self.pass_up)
        pl.when(self.z == 2)(self.pass_down)

    def far(self):
        pl.when(self.z == 1)(self.pass_down)
        pl.when(self.z == 2)(self.pass_up)

    def total(self):
        pl.when(self.z == 0)(lambda: self.sink(self.own).wait_recv())
        pl.when(self.z == 3)(lambda: self.rise(self.own).wait_recv())
        return self.own[...].astype(f32) + (self.below[...].astype(f32) + self.above[...].astype(f32))

    def drain(self):
        pl.when(self.z < 3)(lambda: self.rise(self.own).wait_send())
        pl.when(self.z > 0)(lambda: self.sink(self.own).wait_send())


def back_one(q, g, window_ref, proj, prefix, attended_grad, bias, bias_grad, pads, slots):
    base, begin, end = question(window_ref, q)
    cost = key_cost(begin, end)
    rows = pl.ds(base, WIN)
    cols = slice(g * GW, (g + 1) * GW)
    heads = slice(g * GROUP * WIN, (g + 1) * GROUP * WIN)
    row = lax.broadcasted_iota(jnp.int32, (WIN, GW), 0)
    stack = stack_heads(proj[0, rows, cols] * bf16(DH**-0.5))
    keys = key_tile(proj[1, rows, cols], prefix[0, q, :, cols], prefix[1, q, :, cols])
    values = key_tile(proj[2, rows, cols], prefix[2, q, :, cols], prefix[3, q, :, cols])
    grad = attended_grad[rows, cols]
    grads = stack_heads(jnp.where((row >= begin) & (row < end), grad, jnp.zeros_like(grad)))
    soft = soft_rows(stack, keys, bias[heads, :], cost)
    prob_grad = mm(grads, values, NT)
    weighted = soft * prob_grad
    low = (weighted - soft * jnp.sum(weighted, axis=1, keepdims=True)).astype(bf16)
    bias_grad[heads, :] += low.astype(f32)
    key_grad = mm(low, stack, TN).astype(bf16)
    value_grad = mm(soft.astype(bf16), grads, TN).astype(bf16)
    pads[0, q] = (merge_heads(mm(low, keys)) * DH**-0.5).astype(bf16)
    pads[1, q] = key_grad[:WIN]
    pads[2, q] = value_grad[:WIN]
    for s in range(2):
        part = slice(WIN + s * SLOT, WIN + (s + 1) * SLOT)
        slots[s, q, :, cols] = key_grad[part]
        slots[2 + s, q, :, cols] = value_grad[part]


def table_sums(bias_grad, idx_ref, select_ref):
    lane = lax.broadcasted_iota(jnp.int32, (H, KEYS), 1)
    sums = jnp.zeros((H, KEYS), f32)
    for i in range(WIN):
        line = jnp.where(lane < WIN, bias_grad[pl.ds(i, H, stride=WIN), :], 0.0)
        sums += line if i == 0 else pltpu.roll(line, KEYS - i, 1)
    sums = jnp.concatenate([sums, jnp.zeros((16 - H, KEYS), f32)], axis=0)
    wide = lax.dot_general(
        sums, entry_hot(idx_ref).astype(f32), NT, precision=lax.Precision.HIGHEST, preferred_element_type=f32
    )
    return jnp.sum(jnp.where(select_ref[...] > 0, wide, 0.0), axis=0, keepdims=True)


def backward_part_kernel(
    window_ref, piece_ref, back_ref, idx_ref, select_ref, gains_ref, gain_grad_ref, down_ref,
    normed_hbm, proj_hbm, prefix_hbm, picked_hbm, attended_grad_hbm, after_grad_hbm, hidden_hbm,
    qkv_hbm, prefix_w_hbm, in_grad_hbm, out_grad_hbm,
    hidden_grad_hbm, memory_grad_ref, gain_one_ref, gain_two_ref, table_ref,
    qkv_out, attn_out, in_out, down_out, prefix_out,
    normed, proj, prefix, picked, attended_grad, after, pads, tokens, slots, bias, bias_grad, picked_grad,
    own, rc, rd, re, rx, ry, fat, fat_rc, fat_rd, fat_re, fat_rx, fat_ry,
    down_up, down_down, below, above, fat_below, fat_above, small, small_in, small_z,
    send, recv, z_send, z_recv, small_send, small_recv, io_sem, out_sem,
):
    place = Place()
    z = place.z
    length, width = normed.shape
    steps = length // TILE
    groups = width // GW
    eighth = width // 8

    def io(k, src, dst):
        return pltpu.make_async_copy(src, dst, io_sem.at[k])

    load_own = [io(k, in_grad_hbm.at[k, :, place.c], own.at[k]) for k in range(4)] + [
        io(4, out_grad_hbm.at[:, place.c], own.at[4])
    ]
    load_proj, load_prefix = io(5, proj_hbm, proj), io(6, prefix_hbm, prefix)
    load_grad, load_normed = io(7, attended_grad_hbm, attended_grad), io(8, normed_hbm, normed)
    load_picked, load_after = io(9, picked_hbm, picked), io(10, after_grad_hbm, after)
    for copy in [load_proj, load_prefix, load_grad] + load_own + [load_normed, load_picked, load_after]:
        copy.start()

    barrier = pltpu.get_barrier_semaphore()
    for o in ((0, 0, 1), (0, 1, 0), (1, 0, 0)):
        pl.semaphore_signal(barrier, inc=1, device_id={"fsdp": place.at(*o)}, device_id_type=MESH)

    @pl.when(z > 0)
    def _():
        pl.semaphore_signal(barrier, inc=1, device_id={"dp": z - 1}, device_id_type=MESH)

    @pl.when(z < 3)
    def _():
        pl.semaphore_signal(barrier, inc=1, device_id={"dp": z + 1}, device_id_type=MESH)

    table_bias(gains_ref, idx_ref, select_ref, bias)
    bias_grad[...] = jnp.zeros_like(bias_grad)
    pl.semaphore_wait(barrier, 5 - (z // 3) - (3 - z) // 3)

    bufs = (rc, rd, re, rx, ry)
    fat_bufs = (fat_rc, fat_rd, fat_re, fat_rx, fat_ry)
    plain = [Scatter(place, in_grad_hbm.at[u, :, 1 - place.c], own.at[u], bufs, u, send.at[u], recv.at[u]) for u in range(4)]
    plain.append(Scatter(place, out_grad_hbm.at[:, 1 - place.c], own.at[4], bufs, 4, send.at[4], recv.at[4]))
    thick = [
        Scatter(place, fat.at[g, :, 1 - place.c], fat.at[g, :, place.c], fat_bufs, g, send.at[5 + g], recv.at[5 + g])
        for g in range(groups)
    ]
    down_lines = [
        Line(place, down_ref.at[u], below.at[5 + u], above.at[5 + u], down_up.at[u], down_down.at[u], 5 + u, z_send, z_recv)
        for u in range(4)
    ]
    plain_lines = [
        Line(place, s.mine(0, 0), below.at[u], above.at[u], rx.at[u], ry.at[u], u, z_send, z_recv) for u, s in enumerate(plain)
    ]
    thick_lines = [
        Line(place, s.mine(0, 0), fat_below.at[g], fat_above.at[g], fat_rx.at[g], fat_ry.at[g], 9 + g, z_send, z_recv)
        for g, s in enumerate(thick)
    ]

    def each(items, name):
        for item in items:
            getattr(item, name)()

    def settle(scatters, lines):
        for s, line in zip(scatters, lines):
            s.settle()
            line.start()

    each(plain, "core")
    each(down_lines, "start")
    for copy in (load_proj, load_prefix, load_grad):
        copy.wait()

    def attend_back_some(g, first, count):
        loop(count, lambda q: back_one(q + first, g, window_ref, proj, prefix, attended_grad, bias, bias_grad, pads, slots))

    def unit_grads(g):
        cols = slice(g * GW, (g + 1) * GW)
        loop(
            length // BLOCK,
            lambda b: unpad(
                b, piece_ref, [pads.at[s] for s in range(3)], [tokens.at[s, :, cols] for s in range(3)]
            ),
        )
        flat = picked[...].reshape(QPR * SLOT, width)

        def qkv_unit(s):
            part = mm(normed[...], tokens[s, :, cols], TN).astype(bf16)
            fat[g, :, :, :, pl.ds(pl.multiple_of(s * GW, GW), GW)] = part.reshape(4, 2, eighth, GW)

        def prefix_unit(s):
            part = mm(flat, slots[s, :, :, cols].reshape(QPR * SLOT, GW), TN).astype(bf16)
            fat[g, :, :, :, pl.ds(pl.multiple_of((3 + s) * GW, GW), GW)] = part.reshape(4, 2, eighth, GW)

        loop(3, qkv_unit)
        loop(4, prefix_unit)

    def keep_fat(g):
        return [
            pltpu.make_async_copy(
                fat_rc.at[g, 0, :, s * GW : (s + 1) * GW],
                (qkv_out if s < 3 else prefix_out).at[:, pl.ds((s % 3 if s < 3 else s - 3) * width + g * GW, GW)],
                out_sem.at[9 + 7 * g + s],
            )
            for s in range(7)
        ]

    def store_fat(g):
        fat_rc[g, 0] = thick_lines[g].total().astype(bf16)
        for copy in keep_fat(g):
            copy.start()

    keep_plain = [
        pltpu.make_async_copy(rc.at[u, 0], in_out.at[:, u * width : (u + 1) * width], out_sem.at[u]) for u in range(4)
    ]
    keep_plain.append(pltpu.make_async_copy(rc.at[4, 0], attn_out, out_sem.at[4]))
    keep_down = [
        pltpu.make_async_copy(down_up.at[u], down_out.at[u * eighth : (u + 1) * eighth, :], out_sem.at[5 + u])
        for u in range(4)
    ]

    half = QPR // 2
    attend_back_some(0, 0, half)
    for copy in load_own:
        copy.wait()
    each(plain, "fold")
    each(down_lines, "near")
    attend_back_some(0, half, half)
    each(plain, "relay")
    each(down_lines, "far")
    load_normed.wait()
    load_picked.wait()
    unit_grads(0)
    thick[0].core()
    attend_back_some(1, 0, half)
    settle(plain, plain_lines)
    thick[0].fold()
    attend_back_some(1, half, half)
    thick[0].relay()
    each(plain_lines, "near")
    for u in range(4):
        total = down_lines[u].total().astype(bf16)
        down_lines[u].drain()
        down_up[u] = total
        keep_down[u].start()
    unit_grads(1)
    thick[1].core()
    attend_back_some(2, 0, half)
    settle(thick[0:1], thick_lines[0:1])
    thick[1].fold()
    each(plain_lines, "far")
    attend_back_some(2, half, half)
    load_qkv = io(5, qkv_hbm, proj.at[:, 0:width, :])
    load_qkv.start()
    thick[1].relay()
    thick_lines[0].near()
    unit_grads(2)
    thick[2].core()
    hidden = normed
    load_hidden = io(8, hidden_hbm, hidden)
    load_hidden.start()
    for u in range(5):
        rc[u, 0] = plain_lines[u].total().astype(bf16)
        keep_plain[u].start()
    load_after.wait()
    load_hidden.wait()
    load_qkv.wait()
    row = lax.broadcasted_iota(jnp.int32, (8, width), 0)
    small[0] = jnp.where(row == 1, gain_grad_ref[0:1, :], 0.0)
    small[0, 2:3, 0 : NB * H] = table_sums(bias_grad, idx_ref, select_ref)
    gain = gains_ref[0:1, :]

    def hidden_back(i):
        rows = rows_of(i)
        grad = mm(tokens[0, rows, :], proj[0, 0:width, :], NT)
        for s in range(1, 3):
            grad += mm(tokens[s, rows, :], proj[s, 0:width, :], NT)
        values = hidden[rows, :].astype(f32)
        scale = lax.rsqrt(jnp.mean(values * values, axis=1, keepdims=True) + epsilon)
        unit = values * scale
        small[0, 0:1, :] += jnp.sum(grad * unit, axis=0, keepdims=True)
        pulled = grad * gain
        after[rows, :] += scale * (pulled - unit * jnp.mean(pulled * unit, axis=1, keepdims=True))

    loop(steps // 2, hidden_back)
    settle(thick[1:2], thick_lines[1:2])
    thick[2].fold()
    thick_lines[0].far()
    loop(steps - steps // 2, lambda i: hidden_back(i + steps // 2))
    keep_hidden = io(10, after, hidden_grad_hbm)
    keep_hidden.start()
    thick[2].relay()
    thick_lines[1].near()

    def swap(k, o):
        return pltpu.make_async_remote_copy(
            src_ref=small.at[k], dst_ref=small_in.at[k], send_sem=small_send.at[k], recv_sem=small_recv.at[k],
            device_id={"fsdp": place.at(*o)}, device_id_type=MESH,
        )

    swaps = [swap(0, (0, 0, 1)), swap(1, (0, 1, 0)), swap(2, (1, 0, 0))]
    swaps[0].start()
    load_prefix_w = [io(5 + s, prefix_w_hbm.at[s], proj.at[s, 0:width, :]) for s in range(3)]
    load_prefix_w.append(io(9, prefix_w_hbm.at[3], attended_grad.at[0:width, :]))
    for copy in load_prefix_w:
        copy.start()
    store_fat(0)
    swaps[0].wait_recv()
    small[1] = small[0] + small_in[0]
    swaps[1].start()
    for copy in load_prefix_w:
        copy.wait()
    total = mm(slots[3].reshape(QPR * SLOT, width), attended_grad[0:width, :], NT)
    for s in range(3):
        total += mm(slots[s].reshape(QPR * SLOT, width), proj[s, 0:width, :], NT)
    picked_grad[...] = total.reshape(QPR, SLOT, width)
    for m in range(QPR):
        memory_grad_ref[m] = picked_grad[back_ref[m], 0:PAIRS, :]
    swaps[1].wait_recv()
    small[2] = small[1] + small_in[1]
    swaps[2].start()
    settle(thick[2:3], thick_lines[2:3])
    thick_lines[1].far()
    swaps[2].wait_recv()
    small[3] = small[2] + small_in[2]
    small_line = Line(
        place, small.at[3], small_z.at[0], small_z.at[1], small_z.at[2], small_z.at[3], 12, z_send, z_recv
    )
    small_line.start()
    small_line.near()
    thick_lines[2].near()
    store_fat(1)
    small_line.far()
    thick_lines[2].far()
    sums = small_line.total()
    shift = lax.rem(8 - place.me, 8)
    wide_roll = pltpu.roll(sums, shift * eighth, 1)
    gain_one_ref[...] = wide_roll[0:1, 0:eighth]
    gain_two_ref[...] = wide_roll[1:2, 0:eighth]
    entries = NB * H // 8
    table_roll = pltpu.roll(sums, lax.rem(width - place.me * entries, width), 1)
    table_ref[...] = table_roll[2:3, 0:entries]
    store_fat(2)
    keep_hidden.wait()
    each(plain + thick, "drain")
    each(plain_lines + thick_lines + [small_line], "drain")
    for copy in keep_plain + keep_down + [c for g in range(groups) for c in keep_fat(g)]:
        copy.wait()
    for copy in swaps:
        copy.wait_send()


def backward_part(
    windows, pieces, back, idx, select, gains, gain_grad, down_share,
    normed, proj, prefix, picked, attended_grad, after_grad, hidden, qkv, prefix_w, in_grad, out_grad,
):
    length, width = hidden.shape
    eighth = width // 8
    groups = width // GW
    thick = 7 * GW
    sds = jax.ShapeDtypeStruct
    vm = lambda shape, dtype=bf16: pltpu.VMEM(shape, dtype)
    return pl.pallas_call(
        backward_part_kernel,
        out_shape=(
            sds((length, width), f32),
            sds((QPR, PAIRS, width), f32),
            sds((1, eighth), f32),
            sds((1, eighth), f32),
            sds((1, NB * H // 8), f32),
            sds((eighth, 3 * width), bf16),
            sds((eighth, width), bf16),
            sds((eighth, 4 * width), bf16),
            sds((4 * eighth, width), bf16),
            sds((eighth, 4 * width), bf16),
        ),
        in_specs=[SMEM] * 3 + [VMEM] * 5 + [ANY] * 11,
        out_specs=(ANY,) + (VMEM,) * 4 + (ANY,) * 5,
        scratch_shapes=[
            vm((length, width)),
            vm((3, length, width)),
            vm((4, QPR, SLOT, width)),
            vm((QPR, SLOT, width)),
            vm((length, width)),
            vm((length, width), f32),
            vm((3, QPR, WIN, GW)),
            vm((3, length, width)),
            vm((4, QPR, SLOT, width)),
            vm((H * WIN, KEYS), f32),
            vm((H * WIN, KEYS), f32),
            vm((QPR, SLOT, width), f32),
            vm((5, 4, eighth, width)),
            vm((5, 4, eighth, width)),
            vm((5, eighth // 2, width)),
            vm((5, eighth // 2, width)),
            vm((5, eighth, width)),
            vm((5, eighth, width)),
            vm((groups, 4, 2, eighth, thick)),
            vm((groups, 4, eighth, thick)),
            vm((groups, eighth // 2, thick)),
            vm((groups, eighth // 2, thick)),
            vm((groups, eighth, thick)),
            vm((groups, eighth, thick)),
            vm((4, eighth, width)),
            vm((4, eighth, width)),
            vm((9, eighth, width)),
            vm((9, eighth, width)),
            vm((groups, eighth, thick)),
            vm((groups, eighth, thick)),
            vm((4, 8, width), f32),
            vm((3, 8, width), f32),
            vm((4, 8, width), f32),
            pltpu.SemaphoreType.DMA((8, Scatter.COPIES)),
            pltpu.SemaphoreType.DMA((8, Scatter.COPIES)),
            pltpu.SemaphoreType.DMA((13, 2)),
            pltpu.SemaphoreType.DMA((13, 2)),
            pltpu.SemaphoreType.DMA((3,)),
            pltpu.SemaphoreType.DMA((3,)),
            pltpu.SemaphoreType.DMA((11,)),
            pltpu.SemaphoreType.DMA((9 + 7 * groups,)),
        ],
        compiler_params=pltpu.CompilerParams(
            collective_id=1, has_side_effects=True, vmem_limit_bytes=62 << 20
        ),
        name="backward_part",
    )(
        windows, pieces, back, idx, select, gains, gain_grad, down_share,
        normed, proj, prefix, picked, attended_grad, after_grad, hidden, qkv, prefix_w,
        in_grad.reshape(-1, 4, 2, eighth, width), out_grad.reshape(4, 2, eighth, width),
    )


def rms_scale(values, norm_gain):
    return (
        values * lax.rsqrt(jnp.mean(values * values, axis=-1, keepdims=True) + epsilon) * norm_gain
    )


def prefix_kernel(row_ref, memory_ref, w_ref, picked_ref, prefix_ref):
    width = w_ref.shape[0]
    for q in range(QPR):
        picked_ref[q] = memory_ref[row_ref[q]]
    picked = picked_ref[...].reshape(QPR * SLOT, width)
    for at in range(0, w_ref.shape[1], width):
        part = mm(picked, w_ref[:, at : at + width]).astype(bf16)
        prefix_ref[:, :, at : at + width] = part.reshape(QPR, SLOT, width)


def make_prefix(chosen, memory, w_prefix):
    padded = jnp.pad(memory, ((0, 0), (0, SLOT - PAIRS), (0, 0)))
    return pl.pallas_call(
        prefix_kernel,
        out_shape=(
            jax.ShapeDtypeStruct(padded.shape, bf16),
            jax.ShapeDtypeStruct((QPR, SLOT, w_prefix.shape[1]), bf16),
        ),
        in_specs=[SMEM, VMEM, VMEM],
        out_specs=(VMEM, VMEM),
        compiler_params=pltpu.CompilerParams(vmem_limit_bytes=40 << 20),
        name="make_prefix",
    )(chosen, padded, w_prefix)


def memory_kernel(row_ref, slot_ref, w_ref, out_ref, held):
    width = w_ref.shape[0]
    slots = slot_ref[...].reshape(QPR * SLOT, w_ref.shape[1])
    held[...] = mm(slots, w_ref[...], NT).reshape(QPR, SLOT, width)
    for q in range(QPR):
        out_ref[row_ref[q]] = held[q, :PAIRS, :]


def memory_back(chosen, slot_grad, w_prefix):
    width = w_prefix.shape[0]
    return pl.pallas_call(
        memory_kernel,
        out_shape=jax.ShapeDtypeStruct((QPR, PAIRS, width), f32),
        in_specs=[SMEM, VMEM, VMEM],
        out_specs=VMEM,
        scratch_shapes=[pltpu.VMEM((QPR, SLOT, width), f32)],
        compiler_params=pltpu.CompilerParams(vmem_limit_bytes=40 << 20),
        name="memory_back",
    )(chosen, slot_grad, w_prefix)


def plain_row_pass(hidden, segments, memory, chosen, buckets, cotangent, full):
    attn_gain, ffn_gain, rel_table, w_qkv, w_attn_out, w_in, w_down, w_prefix = full
    length, width = hidden.shape
    starts = row_starts(segments)
    idx = near_buckets(buckets, length)
    table = jnp.pad(rel_table.reshape(NB, H).T, ((0, 16 - H), (0, 0)))
    tokens = hidden.astype(f32)
    gain_one = attn_gain.astype(f32)
    gain_two = ffn_gain.astype(f32)

    normed = rms_scale(tokens, gain_one).astype(bf16)
    projected = mm(normed, w_qkv).astype(bf16)
    picked, prefix = make_prefix(chosen, memory, w_prefix)
    attended = attend(starts, projected, prefix, table, idx)
    after_attn = tokens + mm(attended, w_attn_out)
    normed_ffn = rms_scale(after_attn, gain_two).astype(bf16)
    hidden_pre = mm(normed_ffn, w_in)
    activation = jax.nn.gelu(hidden_pre).astype(bf16)
    output = (after_attn + mm(activation, w_down)).astype(bf16)

    grad_out = cotangent.astype(f32)
    down_grad = mm(activation, cotangent, TN)
    act_grad = mm(cotangent, w_down, NT)
    pre_grad = jax.vjp(jax.nn.gelu, hidden_pre)[1](act_grad)[0].astype(bf16)
    in_grad = mm(normed_ffn, pre_grad, TN)
    normed_ffn_grad = mm(pre_grad, w_in, NT)
    residual_part, ffn_gain_grad = jax.vjp(rms_scale, after_attn, gain_two)[1](normed_ffn_grad)
    after_grad = grad_out + residual_part
    attn_branch = after_grad.astype(bf16)
    attn_out_grad = mm(attended, attn_branch, TN)
    attended_grad = mm(attn_branch, w_attn_out, NT).astype(bf16)
    token_grad, slot_grad, table_grad = attend_back(
        starts, projected, prefix, attended_grad, table, idx
    )
    qkv_grad = mm(normed, token_grad, TN)
    normed_grad = mm(token_grad, w_qkv, NT)
    flat = (QPR * SLOT, -1)
    prefix_grad = mm(picked.reshape(flat), slot_grad.reshape(flat), TN)
    memory_grad = memory_back(chosen, slot_grad, w_prefix)
    norm_part, attn_gain_grad = jax.vjp(rms_scale, tokens, gain_one)[1](normed_grad)
    hidden_grad = after_grad + norm_part
    small = jnp.concatenate([attn_gain_grad, ffn_gain_grad, table_grad[:, :H].reshape(NB * H)])
    return output, hidden_grad, memory_grad, small, (qkv_grad, attn_out_grad, in_grad, down_grad, prefix_grad)


def near_row_pass(hidden, segments, memory, chosen, buckets, cotangent, shards):
    attn_gain, ffn_gain, rel_table, w_qkv, w_attn_out, w_in, w_down, w_prefix = shards
    length, width = hidden.shape
    windows, pieces = layout_tables(segments)
    idx, select = near_buckets(buckets, length), head_select()
    padded = jnp.pad(memory, ((0, 0), (0, SLOT - PAIRS), (0, 0)))
    (
        output, normed, proj, prefix, picked, gains, ffn_gain_grad, attended_grad, after_grad,
        full_qkv, full_prefix, in_grad, attn_out_grad, down_share,
    ) = forward_part(
        windows, pieces, chosen, padded,
        pack_small(attn_gain, ffn_gain, rel_table, width), idx, select,
        hidden, cotangent, w_qkv, w_prefix, w_attn_out, w_in, w_down,
    )
    ids = jnp.arange(QPR, dtype=jnp.int32)
    back = jnp.sum(jnp.where(chosen[None, :] == ids[:, None], ids[None, :], 0), axis=1)
    return (output,) + tuple(
        backward_part(
            windows, pieces, back, idx, select, gains, ffn_gain_grad, down_share, normed, proj, prefix, picked,
            attended_grad, after_grad, hidden, full_qkv, full_prefix, in_grad, attn_out_grad,
        )
    )


def near_local(
    hidden, segment_ids, memory, memory_row, buckets, attn_gain, ffn_gain, rel_table,
    w_qkv, w_attn_out, w_in, w_down, w_prefix, cotangent,
):
    shards = (attn_gain, ffn_gain, rel_table, w_qkv, w_attn_out, w_in, w_down, w_prefix)
    output, hidden_grad, memory_grad, *rest = near_row_pass(
        hidden[0], segment_ids[0], memory[0], memory_row[0], buckets, cotangent[0], shards
    )
    return (output[None], hidden_grad[None], memory_grad[None]) + tuple(x[0] for x in rest[:3]) + tuple(
        x.astype(f32) for x in rest[3:]
    )


def plain_local(
    hidden, segment_ids, memory, memory_row, buckets, attn_gain, ffn_gain, rel_table,
    w_qkv, w_attn_out, w_in, w_down, w_prefix, cotangent,
):
    sizes = (attn_gain.shape[0], ffn_gain.shape[0], rel_table.shape[0])
    small = lax.all_gather(jnp.concatenate([attn_gain, ffn_gain, rel_table]), "fsdp", axis=0)
    cuts = (0, sizes[0], sizes[0] + sizes[1], sum(sizes))
    full = tuple(small[:, cuts[i] : cuts[i + 1]].reshape(-1) for i in range(3)) + tuple(
        lax.all_gather(w, "fsdp", axis=0, tiled=True)
        for w in (w_qkv, w_attn_out, w_in, w_down, w_prefix)
    )
    outs = []
    total = None
    for r in range(hidden.shape[0]):
        *own, small_grad, grads = plain_row_pass(
            hidden[r], segment_ids[r], memory[r], memory_row[r], buckets, cotangent[r], full
        )
        outs.append(own)
        fresh = (small_grad,) + grads
        total = fresh if total is None else jax.tree.map(jnp.add, total, fresh)
    output, hidden_grad, memory_grad = (jnp.stack(x) for x in zip(*outs))
    small_grad = lax.psum(total[0], ("fsdp", "dp"))
    me = lax.axis_index("fsdp")
    bases = (0, full[0].shape[0], full[0].shape[0] + full[1].shape[0])
    shares = [
        lax.dynamic_slice_in_dim(small_grad, base + me * size, size) for base, size in zip(bases, sizes)
    ]
    for gradient in total[1:]:
        share = lax.psum_scatter(
            gradient.astype(bf16), "fsdp", scatter_dimension=0, tiled=True
        )
        shares.append(lax.psum(share, "dp").astype(f32))
    return (output, hidden_grad, memory_grad) + tuple(shares)


def solution(mesh):
    rows = ("fsdp", "dp")
    placed = (
        P(rows, None, None), P(rows, None), P(rows, None, None, None), P(rows, None), P(),
        P("fsdp"), P("fsdp"), P("fsdp"),
        P("fsdp", None), P("fsdp", None), P("fsdp", None), P("fsdp", None), P("fsdp", None),
        P(rows, None, None),
    )
    near = mesh.shape["fsdp"] == 8 and mesh.shape["dp"] == 4
    return jax.shard_map(
        near_local if near else plain_local,
        mesh=mesh,
        in_specs=placed,
        out_specs=(
            P(rows, None, None), P(rows, None, None), P(rows, None, None, None),
            P("fsdp"), P("fsdp"), P("fsdp"),
            P("fsdp", None), P("fsdp", None), P("fsdp", None), P("fsdp", None), P("fsdp", None),
        ),
        check_vma=False,
    )
```

```python
import functools
import jax
import jax.numpy as jnp
from jax import lax
from jax.experimental import pallas as pl
from jax.experimental.pallas import tpu as pltpu
from jax.sharding import PartitionSpec as P

H = 12
DH = 64
NB = 32
QLEN = 64
QPR = 20
PAIRS = 10

WIN = 96
SLOT = 16
KEYS = WIN + 2 * SLOT
GROUP = 4
GW = GROUP * DH
STACK = GROUP * WIN
TILE = 256
BLOCK = 16
SPAN = 5
OVERLAP = 6

epsilon = 1e-06
masked_out = -1e30
f32 = jnp.float32
bf16 = jnp.bfloat16
NT = (((1,), (1,)), ((), ()))
TN = (((0,), (0,)), ((), ()))
MESH = pl.DeviceIdType.MESH
ANY = pl.BlockSpec(memory_space=pl.ANY)
SMEM = pl.BlockSpec(memory_space=pltpu.SMEM)
VMEM = pl.BlockSpec(memory_space=pltpu.VMEM)


def mm(a, b, dims=(((1,), (0,)), ((), ()))):
    return lax.dot_general(a, b, dims, preferred_element_type=f32)


def row_starts(segments):
    ids = jnp.arange(QPR + 1, dtype=jnp.int32)
    return jnp.sum((segments[None, :] < ids[:, None]).astype(jnp.int32), axis=1)


def near_buckets(buckets, length):
    back = buckets[length - QLEN : length][::-1]
    ahead = buckets[length : length + QLEN - 1][::-1]
    return jnp.concatenate([back, buckets[length - 1 : length], ahead])[None, :]


def head_select():
    entry = jnp.arange(NB * H, dtype=jnp.int32)[None, :]
    head = jnp.arange(16, dtype=jnp.int32)[:, None]
    return (entry % H == head).astype(f32)


def pack_small(attn_gain, ffn_gain, rel_table, width):
    lines = [jnp.pad(v.astype(f32), (0, width - v.shape[0])) for v in (attn_gain, ffn_gain, rel_table)]
    return jnp.concatenate([jnp.stack(lines), jnp.zeros((5, width), f32)])


def loop(n, body, unroll=1):
    def step(i, carry):
        body(i)
        return carry

    lax.fori_loop(0, n, step, 0, unroll=unroll)


def each(items, name):
    for item in items:
        getattr(item, name)()


def rows_of(i):
    return pl.ds(pl.multiple_of(i * TILE, TILE), TILE)


class Place:
    def __init__(self):
        me = lax.axis_index("fsdp")
        self.me, self.c, self.x, self.y = me, me % 2, (me // 2) % 2, me // 4
        self.z = lax.axis_index("dp")

    def at(self, dy, dx, dc):
        return 4 * ((self.y + dy) % 2) + 2 * ((self.x + dx) % 2) + (self.c + dc) % 2


OTHERS = [(dy, dx, dc) for dy in (0, 1) for dx in (0, 1) for dc in (0, 1)][1:]


def greet(peers):
    barrier = pltpu.get_barrier_semaphore()
    for peer in peers:
        pl.semaphore_signal(barrier, inc=1, device_id=peer, device_id_type=MESH)
    pl.semaphore_wait(barrier, len(peers))


class Gather:
    COPIES = 8

    def __init__(self, place, shard, full, down, k, send, recv, own_sem, share=(0, 1)):
        self.p, self.shard, self.full, self.down = place, shard, full, down
        self.send, self.recv, self.own_sem = send.at[k], recv.at[k], own_sem.at[k]
        self.all_rows = shard.shape[0]
        self.rows = self.all_rows // share[1]
        self.skip = share[0] * self.rows
        self.half = self.rows // 2

    def piece(self, dy, dx, dc, part=None):
        f = self.p.at(dy, dx, dc)
        begin = (f % 2 if self.down else f) * self.all_rows + self.skip
        size = self.rows
        if part is not None:
            begin, size = begin + part * self.half, self.half
        if len(self.full.shape) == 5:
            rows = slice(None) if part is None else pl.ds(part * self.half, self.half)
            return self.full.at[:, f // 2, f % 2, rows, :]
        rows = pl.ds(pl.multiple_of(begin, 16), size)
        return self.full.at[f // 2, rows, :] if self.down else self.full.at[:, rows, :]

    def copy(self, k, src, dst, dy, dx, dc):
        return pltpu.make_async_remote_copy(
            src_ref=src, dst_ref=dst, send_sem=self.send.at[k], recv_sem=self.recv.at[k],
            device_id={"fsdp": self.p.at(dy, dx, dc)}, device_id_type=MESH,
        )

    def own(self):
        if self.down:
            return [
                pltpu.make_async_copy(
                    self.shard.at[pl.ds(self.skip, self.rows), :], self.piece(0, 0, 0), self.own_sem.at[0]
                )
            ]
        width = self.full.shape[-1]
        return [
            pltpu.make_async_copy(
                self.shard.at[:, s * width : (s + 1) * width], self.piece(0, 0, 0).at[s], self.own_sem.at[s]
            )
            for s in range(self.full.shape[0])
        ]

    def load(self):
        for copy in self.own():
            copy.start()

    def first(self):
        for copy in self.own():
            copy.wait()
        mine = self.piece(0, 0, 0)
        self.copy(0, mine, mine, 0, 1, 0).start()
        self.copy(1, mine, mine, 1, 0, 0).start()
        self.copy(2, mine, mine, 0, 0, 1).start()

    def landed(self, k, piece):
        self.copy(k, piece, piece, 0, 0, 1).wait_recv()

    def relay(self):
        from_x, from_y = self.piece(0, 1, 0), self.piece(1, 0, 0)
        self.landed(0, from_x)
        top = self.piece(0, 1, 0, 0)
        self.copy(3, top, top, 1, 0, 0).start()
        self.copy(4, from_x, from_x, 0, 0, 1).start()
        self.landed(1, from_y)
        low = self.piece(1, 0, 0, 1)
        self.copy(5, low, low, 0, 1, 0).start()
        self.copy(6, from_y, from_y, 0, 0, 1).start()

    def last(self):
        self.landed(3, self.piece(1, 1, 0, 0))
        self.landed(5, self.piece(1, 1, 0, 1))
        far = self.piece(1, 1, 0)
        self.copy(7, far, far, 0, 0, 1).start()

    def finish(self):
        self.landed(2, self.piece(0, 0, 1))
        self.landed(4, self.piece(0, 1, 1))
        self.landed(6, self.piece(1, 0, 1))
        self.landed(7, self.piece(1, 1, 1))

    def drain(self):
        whole, part = self.piece(0, 0, 0), self.piece(0, 0, 0, 0)
        for k in range(self.COPIES):
            src = part if k in (3, 5) else whole
            self.copy(k, src, src, 0, 0, 1).wait_send()


class Scatter:
    COPIES = 7

    def __init__(self, place, other, own, bufs, u, send, recv):
        self.p, self.other, self.own = place, other, own
        self.rc, self.rd, self.re, self.rx, self.ry = bufs if u is None else (b.at[u] for b in bufs)
        self.send, self.recv = send, recv
        self.half = self.rd.shape[0]

    def mine(self, dy, dx):
        return self.own.at[2 * ((self.p.y + dy) % 2) + (self.p.x + dx) % 2]

    def copy(self, k, src, dst, dy, dx, dc):
        return pltpu.make_async_remote_copy(
            src_ref=src, dst_ref=dst, send_sem=self.send.at[k], recv_sem=self.recv.at[k],
            device_id={"fsdp": self.p.at(dy, dx, dc)}, device_id_type=MESH,
        )

    def part(self, k):
        low, high = pl.ds(0, self.half), pl.ds(self.half, self.half)
        if k == 0:
            return self.copy(0, self.other, self.rc, 0, 0, 1)
        if k == 1:
            return self.copy(1, self.mine(1, 1).at[low], self.rd, 0, 1, 0)
        if k == 2:
            return self.copy(2, self.mine(1, 1).at[high], self.re, 1, 0, 0)
        if k == 3:
            return self.copy(3, self.mine(0, 1).at[low], self.rx.at[low], 0, 1, 0)
        if k == 4:
            return self.copy(4, self.mine(1, 0).at[high], self.ry.at[high], 1, 0, 0)
        if k == 5:
            return self.copy(5, self.mine(0, 1).at[high], self.rx.at[high], 0, 1, 0)
        return self.copy(6, self.mine(1, 0).at[low], self.ry.at[low], 1, 0, 0)

    def core(self):
        self.part(0).start()

    def fold(self):
        self.part(0).wait_recv()
        self.own[...] = (self.own[...].astype(f32) + self.rc[...].astype(f32)).astype(bf16)
        for k in (1, 2, 3, 4):
            self.part(k).start()

    def relay(self):
        low, high = pl.ds(0, self.half), pl.ds(self.half, self.half)
        nx, ny = self.mine(0, 1).at[high], self.mine(1, 0).at[low]
        self.part(1).wait_recv()
        ny[...] = (ny[...].astype(f32) + self.rd[...].astype(f32)).astype(bf16)
        self.part(6).start()
        self.part(2).wait_recv()
        nx[...] = (nx[...].astype(f32) + self.re[...].astype(f32)).astype(bf16)
        self.part(5).start()

    def total(self):
        for k in (3, 4, 5, 6):
            self.part(k).wait_recv()
        return self.mine(0, 0)[...].astype(f32) + (self.rx[...].astype(f32) + self.ry[...].astype(f32))

    def settle(self):
        total = self.total().astype(bf16)
        self.mine(0, 0)[...] = total

    def drain(self):
        for k in range(self.COPIES):
            self.part(k).wait_send()


GELU_A = 0.7978845608028654
GELU_B = 0.044715


def gelu_pair(v):
    square = v * v
    t = jnp.tanh(v * (GELU_A + (GELU_A * GELU_B) * square))
    half = 0.5 + 0.5 * t
    slope = half + (0.5 * v) * (1.0 - t * t) * (GELU_A + (3.0 * GELU_A * GELU_B) * square)
    return v * half, slope


def stack_heads(block):
    lane = lax.broadcasted_iota(jnp.int32, (1, GW), 1)
    parts = []
    for h in range(GROUP):
        mask = jnp.where((lane >= h * DH) & (lane < (h + 1) * DH), 1.0, 0.0).astype(bf16)
        parts.append(block * mask)
    return jnp.concatenate(parts, axis=0)


def merge_heads(stacked):
    lane = lax.broadcasted_iota(jnp.int32, (WIN, GW), 1)
    out = stacked[:WIN]
    for h in range(1, GROUP):
        out = jnp.where(lane >= h * DH, stacked[h * WIN : (h + 1) * WIN], out)
    return out


def key_tile(tokens, low, high):
    return jnp.concatenate([tokens, low, high], axis=0)


def key_cost(begin, end):
    row = lax.broadcasted_iota(jnp.int32, (KEYS, KEYS), 0)
    token = (row >= begin) & (row < end)
    first = (row >= WIN) & (row < WIN + PAIRS)
    second = (row >= WIN + SLOT) & (row < WIN + SLOT + PAIRS)
    return jnp.where(token | first | second, 0.0, masked_out).astype(f32)


def soft_columns(keys, stack, bias_block, cost):
    logits = mm(keys, stack, NT) + (bias_block + jnp.concatenate([cost] * (STACK // KEYS), axis=1))
    peak = jnp.max(logits, axis=0, keepdims=True)
    raw = jnp.exp(logits - peak)
    return raw * (1.0 / jnp.sum(raw, axis=0, keepdims=True))


def table_bias(gains, idx_ref, select_ref, bias):
    wide = jnp.where(select_ref[...] > 0, jnp.broadcast_to(gains[2:3, : NB * H], (16, NB * H)), 0.0)
    lines = mm(wide.astype(bf16), entry_hot(idx_ref))
    lane = lax.broadcasted_iota(jnp.int32, (WIN, KEYS), 1)
    for g in range(H // GROUP):
        blocks = []
        for h in range(g * GROUP, (g + 1) * GROUP):
            rolled = pltpu.roll(jnp.broadcast_to(lines[h : h + 1, :], (WIN, KEYS)), 0, 1, stride=1, stride_axis=0)
            blocks.append(jnp.where(lane < WIN, rolled, 0.0))
        bias[g] = jnp.concatenate(blocks, axis=0).T


def entry_hot(idx_ref):
    off = lax.broadcasted_iota(jnp.int32, (NB * H, KEYS), 0) - H * idx_ref[...]
    return jnp.where((off >= 0) & (off < H), 1.0, 0.0).astype(bf16)


def question(window_ref, q):
    return window_ref[3 * q] * BLOCK, window_ref[3 * q + 1], window_ref[3 * q + 2]


def attend_one(q, window_ref, proj, prefix, bias, pad):
    base, begin, end = question(window_ref, q)
    cost = key_cost(begin, end)
    rows = pl.ds(base, WIN)
    width = proj.shape[2]
    for g in range(width // GW):
        cols = slice(g * GW, (g + 1) * GW)
        stack = stack_heads(proj[0, rows, cols] * bf16(DH**-0.5))
        keys = key_tile(proj[1, rows, cols], prefix[0, q, :, cols], prefix[1, q, :, cols])
        values = key_tile(proj[2, rows, cols], prefix[2, q, :, cols], prefix[3, q, :, cols])
        soft = soft_columns(keys, stack, bias[g], cost).astype(bf16)
        pad[q, :, cols] = merge_heads(mm(soft, values, TN)).astype(bf16)


def back_one(q, g, window_ref, proj, prefix, attended_grad, bias, bias_grad, pads, slots):
    base, begin, end = question(window_ref, q)
    cost = key_cost(begin, end)
    rows = pl.ds(base, WIN)
    cols = slice(g * GW, (g + 1) * GW)
    row = lax.broadcasted_iota(jnp.int32, (WIN, GW), 0)
    stack = stack_heads(proj[0, rows, cols] * bf16(DH**-0.5))
    keys = key_tile(proj[1, rows, cols], prefix[0, q, :, cols], prefix[1, q, :, cols])
    values = key_tile(proj[2, rows, cols], prefix[2, q, :, cols], prefix[3, q, :, cols])
    grad = attended_grad[rows, cols]
    grads = stack_heads(jnp.where((row >= begin) & (row < end), grad, jnp.zeros_like(grad)))
    soft = soft_columns(keys, stack, bias[g], cost)
    prob_grad = mm(values, grads, NT)
    mean = jnp.sum(soft * prob_grad, axis=0, keepdims=True)
    low = (soft * (prob_grad - mean)).astype(bf16)
    bias_grad[g] += low.astype(f32)
    key_grad = mm(low, stack).astype(bf16)
    value_grad = mm(soft.astype(bf16), grads).astype(bf16)
    pads[0, q] = (merge_heads(mm(low, keys, TN)) * DH**-0.5).astype(bf16)
    pads[1, q] = key_grad[:WIN]
    pads[2, q] = value_grad[:WIN]
    for s in range(2):
        part = slice(WIN + s * SLOT, WIN + (s + 1) * SLOT)
        slots[s, q, :, cols] = key_grad[part]
        slots[2 + s, q, :, cols] = value_grad[part]


def table_sums(bias_grad, lines, idx_ref, select_ref):
    lane = lax.broadcasted_iota(jnp.int32, (H, KEYS), 1)
    for g in range(H // GROUP):
        lines[g * STACK : (g + 1) * STACK, :] = bias_grad[g].T
    sums = jnp.zeros((H, KEYS), f32)
    for i in range(WIN):
        line = jnp.where(lane < WIN, lines[pl.ds(i, H, stride=WIN), :], 0.0)
        sums += line if i == 0 else pltpu.roll(line, KEYS - i, 1)
    sums = jnp.concatenate([sums, jnp.zeros((16 - H, KEYS), f32)], axis=0)
    wide = lax.dot_general(
        sums, entry_hot(idx_ref).astype(f32), NT, precision=lax.Precision.HIGHEST, preferred_element_type=f32
    )
    return jnp.sum(jnp.where(select_ref[...] > 0, wide, 0.0), axis=0, keepdims=True)


def unpad(b, piece_ref, pads, outs):
    row = lax.broadcasted_iota(jnp.int32, (BLOCK, 1), 0)
    sums = [jnp.zeros((BLOCK, pad.shape[-1]), bf16) for pad in pads]
    for k in range(OVERLAP):
        at = 4 * (OVERLAP * b + k)
        q, off = piece_ref[at], piece_ref[at + 1] * BLOCK
        mine = (row >= piece_ref[at + 2]) & (row < piece_ref[at + 3])
        for s, pad in enumerate(pads):
            sums[s] = jnp.where(mine, pad[q, pl.ds(off, BLOCK), :], sums[s])
    for total, out in zip(sums, outs):
        out[pl.ds(pl.multiple_of(b * BLOCK, BLOCK), BLOCK), :] = total


def layout_tables(segments):
    length = segments.shape[0]
    starts = row_starts(segments)
    low, high = starts[:-1], starts[1:]
    base = jnp.minimum(low // BLOCK, (length - WIN) // BLOCK)
    windows = jnp.stack([base, low - BLOCK * base, high - BLOCK * base], axis=1).reshape(-1)
    at = jnp.arange(length // BLOCK, dtype=jnp.int32)[:, None] * BLOCK
    ids = jnp.arange(QPR, dtype=jnp.int32)
    q = jnp.sum((high[None, :] <= at).astype(jnp.int32), axis=1, keepdims=True)
    q = jnp.minimum(q + jnp.arange(OVERLAP, dtype=jnp.int32)[None, :], QPR - 1)
    hot = (q[:, :, None] == ids).astype(jnp.int32)
    pick = lambda v: jnp.sum(hot * v, axis=2)
    begin, end = jnp.clip(pick(low) - at, 0, BLOCK), jnp.clip(pick(high) - at, 0, BLOCK)
    off = jnp.clip(at // BLOCK - pick(base), 0, (WIN - BLOCK) // BLOCK)
    return windows, jnp.stack([q, off, begin, end], axis=2).reshape(-1)


def back_order(chosen):
    ids = jnp.arange(QPR, dtype=jnp.int32)
    return jnp.sum(jnp.where(chosen[None, :] == ids[:, None], ids[None, :], 0), axis=1)


def forward_part_kernel(
    window_ref, piece_ref, chosen_ref, memory_ref, small_ref, idx_ref, select_ref,
    hidden_hbm, cot_hbm, qkv_w, prefix_w, out_w, in_w, down_w,
    output_hbm, normed_hbm, proj_hbm, prefix_hbm, picked_hbm, gains_ref, gain_grad_ref,
    attended_grad_hbm, after_grad_hbm, qkv_hbm, prefix_w_hbm, out_grad_hbm, sums_ref,
    w_qkv, w_prefix, w_out, w_in, w_down, hidden, cot, normed, act, slope, prefix, picked, pad, attended,
    after, down_grads, bias, small_all,
    rc, rd, re, rx, ry, send, recv, g_send, g_recv, own_sem, small_send, small_recv, io_sem,
):
    place = Place()
    length, width = hidden.shape
    steps = length // TILE
    chunks = w_in.shape[0]
    proj = slope
    weights = ((qkv_w, w_qkv), (prefix_w, w_prefix), (out_w, w_out), (in_w, w_in))
    g_qkv, g_prefix, g_out, g_in = (
        Gather(place, shard, full, False, k, g_send, g_recv, own_sem) for k, (shard, full) in enumerate(weights)
    )
    g_down, g_rest = (
        Gather(place, down_w, w_down, True, 4 + k, g_send, g_recv, own_sem, (k, 2)) for k in range(2)
    )

    def io(k, src, dst):
        return pltpu.make_async_copy(src, dst, io_sem.at[k])

    load_hidden, load_cot = io(0, hidden_hbm, hidden), io(1, cot_hbm, cot)
    for g in (g_qkv, g_prefix, g_out, g_in, g_down, g_rest):
        g.load()
    load_hidden.start()
    load_cot.start()
    row = lax.broadcasted_iota(jnp.int32, small_ref.shape, 0)
    small_all[0] = jnp.where(
        row < 2,
        pltpu.roll(small_ref[...], place.me * (width // 8), 1),
        pltpu.roll(small_ref[...], place.me * (NB * H // 8), 1),
    )
    greet([{"fsdp": place.at(*o)} for o in OTHERS])

    def small_copy(k):
        return pltpu.make_async_remote_copy(
            src_ref=small_all.at[0], dst_ref=small_all.at[k + 1],
            send_sem=small_send.at[k], recv_sem=small_recv.at[k],
            device_id={"fsdp": place.at(*OTHERS[k])}, device_id_type=MESH,
        )

    for k in range(7):
        small_copy(k).start()
    g_qkv.first()
    g_prefix.first()
    load_hidden.wait()
    for q in range(QPR):
        picked[q] = memory_ref[chosen_ref[q]]
    keep_picked = io(2, picked, picked_hbm)
    keep_picked.start()
    for k in range(7):
        small_copy(k).wait_recv()
    gains_ref[...] = jnp.sum(small_all[...], axis=0)
    gain_one, gain_two = gains_ref[0:1, :], gains_ref[1:2, :]

    def norm(i):
        rows = rows_of(i)
        values = hidden[rows, :].astype(f32)
        scale = lax.rsqrt(jnp.mean(values * values, axis=1, keepdims=True) + epsilon)
        normed[rows, :] = (values * scale * gain_one).astype(bf16)

    loop(steps, norm)
    keep_normed = io(3, normed, normed_hbm)
    keep_normed.start()
    table_bias(gains_ref, idx_ref, select_ref, bias)
    g_qkv.relay()
    g_out.first()
    g_prefix.relay()
    g_in.first()
    g_qkv.last()
    g_qkv.finish()
    keep_qkv = io(4, w_qkv, qkv_hbm)
    keep_qkv.start()

    def project(step):
        s, rows = step // steps, rows_of(step % steps)
        proj[s, rows, :] = mm(normed[rows, :], w_qkv[s]).astype(bf16)

    loop(3 * steps, project)
    keep_proj = io(5, proj.at[0:3], proj_hbm)
    keep_proj.start()
    g_prefix.last()
    g_prefix.finish()
    keep_prefix_w = io(6, w_prefix, prefix_w_hbm)
    keep_prefix_w.start()

    def make_prefix_slot(s):
        part = mm(picked[...].reshape(QPR * SLOT, width), w_prefix[s].reshape(width, width))
        prefix[s] = part.astype(bf16).reshape(QPR, SLOT, width)

    loop(4, make_prefix_slot)
    keep_prefix = io(7, prefix, prefix_hbm)
    keep_prefix.start()
    g_out.relay()

    def attend_some(step):
        for i in range(SPAN):
            attend_one(step * SPAN + i, window_ref, proj, prefix, bias, pad)

    loop(QPR // SPAN, attend_some)
    g_out.last()
    g_in.relay()
    g_down.first()
    g_rest.first()
    loop(length // BLOCK, lambda b: unpad(b, piece_ref, (pad,), (attended,)), 4)
    g_out.finish()
    keep_normed.wait()

    def attn_out(i):
        rows = rows_of(i)
        values = hidden[rows, :].astype(f32) + mm(attended[rows, :], w_out[0])
        after[rows, :] = values
        scale = lax.rsqrt(jnp.mean(values * values, axis=1, keepdims=True) + epsilon)
        normed[rows, :] = (values * scale * gain_two).astype(bf16)

    loop(steps, attn_out)
    g_in.last()
    g_in.finish()
    keep_proj.wait()

    def hidden_chunk(step):
        j, rows = step // steps, rows_of(step % steps)
        act_part, slope_part = gelu_pair(mm(normed[rows, :], w_in[j]))
        act[j, rows, :] = act_part.astype(bf16)
        slope[j, rows, :] = slope_part.astype(bf16)

    def hidden_some(part):
        loop(chunks * steps // 2, lambda step: hidden_chunk(step + part * chunks * steps // 2))

    hidden_some(0)
    g_down.relay()
    hidden_some(1)
    g_rest.relay()
    g_down.last()
    load_cot.wait()

    def down_chunk(step):
        j, c = step // 2, step % 2
        cols = pl.ds(pl.multiple_of(c * (width // 2), 128), width // 2)
        part = mm(act[j, :, cols], cot[...], TN)
        down_grads[j, c] = part.astype(bf16).reshape(4, width // 8, width)

    loop(chunks * 2, down_chunk)
    me, other = place.c, 1 - place.c
    downs = [
        Scatter(place, down_grads.at[:, other, u], down_grads.at[:, me, u], (rc, rd, re, rx, ry), u, send.at[u], recv.at[u])
        for u in range(4)
    ]
    each(downs, "core")
    g_rest.last()
    g_down.finish()
    g_rest.finish()

    def slope_chunk(step):
        j, rows = step // steps, rows_of(step % steps)
        act_grad = mm(cot[rows, :], w_down[j], NT)
        slope[j, rows, :] = (act_grad * slope[j, rows, :].astype(f32)).astype(bf16)

    def slope_some(part):
        loop(chunks * steps // 2, lambda step: slope_chunk(step + part * chunks * steps // 2))

    slope_some(0)
    each(downs, "fold")
    slope_some(1)
    keep_prefix_w.wait()
    keep_qkv.wait()
    g_qkv.drain()
    g_prefix.drain()
    in_grads, out_grad = w_prefix, w_qkv
    ins = [
        Scatter(
            place, in_grads.at[u, :, other], in_grads.at[u, :, me],
            (pad.at[4 * u : 4 * u + 4], rd.at[4 + u], re.at[4 + u], pad.at[16 + u], ry.at[4 + u]),
            None, send.at[4 + u], recv.at[4 + u],
        )
        for u in range(4)
    ]

    def in_chunk(step):
        j, c = step // 2, step % 2
        cols = pl.ds(pl.multiple_of(c * (width // 2), 128), width // 2)
        part = mm(normed[:, cols], slope[j], TN).astype(bf16)
        in_grads[j, pl.ds(c * 2, 2)] = part.reshape(2, 2, width // 8, width)

    loop(chunks * 2, in_chunk)
    each(ins, "core")
    each(downs, "relay")

    def out_rows(i):
        rows = rows_of(i)
        total = after[rows, :]
        for j in range(chunks):
            total += mm(act[j, rows, :], w_down[j])
        hidden[rows, :] = total.astype(bf16)

    loop(steps, out_rows)
    keep_output = io(8, hidden, output_hbm)
    keep_output.start()
    each(ins, "fold")
    gain_grad_ref[...] = jnp.zeros_like(gain_grad_ref)
    attended_grad = act.at[0]

    def back_rows(i):
        rows = rows_of(i)
        grad = mm(slope[0, rows, :], w_in[0], NT)
        for j in range(1, chunks):
            grad += mm(slope[j, rows, :], w_in[j], NT)
        values = after[rows, :]
        scale = lax.rsqrt(jnp.mean(values * values, axis=1, keepdims=True) + epsilon)
        unit = values * scale
        gain_grad_ref[0:1, :] += jnp.sum(grad * unit, axis=0, keepdims=True)
        pulled = grad * gain_two
        mixed = pulled - unit * jnp.mean(pulled * unit, axis=1, keepdims=True)
        result = cot[rows, :].astype(f32) + scale * mixed
        after[rows, :] = result
        low = result.astype(bf16)
        normed[rows, :] = low
        attended_grad[rows, :] = mm(low, w_out[0], NT).astype(bf16)

    loop(steps, back_rows)
    keep_after = io(9, after, after_grad_hbm)
    keep_after.start()
    keep_attended = io(10, attended_grad, attended_grad_hbm)
    keep_attended.start()
    for u in range(4):
        sums_ref[u] = downs[u].total().astype(bf16)
    for c in range(2):
        cols = slice(c * (width // 2), (c + 1) * (width // 2))
        out_grad[0, cols, :] = mm(attended[:, cols], normed[...], TN).astype(bf16)
    keep_out = io(11, out_grad.at[0], out_grad_hbm)
    keep_out.start()
    each(ins, "relay")
    for u in range(4):
        sums_ref[4 + u] = ins[u].total().astype(bf16)
    for k in range(7):
        small_copy(k).wait_send()
    each((g_out, g_in, g_down, g_rest), "drain")
    each(downs + ins, "drain")
    for copy in (keep_picked, keep_prefix, keep_output, keep_after, keep_attended, keep_out):
        copy.wait()


def forward_part(windows, pieces, chosen, memory, small, idx, select, hidden, cot, w_qkv, w_prefix, w_out, w_in, w_down):
    length, width = hidden.shape
    chunks = w_in.shape[1] // width
    eighth = width // 8
    units = w_down.shape[0] // eighth
    sds = jax.ShapeDtypeStruct
    return pl.pallas_call(
        forward_part_kernel,
        out_shape=(
            sds((length, width), bf16),
            sds((length, width), bf16),
            sds((3, length, width), bf16),
            sds((4, QPR, SLOT, width), bf16),
            sds((QPR, SLOT, width), bf16),
            sds(small.shape, f32),
            sds((8, width), f32),
            sds((length, width), bf16),
            sds((length, width), f32),
            sds((3, width, width), bf16),
            sds((4, 4, 2, eighth, width), bf16),
            sds((width, width), bf16),
            sds((2 * units, eighth, width), bf16),
        ),
        in_specs=[SMEM] * 3 + [VMEM] * 4 + [ANY] * 7,
        out_specs=(ANY,) * 5 + (VMEM,) * 2 + (ANY,) * 5 + (VMEM,),
        scratch_shapes=[
            pltpu.VMEM((3, width, width), bf16),
            pltpu.VMEM((4, 4, 2, eighth, width), bf16),
            pltpu.VMEM((1, width, width), bf16),
            pltpu.VMEM((chunks, width, width), bf16),
            pltpu.VMEM((chunks, width, width), bf16),
            pltpu.VMEM((length, width), bf16),
            pltpu.VMEM((length, width), bf16),
            pltpu.VMEM((length, width), bf16),
            pltpu.VMEM((chunks, length, width), bf16),
            pltpu.VMEM((chunks, length, width), bf16),
            pltpu.VMEM((4, QPR, SLOT, width), bf16),
            pltpu.VMEM((QPR, SLOT, width), bf16),
            pltpu.VMEM((QPR, WIN, width), bf16),
            pltpu.VMEM((length, width), bf16),
            pltpu.VMEM((length, width), f32),
            pltpu.VMEM((4, 2, units, eighth, width), bf16),
            pltpu.VMEM((H // GROUP, KEYS, STACK), f32),
            pltpu.VMEM((8,) + small.shape, f32),
            pltpu.VMEM((units, 4, eighth, width), bf16),
            pltpu.VMEM((2 * units, eighth // 2, width), bf16),
            pltpu.VMEM((2 * units, eighth // 2, width), bf16),
            pltpu.VMEM((units, eighth, width), bf16),
            pltpu.VMEM((2 * units, eighth, width), bf16),
            pltpu.SemaphoreType.DMA((2 * units, Scatter.COPIES)),
            pltpu.SemaphoreType.DMA((2 * units, Scatter.COPIES)),
            pltpu.SemaphoreType.DMA((6, Gather.COPIES)),
            pltpu.SemaphoreType.DMA((6, Gather.COPIES)),
            pltpu.SemaphoreType.DMA((6, 4)),
            pltpu.SemaphoreType.DMA((7,)),
            pltpu.SemaphoreType.DMA((7,)),
            pltpu.SemaphoreType.DMA((12,)),
        ],
        compiler_params=pltpu.CompilerParams(
            collective_id=0, has_side_effects=True, vmem_limit_bytes=62 << 20
        ),
        name="forward_part",
    )(windows, pieces, chosen, memory, small, idx, select, hidden, cot, w_qkv, w_prefix, w_out, w_in, w_down)


class Line:
    def __init__(self, place, own, below, above, up, down, k, send, recv):
        self.z, self.own, self.below, self.above, self.up, self.down = place.z, own, below, above, up, down
        self.send, self.recv = send.at[k], recv.at[k]

    def rise(self, src):
        return pltpu.make_async_remote_copy(
            src_ref=src, dst_ref=self.below, send_sem=self.send.at[0], recv_sem=self.recv.at[0],
            device_id={"dp": self.z + 1}, device_id_type=MESH,
        )

    def sink(self, src):
        return pltpu.make_async_remote_copy(
            src_ref=src, dst_ref=self.above, send_sem=self.send.at[1], recv_sem=self.recv.at[1],
            device_id={"dp": self.z - 1}, device_id_type=MESH,
        )

    def start(self):
        @pl.when(self.z == 0)
        def _():
            self.below[...] = jnp.zeros_like(self.below)
            self.rise(self.own).start()

        @pl.when(self.z == 3)
        def _():
            self.above[...] = jnp.zeros_like(self.above)
            self.sink(self.own).start()

    def pass_up(self):
        self.rise(self.own).wait_recv()
        self.up[...] = (self.below[...].astype(f32) + self.own[...].astype(f32)).astype(self.up.dtype)
        self.rise(self.up).start()

    def pass_down(self):
        self.sink(self.own).wait_recv()
        self.down[...] = (self.above[...].astype(f32) + self.own[...].astype(f32)).astype(self.down.dtype)
        self.sink(self.down).start()

    def near(self):
        pl.when(self.z == 1)(self.pass_up)
        pl.when(self.z == 2)(self.pass_down)

    def far(self):
        pl.when(self.z == 1)(self.pass_down)
        pl.when(self.z == 2)(self.pass_up)

    def total(self):
        pl.when(self.z == 0)(lambda: self.sink(self.own).wait_recv())
        pl.when(self.z == 3)(lambda: self.rise(self.own).wait_recv())
        return self.own[...].astype(f32) + (self.below[...].astype(f32) + self.above[...].astype(f32))

    def drain(self):
        pl.when(self.z < 3)(lambda: self.rise(self.own).wait_send())
        pl.when(self.z > 0)(lambda: self.sink(self.own).wait_send())


CUTS = (((0, 7),), ((0, 7),), ((0, 2), (2, 4), (4, 6), (6, 7)))


def backward_part_kernel(
    window_ref, piece_ref, back_ref, idx_ref, select_ref, gains_ref, gain_grad_ref, sums_ref,
    normed_hbm, proj_hbm, prefix_hbm, picked_hbm, attended_grad_hbm, after_grad_hbm, hidden_hbm,
    qkv_hbm, prefix_w_hbm, out_grad_hbm,
    hidden_grad_hbm, memory_grad_ref, gain_one_ref, gain_two_ref, table_ref,
    qkv_out, attn_out, in_out, down_out, prefix_out,
    normed, proj, prefix, picked, attended_grad, after, pads, tokens, slots, bias, bias_grad, lines, picked_grad,
    own, rc, rd, re, rx, ry, fat, fat_rc, fat_rd, fat_re, fat_rx, fat_ry,
    up, down, below, above, fat_below, fat_above, small, small_in, small_z,
    send, recv, z_send, z_recv, small_send, small_recv, io_sem, out_sem,
):
    place = Place()
    z = place.z
    length, width = normed.shape
    steps = length // TILE
    groups = width // GW
    eighth = width // 8
    me, other = place.c, 1 - place.c

    def io(k, src, dst):
        return pltpu.make_async_copy(src, dst, io_sem.at[k])

    load_own = io(4, out_grad_hbm.at[:, me], own)
    load_proj, load_prefix = io(5, proj_hbm, proj), io(6, prefix_hbm, prefix)
    load_grad, load_normed = io(7, attended_grad_hbm, attended_grad), io(8, normed_hbm, normed)
    load_picked, load_after = io(9, picked_hbm, picked), io(10, after_grad_hbm, after)
    for copy in (load_proj, load_prefix, load_grad, load_own, load_normed, load_picked, load_after):
        copy.start()

    barrier = pltpu.get_barrier_semaphore()
    for o in ((0, 0, 1), (0, 1, 0), (1, 0, 0)):
        pl.semaphore_signal(barrier, inc=1, device_id={"fsdp": place.at(*o)}, device_id_type=MESH)

    @pl.when(z > 0)
    def _():
        pl.semaphore_signal(barrier, inc=1, device_id={"dp": z - 1}, device_id_type=MESH)

    @pl.when(z < 3)
    def _():
        pl.semaphore_signal(barrier, inc=1, device_id={"dp": z + 1}, device_id_type=MESH)

    table_bias(gains_ref, idx_ref, select_ref, bias)
    bias_grad[...] = jnp.zeros_like(bias_grad)
    pl.semaphore_wait(barrier, 5 - (z // 3) - (3 - z) // 3)

    out_unit = Scatter(place, out_grad_hbm.at[:, other], own, (rc, rd, re, rx, ry), None, send.at[0], recv.at[0])
    out_line = Line(place, out_unit.mine(0, 0), below.at[8], above.at[8], rx, ry, 8, z_send, z_recv)
    sum_lines = [
        Line(place, sums_ref.at[u], below.at[u], above.at[u], up.at[u], down.at[u], u, z_send, z_recv) for u in range(8)
    ]
    units, unit_lines, cuts = [], [], []
    for g in range(groups):
        for first, last in CUTS[g]:
            cols = slice(first * GW, last * GW)
            k = len(units)
            bufs = (
                fat_rc.at[g, :, :, cols], fat_rd.at[g, :, cols], fat_re.at[g, :, cols],
                fat_rx.at[g, :, cols], fat_ry.at[g, :, cols],
            )
            unit = Scatter(
                place, fat.at[g, :, other, :, cols], fat.at[g, :, me, :, cols], bufs, None, send.at[1 + k], recv.at[1 + k]
            )
            units.append(unit)
            cuts.append((g, first, last))
            unit_lines.append(
                Line(
                    place, unit.mine(0, 0), fat_below.at[g, :, cols], fat_above.at[g, :, cols],
                    fat_rx.at[g, :, cols], fat_ry.at[g, :, cols], 9 + k, z_send, z_recv,
                )
            )

    def settle(unit, line):
        unit.settle()
        line.start()

    def keep_block(g, s):
        out, at = (qkv_out, s) if s < 3 else (prefix_out, s - 3)
        return pltpu.make_async_copy(
            fat_rc.at[g, 0, :, s * GW : (s + 1) * GW],
            out.at[:, at * width + g * GW : at * width + (g + 1) * GW],
            out_sem.at[9 + 7 * g + s],
        )

    def store_unit(k):
        g, first, last = cuts[k]
        fat_rc[g, 0, :, first * GW : last * GW] = unit_lines[k].total().astype(bf16)
        for s in range(first, last):
            keep_block(g, s).start()

    def keep_sum(u):
        if u < 4:
            return pltpu.make_async_copy(up.at[u], down_out.at[u * eighth : (u + 1) * eighth, :], out_sem.at[u])
        return pltpu.make_async_copy(up.at[u], in_out.at[:, (u - 4) * width : (u - 3) * width], out_sem.at[u])

    def store_sum(u):
        total = sum_lines[u].total().astype(bf16)
        sum_lines[u].drain()
        up[u] = total
        keep_sum(u).start()

    keep_out = pltpu.make_async_copy(rc.at[0], attn_out, out_sem.at[8])

    def store_out():
        rc[0] = out_line.total().astype(bf16)
        keep_out.start()

    def near(*which):
        for u in which:
            sum_lines[u].near()

    def far(*which):
        for u in which:
            sum_lines[u].far()

    def store(*which):
        for u in which:
            store_sum(u)

    out_unit.core()
    each(sum_lines, "start")
    for copy in (load_proj, load_prefix, load_grad, load_own):
        copy.wait()

    def attend_back_all(g, pumps):
        def span(step):
            for i in range(SPAN):
                back_one(
                    step * SPAN + i, g, window_ref, proj, prefix, attended_grad, bias, bias_grad, pads, slots
                )
            for at, pump in enumerate(pumps):
                if pump is not None:
                    pl.when(step == at)(pump)

        loop(QPR // SPAN, span)

    def unit_grads(g):
        cols = slice(g * GW, (g + 1) * GW)
        loop(
            length // BLOCK,
            lambda b: unpad(
                b, piece_ref, [pads.at[s] for s in range(3)], [tokens.at[s, :, cols] for s in range(3)]
            ),
            4,
        )
        flat = picked[...].reshape(QPR * SLOT, width)

        def qkv_unit(s):
            part = mm(normed[...], tokens[s, :, cols], TN).astype(bf16)
            fat[g, :, :, :, pl.ds(pl.multiple_of(s * GW, GW), GW)] = part.reshape(4, 2, eighth, GW)

        def prefix_unit(s):
            part = mm(flat, slots[s, :, :, cols].reshape(QPR * SLOT, GW), TN).astype(bf16)
            fat[g, :, :, :, pl.ds(pl.multiple_of((3 + s) * GW, GW), GW)] = part.reshape(4, 2, eighth, GW)

        loop(3, qkv_unit)
        loop(4, prefix_unit)

    def both(*actions):
        def run():
            for action in actions:
                action()

        return run

    attend_back_all(0, (out_unit.fold, None, lambda: near(0), both(out_unit.relay, lambda: near(1))))
    load_normed.wait()
    load_picked.wait()
    unit_grads(0)
    units[0].core()
    near(2)
    far(0)
    settle(out_unit, out_line)
    attend_back_all(
        1,
        (
            both(lambda: near(3), lambda: far(1)),
            both(units[0].fold, lambda: near(4), lambda: far(2)),
            both(lambda: far(3), lambda: store(0)),
            both(lambda: near(5), lambda: store(1)),
        ),
    )
    unit_grads(1)
    units[1].core()
    units[0].relay()
    near(6)
    far(4)
    store(2)
    attend_back_all(
        2,
        (
            both(lambda: near(7), lambda: far(5), lambda: store(3)),
            both(units[1].fold, lambda: settle(units[0], unit_lines[0])),
            both(out_line.near, lambda: far(6), lambda: store(4)),
            both(lambda: far(7), lambda: store(5)),
        ),
    )
    load_qkv = io(5, qkv_hbm, proj.at[:, 0:width, :])
    load_qkv.start()
    unit_grads(2)
    each(units[2:], "core")
    hidden = normed
    load_hidden = io(8, hidden_hbm, hidden)
    load_hidden.start()
    units[1].relay()
    unit_lines[0].near()
    out_line.far()
    store(6, 7)
    load_after.wait()
    load_qkv.wait()
    load_hidden.wait()
    row = lax.broadcasted_iota(jnp.int32, (8, width), 0)
    small[0] = jnp.where(row == 1, gain_grad_ref[0:1, :], 0.0)
    gain = gains_ref[0:1, :]

    def hidden_back(i):
        rows = rows_of(i)
        grad = mm(tokens[0, rows, :], proj[0, 0:width, :], NT)
        for s in range(1, 3):
            grad += mm(tokens[s, rows, :], proj[s, 0:width, :], NT)
        values = hidden[rows, :].astype(f32)
        scale = lax.rsqrt(jnp.mean(values * values, axis=1, keepdims=True) + epsilon)
        unit = values * scale
        small[0, 0:1, :] += jnp.sum(grad * unit, axis=0, keepdims=True)
        pulled = grad * gain
        after[rows, :] += scale * (pulled - unit * jnp.mean(pulled * unit, axis=1, keepdims=True))

    tail_pumps = (
        lambda: each(units[2:4], "fold"),
        both(lambda: each(units[4:6], "fold"), lambda: settle(units[1], unit_lines[1]), unit_lines[0].far),
        lambda: each(units[2:4], "relay"),
        lambda: each(units[4:6], "relay"),
    )

    def hidden_step(i):
        hidden_back(i)
        for at, pump in enumerate(tail_pumps):
            pl.when(i == at)(pump)

    loop(steps, hidden_step)
    keep_hidden = io(10, after, hidden_grad_hbm)
    keep_hidden.start()
    load_prefix_w = [io(5 + s, prefix_w_hbm.at[s], proj.at[s, 0:width, :]) for s in range(3)]
    load_prefix_w.append(io(9, prefix_w_hbm.at[3], attended_grad.at[0:width, :]))
    for copy in load_prefix_w:
        copy.start()
    small[0, 2:3, 0 : NB * H] = table_sums(bias_grad, lines, idx_ref, select_ref)

    def swap(k, o):
        return pltpu.make_async_remote_copy(
            src_ref=small.at[k], dst_ref=small_in.at[k], send_sem=small_send.at[k], recv_sem=small_recv.at[k],
            device_id={"fsdp": place.at(*o)}, device_id_type=MESH,
        )

    swaps = [swap(0, (0, 0, 1)), swap(1, (0, 1, 0)), swap(2, (1, 0, 0))]
    swaps[0].start()
    settle(units[2], unit_lines[2])
    settle(units[3], unit_lines[3])
    swaps[0].wait_recv()
    small[1] = small[0] + small_in[0]
    swaps[1].start()
    unit_lines[1].near()
    store_out()
    settle(units[4], unit_lines[4])
    settle(units[5], unit_lines[5])
    swaps[1].wait_recv()
    small[2] = small[1] + small_in[1]
    swaps[2].start()
    unit_lines[2].near()
    for copy in load_prefix_w:
        copy.wait()
    total = mm(slots[3].reshape(QPR * SLOT, width), attended_grad[0:width, :], NT)
    for s in range(3):
        total += mm(slots[s].reshape(QPR * SLOT, width), proj[s, 0:width, :], NT)
    picked_grad[...] = total.reshape(QPR, SLOT, width)
    swaps[2].wait_recv()
    small[3] = small[2] + small_in[2]
    small_line = Line(
        place, small.at[3], small_z.at[0], small_z.at[1], small_z.at[2], small_z.at[3], 15, z_send, z_recv
    )
    small_line.start()
    unit_lines[3].near()
    unit_lines[1].far()
    unit_lines[4].near()
    unit_lines[5].near()
    small_line.near()
    unit_lines[2].far()
    unit_lines[3].far()
    for m in range(QPR):
        memory_grad_ref[m] = picked_grad[back_ref[m], 0:PAIRS, :]
    store_unit(0)
    unit_lines[4].far()
    unit_lines[5].far()
    small_line.far()
    store_unit(1)
    store_unit(2)
    store_unit(3)
    sums = small_line.total()
    shift = lax.rem(8 - place.me, 8)
    wide_roll = pltpu.roll(sums, shift * eighth, 1)
    gain_one_ref[...] = wide_roll[0:1, 0:eighth]
    gain_two_ref[...] = wide_roll[1:2, 0:eighth]
    entries = NB * H // 8
    table_roll = pltpu.roll(sums, lax.rem(width - place.me * entries, width), 1)
    table_ref[...] = table_roll[2:3, 0:entries]
    store_unit(4)
    store_unit(5)
    keep_hidden.wait()
    out_unit.drain()
    each(units, "drain")
    each([out_line, small_line] + unit_lines, "drain")
    for copy in [keep_out] + [keep_sum(u) for u in range(8)] + [keep_block(g, s) for g in range(groups) for s in range(7)]:
        copy.wait()
    for copy in swaps:
        copy.wait_send()


def backward_part(
    windows, pieces, back, idx, select, gains, gain_grad, sums,
    normed, proj, prefix, picked, attended_grad, after_grad, hidden, qkv, prefix_w, out_grad,
):
    length, width = hidden.shape
    eighth = width // 8
    groups = width // GW
    thick = 7 * GW
    sds = jax.ShapeDtypeStruct
    vm = lambda shape, dtype=bf16: pltpu.VMEM(shape, dtype)
    return pl.pallas_call(
        backward_part_kernel,
        out_shape=(
            sds((length, width), f32),
            sds((QPR, PAIRS, width), f32),
            sds((1, eighth), f32),
            sds((1, eighth), f32),
            sds((1, NB * H // 8), f32),
            sds((eighth, 3 * width), bf16),
            sds((eighth, width), bf16),
            sds((eighth, 4 * width), bf16),
            sds((4 * eighth, width), bf16),
            sds((eighth, 4 * width), bf16),
        ),
        in_specs=[SMEM] * 3 + [VMEM] * 5 + [ANY] * 10,
        out_specs=(ANY,) + (VMEM,) * 4 + (ANY,) * 5,
        scratch_shapes=[
            vm((length, width)),
            vm((3, length, width)),
            vm((4, QPR, SLOT, width)),
            vm((QPR, SLOT, width)),
            vm((length, width)),
            vm((length, width), f32),
            vm((3, QPR, WIN, GW)),
            vm((3, length, width)),
            vm((4, QPR, SLOT, width)),
            vm((groups, KEYS, STACK), f32),
            vm((groups, KEYS, STACK), f32),
            vm((H * WIN, KEYS), f32),
            vm((QPR, SLOT, width), f32),
            vm((4, eighth, width)),
            vm((4, eighth, width)),
            vm((eighth // 2, width)),
            vm((eighth // 2, width)),
            vm((eighth, width)),
            vm((eighth, width)),
            vm((groups, 4, 2, eighth, thick)),
            vm((groups, 4, eighth, thick)),
            vm((groups, eighth // 2, thick)),
            vm((groups, eighth // 2, thick)),
            vm((groups, eighth, thick)),
            vm((groups, eighth, thick)),
            vm((8, eighth, width)),
            vm((8, eighth, width)),
            vm((9, eighth, width)),
            vm((9, eighth, width)),
            vm((groups, eighth, thick)),
            vm((groups, eighth, thick)),
            vm((4, 8, width), f32),
            vm((3, 8, width), f32),
            vm((4, 8, width), f32),
            pltpu.SemaphoreType.DMA((7, Scatter.COPIES)),
            pltpu.SemaphoreType.DMA((7, Scatter.COPIES)),
            pltpu.SemaphoreType.DMA((16, 2)),
            pltpu.SemaphoreType.DMA((16, 2)),
            pltpu.SemaphoreType.DMA((3,)),
            pltpu.SemaphoreType.DMA((3,)),
            pltpu.SemaphoreType.DMA((11,)),
            pltpu.SemaphoreType.DMA((9 + 7 * groups,)),
        ],
        compiler_params=pltpu.CompilerParams(
            collective_id=1, has_side_effects=True, vmem_limit_bytes=62 << 20
        ),
        name="backward_part",
    )(
        windows, pieces, back, idx, select, gains, gain_grad, sums,
        normed, proj, prefix, picked, attended_grad, after_grad, hidden, qkv, prefix_w,
        out_grad.reshape(4, 2, eighth, width),
    )


def near_local(
    hidden, segment_ids, memory, memory_row, buckets, attn_gain, ffn_gain, rel_table,
    w_qkv, w_attn_out, w_in, w_down, w_prefix, cotangent,
):
    length, width = hidden.shape[1:]
    windows, pieces = layout_tables(segment_ids[0])
    idx, select = near_buckets(buckets, length), head_select()
    padded = jnp.pad(memory[0], ((0, 0), (0, SLOT - PAIRS), (0, 0)))
    (
        output, normed, proj, prefix, picked, gains, ffn_gain_grad, attended_grad, after_grad,
        full_qkv, full_prefix, attn_out_grad, sums,
    ) = forward_part(
        windows, pieces, memory_row[0], padded, pack_small(attn_gain, ffn_gain, rel_table, width), idx, select,
        hidden[0], cotangent[0], w_qkv, w_prefix, w_attn_out, w_in, w_down,
    )
    hidden_grad, memory_grad, *rest = backward_part(
        windows, pieces, back_order(memory_row[0]), idx, select, gains, ffn_gain_grad, sums, normed, proj, prefix,
        picked, attended_grad, after_grad, hidden[0], full_qkv, full_prefix.reshape(4, width, width), attn_out_grad,
    )
    return (output[None], hidden_grad[None], memory_grad[None]) + tuple(x[0] for x in rest[:3]) + tuple(
        x.astype(f32) for x in rest[3:]
    )


def rms_scale(values, norm_gain):
    return (
        values * lax.rsqrt(jnp.mean(values * values, axis=-1, keepdims=True) + epsilon) * norm_gain
    )


def plain_forward_kernel(window_ref, piece_ref, idx_ref, select_ref, gains_ref, proj, prefix, out, bias, pad):
    table_bias(gains_ref, idx_ref, select_ref, bias)
    loop(QPR, lambda q: attend_one(q, window_ref, proj, prefix, bias, pad), SPAN)
    loop(out.shape[0] // BLOCK, lambda b: unpad(b, piece_ref, (pad,), (out,)))


def plain_attend(tables, proj, prefix):
    _, length, width = proj.shape
    return pl.pallas_call(
        plain_forward_kernel,
        out_shape=jax.ShapeDtypeStruct((length, width), bf16),
        in_specs=[SMEM] * 2 + [VMEM] * 5,
        out_specs=VMEM,
        scratch_shapes=[pltpu.VMEM((H // GROUP, KEYS, STACK), f32), pltpu.VMEM((QPR, WIN, width), bf16)],
        compiler_params=pltpu.CompilerParams(vmem_limit_bytes=40 << 20),
        name="attend",
    )(*tables, proj, prefix)


def plain_backward_kernel(
    window_ref, piece_ref, idx_ref, select_ref, gains_ref, proj, prefix, grad,
    tokens, slots, table_ref, bias, bias_grad, pads, lines,
):
    table_bias(gains_ref, idx_ref, select_ref, bias)
    bias_grad[...] = jnp.zeros_like(bias_grad)
    for g in range(grad.shape[1] // GW):
        loop(QPR, lambda q: back_one(q, g, window_ref, proj, prefix, grad, bias, bias_grad, pads, slots), SPAN)
        cols = slice(g * GW, (g + 1) * GW)
        loop(
            grad.shape[0] // BLOCK,
            lambda b: unpad(
                b, piece_ref, [pads.at[s] for s in range(3)], [tokens.at[s, :, cols] for s in range(3)]
            ),
        )
    table_ref[...] = table_sums(bias_grad, lines, idx_ref, select_ref)


def plain_attend_back(tables, proj, prefix, grad):
    sds = jax.ShapeDtypeStruct
    return pl.pallas_call(
        plain_backward_kernel,
        out_shape=(sds(proj.shape, bf16), sds(prefix.shape, bf16), sds((1, NB * H), f32)),
        in_specs=[SMEM] * 2 + [VMEM] * 6,
        out_specs=(VMEM,) * 3,
        scratch_shapes=[
            pltpu.VMEM((H // GROUP, KEYS, STACK), f32),
            pltpu.VMEM((H // GROUP, KEYS, STACK), f32),
            pltpu.VMEM((3, QPR, WIN, GW), bf16),
            pltpu.VMEM((H * WIN, KEYS), f32),
        ],
        compiler_params=pltpu.CompilerParams(vmem_limit_bytes=48 << 20),
        name="attend_back",
    )(*tables, proj, prefix, grad)


def plain_row_pass(hidden, segments, memory, chosen, buckets, cotangent, full):
    attn_gain, ffn_gain, rel_table, w_qkv, w_attn_out, w_in, w_down, w_prefix = full
    length, width = hidden.shape
    tokens = hidden.astype(f32)
    gain_one = attn_gain.astype(f32)
    gain_two = ffn_gain.astype(f32)
    tables = layout_tables(segments) + (
        near_buckets(buckets, length), head_select(), pack_small(attn_gain, ffn_gain, rel_table, width),
    )

    normed = rms_scale(tokens, gain_one).astype(bf16)
    projected = mm(normed, w_qkv).astype(bf16)
    picked = jnp.take(jnp.pad(memory, ((0, 0), (0, SLOT - PAIRS), (0, 0))), chosen, axis=0).reshape(QPR * SLOT, width)
    prefix = mm(picked, w_prefix).astype(bf16)
    proj = jnp.transpose(projected.reshape(length, 3, width), (1, 0, 2))
    prefix = jnp.transpose(prefix.reshape(QPR, SLOT, 4, width), (2, 0, 1, 3))
    attended = plain_attend(tables, proj, prefix)
    after_attn = tokens + mm(attended, w_attn_out)
    normed_ffn = rms_scale(after_attn, gain_two).astype(bf16)
    hidden_pre = mm(normed_ffn, w_in)
    activation = jax.nn.gelu(hidden_pre).astype(bf16)
    output = (after_attn + mm(activation, w_down)).astype(bf16)

    grad_out = cotangent.astype(f32)
    down_grad = mm(activation, cotangent, TN)
    act_grad = mm(cotangent, w_down, NT)
    pre_grad = jax.vjp(jax.nn.gelu, hidden_pre)[1](act_grad)[0].astype(bf16)
    in_grad = mm(normed_ffn, pre_grad, TN)
    normed_ffn_grad = mm(pre_grad, w_in, NT)
    residual_part, ffn_gain_grad = jax.vjp(rms_scale, after_attn, gain_two)[1](normed_ffn_grad)
    after_grad = grad_out + residual_part
    attn_branch = after_grad.astype(bf16)
    attn_out_grad = mm(attended, attn_branch, TN)
    attended_grad = mm(attn_branch, w_attn_out, NT).astype(bf16)
    token_grad, slot_grad, table_grad = plain_attend_back(tables, proj, prefix, attended_grad)
    token_grad = jnp.transpose(token_grad, (1, 0, 2)).reshape(length, 3 * width)
    slot_grad = jnp.transpose(slot_grad, (1, 2, 0, 3)).reshape(QPR * SLOT, 4 * width)
    qkv_grad = mm(normed, token_grad, TN)
    normed_grad = mm(token_grad, w_qkv, NT)
    prefix_grad = mm(picked, slot_grad, TN)
    picked_grad = mm(slot_grad, w_prefix, NT).reshape(QPR, SLOT, width)[:, :PAIRS]
    memory_grad = jnp.take(picked_grad, back_order(chosen), axis=0)
    norm_part, attn_gain_grad = jax.vjp(rms_scale, tokens, gain_one)[1](normed_grad)
    hidden_grad = after_grad + norm_part
    small = jnp.concatenate([attn_gain_grad, ffn_gain_grad, table_grad[0]])
    return output, hidden_grad, memory_grad, small, (qkv_grad, attn_out_grad, in_grad, down_grad, prefix_grad)


def plain_local(
    hidden, segment_ids, memory, memory_row, buckets, attn_gain, ffn_gain, rel_table,
    w_qkv, w_attn_out, w_in, w_down, w_prefix, cotangent,
):
    sizes = (attn_gain.shape[0], ffn_gain.shape[0], rel_table.shape[0])
    small = lax.all_gather(jnp.concatenate([attn_gain, ffn_gain, rel_table]), "fsdp", axis=0)
    cuts = (0, sizes[0], sizes[0] + sizes[1], sum(sizes))
    full = tuple(small[:, cuts[i] : cuts[i + 1]].reshape(-1) for i in range(3)) + tuple(
        lax.all_gather(w, "fsdp", axis=0, tiled=True) for w in (w_qkv, w_attn_out, w_in, w_down, w_prefix)
    )
    outs = []
    total = None
    for r in range(hidden.shape[0]):
        *own, small_grad, grads = plain_row_pass(
            hidden[r], segment_ids[r], memory[r], memory_row[r], buckets, cotangent[r], full
        )
        outs.append(own)
        fresh = (small_grad,) + grads
        total = fresh if total is None else jax.tree.map(jnp.add, total, fresh)
    output, hidden_grad, memory_grad = (jnp.stack(x) for x in zip(*outs))
    small_grad = lax.psum(total[0], ("fsdp", "dp"))
    me = lax.axis_index("fsdp")
    bases = (0, full[0].shape[0], full[0].shape[0] + full[1].shape[0])
    shares = [
        lax.dynamic_slice_in_dim(small_grad, base + me * size, size) for base, size in zip(bases, sizes)
    ]
    for gradient in total[1:]:
        share = lax.psum_scatter(gradient.astype(bf16), "fsdp", scatter_dimension=0, tiled=True)
        shares.append(lax.psum(share, "dp").astype(f32))
    return (output, hidden_grad, memory_grad) + tuple(shares)


def solution(mesh):
    rows = ("fsdp", "dp")
    placed = (
        P(rows, None, None), P(rows, None), P(rows, None, None, None), P(rows, None), P(),
        P("fsdp"), P("fsdp"), P("fsdp"),
        P("fsdp", None), P("fsdp", None), P("fsdp", None), P("fsdp", None), P("fsdp", None),
        P(rows, None, None),
    )
    near = mesh.shape["fsdp"] == 8 and mesh.shape["dp"] == 4
    return jax.shard_map(
        near_local if near else plain_local,
        mesh=mesh,
        in_specs=placed,
        out_specs=(
            P(rows, None, None), P(rows, None, None), P(rows, None, None, None),
            P("fsdp"), P("fsdp"), P("fsdp"),
            P("fsdp", None), P("fsdp", None), P("fsdp", None), P("fsdp", None), P("fsdp", None),
        ),
        check_vma=False,
    )
```

```python
import functools
import jax
import jax.numpy as jnp
from jax import lax
from jax.experimental import pallas as pl
from jax.experimental.pallas import tpu as pltpu
from jax.sharding import PartitionSpec as P

H = 12
DH = 64
NB = 32
QLEN = 64
QPR = 20
PAIRS = 10

WIN = 96
SLOT = 16
KEYS = WIN + 2 * SLOT
GROUP = 4
GW = GROUP * DH
STACK = GROUP * WIN
TILE = 256
BLOCK = 16
SPAN = 5
OVERLAP = 6

epsilon = 1e-06
masked_out = -1e30
f32 = jnp.float32
bf16 = jnp.bfloat16
NT = (((1,), (1,)), ((), ()))
TN = (((0,), (0,)), ((), ()))
MESH = pl.DeviceIdType.MESH
ANY = pl.BlockSpec(memory_space=pl.ANY)
SMEM = pl.BlockSpec(memory_space=pltpu.SMEM)
VMEM = pl.BlockSpec(memory_space=pltpu.VMEM)


def mm(a, b, dims=(((1,), (0,)), ((), ()))):
    return lax.dot_general(a, b, dims, preferred_element_type=f32)


def row_starts(segments):
    ids = jnp.arange(QPR + 1, dtype=jnp.int32)
    return jnp.sum((segments[None, :] < ids[:, None]).astype(jnp.int32), axis=1)


def near_buckets(buckets, length):
    return lax.slice_in_dim(buckets, length - QLEN, length - QLEN + KEYS).reshape(1, KEYS)


def lines_of(vectors, width):
    return jnp.concatenate(
        [jnp.pad(v.astype(f32), (0, width - v.shape[0]))[None] for v in vectors] + [jnp.zeros((8 - len(vectors), width), f32)]
    )


def loop(n, body, unroll=1):
    def step(i, carry):
        body(i)
        return carry

    lax.fori_loop(0, n, step, 0, unroll=unroll)


def each(items, name):
    for item in items:
        getattr(item, name)()


def rows_of(i):
    return pl.ds(pl.multiple_of(i * TILE, TILE), TILE)


class Place:
    def __init__(self):
        me = lax.axis_index("fsdp")
        self.me, self.c, self.x, self.y = me, me % 2, (me // 2) % 2, me // 4
        self.z = lax.axis_index("dp")

    def at(self, dy, dx, dc):
        return 4 * ((self.y + dy) % 2) + 2 * ((self.x + dx) % 2) + (self.c + dc) % 2


OTHERS = [(dy, dx, dc) for dy in (0, 1) for dx in (0, 1) for dc in (0, 1)][1:]


def greet(peers):
    barrier = pltpu.get_barrier_semaphore()
    for peer in peers:
        pl.semaphore_signal(barrier, inc=1, device_id=peer, device_id_type=MESH)
    pl.semaphore_wait(barrier, len(peers))


class Gather:
    COPIES = 8

    def __init__(self, place, shard, full, down, k, send, recv, own_sem, share=(0, 1)):
        self.p, self.shard, self.full, self.down = place, shard, full, down
        self.send, self.recv, self.own_sem = send.at[k], recv.at[k], own_sem.at[k]
        self.all_rows = shard.shape[0]
        self.rows = self.all_rows // share[1]
        self.skip = share[0] * self.rows
        self.half = self.rows // 2

    def piece(self, dy, dx, dc, part=None):
        f = self.p.at(dy, dx, dc)
        begin = (f % 2 if self.down else f) * self.all_rows + self.skip
        size = self.rows
        if part is not None:
            begin, size = begin + part * self.half, self.half
        if len(self.full.shape) == 5:
            rows = slice(None) if part is None else pl.ds(part * self.half, self.half)
            return self.full.at[:, f // 2, f % 2, rows, :]
        rows = pl.ds(pl.multiple_of(begin, 16), size)
        return self.full.at[f // 2, rows, :] if self.down else self.full.at[:, rows, :]

    def copy(self, k, src, dst, dy, dx, dc):
        return pltpu.make_async_remote_copy(
            src_ref=src, dst_ref=dst, send_sem=self.send.at[k], recv_sem=self.recv.at[k],
            device_id={"fsdp": self.p.at(dy, dx, dc)}, device_id_type=MESH,
        )

    def own(self):
        if self.down:
            return [
                pltpu.make_async_copy(
                    self.shard.at[pl.ds(self.skip, self.rows), :], self.piece(0, 0, 0), self.own_sem.at[0]
                )
            ]
        width = self.full.shape[-1]
        return [
            pltpu.make_async_copy(
                self.shard.at[:, s * width : (s + 1) * width], self.piece(0, 0, 0).at[s], self.own_sem.at[s]
            )
            for s in range(self.full.shape[0])
        ]

    def load(self):
        for copy in self.own():
            copy.start()

    def first(self):
        for copy in self.own():
            copy.wait()
        mine = self.piece(0, 0, 0)
        self.copy(0, mine, mine, 0, 1, 0).start()
        self.copy(1, mine, mine, 1, 0, 0).start()
        self.copy(2, mine, mine, 0, 0, 1).start()

    def landed(self, k, piece):
        self.copy(k, piece, piece, 0, 0, 1).wait_recv()

    def relay(self):
        from_x, from_y = self.piece(0, 1, 0), self.piece(1, 0, 0)
        self.landed(0, from_x)
        top = self.piece(0, 1, 0, 0)
        self.copy(3, top, top, 1, 0, 0).start()
        self.copy(4, from_x, from_x, 0, 0, 1).start()
        self.landed(1, from_y)
        low = self.piece(1, 0, 0, 1)
        self.copy(5, low, low, 0, 1, 0).start()
        self.copy(6, from_y, from_y, 0, 0, 1).start()

    def last(self):
        self.landed(3, self.piece(1, 1, 0, 0))
        self.landed(5, self.piece(1, 1, 0, 1))
        far = self.piece(1, 1, 0)
        self.copy(7, far, far, 0, 0, 1).start()

    def finish(self):
        self.landed(2, self.piece(0, 0, 1))
        self.landed(4, self.piece(0, 1, 1))
        self.landed(6, self.piece(1, 0, 1))
        self.landed(7, self.piece(1, 1, 1))

    def drain(self):
        whole, part = self.piece(0, 0, 0), self.piece(0, 0, 0, 0)
        for k in range(self.COPIES):
            src = part if k in (3, 5) else whole
            self.copy(k, src, src, 0, 0, 1).wait_send()


class Scatter:
    COPIES = 7

    def __init__(self, place, other, own, bufs, u, send, recv):
        self.p, self.other, self.own = place, other, own
        self.rc, self.rd, self.re, self.rx, self.ry = bufs if u is None else (b.at[u] for b in bufs)
        self.send, self.recv = send, recv
        self.half = self.rd.shape[0]

    def mine(self, dy, dx):
        return self.own.at[2 * ((self.p.y + dy) % 2) + (self.p.x + dx) % 2]

    def copy(self, k, src, dst, dy, dx, dc):
        return pltpu.make_async_remote_copy(
            src_ref=src, dst_ref=dst, send_sem=self.send.at[k], recv_sem=self.recv.at[k],
            device_id={"fsdp": self.p.at(dy, dx, dc)}, device_id_type=MESH,
        )

    def part(self, k):
        low, high = pl.ds(0, self.half), pl.ds(self.half, self.half)
        if k == 0:
            return self.copy(0, self.other, self.rc, 0, 0, 1)
        if k == 1:
            return self.copy(1, self.mine(1, 1).at[low], self.rd, 0, 1, 0)
        if k == 2:
            return self.copy(2, self.mine(1, 1).at[high], self.re, 1, 0, 0)
        if k == 3:
            return self.copy(3, self.mine(0, 1).at[low], self.rx.at[low], 0, 1, 0)
        if k == 4:
            return self.copy(4, self.mine(1, 0).at[high], self.ry.at[high], 1, 0, 0)
        if k == 5:
            return self.copy(5, self.mine(0, 1).at[high], self.rx.at[high], 0, 1, 0)
        return self.copy(6, self.mine(1, 0).at[low], self.ry.at[low], 1, 0, 0)

    def core(self):
        self.part(0).start()

    def fold(self):
        self.part(0).wait_recv()
        self.own[...] = (self.own[...].astype(f32) + self.rc[...].astype(f32)).astype(bf16)
        for k in (1, 2, 3, 4):
            self.part(k).start()

    def relay(self):
        low, high = pl.ds(0, self.half), pl.ds(self.half, self.half)
        nx, ny = self.mine(0, 1).at[high], self.mine(1, 0).at[low]
        self.part(1).wait_recv()
        ny[...] = (ny[...].astype(f32) + self.rd[...].astype(f32)).astype(bf16)
        self.part(6).start()
        self.part(2).wait_recv()
        nx[...] = (nx[...].astype(f32) + self.re[...].astype(f32)).astype(bf16)
        self.part(5).start()

    def total(self):
        for k in (3, 4, 5, 6):
            self.part(k).wait_recv()
        return self.mine(0, 0)[...].astype(f32) + (self.rx[...].astype(f32) + self.ry[...].astype(f32))

    def settle(self):
        total = self.total().astype(bf16)
        self.mine(0, 0)[...] = total

    def drain(self):
        for k in range(self.COPIES):
            self.part(k).wait_send()


GELU_A = 0.7978845608028654
GELU_B = 0.044715


def gelu_pair(v):
    square = v * v
    t = jnp.tanh(v * (GELU_A + (GELU_A * GELU_B) * square))
    half = 0.5 + 0.5 * t
    slope = half + (0.5 * v) * (1.0 - t * t) * (GELU_A + (3.0 * GELU_A * GELU_B) * square)
    return v * half, slope


def stack_heads(block):
    lane = lax.broadcasted_iota(jnp.int32, (1, GW), 1)
    parts = []
    for h in range(GROUP):
        mask = jnp.where((lane >= h * DH) & (lane < (h + 1) * DH), 1.0, 0.0).astype(bf16)
        parts.append(block * mask)
    return jnp.concatenate(parts, axis=0)


def merge_heads(stacked):
    lane = lax.broadcasted_iota(jnp.int32, (WIN, GW), 1)
    out = stacked[:WIN]
    for h in range(1, GROUP):
        out = jnp.where(lane >= h * DH, stacked[h * WIN : (h + 1) * WIN], out)
    return out


def key_tile(tokens, low, high):
    return jnp.concatenate([tokens, low, high], axis=0)


def key_cost(begin, end):
    row = lax.broadcasted_iota(jnp.int32, (KEYS, KEYS), 0)
    token = (row >= begin) & (row < end)
    first = (row >= WIN) & (row < WIN + PAIRS)
    second = (row >= WIN + SLOT) & (row < WIN + SLOT + PAIRS)
    return jnp.where(token | first | second, 0.0, masked_out).astype(f32)


def soft_columns(keys, stack, bias_block, cost):
    logits = mm(keys, stack, NT) + (bias_block + jnp.concatenate([cost] * (STACK // KEYS), axis=1))
    peak = jnp.max(logits, axis=0, keepdims=True)
    raw = jnp.exp(logits - peak)
    return raw * (1.0 / jnp.sum(raw, axis=0, keepdims=True))


def mirror():
    total = lax.broadcasted_iota(jnp.int32, (KEYS, KEYS), 0) + lax.broadcasted_iota(jnp.int32, (KEYS, KEYS), 1)
    return jnp.where((total == QLEN - 1) | (total == QLEN - 1 + KEYS), 1.0, 0.0).astype(f32)


def head_select():
    entry = lax.broadcasted_iota(jnp.int32, (16, NB * H), 1)
    return lax.rem(entry, H) == lax.broadcasted_iota(jnp.int32, (16, NB * H), 0)


def table_bias(gains, idx_ref, bias):
    wide = jnp.where(head_select(), jnp.broadcast_to(gains[2:3, : NB * H], (16, NB * H)), 0.0)
    lines = mm(mm(wide.astype(bf16), entry_hot(idx_ref)).astype(bf16), mirror().astype(bf16))
    lane = lax.broadcasted_iota(jnp.int32, (WIN, KEYS), 1)
    for g in range(H // GROUP):
        blocks = []
        for h in range(g * GROUP, (g + 1) * GROUP):
            rolled = pltpu.roll(jnp.broadcast_to(lines[h : h + 1, :], (WIN, KEYS)), 0, 1, stride=1, stride_axis=0)
            blocks.append(jnp.where(lane < WIN, rolled, 0.0))
        bias[g] = jnp.concatenate(blocks, axis=0).T


def entry_hot(idx_ref):
    off = lax.broadcasted_iota(jnp.int32, (NB * H, KEYS), 0) - H * idx_ref[...]
    return jnp.where((off >= 0) & (off < H), 1.0, 0.0).astype(bf16)


def question(window_ref, q):
    return window_ref[3 * q] * BLOCK, window_ref[3 * q + 1], window_ref[3 * q + 2]


def attend_one(q, window_ref, proj, prefix, bias, pad):
    base, begin, end = question(window_ref, q)
    cost = key_cost(begin, end)
    rows = pl.ds(base, WIN)
    width = proj.shape[2]
    for g in range(width // GW):
        cols = slice(g * GW, (g + 1) * GW)
        stack = stack_heads(proj[0, rows, cols] * bf16(DH**-0.5))
        keys = key_tile(proj[1, rows, cols], prefix[0, q, :, cols], prefix[1, q, :, cols])
        values = key_tile(proj[2, rows, cols], prefix[2, q, :, cols], prefix[3, q, :, cols])
        soft = soft_columns(keys, stack, bias[g], cost).astype(bf16)
        pad[q, :, cols] = merge_heads(mm(soft, values, TN)).astype(bf16)


def back_one(q, g, window_ref, proj, prefix, attended_grad, bias, bias_grad, pads, slots):
    base, begin, end = question(window_ref, q)
    cost = key_cost(begin, end)
    rows = pl.ds(base, WIN)
    cols = slice(g * GW, (g + 1) * GW)
    row = lax.broadcasted_iota(jnp.int32, (WIN, GW), 0)
    stack = stack_heads(proj[0, rows, cols] * bf16(DH**-0.5))
    keys = key_tile(proj[1, rows, cols], prefix[0, q, :, cols], prefix[1, q, :, cols])
    values = key_tile(proj[2, rows, cols], prefix[2, q, :, cols], prefix[3, q, :, cols])
    grad = attended_grad[rows, cols]
    grads = stack_heads(jnp.where((row >= begin) & (row < end), grad, jnp.zeros_like(grad)))
    soft = soft_columns(keys, stack, bias[g], cost)
    prob_grad = mm(values, grads, NT)
    mean = jnp.sum(soft * prob_grad, axis=0, keepdims=True)
    low = (soft * (prob_grad - mean)).astype(bf16)
    bias_grad[g] += low.astype(f32)
    key_grad = mm(low, stack).astype(bf16)
    value_grad = mm(soft.astype(bf16), grads).astype(bf16)
    pads[0, q] = (merge_heads(mm(low, keys, TN)) * DH**-0.5).astype(bf16)
    pads[1, q] = key_grad[:WIN]
    pads[2, q] = value_grad[:WIN]
    for s in range(2):
        part = slice(WIN + s * SLOT, WIN + (s + 1) * SLOT)
        slots[s, q, :, cols] = key_grad[part]
        slots[2 + s, q, :, cols] = value_grad[part]


def table_sums(bias_grad, lines, idx_ref):
    lane = lax.broadcasted_iota(jnp.int32, (H, KEYS), 1)
    for g in range(H // GROUP):
        lines[g * STACK : (g + 1) * STACK, :] = bias_grad[g].T
    sums = jnp.zeros((H, KEYS), f32)
    for i in range(WIN):
        line = jnp.where(lane < WIN, lines[pl.ds(i, H, stride=WIN), :], 0.0)
        sums += line if i == 0 else pltpu.roll(line, KEYS - i, 1)
    sums = jnp.concatenate([sums, jnp.zeros((16 - H, KEYS), f32)], axis=0)
    exact = dict(precision=lax.Precision.HIGHEST, preferred_element_type=f32)
    sums = lax.dot_general(sums, mirror(), NT, **exact)
    wide = lax.dot_general(sums, entry_hot(idx_ref).astype(f32), NT, **exact)
    return jnp.sum(jnp.where(head_select(), wide, 0.0), axis=0, keepdims=True)


def unpad(b, piece_ref, pads, outs):
    row = lax.broadcasted_iota(jnp.int32, (BLOCK, 1), 0)
    sums = [jnp.zeros((BLOCK, pad.shape[-1]), bf16) for pad in pads]
    for k in range(OVERLAP):
        at = 4 * (OVERLAP * b + k)
        q, off = piece_ref[at], piece_ref[at + 1] * BLOCK
        mine = (row >= piece_ref[at + 2]) & (row < piece_ref[at + 3])
        for s, pad in enumerate(pads):
            sums[s] = jnp.where(mine, pad[q, pl.ds(off, BLOCK), :], sums[s])
    for total, out in zip(sums, outs):
        out[pl.ds(pl.multiple_of(b * BLOCK, BLOCK), BLOCK), :] = total


def layout_tables(segments):
    length = segments.shape[0]
    starts = row_starts(segments)
    ids = jnp.arange(QPR, dtype=jnp.int32)
    low, high = starts[:-1], starts[1:]

    def pick(q, v):
        return jnp.sum(jnp.where(q[:, None] == ids[None, :], v[None, :], 0), axis=1)

    entry = jnp.arange(3 * QPR, dtype=jnp.int32)
    q, field = entry // 3, entry % 3
    begin, end = pick(q, low), pick(q, high)
    base = jnp.minimum(begin // BLOCK, (length - WIN) // BLOCK)
    windows = jnp.where(field == 0, base, jnp.where(field == 1, begin, end) - BLOCK * base)

    entry = jnp.arange(4 * OVERLAP * (length // BLOCK), dtype=jnp.int32)
    at, k, field = entry // (4 * OVERLAP) * BLOCK, entry // 4 % OVERLAP, entry % 4
    q = jnp.sum((high[None, :] <= at[:, None]).astype(jnp.int32), axis=1)
    q = jnp.minimum(q + k, QPR - 1)
    begin, end = pick(q, low), pick(q, high)
    base = jnp.minimum(begin // BLOCK, (length - WIN) // BLOCK)
    off = jnp.clip(at // BLOCK - base, 0, (WIN - BLOCK) // BLOCK)
    edge = jnp.clip(jnp.where(field == 2, begin, end) - at, 0, BLOCK)
    return windows, jnp.where(field == 0, q, jnp.where(field == 1, off, edge))


def back_order(chosen):
    ids = jnp.arange(QPR, dtype=jnp.int32)
    return jnp.sum(jnp.where(chosen[None, :] == ids[:, None], ids[None, :], 0), axis=1)


def forward_part_kernel(
    window_ref, piece_ref, chosen_ref, memory_ref, one_ref, two_ref, entry_ref, idx_ref,
    hidden_hbm, cot_hbm, qkv_w, prefix_w, out_w, in_w, down_w,
    output_hbm, normed_hbm, proj_hbm, prefix_hbm, picked_hbm, gains_ref, gain_grad_ref,
    attended_grad_hbm, after_grad_hbm, qkv_hbm, prefix_w_hbm, out_grad_hbm, sums_ref,
    w_qkv, w_prefix, w_out, w_in, w_down, hidden, cot, normed, act, slope, prefix, picked, pad, attended,
    after, down_grads, bias, small_all,
    rc, rd, re, rx, ry, send, recv, g_send, g_recv, own_sem, small_send, small_recv, io_sem,
):
    place = Place()
    length, width = hidden.shape
    steps = length // TILE
    chunks = w_in.shape[0]
    proj = slope
    weights = ((qkv_w, w_qkv), (prefix_w, w_prefix), (out_w, w_out), (in_w, w_in))
    g_qkv, g_prefix, g_out, g_in = (
        Gather(place, shard, full, False, k, g_send, g_recv, own_sem) for k, (shard, full) in enumerate(weights)
    )
    g_down, g_rest = (
        Gather(place, down_w, w_down, True, 4 + k, g_send, g_recv, own_sem, (k, 2)) for k in range(2)
    )

    def io(k, src, dst):
        return pltpu.make_async_copy(src, dst, io_sem.at[k])

    load_hidden, load_cot = io(0, hidden_hbm, hidden), io(1, cot_hbm, cot)
    for g in (g_qkv, g_prefix, g_out, g_in, g_down, g_rest):
        g.load()
    load_hidden.start()
    load_cot.start()
    small_all[0] = jnp.zeros(small_all.shape[1:], f32)
    small_all[0, 0:1, 0 : width // 8] = one_ref[...].astype(f32)
    small_all[0, 1:2, 0 : width // 8] = two_ref[...].astype(f32)
    small_all[0, 2:3, 0 : NB * H // 8] = entry_ref[...].astype(f32)
    raw = small_all[0]
    row = lax.broadcasted_iota(jnp.int32, raw.shape, 0)
    small_all[0] = jnp.where(
        row < 2,
        pltpu.roll(raw, place.me * (width // 8), 1),
        pltpu.roll(raw, place.me * (NB * H // 8), 1),
    )
    greet([{"fsdp": place.at(*o)} for o in OTHERS])

    def small_copy(k):
        return pltpu.make_async_remote_copy(
            src_ref=small_all.at[0], dst_ref=small_all.at[k + 1],
            send_sem=small_send.at[k], recv_sem=small_recv.at[k],
            device_id={"fsdp": place.at(*OTHERS[k])}, device_id_type=MESH,
        )

    for k in range(7):
        small_copy(k).start()
    g_qkv.first()
    g_prefix.first()
    load_hidden.wait()
    for q in range(QPR):
        picked[q] = memory_ref[chosen_ref[q]]
    keep_picked = io(2, picked, picked_hbm)
    keep_picked.start()
    for k in range(7):
        small_copy(k).wait_recv()
    gains_ref[...] = jnp.sum(small_all[...], axis=0)
    gain_one, gain_two = gains_ref[0:1, :], gains_ref[1:2, :]

    def norm(i):
        rows = rows_of(i)
        values = hidden[rows, :].astype(f32)
        scale = lax.rsqrt(jnp.mean(values * values, axis=1, keepdims=True) + epsilon)
        normed[rows, :] = (values * scale * gain_one).astype(bf16)

    loop(steps, norm)
    keep_normed = io(3, normed, normed_hbm)
    keep_normed.start()
    table_bias(gains_ref, idx_ref, bias)
    g_qkv.relay()
    g_out.first()
    g_prefix.relay()
    g_in.first()
    g_qkv.last()
    g_qkv.finish()
    keep_qkv = io(4, w_qkv, qkv_hbm)
    keep_qkv.start()

    def project(step):
        s, rows = step // steps, rows_of(step % steps)
        proj[s, rows, :] = mm(normed[rows, :], w_qkv[s]).astype(bf16)

    loop(3 * steps, project)
    keep_proj = io(5, proj.at[0:3], proj_hbm)
    keep_proj.start()
    g_prefix.last()
    g_prefix.finish()
    keep_prefix_w = io(6, w_prefix, prefix_w_hbm)
    keep_prefix_w.start()

    def make_prefix_slot(s):
        part = mm(picked[...].reshape(QPR * SLOT, width), w_prefix[s].reshape(width, width))
        prefix[s] = part.astype(bf16).reshape(QPR, SLOT, width)

    loop(4, make_prefix_slot)
    keep_prefix = io(7, prefix, prefix_hbm)
    keep_prefix.start()
    g_out.relay()

    def attend_some(step):
        for i in range(SPAN):
            attend_one(step * SPAN + i, window_ref, proj, prefix, bias, pad)

    loop(QPR // SPAN, attend_some)
    g_out.last()
    g_in.relay()
    g_down.first()
    g_rest.first()
    loop(length // BLOCK, lambda b: unpad(b, piece_ref, (pad,), (attended,)), 4)
    g_out.finish()
    keep_normed.wait()

    def attn_out(i):
        rows = rows_of(i)
        values = hidden[rows, :].astype(f32) + mm(attended[rows, :], w_out[0])
        after[rows, :] = values
        scale = lax.rsqrt(jnp.mean(values * values, axis=1, keepdims=True) + epsilon)
        normed[rows, :] = (values * scale * gain_two).astype(bf16)

    loop(steps, attn_out)
    g_in.last()
    g_in.finish()
    keep_proj.wait()

    def hidden_chunk(step):
        j, rows = step // steps, rows_of(step % steps)
        act_part, slope_part = gelu_pair(mm(normed[rows, :], w_in[j]))
        act[j, rows, :] = act_part.astype(bf16)
        slope[j, rows, :] = slope_part.astype(bf16)

    def hidden_some(part):
        loop(chunks * steps // 2, lambda step: hidden_chunk(step + part * chunks * steps // 2))

    hidden_some(0)
    g_down.relay()
    hidden_some(1)
    g_rest.relay()
    g_down.last()
    load_cot.wait()

    def down_chunk(step):
        j, c = step // 2, step % 2
        cols = pl.ds(pl.multiple_of(c * (width // 2), 128), width // 2)
        part = mm(act[j, :, cols], cot[...], TN)
        down_grads[j, c] = part.astype(bf16).reshape(4, width // 8, width)

    loop(chunks * 2, down_chunk)
    me, other = place.c, 1 - place.c
    downs = [
        Scatter(place, down_grads.at[:, other, u], down_grads.at[:, me, u], (rc, rd, re, rx, ry), u, send.at[u], recv.at[u])
        for u in range(4)
    ]
    each(downs, "core")
    g_rest.last()
    g_down.finish()
    g_rest.finish()

    def slope_chunk(step):
        j, rows = step // steps, rows_of(step % steps)
        act_grad = mm(cot[rows, :], w_down[j], NT)
        slope[j, rows, :] = (act_grad * slope[j, rows, :].astype(f32)).astype(bf16)

    def slope_some(part):
        loop(chunks * steps // 2, lambda step: slope_chunk(step + part * chunks * steps // 2))

    slope_some(0)
    each(downs, "fold")
    slope_some(1)
    keep_prefix_w.wait()
    keep_qkv.wait()
    g_qkv.drain()
    g_prefix.drain()
    in_grads, out_grad = w_prefix, w_qkv
    ins = [
        Scatter(
            place, in_grads.at[u, :, other], in_grads.at[u, :, me],
            (pad.at[4 * u : 4 * u + 4], rd.at[4 + u], re.at[4 + u], pad.at[16 + u], ry.at[4 + u]),
            None, send.at[4 + u], recv.at[4 + u],
        )
        for u in range(4)
    ]

    def in_chunk(step):
        j, c = step // 2, step % 2
        cols = pl.ds(pl.multiple_of(c * (width // 2), 128), width // 2)
        part = mm(normed[:, cols], slope[j], TN).astype(bf16)
        in_grads[j, pl.ds(c * 2, 2)] = part.reshape(2, 2, width // 8, width)

    loop(chunks * 2, in_chunk)
    each(ins, "core")
    each(downs, "relay")

    def out_rows(i):
        rows = rows_of(i)
        total = after[rows, :]
        for j in range(chunks):
            total += mm(act[j, rows, :], w_down[j])
        hidden[rows, :] = total.astype(bf16)

    loop(steps, out_rows)
    keep_output = io(8, hidden, output_hbm)
    keep_output.start()
    each(ins, "fold")
    gain_grad_ref[...] = jnp.zeros_like(gain_grad_ref)
    attended_grad = act.at[0]

    def back_rows(i):
        rows = rows_of(i)
        grad = mm(slope[0, rows, :], w_in[0], NT)
        for j in range(1, chunks):
            grad += mm(slope[j, rows, :], w_in[j], NT)
        values = after[rows, :]
        scale = lax.rsqrt(jnp.mean(values * values, axis=1, keepdims=True) + epsilon)
        unit = values * scale
        gain_grad_ref[0:1, :] += jnp.sum(grad * unit, axis=0, keepdims=True)
        pulled = grad * gain_two
        mixed = pulled - unit * jnp.mean(pulled * unit, axis=1, keepdims=True)
        result = cot[rows, :].astype(f32) + scale * mixed
        after[rows, :] = result
        low = result.astype(bf16)
        normed[rows, :] = low
        attended_grad[rows, :] = mm(low, w_out[0], NT).astype(bf16)

    loop(steps, back_rows)
    keep_after = io(9, after, after_grad_hbm)
    keep_after.start()
    keep_attended = io(10, attended_grad, attended_grad_hbm)
    keep_attended.start()
    for u in range(4):
        sums_ref[u] = downs[u].total().astype(bf16)
    for c in range(2):
        cols = slice(c * (width // 2), (c + 1) * (width // 2))
        out_grad[0, cols, :] = mm(attended[:, cols], normed[...], TN).astype(bf16)
    keep_out = io(11, out_grad.at[0], out_grad_hbm)
    keep_out.start()
    each(ins, "relay")
    for u in range(4):
        sums_ref[4 + u] = ins[u].total().astype(bf16)
    for k in range(7):
        small_copy(k).wait_send()
    each((g_out, g_in, g_down, g_rest), "drain")
    each(downs + ins, "drain")
    for copy in (keep_picked, keep_prefix, keep_output, keep_after, keep_attended, keep_out):
        copy.wait()


def forward_part(windows, pieces, chosen, memory, one, two, entries, idx, hidden, cot, w_qkv, w_prefix, w_out, w_in, w_down):
    length, width = hidden.shape
    chunks = w_in.shape[1] // width
    eighth = width // 8
    units = w_down.shape[0] // eighth
    sds = jax.ShapeDtypeStruct
    return pl.pallas_call(
        forward_part_kernel,
        out_shape=(
            sds((length, width), bf16),
            sds((length, width), bf16),
            sds((3, length, width), bf16),
            sds((4, QPR, SLOT, width), bf16),
            sds((QPR, SLOT, width), bf16),
            sds((8, width), f32),
            sds((8, width), f32),
            sds((length, width), bf16),
            sds((length, width), f32),
            sds((3, width, width), bf16),
            sds((4, 4, 2, eighth, width), bf16),
            sds((width, width), bf16),
            sds((2 * units, eighth, width), bf16),
        ),
        in_specs=[SMEM] * 3 + [VMEM] * 5 + [ANY] * 7,
        out_specs=(ANY,) * 5 + (VMEM,) * 2 + (ANY,) * 5 + (VMEM,),
        scratch_shapes=[
            pltpu.VMEM((3, width, width), bf16),
            pltpu.VMEM((4, 4, 2, eighth, width), bf16),
            pltpu.VMEM((1, width, width), bf16),
            pltpu.VMEM((chunks, width, width), bf16),
            pltpu.VMEM((chunks, width, width), bf16),
            pltpu.VMEM((length, width), bf16),
            pltpu.VMEM((length, width), bf16),
            pltpu.VMEM((length, width), bf16),
            pltpu.VMEM((chunks, length, width), bf16),
            pltpu.VMEM((chunks, length, width), bf16),
            pltpu.VMEM((4, QPR, SLOT, width), bf16),
            pltpu.VMEM((QPR, SLOT, width), bf16),
            pltpu.VMEM((QPR, WIN, width), bf16),
            pltpu.VMEM((length, width), bf16),
            pltpu.VMEM((length, width), f32),
            pltpu.VMEM((4, 2, units, eighth, width), bf16),
            pltpu.VMEM((H // GROUP, KEYS, STACK), f32),
            pltpu.VMEM((8, 8, width), f32),
            pltpu.VMEM((units, 4, eighth, width), bf16),
            pltpu.VMEM((2 * units, eighth // 2, width), bf16),
            pltpu.VMEM((2 * units, eighth // 2, width), bf16),
            pltpu.VMEM((units, eighth, width), bf16),
            pltpu.VMEM((2 * units, eighth, width), bf16),
            pltpu.SemaphoreType.DMA((2 * units, Scatter.COPIES)),
            pltpu.SemaphoreType.DMA((2 * units, Scatter.COPIES)),
            pltpu.SemaphoreType.DMA((6, Gather.COPIES)),
            pltpu.SemaphoreType.DMA((6, Gather.COPIES)),
            pltpu.SemaphoreType.DMA((6, 4)),
            pltpu.SemaphoreType.DMA((7,)),
            pltpu.SemaphoreType.DMA((7,)),
            pltpu.SemaphoreType.DMA((12,)),
        ],
        compiler_params=pltpu.CompilerParams(
            collective_id=0, has_side_effects=True, vmem_limit_bytes=62 << 20
        ),
        name="forward_part",
    )(windows, pieces, chosen, memory, one, two, entries, idx, hidden, cot, w_qkv, w_prefix, w_out, w_in, w_down)


class Line:
    def __init__(self, place, own, below, above, up, down, k, send, recv):
        self.z, self.own, self.below, self.above, self.up, self.down = place.z, own, below, above, up, down
        self.send, self.recv = send.at[k], recv.at[k]

    def rise(self, src):
        return pltpu.make_async_remote_copy(
            src_ref=src, dst_ref=self.below, send_sem=self.send.at[0], recv_sem=self.recv.at[0],
            device_id={"dp": self.z + 1}, device_id_type=MESH,
        )

    def sink(self, src):
        return pltpu.make_async_remote_copy(
            src_ref=src, dst_ref=self.above, send_sem=self.send.at[1], recv_sem=self.recv.at[1],
            device_id={"dp": self.z - 1}, device_id_type=MESH,
        )

    def start(self):
        @pl.when(self.z == 0)
        def _():
            self.below[...] = jnp.zeros_like(self.below)
            self.rise(self.own).start()

        @pl.when(self.z == 3)
        def _():
            self.above[...] = jnp.zeros_like(self.above)
            self.sink(self.own).start()

    def pass_up(self):
        self.rise(self.own).wait_recv()
        self.up[...] = (self.below[...].astype(f32) + self.own[...].astype(f32)).astype(self.up.dtype)
        self.rise(self.up).start()

    def pass_down(self):
        self.sink(self.own).wait_recv()
        self.down[...] = (self.above[...].astype(f32) + self.own[...].astype(f32)).astype(self.down.dtype)
        self.sink(self.down).start()

    def near(self):
        pl.when(self.z == 1)(self.pass_up)
        pl.when(self.z == 2)(self.pass_down)

    def far(self):
        pl.when(self.z == 1)(self.pass_down)
        pl.when(self.z == 2)(self.pass_up)

    def total(self):
        pl.when(self.z == 0)(lambda: self.sink(self.own).wait_recv())
        pl.when(self.z == 3)(lambda: self.rise(self.own).wait_recv())
        return self.own[...].astype(f32) + (self.below[...].astype(f32) + self.above[...].astype(f32))

    def drain(self):
        pl.when(self.z < 3)(lambda: self.rise(self.own).wait_send())
        pl.when(self.z > 0)(lambda: self.sink(self.own).wait_send())


CUTS = (((0, 7),), ((0, 2), (2, 4), (4, 6), (6, 7)), ((0, 2), (2, 4), (4, 6), (6, 7)))


def backward_part_kernel(
    window_ref, piece_ref, back_ref, idx_ref, gains_ref, gain_grad_ref, sums_ref,
    normed_hbm, proj_hbm, prefix_hbm, picked_hbm, attended_grad_hbm, after_grad_hbm, hidden_hbm,
    qkv_hbm, prefix_w_hbm, out_grad_hbm,
    hidden_grad_hbm, memory_grad_ref, gain_one_ref, gain_two_ref, table_ref,
    qkv_out, attn_out, in_out, down_out, prefix_out,
    normed, proj, prefix, picked, attended_grad, after, pads, tokens, slots, bias, bias_grad, lines, picked_grad,
    own, rc, rd, re, rx, ry, fat, fat_rc, fat_rd, fat_re, fat_rx, fat_ry,
    up, down, below, above, fat_below, fat_above, small, small_in, small_z,
    send, recv, z_send, z_recv, small_send, small_recv, io_sem, out_sem,
):
    place = Place()
    z = place.z
    length, width = normed.shape
    steps = length // TILE
    groups = width // GW
    eighth = width // 8
    me, other = place.c, 1 - place.c

    def io(k, src, dst):
        return pltpu.make_async_copy(src, dst, io_sem.at[k])

    load_own = io(4, out_grad_hbm.at[:, me], own)
    load_proj, load_prefix = io(5, proj_hbm, proj), io(6, prefix_hbm, prefix)
    load_grad, load_normed = io(7, attended_grad_hbm, attended_grad), io(8, normed_hbm, normed)
    load_picked, load_after = io(9, picked_hbm, picked), io(10, after_grad_hbm, after)
    for copy in (load_proj, load_prefix, load_grad, load_own, load_normed, load_picked, load_after):
        copy.start()

    barrier = pltpu.get_barrier_semaphore()
    for o in ((0, 0, 1), (0, 1, 0), (1, 0, 0)):
        pl.semaphore_signal(barrier, inc=1, device_id={"fsdp": place.at(*o)}, device_id_type=MESH)

    @pl.when(z > 0)
    def _():
        pl.semaphore_signal(barrier, inc=1, device_id={"dp": z - 1}, device_id_type=MESH)

    @pl.when(z < 3)
    def _():
        pl.semaphore_signal(barrier, inc=1, device_id={"dp": z + 1}, device_id_type=MESH)

    table_bias(gains_ref, idx_ref, bias)
    bias_grad[...] = jnp.zeros_like(bias_grad)
    pl.semaphore_wait(barrier, 5 - (z // 3) - (3 - z) // 3)

    out_unit = Scatter(place, out_grad_hbm.at[:, other], own, (rc, rd, re, rx, ry), None, send.at[0], recv.at[0])
    out_line = Line(place, out_unit.mine(0, 0), below.at[8], above.at[8], rx, ry, 8, z_send, z_recv)
    sum_lines = [
        Line(place, sums_ref.at[u], below.at[u], above.at[u], up.at[u], down.at[u], u, z_send, z_recv) for u in range(8)
    ]
    units, unit_lines, cuts = [], [], []
    for g in range(groups):
        for first, last in CUTS[g]:
            cols = slice(first * GW, last * GW)
            k = len(units)
            bufs = (
                fat_rc.at[g, :, :, cols], fat_rd.at[g, :, cols], fat_re.at[g, :, cols],
                fat_rx.at[g, :, cols], fat_ry.at[g, :, cols],
            )
            unit = Scatter(
                place, fat.at[g, :, other, :, cols], fat.at[g, :, me, :, cols], bufs, None, send.at[1 + k], recv.at[1 + k]
            )
            units.append(unit)
            cuts.append((g, first, last))
            unit_lines.append(
                Line(
                    place, unit.mine(0, 0), fat_below.at[g, :, cols], fat_above.at[g, :, cols],
                    fat_rx.at[g, :, cols], fat_ry.at[g, :, cols], 9 + k, z_send, z_recv,
                )
            )

    def settle(unit, line):
        unit.settle()
        line.start()

    def keep_block(g, s):
        out, at = (qkv_out, s) if s < 3 else (prefix_out, s - 3)
        return pltpu.make_async_copy(
            fat_rc.at[g, 0, :, s * GW : (s + 1) * GW],
            out.at[:, at * width + g * GW : at * width + (g + 1) * GW],
            out_sem.at[9 + 7 * g + s],
        )

    def store_unit(k):
        g, first, last = cuts[k]
        fat_rc[g, 0, :, first * GW : last * GW] = unit_lines[k].total().astype(bf16)
        for s in range(first, last):
            keep_block(g, s).start()

    def keep_sum(u):
        if u < 4:
            return pltpu.make_async_copy(up.at[u], down_out.at[u * eighth : (u + 1) * eighth, :], out_sem.at[u])
        return pltpu.make_async_copy(up.at[u], in_out.at[:, (u - 4) * width : (u - 3) * width], out_sem.at[u])

    def store_sum(u):
        total = sum_lines[u].total().astype(bf16)
        sum_lines[u].drain()
        up[u] = total
        keep_sum(u).start()

    keep_out = pltpu.make_async_copy(rc.at[0], attn_out, out_sem.at[8])

    def store_out():
        rc[0] = out_line.total().astype(bf16)
        keep_out.start()

    def near(*which):
        for u in which:
            sum_lines[u].near()

    def far(*which):
        for u in which:
            sum_lines[u].far()

    def store(*which):
        for u in which:
            store_sum(u)

    out_unit.core()
    each(sum_lines, "start")
    for copy in (load_proj, load_prefix, load_grad, load_own):
        copy.wait()

    def attend_back_all(g, pumps):
        def span(step):
            for i in range(SPAN):
                back_one(
                    step * SPAN + i, g, window_ref, proj, prefix, attended_grad, bias, bias_grad, pads, slots
                )
            for at, pump in enumerate(pumps):
                if pump is not None:
                    pl.when(step == at)(pump)

        loop(QPR // SPAN, span)

    def unit_grads(g):
        cols = slice(g * GW, (g + 1) * GW)
        loop(
            length // BLOCK,
            lambda b: unpad(
                b, piece_ref, [pads.at[s] for s in range(3)], [tokens.at[s, :, cols] for s in range(3)]
            ),
            4,
        )
        flat = picked[...].reshape(QPR * SLOT, width)

        def qkv_unit(s):
            part = mm(normed[...], tokens[s, :, cols], TN).astype(bf16)
            fat[g, :, :, :, pl.ds(pl.multiple_of(s * GW, GW), GW)] = part.reshape(4, 2, eighth, GW)

        def prefix_unit(s):
            part = mm(flat, slots[s, :, :, cols].reshape(QPR * SLOT, GW), TN).astype(bf16)
            fat[g, :, :, :, pl.ds(pl.multiple_of((3 + s) * GW, GW), GW)] = part.reshape(4, 2, eighth, GW)

        loop(3, qkv_unit)
        loop(4, prefix_unit)

    def both(*actions):
        def run():
            for action in actions:
                action()

        return run

    attend_back_all(0, (out_unit.fold, None, lambda: near(0), both(out_unit.relay, lambda: near(1))))
    load_normed.wait()
    load_picked.wait()
    unit_grads(0)
    units[0].core()
    near(2)
    far(0)
    settle(out_unit, out_line)
    attend_back_all(
        1,
        (
            both(lambda: near(3), lambda: far(1)),
            both(units[0].fold, lambda: near(4), lambda: far(2)),
            both(lambda: far(3), lambda: store(0)),
            both(lambda: near(5), lambda: store(1)),
        ),
    )
    unit_grads(1)
    second, third = units[1:5], units[5:9]
    second_lines, third_lines = unit_lines[1:5], unit_lines[5:9]
    each(second, "core")
    units[0].relay()
    near(6)
    far(4)
    store(2)
    attend_back_all(
        2,
        (
            both(lambda: near(7), lambda: far(5), lambda: store(3)),
            both(lambda: each(second, "fold"), lambda: settle(units[0], unit_lines[0])),
            both(out_line.near, lambda: far(6), lambda: store(4)),
            both(lambda: far(7), lambda: store(5), lambda: each(second[:2], "relay")),
        ),
    )
    load_qkv = io(5, qkv_hbm, proj.at[:, 0:width, :])
    load_qkv.start()
    unit_grads(2)
    each(third, "core")
    hidden = normed
    load_hidden = io(8, hidden_hbm, hidden)
    load_hidden.start()
    each(second[2:], "relay")
    unit_lines[0].near()
    out_line.far()
    store(6, 7)
    load_after.wait()
    load_qkv.wait()
    load_hidden.wait()
    row = lax.broadcasted_iota(jnp.int32, (8, width), 0)
    small[0] = jnp.where(row == 1, gain_grad_ref[0:1, :], 0.0)
    gain = gains_ref[0:1, :]

    def hidden_back(i):
        rows = rows_of(i)
        grad = mm(tokens[0, rows, :], proj[0, 0:width, :], NT)
        for s in range(1, 3):
            grad += mm(tokens[s, rows, :], proj[s, 0:width, :], NT)
        values = hidden[rows, :].astype(f32)
        scale = lax.rsqrt(jnp.mean(values * values, axis=1, keepdims=True) + epsilon)
        unit = values * scale
        small[0, 0:1, :] += jnp.sum(grad * unit, axis=0, keepdims=True)
        pulled = grad * gain
        after[rows, :] += scale * (pulled - unit * jnp.mean(pulled * unit, axis=1, keepdims=True))

    def settle_all(scatters, lines):
        for unit, line in zip(scatters, lines):
            settle(unit, line)

    tail_pumps = (
        both(lambda: each(third, "fold"), lambda: settle_all(second[:2], second_lines[:2])),
        both(lambda: settle_all(second[2:], second_lines[2:]), unit_lines[0].far),
        both(lambda: each(third[:2], "relay"), lambda: each(second_lines[:2], "near")),
        both(lambda: each(third[2:], "relay"), lambda: each(second_lines[2:], "near")),
    )

    def hidden_step(i):
        hidden_back(i)
        for at, pump in enumerate(tail_pumps):
            pl.when(i == at)(pump)

    loop(steps, hidden_step)
    keep_hidden = io(10, after, hidden_grad_hbm)
    keep_hidden.start()
    load_prefix_w = [io(5 + s, prefix_w_hbm.at[s], proj.at[s, 0:width, :]) for s in range(3)]
    load_prefix_w.append(io(9, prefix_w_hbm.at[3], attended_grad.at[0:width, :]))
    for copy in load_prefix_w:
        copy.start()
    small[0, 2:3, 0 : NB * H] = table_sums(bias_grad, lines, idx_ref)

    def swap(k, o):
        return pltpu.make_async_remote_copy(
            src_ref=small.at[k], dst_ref=small_in.at[k], send_sem=small_send.at[k], recv_sem=small_recv.at[k],
            device_id={"fsdp": place.at(*o)}, device_id_type=MESH,
        )

    swaps = [swap(0, (0, 0, 1)), swap(1, (0, 1, 0)), swap(2, (1, 0, 0))]
    swaps[0].start()
    each(second_lines[:2], "far")
    settle_all(third[:2], third_lines[:2])
    swaps[0].wait_recv()
    small[1] = small[0] + small_in[0]
    swaps[1].start()
    each(second_lines[2:], "far")
    settle_all(third[2:], third_lines[2:])
    store_out()
    swaps[1].wait_recv()
    small[2] = small[1] + small_in[1]
    swaps[2].start()
    each(third_lines[:2], "near")
    for copy in load_prefix_w:
        copy.wait()
    total = mm(slots[3].reshape(QPR * SLOT, width), attended_grad[0:width, :], NT)
    for s in range(3):
        total += mm(slots[s].reshape(QPR * SLOT, width), proj[s, 0:width, :], NT)
    picked_grad[...] = total.reshape(QPR, SLOT, width)
    swaps[2].wait_recv()
    small[3] = small[2] + small_in[2]
    small_line = Line(
        place, small.at[3], small_z.at[0], small_z.at[1], small_z.at[2], small_z.at[3], 18, z_send, z_recv
    )
    small_line.start()
    each(third_lines[2:], "near")
    small_line.near()
    for m in range(QPR):
        memory_grad_ref[m] = picked_grad[back_ref[m], 0:PAIRS, :]
    store_unit(0)
    each(third_lines, "far")
    small_line.far()
    for k in range(1, 7):
        store_unit(k)
    sums = small_line.total()
    shift = lax.rem(8 - place.me, 8)
    wide_roll = pltpu.roll(sums, shift * eighth, 1)
    gain_one_ref[...] = wide_roll[0:1, 0:eighth]
    gain_two_ref[...] = wide_roll[1:2, 0:eighth]
    entries = NB * H // 8
    table_roll = pltpu.roll(sums, lax.rem(width - place.me * entries, width), 1)
    table_ref[...] = table_roll[2:3, 0:entries]
    store_unit(7)
    store_unit(8)
    keep_hidden.wait()
    out_unit.drain()
    each(units, "drain")
    each([out_line, small_line] + unit_lines, "drain")
    for copy in [keep_out] + [keep_sum(u) for u in range(8)] + [keep_block(g, s) for g in range(groups) for s in range(7)]:
        copy.wait()
    for copy in swaps:
        copy.wait_send()


def backward_part(
    windows, pieces, back, idx, gains, gain_grad, sums,
    normed, proj, prefix, picked, attended_grad, after_grad, hidden, qkv, prefix_w, out_grad,
):
    length, width = hidden.shape
    eighth = width // 8
    groups = width // GW
    thick = 7 * GW
    sds = jax.ShapeDtypeStruct
    vm = lambda shape, dtype=bf16: pltpu.VMEM(shape, dtype)
    return pl.pallas_call(
        backward_part_kernel,
        out_shape=(
            sds((length, width), f32),
            sds((QPR, PAIRS, width), f32),
            sds((1, eighth), f32),
            sds((1, eighth), f32),
            sds((1, NB * H // 8), f32),
            sds((eighth, 3 * width), bf16),
            sds((eighth, width), bf16),
            sds((eighth, 4 * width), bf16),
            sds((4 * eighth, width), bf16),
            sds((eighth, 4 * width), bf16),
        ),
        in_specs=[SMEM] * 3 + [VMEM] * 4 + [ANY] * 10,
        out_specs=(ANY,) + (VMEM,) * 4 + (ANY,) * 5,
        scratch_shapes=[
            vm((length, width)),
            vm((3, length, width)),
            vm((4, QPR, SLOT, width)),
            vm((QPR, SLOT, width)),
            vm((length, width)),
            vm((length, width), f32),
            vm((3, QPR, WIN, GW)),
            vm((3, length, width)),
            vm((4, QPR, SLOT, width)),
            vm((groups, KEYS, STACK), f32),
            vm((groups, KEYS, STACK), f32),
            vm((H * WIN, KEYS), f32),
            vm((QPR, SLOT, width), f32),
            vm((4, eighth, width)),
            vm((4, eighth, width)),
            vm((eighth // 2, width)),
            vm((eighth // 2, width)),
            vm((eighth, width)),
            vm((eighth, width)),
            vm((groups, 4, 2, eighth, thick)),
            vm((groups, 4, eighth, thick)),
            vm((groups, eighth // 2, thick)),
            vm((groups, eighth // 2, thick)),
            vm((groups, eighth, thick)),
            vm((groups, eighth, thick)),
            vm((8, eighth, width)),
            vm((8, eighth, width)),
            vm((9, eighth, width)),
            vm((9, eighth, width)),
            vm((groups, eighth, thick)),
            vm((groups, eighth, thick)),
            vm((4, 8, width), f32),
            vm((3, 8, width), f32),
            vm((4, 8, width), f32),
            pltpu.SemaphoreType.DMA((10, Scatter.COPIES)),
            pltpu.SemaphoreType.DMA((10, Scatter.COPIES)),
            pltpu.SemaphoreType.DMA((19, 2)),
            pltpu.SemaphoreType.DMA((19, 2)),
            pltpu.SemaphoreType.DMA((3,)),
            pltpu.SemaphoreType.DMA((3,)),
            pltpu.SemaphoreType.DMA((11,)),
            pltpu.SemaphoreType.DMA((9 + 7 * groups,)),
        ],
        compiler_params=pltpu.CompilerParams(
            collective_id=1, has_side_effects=True, vmem_limit_bytes=62 << 20
        ),
        name="backward_part",
    )(
        windows, pieces, back, idx, gains, gain_grad, sums,
        normed, proj, prefix, picked, attended_grad, after_grad, hidden, qkv, prefix_w,
        out_grad.reshape(4, 2, eighth, width),
    )


def finish_kernel(*refs):
    count = (len(refs) - 2) // 4
    sources, results, held, wide = (refs[i * count : (i + 1) * count] for i in range(4))
    in_sem, out_sem = refs[-2:]
    loads = [pltpu.make_async_copy(src, dst, in_sem.at[k]) for k, (src, dst) in enumerate(zip(sources, held))]
    stores = [
        pltpu.make_async_copy(src if src.dtype != low.dtype else low, dst, out_sem.at[k])
        for k, (src, low, dst) in enumerate(zip(wide, held, results))
    ]
    for copy in loads:
        copy.start()
    for k, copy in enumerate(loads):
        copy.wait()
        if wide[k].dtype != held[k].dtype:
            wide[k][...] = held[k][...].astype(f32)
        stores[k].start()
    for copy in stores:
        copy.wait()


def finish(arrays, kinds):
    sds = jax.ShapeDtypeStruct
    return pl.pallas_call(
        finish_kernel,
        out_shape=tuple(sds(a.shape, kind) for a, kind in zip(arrays, kinds)),
        in_specs=[ANY] * len(arrays),
        out_specs=(ANY,) * len(arrays),
        scratch_shapes=[pltpu.VMEM(a.shape, a.dtype) for a in arrays]
        + [
            pltpu.VMEM(a.shape if kind != a.dtype else (8, 128), kind) for a, kind in zip(arrays, kinds)
        ]
        + [pltpu.SemaphoreType.DMA((len(arrays),)), pltpu.SemaphoreType.DMA((len(arrays),))],
        compiler_params=pltpu.CompilerParams(vmem_limit_bytes=62 << 20),
        name="finish",
    )(*arrays)


def near_local(
    hidden, segment_ids, memory, memory_row, buckets, attn_gain, ffn_gain, rel_table,
    w_qkv, w_attn_out, w_in, w_down, w_prefix, cotangent,
):
    length, width = hidden.shape[1:]
    windows, pieces = layout_tables(segment_ids[0])
    idx = near_buckets(buckets, length)
    padded = jnp.pad(memory[0], ((0, 0), (0, SLOT - PAIRS), (0, 0)))
    (
        output, normed, proj, prefix, picked, gains, ffn_gain_grad, attended_grad, after_grad,
        full_qkv, full_prefix, attn_out_grad, sums,
    ) = forward_part(
        windows, pieces, memory_row[0], padded, attn_gain[None], ffn_gain[None], rel_table[None], idx,
        hidden[0], cotangent[0], w_qkv, w_prefix, w_attn_out, w_in, w_down,
    )
    hidden_grad, memory_grad, *rest = backward_part(
        windows, pieces, back_order(memory_row[0]), idx, gains, ffn_gain_grad, sums, normed, proj, prefix,
        picked, attended_grad, after_grad, hidden[0], full_qkv, full_prefix.reshape(4, width, width), attn_out_grad,
    )
    output, hidden_grad, memory_grad, *grads = finish(
        (output, hidden_grad, memory_grad, *rest[3:]), (bf16,) + (f32,) * 7
    )
    return (output[None], hidden_grad[None], memory_grad[None]) + tuple(x[0] for x in rest[:3]) + tuple(grads)


def rms_scale(values, norm_gain):
    return (
        values * lax.rsqrt(jnp.mean(values * values, axis=-1, keepdims=True) + epsilon) * norm_gain
    )


def plain_forward_kernel(window_ref, piece_ref, idx_ref, gains_ref, proj, prefix, out, bias, pad):
    table_bias(gains_ref, idx_ref, bias)
    loop(QPR, lambda q: attend_one(q, window_ref, proj, prefix, bias, pad), SPAN)
    loop(out.shape[0] // BLOCK, lambda b: unpad(b, piece_ref, (pad,), (out,)))


def plain_attend(tables, proj, prefix):
    _, length, width = proj.shape
    return pl.pallas_call(
        plain_forward_kernel,
        out_shape=jax.ShapeDtypeStruct((length, width), bf16),
        in_specs=[SMEM] * 2 + [VMEM] * 4,
        out_specs=VMEM,
        scratch_shapes=[pltpu.VMEM((H // GROUP, KEYS, STACK), f32), pltpu.VMEM((QPR, WIN, width), bf16)],
        compiler_params=pltpu.CompilerParams(vmem_limit_bytes=40 << 20),
        name="attend",
    )(*tables, proj, prefix)


def plain_backward_kernel(
    window_ref, piece_ref, idx_ref, gains_ref, proj, prefix, grad,
    tokens, slots, table_ref, bias, bias_grad, pads, lines,
):
    table_bias(gains_ref, idx_ref, bias)
    bias_grad[...] = jnp.zeros_like(bias_grad)
    for g in range(grad.shape[1] // GW):
        loop(QPR, lambda q: back_one(q, g, window_ref, proj, prefix, grad, bias, bias_grad, pads, slots), SPAN)
        cols = slice(g * GW, (g + 1) * GW)
        loop(
            grad.shape[0] // BLOCK,
            lambda b: unpad(
                b, piece_ref, [pads.at[s] for s in range(3)], [tokens.at[s, :, cols] for s in range(3)]
            ),
        )
    table_ref[...] = table_sums(bias_grad, lines, idx_ref)


def plain_attend_back(tables, proj, prefix, grad):
    sds = jax.ShapeDtypeStruct
    return pl.pallas_call(
        plain_backward_kernel,
        out_shape=(sds(proj.shape, bf16), sds(prefix.shape, bf16), sds((1, NB * H), f32)),
        in_specs=[SMEM] * 2 + [VMEM] * 5,
        out_specs=(VMEM,) * 3,
        scratch_shapes=[
            pltpu.VMEM((H // GROUP, KEYS, STACK), f32),
            pltpu.VMEM((H // GROUP, KEYS, STACK), f32),
            pltpu.VMEM((3, QPR, WIN, GW), bf16),
            pltpu.VMEM((H * WIN, KEYS), f32),
        ],
        compiler_params=pltpu.CompilerParams(vmem_limit_bytes=48 << 20),
        name="attend_back",
    )(*tables, proj, prefix, grad)


def plain_row_pass(hidden, segments, memory, chosen, buckets, cotangent, full):
    attn_gain, ffn_gain, rel_table, w_qkv, w_attn_out, w_in, w_down, w_prefix = full
    length, width = hidden.shape
    tokens = hidden.astype(f32)
    gain_one = attn_gain.astype(f32)
    gain_two = ffn_gain.astype(f32)
    tables = layout_tables(segments) + (
        near_buckets(buckets, length), lines_of((attn_gain, ffn_gain, rel_table), width),
    )

    normed = rms_scale(tokens, gain_one).astype(bf16)
    projected = mm(normed, w_qkv).astype(bf16)
    picked = jnp.take(jnp.pad(memory, ((0, 0), (0, SLOT - PAIRS), (0, 0))), chosen, axis=0).reshape(QPR * SLOT, width)
    prefix = mm(picked, w_prefix).astype(bf16)
    proj = jnp.transpose(projected.reshape(length, 3, width), (1, 0, 2))
    prefix = jnp.transpose(prefix.reshape(QPR, SLOT, 4, width), (2, 0, 1, 3))
    attended = plain_attend(tables, proj, prefix)
    after_attn = tokens + mm(attended, w_attn_out)
    normed_ffn = rms_scale(after_attn, gain_two).astype(bf16)
    hidden_pre = mm(normed_ffn, w_in)
    activation = jax.nn.gelu(hidden_pre).astype(bf16)
    output = (after_attn + mm(activation, w_down)).astype(bf16)

    grad_out = cotangent.astype(f32)
    down_grad = mm(activation, cotangent, TN)
    act_grad = mm(cotangent, w_down, NT)
    pre_grad = jax.vjp(jax.nn.gelu, hidden_pre)[1](act_grad)[0].astype(bf16)
    in_grad = mm(normed_ffn, pre_grad, TN)
    normed_ffn_grad = mm(pre_grad, w_in, NT)
    residual_part, ffn_gain_grad = jax.vjp(rms_scale, after_attn, gain_two)[1](normed_ffn_grad)
    after_grad = grad_out + residual_part
    attn_branch = after_grad.astype(bf16)
    attn_out_grad = mm(attended, attn_branch, TN)
    attended_grad = mm(attn_branch, w_attn_out, NT).astype(bf16)
    token_grad, slot_grad, table_grad = plain_attend_back(tables, proj, prefix, attended_grad)
    token_grad = jnp.transpose(token_grad, (1, 0, 2)).reshape(length, 3 * width)
    slot_grad = jnp.transpose(slot_grad, (1, 2, 0, 3)).reshape(QPR * SLOT, 4 * width)
    qkv_grad = mm(normed, token_grad, TN)
    normed_grad = mm(token_grad, w_qkv, NT)
    prefix_grad = mm(picked, slot_grad, TN)
    picked_grad = mm(slot_grad, w_prefix, NT).reshape(QPR, SLOT, width)[:, :PAIRS]
    memory_grad = jnp.take(picked_grad, back_order(chosen), axis=0)
    norm_part, attn_gain_grad = jax.vjp(rms_scale, tokens, gain_one)[1](normed_grad)
    hidden_grad = after_grad + norm_part
    small = jnp.concatenate([attn_gain_grad, ffn_gain_grad, table_grad[0]])
    return output, hidden_grad, memory_grad, small, (qkv_grad, attn_out_grad, in_grad, down_grad, prefix_grad)


def plain_local(
    hidden, segment_ids, memory, memory_row, buckets, attn_gain, ffn_gain, rel_table,
    w_qkv, w_attn_out, w_in, w_down, w_prefix, cotangent,
):
    sizes = (attn_gain.shape[0], ffn_gain.shape[0], rel_table.shape[0])
    small = lax.all_gather(jnp.concatenate([attn_gain, ffn_gain, rel_table]), "fsdp", axis=0)
    cuts = (0, sizes[0], sizes[0] + sizes[1], sum(sizes))
    full = tuple(small[:, cuts[i] : cuts[i + 1]].reshape(-1) for i in range(3)) + tuple(
        lax.all_gather(w, "fsdp", axis=0, tiled=True) for w in (w_qkv, w_attn_out, w_in, w_down, w_prefix)
    )
    outs = []
    total = None
    for r in range(hidden.shape[0]):
        *own, small_grad, grads = plain_row_pass(
            hidden[r], segment_ids[r], memory[r], memory_row[r], buckets, cotangent[r], full
        )
        outs.append(own)
        fresh = (small_grad,) + grads
        total = fresh if total is None else jax.tree.map(jnp.add, total, fresh)
    output, hidden_grad, memory_grad = (jnp.stack(x) for x in zip(*outs))
    small_grad = lax.psum(total[0], ("fsdp", "dp"))
    me = lax.axis_index("fsdp")
    bases = (0, full[0].shape[0], full[0].shape[0] + full[1].shape[0])
    shares = [
        lax.dynamic_slice_in_dim(small_grad, base + me * size, size) for base, size in zip(bases, sizes)
    ]
    for gradient in total[1:]:
        share = lax.psum_scatter(gradient.astype(bf16), "fsdp", scatter_dimension=0, tiled=True)
        shares.append(lax.psum(share, "dp").astype(f32))
    return (output, hidden_grad, memory_grad) + tuple(shares)


def solution(mesh):
    rows = ("fsdp", "dp")
    placed = (
        P(rows, None, None), P(rows, None), P(rows, None, None, None), P(rows, None), P(),
        P("fsdp"), P("fsdp"), P("fsdp"),
        P("fsdp", None), P("fsdp", None), P("fsdp", None), P("fsdp", None), P("fsdp", None),
        P(rows, None, None),
    )
    near = mesh.shape["fsdp"] == 8 and mesh.shape["dp"] == 4
    return jax.shard_map(
        near_local if near else plain_local,
        mesh=mesh,
        in_specs=placed,
        out_specs=(
            P(rows, None, None), P(rows, None, None), P(rows, None, None, None),
            P("fsdp"), P("fsdp"), P("fsdp"),
            P("fsdp", None), P("fsdp", None), P("fsdp", None), P("fsdp", None), P("fsdp", None),
        ),
        check_vma=False,
    )
```

```python
import functools
import jax
import jax.numpy as jnp
from jax import lax
from jax.experimental import pallas as pl
from jax.experimental.pallas import tpu as pltpu
from jax.sharding import PartitionSpec as P

H = 12
DH = 64
NB = 32
QLEN = 64
QPR = 20
PAIRS = 10

WIN = 96
SLOT = 16
KEYS = WIN + 2 * SLOT
GROUP = 4
GW = GROUP * DH
STACK = GROUP * WIN
TILE = 256
BLOCK = 16
SPAN = 5
OVERLAP = 6

epsilon = 1e-06
masked_out = -1e30
f32 = jnp.float32
bf16 = jnp.bfloat16
NT = (((1,), (1,)), ((), ()))
TN = (((0,), (0,)), ((), ()))
MESH = pl.DeviceIdType.MESH
ANY = pl.BlockSpec(memory_space=pl.ANY)
SMEM = pl.BlockSpec(memory_space=pltpu.SMEM)
VMEM = pl.BlockSpec(memory_space=pltpu.VMEM)


def mm(a, b, dims=(((1,), (0,)), ((), ()))):
    return lax.dot_general(a, b, dims, preferred_element_type=f32)


def row_starts(segments):
    ids = jnp.arange(QPR + 1, dtype=jnp.int32)
    return jnp.sum((segments[None, :] < ids[:, None]).astype(jnp.int32), axis=1)


def near_buckets(buckets, length):
    return lax.slice_in_dim(buckets, length - QLEN, length - QLEN + KEYS).reshape(1, KEYS)


def lines_of(vectors, width):
    return jnp.concatenate(
        [jnp.pad(v.astype(f32), (0, width - v.shape[0]))[None] for v in vectors] + [jnp.zeros((8 - len(vectors), width), f32)]
    )


def loop(n, body, unroll=1):
    def step(i, carry):
        body(i)
        return carry

    lax.fori_loop(0, n, step, 0, unroll=unroll)


def each(items, name):
    for item in items:
        getattr(item, name)()


def rows_of(i):
    return pl.ds(pl.multiple_of(i * TILE, TILE), TILE)


class Place:
    def __init__(self):
        me = lax.axis_index("fsdp")
        self.me, self.c, self.x, self.y = me, me % 2, (me // 2) % 2, me // 4
        self.z = lax.axis_index("dp")

    def at(self, dy, dx, dc):
        return 4 * ((self.y + dy) % 2) + 2 * ((self.x + dx) % 2) + (self.c + dc) % 2


OTHERS = [(dy, dx, dc) for dy in (0, 1) for dx in (0, 1) for dc in (0, 1)][1:]


def greet(peers):
    barrier = pltpu.get_barrier_semaphore()
    for peer in peers:
        pl.semaphore_signal(barrier, inc=1, device_id=peer, device_id_type=MESH)
    pl.semaphore_wait(barrier, len(peers))


class Gather:
    COPIES = 8

    def __init__(self, place, shard, full, down, k, send, recv, own_sem, share=(0, 1)):
        self.p, self.shard, self.full, self.down = place, shard, full, down
        self.send, self.recv, self.own_sem = send.at[k], recv.at[k], own_sem.at[k]
        self.all_rows = shard.shape[0]
        self.rows = self.all_rows // share[1]
        self.skip = share[0] * self.rows
        self.half = self.rows // 2

    def piece(self, dy, dx, dc, part=None):
        f = self.p.at(dy, dx, dc)
        begin = (f % 2 if self.down else f) * self.all_rows + self.skip
        size = self.rows
        if part is not None:
            begin, size = begin + part * self.half, self.half
        if len(self.full.shape) == 5:
            rows = slice(None) if part is None else pl.ds(part * self.half, self.half)
            return self.full.at[:, f // 2, f % 2, rows, :]
        rows = pl.ds(pl.multiple_of(begin, 16), size)
        return self.full.at[f // 2, rows, :] if self.down else self.full.at[:, rows, :]

    def copy(self, k, src, dst, dy, dx, dc):
        return pltpu.make_async_remote_copy(
            src_ref=src, dst_ref=dst, send_sem=self.send.at[k], recv_sem=self.recv.at[k],
            device_id={"fsdp": self.p.at(dy, dx, dc)}, device_id_type=MESH,
        )

    def own(self):
        if self.down:
            return [
                pltpu.make_async_copy(
                    self.shard.at[pl.ds(self.skip, self.rows), :], self.piece(0, 0, 0), self.own_sem.at[0]
                )
            ]
        width = self.full.shape[-1]
        return [
            pltpu.make_async_copy(
                self.shard.at[:, s * width : (s + 1) * width], self.piece(0, 0, 0).at[s], self.own_sem.at[s]
            )
            for s in range(self.full.shape[0])
        ]

    def load(self):
        for copy in self.own():
            copy.start()

    def first(self):
        for copy in self.own():
            copy.wait()
        mine = self.piece(0, 0, 0)
        self.copy(0, mine, mine, 0, 1, 0).start()
        self.copy(1, mine, mine, 1, 0, 0).start()
        self.copy(2, mine, mine, 0, 0, 1).start()

    def landed(self, k, piece):
        self.copy(k, piece, piece, 0, 0, 1).wait_recv()

    def relay(self):
        from_x, from_y = self.piece(0, 1, 0), self.piece(1, 0, 0)
        self.landed(0, from_x)
        top = self.piece(0, 1, 0, 0)
        self.copy(3, top, top, 1, 0, 0).start()
        self.copy(4, from_x, from_x, 0, 0, 1).start()
        self.landed(1, from_y)
        low = self.piece(1, 0, 0, 1)
        self.copy(5, low, low, 0, 1, 0).start()
        self.copy(6, from_y, from_y, 0, 0, 1).start()

    def last(self):
        self.landed(3, self.piece(1, 1, 0, 0))
        self.landed(5, self.piece(1, 1, 0, 1))
        far = self.piece(1, 1, 0)
        self.copy(7, far, far, 0, 0, 1).start()

    def finish(self):
        self.landed(2, self.piece(0, 0, 1))
        self.landed(4, self.piece(0, 1, 1))
        self.landed(6, self.piece(1, 0, 1))
        self.landed(7, self.piece(1, 1, 1))

    def drain(self):
        whole, part = self.piece(0, 0, 0), self.piece(0, 0, 0, 0)
        for k in range(self.COPIES):
            src = part if k in (3, 5) else whole
            self.copy(k, src, src, 0, 0, 1).wait_send()


class Scatter:
    COPIES = 7

    def __init__(self, place, other, own, bufs, u, send, recv):
        self.p, self.other, self.own = place, other, own
        self.rc, self.rd, self.re, self.rx, self.ry = bufs if u is None else (b.at[u] for b in bufs)
        self.send, self.recv = send, recv
        self.half = self.rd.shape[0]

    def mine(self, dy, dx):
        return self.own.at[2 * ((self.p.y + dy) % 2) + (self.p.x + dx) % 2]

    def copy(self, k, src, dst, dy, dx, dc):
        return pltpu.make_async_remote_copy(
            src_ref=src, dst_ref=dst, send_sem=self.send.at[k], recv_sem=self.recv.at[k],
            device_id={"fsdp": self.p.at(dy, dx, dc)}, device_id_type=MESH,
        )

    def part(self, k):
        low, high = pl.ds(0, self.half), pl.ds(self.half, self.half)
        if k == 0:
            return self.copy(0, self.other, self.rc, 0, 0, 1)
        if k == 1:
            return self.copy(1, self.mine(1, 1).at[low], self.rd, 0, 1, 0)
        if k == 2:
            return self.copy(2, self.mine(1, 1).at[high], self.re, 1, 0, 0)
        if k == 3:
            return self.copy(3, self.mine(0, 1).at[low], self.rx.at[low], 0, 1, 0)
        if k == 4:
            return self.copy(4, self.mine(1, 0).at[high], self.ry.at[high], 1, 0, 0)
        if k == 5:
            return self.copy(5, self.mine(0, 1).at[high], self.rx.at[high], 0, 1, 0)
        return self.copy(6, self.mine(1, 0).at[low], self.ry.at[low], 1, 0, 0)

    def core(self):
        self.part(0).start()

    def fold(self):
        self.part(0).wait_recv()
        self.own[...] = (self.own[...].astype(f32) + self.rc[...].astype(f32)).astype(bf16)
        for k in (1, 2, 3, 4):
            self.part(k).start()

    def relay(self):
        low, high = pl.ds(0, self.half), pl.ds(self.half, self.half)
        nx, ny = self.mine(0, 1).at[high], self.mine(1, 0).at[low]
        self.part(1).wait_recv()
        ny[...] = (ny[...].astype(f32) + self.rd[...].astype(f32)).astype(bf16)
        self.part(6).start()
        self.part(2).wait_recv()
        nx[...] = (nx[...].astype(f32) + self.re[...].astype(f32)).astype(bf16)
        self.part(5).start()

    def total(self):
        for k in (3, 4, 5, 6):
            self.part(k).wait_recv()
        return self.mine(0, 0)[...].astype(f32) + (self.rx[...].astype(f32) + self.ry[...].astype(f32))

    def settle(self):
        total = self.total().astype(bf16)
        self.mine(0, 0)[...] = total

    def drain(self):
        for k in range(self.COPIES):
            self.part(k).wait_send()


GELU_A = 0.7978845608028654
GELU_B = 0.044715


def gelu_pair(v):
    square = v * v
    t = jnp.tanh(v * (GELU_A + (GELU_A * GELU_B) * square))
    half = 0.5 + 0.5 * t
    slope = half + (0.5 * v) * (1.0 - t * t) * (GELU_A + (3.0 * GELU_A * GELU_B) * square)
    return v * half, slope


def stack_heads(block):
    lane = lax.broadcasted_iota(jnp.int32, (1, GW), 1)
    parts = []
    for h in range(GROUP):
        mask = jnp.where((lane >= h * DH) & (lane < (h + 1) * DH), 1.0, 0.0).astype(bf16)
        parts.append(block * mask)
    return jnp.concatenate(parts, axis=0)


def merge_heads(stacked):
    lane = lax.broadcasted_iota(jnp.int32, (WIN, GW), 1)
    out = stacked[:WIN]
    for h in range(1, GROUP):
        out = jnp.where(lane >= h * DH, stacked[h * WIN : (h + 1) * WIN], out)
    return out


def key_tile(tokens, low, high):
    return jnp.concatenate([tokens, low, high], axis=0)


def key_cost(begin, end):
    row = lax.broadcasted_iota(jnp.int32, (KEYS, KEYS), 0)
    token = (row >= begin) & (row < end)
    first = (row >= WIN) & (row < WIN + PAIRS)
    second = (row >= WIN + SLOT) & (row < WIN + SLOT + PAIRS)
    return jnp.where(token | first | second, 0.0, masked_out).astype(f32)


def soft_columns(keys, stack, bias_block, cost):
    logits = mm(keys, stack, NT) + (bias_block + jnp.concatenate([cost] * (STACK // KEYS), axis=1))
    peak = jnp.max(logits, axis=0, keepdims=True)
    raw = jnp.exp(logits - peak)
    return raw * (1.0 / jnp.sum(raw, axis=0, keepdims=True))


def mirror():
    total = lax.broadcasted_iota(jnp.int32, (KEYS, KEYS), 0) + lax.broadcasted_iota(jnp.int32, (KEYS, KEYS), 1)
    return jnp.where((total == QLEN - 1) | (total == QLEN - 1 + KEYS), 1.0, 0.0).astype(f32)


def head_select():
    entry = lax.broadcasted_iota(jnp.int32, (16, NB * H), 1)
    return lax.rem(entry, H) == lax.broadcasted_iota(jnp.int32, (16, NB * H), 0)


def table_bias(gains, idx_ref, bias):
    wide = jnp.where(head_select(), jnp.broadcast_to(gains[2:3, : NB * H], (16, NB * H)), 0.0)
    lines = mm(mm(wide.astype(bf16), entry_hot(idx_ref)).astype(bf16), mirror().astype(bf16))
    lane = lax.broadcasted_iota(jnp.int32, (WIN, KEYS), 1)
    for g in range(H // GROUP):
        blocks = []
        for h in range(g * GROUP, (g + 1) * GROUP):
            rolled = pltpu.roll(jnp.broadcast_to(lines[h : h + 1, :], (WIN, KEYS)), 0, 1, stride=1, stride_axis=0)
            blocks.append(jnp.where(lane < WIN, rolled, 0.0))
        bias[g] = jnp.concatenate(blocks, axis=0).T


def entry_hot(idx_ref):
    off = lax.broadcasted_iota(jnp.int32, (NB * H, KEYS), 0) - H * idx_ref[...]
    return jnp.where((off >= 0) & (off < H), 1.0, 0.0).astype(bf16)


def question(window_ref, q):
    return window_ref[3 * q] * BLOCK, window_ref[3 * q + 1], window_ref[3 * q + 2]


def attend_one(q, window_ref, proj, prefix, bias, pad):
    base, begin, end = question(window_ref, q)
    cost = key_cost(begin, end)
    rows = pl.ds(base, WIN)
    width = proj.shape[2]
    for g in range(width // GW):
        cols = slice(g * GW, (g + 1) * GW)
        stack = stack_heads(proj[0, rows, cols] * bf16(DH**-0.5))
        keys = key_tile(proj[1, rows, cols], prefix[0, q, :, cols], prefix[1, q, :, cols])
        values = key_tile(proj[2, rows, cols], prefix[2, q, :, cols], prefix[3, q, :, cols])
        soft = soft_columns(keys, stack, bias[g], cost).astype(bf16)
        pad[q, :, cols] = merge_heads(mm(soft, values, TN)).astype(bf16)


def back_one(q, g, window_ref, proj, prefix, attended_grad, bias, bias_grad, pads, slots):
    base, begin, end = question(window_ref, q)
    cost = key_cost(begin, end)
    rows = pl.ds(base, WIN)
    cols = slice(g * GW, (g + 1) * GW)
    row = lax.broadcasted_iota(jnp.int32, (WIN, GW), 0)
    stack = stack_heads(proj[0, rows, cols] * bf16(DH**-0.5))
    keys = key_tile(proj[1, rows, cols], prefix[0, q, :, cols], prefix[1, q, :, cols])
    values = key_tile(proj[2, rows, cols], prefix[2, q, :, cols], prefix[3, q, :, cols])
    grad = attended_grad[rows, cols]
    grads = stack_heads(jnp.where((row >= begin) & (row < end), grad, jnp.zeros_like(grad)))
    soft = soft_columns(keys, stack, bias[g], cost)
    prob_grad = mm(values, grads, NT)
    mean = jnp.sum(soft * prob_grad, axis=0, keepdims=True)
    low = (soft * (prob_grad - mean)).astype(bf16)
    bias_grad[g] += low.astype(f32)
    key_grad = mm(low, stack).astype(bf16)
    value_grad = mm(soft.astype(bf16), grads).astype(bf16)
    pads[0, q] = (merge_heads(mm(low, keys, TN)) * DH**-0.5).astype(bf16)
    pads[1, q] = key_grad[:WIN]
    pads[2, q] = value_grad[:WIN]
    for s in range(2):
        part = slice(WIN + s * SLOT, WIN + (s + 1) * SLOT)
        slots[s, q, :, cols] = key_grad[part]
        slots[2 + s, q, :, cols] = value_grad[part]


def table_sums(bias_grad, lines, idx_ref):
    lane = lax.broadcasted_iota(jnp.int32, (H, KEYS), 1)
    for g in range(H // GROUP):
        lines[g * STACK : (g + 1) * STACK, :] = bias_grad[g].T
    sums = jnp.zeros((H, KEYS), f32)
    for i in range(WIN):
        line = jnp.where(lane < WIN, lines[pl.ds(i, H, stride=WIN), :], 0.0)
        sums += line if i == 0 else pltpu.roll(line, KEYS - i, 1)
    sums = jnp.concatenate([sums, jnp.zeros((16 - H, KEYS), f32)], axis=0)
    exact = dict(precision=lax.Precision.HIGHEST, preferred_element_type=f32)
    sums = lax.dot_general(sums, mirror(), NT, **exact)
    wide = lax.dot_general(sums, entry_hot(idx_ref).astype(f32), NT, **exact)
    return jnp.sum(jnp.where(head_select(), wide, 0.0), axis=0, keepdims=True)


def unpad(b, piece_ref, pads, outs):
    row = lax.broadcasted_iota(jnp.int32, (BLOCK, 1), 0)
    sums = [jnp.zeros((BLOCK, pad.shape[-1]), bf16) for pad in pads]
    for k in range(OVERLAP):
        at = 4 * (OVERLAP * b + k)
        q, off = piece_ref[at], piece_ref[at + 1] * BLOCK
        mine = (row >= piece_ref[at + 2]) & (row < piece_ref[at + 3])
        for s, pad in enumerate(pads):
            sums[s] = jnp.where(mine, pad[q, pl.ds(off, BLOCK), :], sums[s])
    for total, out in zip(sums, outs):
        out[pl.ds(pl.multiple_of(b * BLOCK, BLOCK), BLOCK), :] = total


def layout_tables(segments):
    length = segments.shape[0]
    starts = row_starts(segments)
    ids = jnp.arange(QPR, dtype=jnp.int32)
    low, high = starts[:-1], starts[1:]

    def pick(q, v):
        return jnp.sum(jnp.where(q[:, None] == ids[None, :], v[None, :], 0), axis=1)

    entry = jnp.arange(3 * QPR, dtype=jnp.int32)
    q, field = entry // 3, entry % 3
    begin, end = pick(q, low), pick(q, high)
    base = jnp.minimum(begin // BLOCK, (length - WIN) // BLOCK)
    windows = jnp.where(field == 0, base, jnp.where(field == 1, begin, end) - BLOCK * base)

    entry = jnp.arange(4 * OVERLAP * (length // BLOCK), dtype=jnp.int32)
    at, k, field = entry // (4 * OVERLAP) * BLOCK, entry // 4 % OVERLAP, entry % 4
    q = jnp.sum((high[None, :] <= at[:, None]).astype(jnp.int32), axis=1)
    q = jnp.minimum(q + k, QPR - 1)
    begin, end = pick(q, low), pick(q, high)
    base = jnp.minimum(begin // BLOCK, (length - WIN) // BLOCK)
    off = jnp.clip(at // BLOCK - base, 0, (WIN - BLOCK) // BLOCK)
    edge = jnp.clip(jnp.where(field == 2, begin, end) - at, 0, BLOCK)
    return windows, jnp.where(field == 0, q, jnp.where(field == 1, off, edge))


def back_order(chosen):
    ids = jnp.arange(QPR, dtype=jnp.int32)
    return jnp.sum(jnp.where(chosen[None, :] == ids[:, None], ids[None, :], 0), axis=1)


def forward_part_kernel(
    window_ref, piece_ref, chosen_ref, memory_ref, one_ref, two_ref, entry_ref, idx_ref,
    hidden_hbm, cot_hbm, qkv_w, prefix_w, out_w, in_w, down_w,
    output_hbm, normed_hbm, proj_hbm, prefix_hbm, picked_hbm, gains_ref, gain_grad_ref,
    attended_grad_hbm, after_grad_hbm, qkv_hbm, prefix_w_hbm, out_grad_hbm, sums_ref,
    w_qkv, w_prefix, w_out, w_in, w_down, hidden, cot, normed, act, slope, prefix, picked, pad, attended,
    after, down_grads, bias, small_all,
    rc, rd, re, rx, ry, send, recv, g_send, g_recv, own_sem, small_send, small_recv, io_sem,
):
    place = Place()
    length, width = hidden.shape
    steps = length // TILE
    chunks = w_in.shape[0]
    proj = slope
    weights = ((qkv_w, w_qkv), (prefix_w, w_prefix), (out_w, w_out), (in_w, w_in))
    g_qkv, g_prefix, g_out, g_in = (
        Gather(place, shard, full, False, k, g_send, g_recv, own_sem) for k, (shard, full) in enumerate(weights)
    )
    g_down, g_rest = (
        Gather(place, down_w, w_down, True, 4 + k, g_send, g_recv, own_sem, (k, 2)) for k in range(2)
    )

    def io(k, src, dst):
        return pltpu.make_async_copy(src, dst, io_sem.at[k])

    load_hidden, load_cot = io(0, hidden_hbm, hidden), io(1, cot_hbm, cot)
    for g in (g_qkv, g_prefix, g_out, g_in, g_down, g_rest):
        g.load()
    load_hidden.start()
    load_cot.start()
    small_all[0] = jnp.zeros(small_all.shape[1:], f32)
    small_all[0, 0:1, 0 : width // 8] = one_ref[...].astype(f32)
    small_all[0, 1:2, 0 : width // 8] = two_ref[...].astype(f32)
    small_all[0, 2:3, 0 : NB * H // 8] = entry_ref[...].astype(f32)
    raw = small_all[0]
    row = lax.broadcasted_iota(jnp.int32, raw.shape, 0)
    small_all[0] = jnp.where(
        row < 2,
        pltpu.roll(raw, place.me * (width // 8), 1),
        pltpu.roll(raw, place.me * (NB * H // 8), 1),
    )
    greet([{"fsdp": place.at(*o)} for o in OTHERS])

    def small_copy(k):
        return pltpu.make_async_remote_copy(
            src_ref=small_all.at[0], dst_ref=small_all.at[k + 1],
            send_sem=small_send.at[k], recv_sem=small_recv.at[k],
            device_id={"fsdp": place.at(*OTHERS[k])}, device_id_type=MESH,
        )

    for k in range(7):
        small_copy(k).start()
    g_qkv.first()
    g_prefix.first()
    load_hidden.wait()
    for q in range(QPR):
        picked[q] = memory_ref[chosen_ref[q]]
    keep_picked = io(2, picked, picked_hbm)
    keep_picked.start()
    for k in range(7):
        small_copy(k).wait_recv()
    gains_ref[...] = jnp.sum(small_all[...], axis=0)
    gain_one, gain_two = gains_ref[0:1, :], gains_ref[1:2, :]

    def norm(i):
        rows = rows_of(i)
        values = hidden[rows, :].astype(f32)
        scale = lax.rsqrt(jnp.mean(values * values, axis=1, keepdims=True) + epsilon)
        normed[rows, :] = (values * scale * gain_one).astype(bf16)

    loop(steps, norm)
    keep_normed = io(3, normed, normed_hbm)
    keep_normed.start()
    table_bias(gains_ref, idx_ref, bias)
    g_qkv.relay()
    g_out.first()
    g_prefix.relay()
    g_in.first()
    g_qkv.last()
    g_qkv.finish()
    keep_qkv = io(4, w_qkv, qkv_hbm)
    keep_qkv.start()

    def project(step):
        s, rows = step // steps, rows_of(step % steps)
        proj[s, rows, :] = mm(normed[rows, :], w_qkv[s]).astype(bf16)

    loop(3 * steps, project)
    keep_proj = io(5, proj.at[0:3], proj_hbm)
    keep_proj.start()
    g_prefix.last()
    g_prefix.finish()
    keep_prefix_w = io(6, w_prefix, prefix_w_hbm)
    keep_prefix_w.start()

    def make_prefix_slot(s):
        part = mm(picked[...].reshape(QPR * SLOT, width), w_prefix[s].reshape(width, width))
        prefix[s] = part.astype(bf16).reshape(QPR, SLOT, width)

    loop(4, make_prefix_slot)
    keep_prefix = io(7, prefix, prefix_hbm)
    keep_prefix.start()
    g_out.relay()

    def attend_some(step):
        for i in range(SPAN):
            attend_one(step * SPAN + i, window_ref, proj, prefix, bias, pad)

    loop(QPR // SPAN, attend_some)
    g_out.last()
    g_in.relay()
    g_down.first()
    g_rest.first()
    loop(length // BLOCK, lambda b: unpad(b, piece_ref, (pad,), (attended,)), 4)
    g_out.finish()
    keep_normed.wait()

    def attn_out(i):
        rows = rows_of(i)
        values = hidden[rows, :].astype(f32) + mm(attended[rows, :], w_out[0])
        after[rows, :] = values
        scale = lax.rsqrt(jnp.mean(values * values, axis=1, keepdims=True) + epsilon)
        normed[rows, :] = (values * scale * gain_two).astype(bf16)

    loop(steps, attn_out)
    g_in.last()
    g_in.finish()
    keep_proj.wait()

    def hidden_chunk(step):
        j, rows = step // steps, rows_of(step % steps)
        act_part, slope_part = gelu_pair(mm(normed[rows, :], w_in[j]))
        act[j, rows, :] = act_part.astype(bf16)
        slope[j, rows, :] = slope_part.astype(bf16)

    def hidden_some(part):
        loop(chunks * steps // 2, lambda step: hidden_chunk(step + part * chunks * steps // 2))

    hidden_some(0)
    g_down.relay()
    hidden_some(1)
    g_rest.relay()
    g_down.last()
    load_cot.wait()

    def down_chunk(step):
        j, c = step // 2, step % 2
        cols = pl.ds(pl.multiple_of(c * (width // 2), 128), width // 2)
        part = mm(act[j, :, cols], cot[...], TN)
        down_grads[j, c] = part.astype(bf16).reshape(4, width // 8, width)

    loop(chunks * 2, down_chunk)
    me, other = place.c, 1 - place.c
    downs = [
        Scatter(place, down_grads.at[:, other, u], down_grads.at[:, me, u], (rc, rd, re, rx, ry), u, send.at[u], recv.at[u])
        for u in range(4)
    ]
    each(downs, "core")
    g_rest.last()
    g_down.finish()
    g_rest.finish()

    def slope_chunk(step):
        j, rows = step // steps, rows_of(step % steps)
        act_grad = mm(cot[rows, :], w_down[j], NT)
        slope[j, rows, :] = (act_grad * slope[j, rows, :].astype(f32)).astype(bf16)

    def slope_some(part):
        loop(chunks * steps // 2, lambda step: slope_chunk(step + part * chunks * steps // 2))

    each(downs, "fold")
    slope_some(0)
    slope_some(1)
    keep_prefix_w.wait()
    keep_qkv.wait()
    g_qkv.drain()
    g_prefix.drain()
    in_grads, out_grad = w_prefix, w_qkv
    ins = [
        Scatter(
            place, in_grads.at[u, :, other], in_grads.at[u, :, me],
            (pad.at[4 * u : 4 * u + 4], rd.at[4 + u], re.at[4 + u], pad.at[16 + u], ry.at[4 + u]),
            None, send.at[4 + u], recv.at[4 + u],
        )
        for u in range(4)
    ]

    def in_chunk(step):
        j, c = step // 2, step % 2
        cols = pl.ds(pl.multiple_of(c * (width // 2), 128), width // 2)
        part = mm(normed[:, cols], slope[j], TN).astype(bf16)
        in_grads[j, pl.ds(c * 2, 2)] = part.reshape(2, 2, width // 8, width)

    loop(chunks * 2, in_chunk)
    each(ins, "core")
    each(downs, "relay")

    def out_rows(i):
        rows = rows_of(i)
        total = after[rows, :]
        for j in range(chunks):
            total += mm(act[j, rows, :], w_down[j])
        hidden[rows, :] = total.astype(bf16)

    loop(steps, out_rows)
    keep_output = io(8, hidden, output_hbm)
    keep_output.start()
    each(ins, "fold")
    gain_grad_ref[...] = jnp.zeros_like(gain_grad_ref)
    attended_grad = act.at[0]

    def back_rows(i):
        rows = rows_of(i)
        grad = mm(slope[0, rows, :], w_in[0], NT)
        for j in range(1, chunks):
            grad += mm(slope[j, rows, :], w_in[j], NT)
        values = after[rows, :]
        scale = lax.rsqrt(jnp.mean(values * values, axis=1, keepdims=True) + epsilon)
        unit = values * scale
        gain_grad_ref[0:1, :] += jnp.sum(grad * unit, axis=0, keepdims=True)
        pulled = grad * gain_two
        mixed = pulled - unit * jnp.mean(pulled * unit, axis=1, keepdims=True)
        result = cot[rows, :].astype(f32) + scale * mixed
        after[rows, :] = result
        low = result.astype(bf16)
        normed[rows, :] = low
        attended_grad[rows, :] = mm(low, w_out[0], NT).astype(bf16)

    loop(steps, back_rows)
    keep_after = io(9, after, after_grad_hbm)
    keep_after.start()
    keep_attended = io(10, attended_grad, attended_grad_hbm)
    keep_attended.start()
    for u in range(4):
        sums_ref[u] = downs[u].total().astype(bf16)
    for c in range(2):
        cols = slice(c * (width // 2), (c + 1) * (width // 2))
        out_grad[0, cols, :] = mm(attended[:, cols], normed[...], TN).astype(bf16)
    keep_out = io(11, out_grad.at[0], out_grad_hbm)
    keep_out.start()
    each(ins, "relay")
    for u in range(4):
        sums_ref[4 + u] = ins[u].total().astype(bf16)
    for k in range(7):
        small_copy(k).wait_send()
    each((g_out, g_in, g_down, g_rest), "drain")
    each(downs + ins, "drain")
    for copy in (keep_picked, keep_prefix, keep_output, keep_after, keep_attended, keep_out):
        copy.wait()


def forward_part(windows, pieces, chosen, memory, one, two, entries, idx, hidden, cot, w_qkv, w_prefix, w_out, w_in, w_down):
    length, width = hidden.shape
    chunks = w_in.shape[1] // width
    eighth = width // 8
    units = w_down.shape[0] // eighth
    sds = jax.ShapeDtypeStruct
    return pl.pallas_call(
        forward_part_kernel,
        out_shape=(
            sds((length, width), bf16),
            sds((length, width), bf16),
            sds((3, length, width), bf16),
            sds((4, QPR, SLOT, width), bf16),
            sds((QPR, SLOT, width), bf16),
            sds((8, width), f32),
            sds((8, width), f32),
            sds((length, width), bf16),
            sds((length, width), f32),
            sds((3, width, width), bf16),
            sds((4, 4, 2, eighth, width), bf16),
            sds((width, width), bf16),
            sds((2 * units, eighth, width), bf16),
        ),
        in_specs=[SMEM] * 3 + [VMEM] * 5 + [ANY] * 7,
        out_specs=(ANY,) * 5 + (VMEM,) * 2 + (ANY,) * 5 + (VMEM,),
        scratch_shapes=[
            pltpu.VMEM((3, width, width), bf16),
            pltpu.VMEM((4, 4, 2, eighth, width), bf16),
            pltpu.VMEM((1, width, width), bf16),
            pltpu.VMEM((chunks, width, width), bf16),
            pltpu.VMEM((chunks, width, width), bf16),
            pltpu.VMEM((length, width), bf16),
            pltpu.VMEM((length, width), bf16),
            pltpu.VMEM((length, width), bf16),
            pltpu.VMEM((chunks, length, width), bf16),
            pltpu.VMEM((chunks, length, width), bf16),
            pltpu.VMEM((4, QPR, SLOT, width), bf16),
            pltpu.VMEM((QPR, SLOT, width), bf16),
            pltpu.VMEM((QPR, WIN, width), bf16),
            pltpu.VMEM((length, width), bf16),
            pltpu.VMEM((length, width), f32),
            pltpu.VMEM((4, 2, units, eighth, width), bf16),
            pltpu.VMEM((H // GROUP, KEYS, STACK), f32),
            pltpu.VMEM((8, 8, width), f32),
            pltpu.VMEM((units, 4, eighth, width), bf16),
            pltpu.VMEM((2 * units, eighth // 2, width), bf16),
            pltpu.VMEM((2 * units, eighth // 2, width), bf16),
            pltpu.VMEM((units, eighth, width), bf16),
            pltpu.VMEM((2 * units, eighth, width), bf16),
            pltpu.SemaphoreType.DMA((2 * units, Scatter.COPIES)),
            pltpu.SemaphoreType.DMA((2 * units, Scatter.COPIES)),
            pltpu.SemaphoreType.DMA((6, Gather.COPIES)),
            pltpu.SemaphoreType.DMA((6, Gather.COPIES)),
            pltpu.SemaphoreType.DMA((6, 4)),
            pltpu.SemaphoreType.DMA((7,)),
            pltpu.SemaphoreType.DMA((7,)),
            pltpu.SemaphoreType.DMA((12,)),
        ],
        compiler_params=pltpu.CompilerParams(
            collective_id=0, has_side_effects=True, vmem_limit_bytes=62 << 20
        ),
        name="forward_part",
    )(windows, pieces, chosen, memory, one, two, entries, idx, hidden, cot, w_qkv, w_prefix, w_out, w_in, w_down)


class Line:
    def __init__(self, place, own, below, above, up, down, k, send, recv):
        self.z, self.own, self.below, self.above, self.up, self.down = place.z, own, below, above, up, down
        self.send, self.recv = send.at[k], recv.at[k]

    def rise(self, src):
        return pltpu.make_async_remote_copy(
            src_ref=src, dst_ref=self.below, send_sem=self.send.at[0], recv_sem=self.recv.at[0],
            device_id={"dp": self.z + 1}, device_id_type=MESH,
        )

    def sink(self, src):
        return pltpu.make_async_remote_copy(
            src_ref=src, dst_ref=self.above, send_sem=self.send.at[1], recv_sem=self.recv.at[1],
            device_id={"dp": self.z - 1}, device_id_type=MESH,
        )

    def start(self):
        @pl.when(self.z == 0)
        def _():
            self.below[...] = jnp.zeros_like(self.below)
            self.rise(self.own).start()

        @pl.when(self.z == 3)
        def _():
            self.above[...] = jnp.zeros_like(self.above)
            self.sink(self.own).start()

    def pass_up(self):
        self.rise(self.own).wait_recv()
        self.up[...] = (self.below[...].astype(f32) + self.own[...].astype(f32)).astype(self.up.dtype)
        self.rise(self.up).start()

    def pass_down(self):
        self.sink(self.own).wait_recv()
        self.down[...] = (self.above[...].astype(f32) + self.own[...].astype(f32)).astype(self.down.dtype)
        self.sink(self.down).start()

    def near(self):
        pl.when(self.z == 1)(self.pass_up)
        pl.when(self.z == 2)(self.pass_down)

    def far(self):
        pl.when(self.z == 1)(self.pass_down)
        pl.when(self.z == 2)(self.pass_up)

    def total(self):
        pl.when(self.z == 0)(lambda: self.sink(self.own).wait_recv())
        pl.when(self.z == 3)(lambda: self.rise(self.own).wait_recv())
        return self.own[...].astype(f32) + (self.below[...].astype(f32) + self.above[...].astype(f32))

    def drain(self):
        pl.when(self.z < 3)(lambda: self.rise(self.own).wait_send())
        pl.when(self.z > 0)(lambda: self.sink(self.own).wait_send())


CUTS = (((0, 7),), ((0, 2), (2, 4), (4, 6), (6, 7)), ((0, 2), (2, 4), (4, 6), (6, 7)))


def backward_part_kernel(
    window_ref, piece_ref, back_ref, idx_ref, gains_ref, gain_grad_ref, sums_ref,
    normed_hbm, proj_hbm, prefix_hbm, picked_hbm, attended_grad_hbm, after_grad_hbm, hidden_hbm,
    qkv_hbm, prefix_w_hbm, out_grad_hbm,
    hidden_grad_hbm, memory_grad_ref, gain_one_ref, gain_two_ref, table_ref,
    qkv_out, attn_out, in_out, down_out, prefix_out,
    normed, proj, prefix, picked, attended_grad, after, pads, tokens, slots, bias, bias_grad, lines, picked_grad,
    own, rc, rd, re, rx, ry, fat, fat_rc, fat_rd, fat_re, fat_rx, fat_ry,
    up, down, below, above, fat_below, fat_above, small, small_in, small_z,
    send, recv, z_send, z_recv, small_send, small_recv, io_sem, out_sem,
):
    place = Place()
    z = place.z
    length, width = normed.shape
    steps = length // TILE
    groups = width // GW
    eighth = width // 8
    me, other = place.c, 1 - place.c

    def io(k, src, dst):
        return pltpu.make_async_copy(src, dst, io_sem.at[k])

    load_own = io(4, out_grad_hbm.at[:, me], own)
    load_proj, load_prefix = io(5, proj_hbm, proj), io(6, prefix_hbm, prefix)
    load_grad, load_normed = io(7, attended_grad_hbm, attended_grad), io(8, normed_hbm, normed)
    load_picked, load_after = io(9, picked_hbm, picked), io(10, after_grad_hbm, after)
    for copy in (load_proj, load_prefix, load_grad, load_own, load_normed, load_picked, load_after):
        copy.start()

    barrier = pltpu.get_barrier_semaphore()
    for o in ((0, 0, 1), (0, 1, 0), (1, 0, 0)):
        pl.semaphore_signal(barrier, inc=1, device_id={"fsdp": place.at(*o)}, device_id_type=MESH)

    @pl.when(z > 0)
    def _():
        pl.semaphore_signal(barrier, inc=1, device_id={"dp": z - 1}, device_id_type=MESH)

    @pl.when(z < 3)
    def _():
        pl.semaphore_signal(barrier, inc=1, device_id={"dp": z + 1}, device_id_type=MESH)

    table_bias(gains_ref, idx_ref, bias)
    bias_grad[...] = jnp.zeros_like(bias_grad)
    pl.semaphore_wait(barrier, 5 - (z // 3) - (3 - z) // 3)

    out_unit = Scatter(place, out_grad_hbm.at[:, other], own, (rc, rd, re, rx, ry), None, send.at[0], recv.at[0])
    out_line = Line(place, out_unit.mine(0, 0), below.at[8], above.at[8], rx, ry, 8, z_send, z_recv)
    sum_lines = [
        Line(place, sums_ref.at[u], below.at[u], above.at[u], up.at[u], down.at[u], u, z_send, z_recv) for u in range(8)
    ]
    units, unit_lines, cuts = [], [], []
    for g in range(groups):
        for first, last in CUTS[g]:
            cols = slice(first * GW, last * GW)
            k = len(units)
            bufs = (
                fat_rc.at[g, :, :, cols], fat_rd.at[g, :, cols], fat_re.at[g, :, cols],
                fat_rx.at[g, :, cols], fat_ry.at[g, :, cols],
            )
            unit = Scatter(
                place, fat.at[g, :, other, :, cols], fat.at[g, :, me, :, cols], bufs, None, send.at[1 + k], recv.at[1 + k]
            )
            units.append(unit)
            cuts.append((g, first, last))
            unit_lines.append(
                Line(
                    place, unit.mine(0, 0), fat_below.at[g, :, cols], fat_above.at[g, :, cols],
                    fat_rx.at[g, :, cols], fat_ry.at[g, :, cols], 9 + k, z_send, z_recv,
                )
            )

    def settle(unit, line):
        unit.settle()
        line.start()

    def keep_block(g, s):
        out, at = (qkv_out, s) if s < 3 else (prefix_out, s - 3)
        return pltpu.make_async_copy(
            fat_rc.at[g, 0, :, s * GW : (s + 1) * GW],
            out.at[:, at * width + g * GW : at * width + (g + 1) * GW],
            out_sem.at[9 + 7 * g + s],
        )

    def store_unit(k):
        g, first, last = cuts[k]
        fat_rc[g, 0, :, first * GW : last * GW] = unit_lines[k].total().astype(bf16)
        for s in range(first, last):
            keep_block(g, s).start()

    def keep_sum(u):
        if u < 4:
            return pltpu.make_async_copy(up.at[u], down_out.at[u * eighth : (u + 1) * eighth, :], out_sem.at[u])
        return pltpu.make_async_copy(up.at[u], in_out.at[:, (u - 4) * width : (u - 3) * width], out_sem.at[u])

    def store_sum(u):
        total = sum_lines[u].total().astype(bf16)
        sum_lines[u].drain()
        up[u] = total
        keep_sum(u).start()

    keep_out = pltpu.make_async_copy(rc.at[0], attn_out, out_sem.at[8])

    def store_out():
        rc[0] = out_line.total().astype(bf16)
        keep_out.start()

    def near(*which):
        for u in which:
            sum_lines[u].near()

    def far(*which):
        for u in which:
            sum_lines[u].far()

    def store(*which):
        for u in which:
            store_sum(u)

    out_unit.core()
    each(sum_lines, "start")
    for copy in (load_proj, load_prefix, load_grad, load_own):
        copy.wait()

    def attend_back_all(g, pumps):
        def span(step):
            for i in range(SPAN):
                back_one(
                    step * SPAN + i, g, window_ref, proj, prefix, attended_grad, bias, bias_grad, pads, slots
                )
            for at, pump in enumerate(pumps):
                if pump is not None:
                    pl.when(step == at)(pump)

        loop(QPR // SPAN, span)

    def unit_grads(g):
        cols = slice(g * GW, (g + 1) * GW)
        loop(
            length // BLOCK,
            lambda b: unpad(
                b, piece_ref, [pads.at[s] for s in range(3)], [tokens.at[s, :, cols] for s in range(3)]
            ),
            4,
        )
        flat = picked[...].reshape(QPR * SLOT, width)

        def qkv_unit(s):
            part = mm(normed[...], tokens[s, :, cols], TN).astype(bf16)
            fat[g, :, :, :, pl.ds(pl.multiple_of(s * GW, GW), GW)] = part.reshape(4, 2, eighth, GW)

        def prefix_unit(s):
            part = mm(flat, slots[s, :, :, cols].reshape(QPR * SLOT, GW), TN).astype(bf16)
            fat[g, :, :, :, pl.ds(pl.multiple_of((3 + s) * GW, GW), GW)] = part.reshape(4, 2, eighth, GW)

        loop(3, qkv_unit)
        loop(4, prefix_unit)

    def both(*actions):
        def run():
            for action in actions:
                action()

        return run

    attend_back_all(0, (out_unit.fold, None, lambda: near(0), both(out_unit.relay, lambda: near(1))))
    load_normed.wait()
    load_picked.wait()
    unit_grads(0)
    units[0].core()
    near(2)
    far(0)
    settle(out_unit, out_line)
    attend_back_all(
        1,
        (
            both(lambda: near(3), lambda: far(1)),
            both(units[0].fold, lambda: near(4), lambda: far(2)),
            both(lambda: far(3), lambda: store(0)),
            both(lambda: near(5), lambda: store(1)),
        ),
    )
    unit_grads(1)
    second, third = units[1:5], units[5:9]
    second_lines, third_lines = unit_lines[1:5], unit_lines[5:9]
    each(second, "core")
    units[0].relay()
    near(6)
    far(4)
    store(2)
    attend_back_all(
        2,
        (
            both(lambda: near(7), lambda: far(5), lambda: store(3)),
            both(lambda: each(second, "fold"), lambda: settle(units[0], unit_lines[0])),
            both(out_line.near, lambda: far(6), lambda: store(4)),
            both(lambda: far(7), lambda: store(5), lambda: each(second[:2], "relay")),
        ),
    )
    load_qkv = io(5, qkv_hbm, proj.at[:, 0:width, :])
    load_qkv.start()
    unit_grads(2)
    each(third, "core")
    hidden = normed
    load_hidden = io(8, hidden_hbm, hidden)
    load_hidden.start()
    each(second[2:], "relay")
    unit_lines[0].near()
    out_line.far()
    store(6, 7)
    load_after.wait()
    load_qkv.wait()
    load_hidden.wait()
    row = lax.broadcasted_iota(jnp.int32, (8, width), 0)
    small[0] = jnp.where(row == 1, gain_grad_ref[0:1, :], 0.0)
    gain = gains_ref[0:1, :]

    def hidden_back(i):
        rows = rows_of(i)
        grad = mm(tokens[0, rows, :], proj[0, 0:width, :], NT)
        for s in range(1, 3):
            grad += mm(tokens[s, rows, :], proj[s, 0:width, :], NT)
        values = hidden[rows, :].astype(f32)
        scale = lax.rsqrt(jnp.mean(values * values, axis=1, keepdims=True) + epsilon)
        unit = values * scale
        small[0, 0:1, :] += jnp.sum(grad * unit, axis=0, keepdims=True)
        pulled = grad * gain
        after[rows, :] += scale * (pulled - unit * jnp.mean(pulled * unit, axis=1, keepdims=True))

    def settle_all(scatters, lines):
        for unit, line in zip(scatters, lines):
            settle(unit, line)

    tail_pumps = (
        both(lambda: each(third, "fold"), lambda: settle_all(second[:2], second_lines[:2])),
        both(lambda: settle_all(second[2:], second_lines[2:]), unit_lines[0].far),
        both(lambda: each(third[:2], "relay"), lambda: each(second_lines[:2], "near")),
        both(lambda: each(third[2:], "relay"), lambda: each(second_lines[2:], "near")),
    )

    def hidden_step(i):
        hidden_back(i)
        for at, pump in enumerate(tail_pumps):
            pl.when(i == at)(pump)

    loop(steps, hidden_step)
    keep_hidden = io(10, after, hidden_grad_hbm)
    keep_hidden.start()
    load_prefix_w = [io(5 + s, prefix_w_hbm.at[s], proj.at[s, 0:width, :]) for s in range(3)]
    load_prefix_w.append(io(9, prefix_w_hbm.at[3], attended_grad.at[0:width, :]))
    for copy in load_prefix_w:
        copy.start()
    small[0, 2:3, 0 : NB * H] = table_sums(bias_grad, lines, idx_ref)

    def swap(k, o):
        return pltpu.make_async_remote_copy(
            src_ref=small.at[k], dst_ref=small_in.at[k], send_sem=small_send.at[k], recv_sem=small_recv.at[k],
            device_id={"fsdp": place.at(*o)}, device_id_type=MESH,
        )

    swaps = [swap(0, (0, 0, 1)), swap(1, (0, 1, 0)), swap(2, (1, 0, 0))]
    swaps[0].start()
    each(second_lines[:2], "far")
    settle_all(third[:2], third_lines[:2])
    swaps[0].wait_recv()
    small[1] = small[0] + small_in[0]
    swaps[1].start()
    each(second_lines[2:], "far")
    settle_all(third[2:], third_lines[2:])
    store_out()
    swaps[1].wait_recv()
    small[2] = small[1] + small_in[1]
    swaps[2].start()
    each(third_lines[:2], "near")
    for copy in load_prefix_w:
        copy.wait()
    total = mm(slots[3].reshape(QPR * SLOT, width), attended_grad[0:width, :], NT)
    for s in range(3):
        total += mm(slots[s].reshape(QPR * SLOT, width), proj[s, 0:width, :], NT)
    picked_grad[...] = total.reshape(QPR, SLOT, width)
    swaps[2].wait_recv()
    small[3] = small[2] + small_in[2]
    small_line = Line(
        place, small.at[3], small_z.at[0], small_z.at[1], small_z.at[2], small_z.at[3], 18, z_send, z_recv
    )
    small_line.start()
    each(third_lines[2:], "near")
    small_line.near()
    for m in range(QPR):
        memory_grad_ref[m] = picked_grad[back_ref[m], 0:PAIRS, :]
    store_unit(0)
    each(third_lines, "far")
    small_line.far()
    for k in range(1, 7):
        store_unit(k)
    sums = small_line.total()
    shift = lax.rem(8 - place.me, 8)
    wide_roll = pltpu.roll(sums, shift * eighth, 1)
    gain_one_ref[...] = wide_roll[0:1, 0:eighth]
    gain_two_ref[...] = wide_roll[1:2, 0:eighth]
    entries = NB * H // 8
    table_roll = pltpu.roll(sums, lax.rem(width - place.me * entries, width), 1)
    table_ref[...] = table_roll[2:3, 0:entries]
    store_unit(7)
    store_unit(8)
    keep_hidden.wait()
    out_unit.drain()
    each(units, "drain")
    each([out_line, small_line] + unit_lines, "drain")
    for copy in [keep_out] + [keep_sum(u) for u in range(8)] + [keep_block(g, s) for g in range(groups) for s in range(7)]:
        copy.wait()
    for copy in swaps:
        copy.wait_send()


def backward_part(
    windows, pieces, back, idx, gains, gain_grad, sums,
    normed, proj, prefix, picked, attended_grad, after_grad, hidden, qkv, prefix_w, out_grad,
):
    length, width = hidden.shape
    eighth = width // 8
    groups = width // GW
    thick = 7 * GW
    sds = jax.ShapeDtypeStruct
    vm = lambda shape, dtype=bf16: pltpu.VMEM(shape, dtype)
    return pl.pallas_call(
        backward_part_kernel,
        out_shape=(
            sds((length, width), f32),
            sds((QPR, PAIRS, width), f32),
            sds((1, eighth), f32),
            sds((1, eighth), f32),
            sds((1, NB * H // 8), f32),
            sds((eighth, 3 * width), bf16),
            sds((eighth, width), bf16),
            sds((eighth, 4 * width), bf16),
            sds((4 * eighth, width), bf16),
            sds((eighth, 4 * width), bf16),
        ),
        in_specs=[SMEM] * 3 + [VMEM] * 4 + [ANY] * 10,
        out_specs=(ANY,) + (VMEM,) * 4 + (ANY,) * 5,
        scratch_shapes=[
            vm((length, width)),
            vm((3, length, width)),
            vm((4, QPR, SLOT, width)),
            vm((QPR, SLOT, width)),
            vm((length, width)),
            vm((length, width), f32),
            vm((3, QPR, WIN, GW)),
            vm((3, length, width)),
            vm((4, QPR, SLOT, width)),
            vm((groups, KEYS, STACK), f32),
            vm((groups, KEYS, STACK), f32),
            vm((H * WIN, KEYS), f32),
            vm((QPR, SLOT, width), f32),
            vm((4, eighth, width)),
            vm((4, eighth, width)),
            vm((eighth // 2, width)),
            vm((eighth // 2, width)),
            vm((eighth, width)),
            vm((eighth, width)),
            vm((groups, 4, 2, eighth, thick)),
            vm((groups, 4, eighth, thick)),
            vm((groups, eighth // 2, thick)),
            vm((groups, eighth // 2, thick)),
            vm((groups, eighth, thick)),
            vm((groups, eighth, thick)),
            vm((8, eighth, width)),
            vm((8, eighth, width)),
            vm((9, eighth, width)),
            vm((9, eighth, width)),
            vm((groups, eighth, thick)),
            vm((groups, eighth, thick)),
            vm((4, 8, width), f32),
            vm((3, 8, width), f32),
            vm((4, 8, width), f32),
            pltpu.SemaphoreType.DMA((10, Scatter.COPIES)),
            pltpu.SemaphoreType.DMA((10, Scatter.COPIES)),
            pltpu.SemaphoreType.DMA((19, 2)),
            pltpu.SemaphoreType.DMA((19, 2)),
            pltpu.SemaphoreType.DMA((3,)),
            pltpu.SemaphoreType.DMA((3,)),
            pltpu.SemaphoreType.DMA((11,)),
            pltpu.SemaphoreType.DMA((9 + 7 * groups,)),
        ],
        compiler_params=pltpu.CompilerParams(
            collective_id=1, has_side_effects=True, vmem_limit_bytes=62 << 20
        ),
        name="backward_part",
    )(
        windows, pieces, back, idx, gains, gain_grad, sums,
        normed, proj, prefix, picked, attended_grad, after_grad, hidden, qkv, prefix_w,
        out_grad.reshape(4, 2, eighth, width),
    )


def finish_kernel(*refs):
    count = (len(refs) - 2) // 4
    sources, results, held, wide = (refs[i * count : (i + 1) * count] for i in range(4))
    in_sem, out_sem = refs[-2:]
    loads = [pltpu.make_async_copy(src, dst, in_sem.at[k]) for k, (src, dst) in enumerate(zip(sources, held))]
    stores = [
        pltpu.make_async_copy(src if src.dtype != low.dtype else low, dst, out_sem.at[k])
        for k, (src, low, dst) in enumerate(zip(wide, held, results))
    ]
    for copy in loads:
        copy.start()
    for k, copy in enumerate(loads):
        copy.wait()
        if wide[k].dtype != held[k].dtype:
            wide[k][...] = held[k][...].astype(f32)
        stores[k].start()
    for copy in stores:
        copy.wait()


def finish(arrays, kinds):
    sds = jax.ShapeDtypeStruct
    return pl.pallas_call(
        finish_kernel,
        out_shape=tuple(sds(a.shape, kind) for a, kind in zip(arrays, kinds)),
        in_specs=[ANY] * len(arrays),
        out_specs=(ANY,) * len(arrays),
        scratch_shapes=[pltpu.VMEM(a.shape, a.dtype) for a in arrays]
        + [
            pltpu.VMEM(a.shape if kind != a.dtype else (8, 128), kind) for a, kind in zip(arrays, kinds)
        ]
        + [pltpu.SemaphoreType.DMA((len(arrays),)), pltpu.SemaphoreType.DMA((len(arrays),))],
        compiler_params=pltpu.CompilerParams(vmem_limit_bytes=62 << 20),
        name="finish",
    )(*arrays)


def near_local(
    hidden, segment_ids, memory, memory_row, buckets, attn_gain, ffn_gain, rel_table,
    w_qkv, w_attn_out, w_in, w_down, w_prefix, cotangent,
):
    length, width = hidden.shape[1:]
    windows, pieces = layout_tables(segment_ids[0])
    idx = near_buckets(buckets, length)
    padded = jnp.pad(memory[0], ((0, 0), (0, SLOT - PAIRS), (0, 0)))
    (
        output, normed, proj, prefix, picked, gains, ffn_gain_grad, attended_grad, after_grad,
        full_qkv, full_prefix, attn_out_grad, sums,
    ) = forward_part(
        windows, pieces, memory_row[0], padded, attn_gain[None], ffn_gain[None], rel_table[None], idx,
        hidden[0], cotangent[0], w_qkv, w_prefix, w_attn_out, w_in, w_down,
    )
    hidden_grad, memory_grad, *rest = backward_part(
        windows, pieces, back_order(memory_row[0]), idx, gains, ffn_gain_grad, sums, normed, proj, prefix,
        picked, attended_grad, after_grad, hidden[0], full_qkv, full_prefix.reshape(4, width, width), attn_out_grad,
    )
    output, hidden_grad, memory_grad, *grads = finish(
        (output, hidden_grad, memory_grad, *rest[3:]), (bf16,) + (f32,) * 7
    )
    return (output[None], hidden_grad[None], memory_grad[None]) + tuple(x[0] for x in rest[:3]) + tuple(grads)


def rms_scale(values, norm_gain):
    return (
        values * lax.rsqrt(jnp.mean(values * values, axis=-1, keepdims=True) + epsilon) * norm_gain
    )


def plain_forward_kernel(window_ref, piece_ref, idx_ref, gains_ref, proj, prefix, out, bias, pad):
    table_bias(gains_ref, idx_ref, bias)
    loop(QPR, lambda q: attend_one(q, window_ref, proj, prefix, bias, pad), SPAN)
    loop(out.shape[0] // BLOCK, lambda b: unpad(b, piece_ref, (pad,), (out,)))


def plain_attend(tables, proj, prefix):
    _, length, width = proj.shape
    return pl.pallas_call(
        plain_forward_kernel,
        out_shape=jax.ShapeDtypeStruct((length, width), bf16),
        in_specs=[SMEM] * 2 + [VMEM] * 4,
        out_specs=VMEM,
        scratch_shapes=[pltpu.VMEM((H // GROUP, KEYS, STACK), f32), pltpu.VMEM((QPR, WIN, width), bf16)],
        compiler_params=pltpu.CompilerParams(vmem_limit_bytes=40 << 20),
        name="attend",
    )(*tables, proj, prefix)


def plain_backward_kernel(
    window_ref, piece_ref, idx_ref, gains_ref, proj, prefix, grad,
    tokens, slots, table_ref, bias, bias_grad, pads, lines,
):
    table_bias(gains_ref, idx_ref, bias)
    bias_grad[...] = jnp.zeros_like(bias_grad)
    for g in range(grad.shape[1] // GW):
        loop(QPR, lambda q: back_one(q, g, window_ref, proj, prefix, grad, bias, bias_grad, pads, slots), SPAN)
        cols = slice(g * GW, (g + 1) * GW)
        loop(
            grad.shape[0] // BLOCK,
            lambda b: unpad(
                b, piece_ref, [pads.at[s] for s in range(3)], [tokens.at[s, :, cols] for s in range(3)]
            ),
        )
    table_ref[...] = table_sums(bias_grad, lines, idx_ref)


def plain_attend_back(tables, proj, prefix, grad):
    sds = jax.ShapeDtypeStruct
    return pl.pallas_call(
        plain_backward_kernel,
        out_shape=(sds(proj.shape, bf16), sds(prefix.shape, bf16), sds((1, NB * H), f32)),
        in_specs=[SMEM] * 2 + [VMEM] * 5,
        out_specs=(VMEM,) * 3,
        scratch_shapes=[
            pltpu.VMEM((H // GROUP, KEYS, STACK), f32),
            pltpu.VMEM((H // GROUP, KEYS, STACK), f32),
            pltpu.VMEM((3, QPR, WIN, GW), bf16),
            pltpu.VMEM((H * WIN, KEYS), f32),
        ],
        compiler_params=pltpu.CompilerParams(vmem_limit_bytes=48 << 20),
        name="attend_back",
    )(*tables, proj, prefix, grad)


def plain_row_pass(hidden, segments, memory, chosen, buckets, cotangent, full):
    attn_gain, ffn_gain, rel_table, w_qkv, w_attn_out, w_in, w_down, w_prefix = full
    length, width = hidden.shape
    tokens = hidden.astype(f32)
    gain_one = attn_gain.astype(f32)
    gain_two = ffn_gain.astype(f32)
    tables = layout_tables(segments) + (
        near_buckets(buckets, length), lines_of((attn_gain, ffn_gain, rel_table), width),
    )

    normed = rms_scale(tokens, gain_one).astype(bf16)
    projected = mm(normed, w_qkv).astype(bf16)
    picked = jnp.take(jnp.pad(memory, ((0, 0), (0, SLOT - PAIRS), (0, 0))), chosen, axis=0).reshape(QPR * SLOT, width)
    prefix = mm(picked, w_prefix).astype(bf16)
    proj = jnp.transpose(projected.reshape(length, 3, width), (1, 0, 2))
    prefix = jnp.transpose(prefix.reshape(QPR, SLOT, 4, width), (2, 0, 1, 3))
    attended = plain_attend(tables, proj, prefix)
    after_attn = tokens + mm(attended, w_attn_out)
    normed_ffn = rms_scale(after_attn, gain_two).astype(bf16)
    hidden_pre = mm(normed_ffn, w_in)
    activation = jax.nn.gelu(hidden_pre).astype(bf16)
    output = (after_attn + mm(activation, w_down)).astype(bf16)

    grad_out = cotangent.astype(f32)
    down_grad = mm(activation, cotangent, TN)
    act_grad = mm(cotangent, w_down, NT)
    pre_grad = jax.vjp(jax.nn.gelu, hidden_pre)[1](act_grad)[0].astype(bf16)
    in_grad = mm(normed_ffn, pre_grad, TN)
    normed_ffn_grad = mm(pre_grad, w_in, NT)
    residual_part, ffn_gain_grad = jax.vjp(rms_scale, after_attn, gain_two)[1](normed_ffn_grad)
    after_grad = grad_out + residual_part
    attn_branch = after_grad.astype(bf16)
    attn_out_grad = mm(attended, attn_branch, TN)
    attended_grad = mm(attn_branch, w_attn_out, NT).astype(bf16)
    token_grad, slot_grad, table_grad = plain_attend_back(tables, proj, prefix, attended_grad)
    token_grad = jnp.transpose(token_grad, (1, 0, 2)).reshape(length, 3 * width)
    slot_grad = jnp.transpose(slot_grad, (1, 2, 0, 3)).reshape(QPR * SLOT, 4 * width)
    qkv_grad = mm(normed, token_grad, TN)
    normed_grad = mm(token_grad, w_qkv, NT)
    prefix_grad = mm(picked, slot_grad, TN)
    picked_grad = mm(slot_grad, w_prefix, NT).reshape(QPR, SLOT, width)[:, :PAIRS]
    memory_grad = jnp.take(picked_grad, back_order(chosen), axis=0)
    norm_part, attn_gain_grad = jax.vjp(rms_scale, tokens, gain_one)[1](normed_grad)
    hidden_grad = after_grad + norm_part
    small = jnp.concatenate([attn_gain_grad, ffn_gain_grad, table_grad[0]])
    return output, hidden_grad, memory_grad, small, (qkv_grad, attn_out_grad, in_grad, down_grad, prefix_grad)


def plain_local(
    hidden, segment_ids, memory, memory_row, buckets, attn_gain, ffn_gain, rel_table,
    w_qkv, w_attn_out, w_in, w_down, w_prefix, cotangent,
):
    sizes = (attn_gain.shape[0], ffn_gain.shape[0], rel_table.shape[0])
    small = lax.all_gather(jnp.concatenate([attn_gain, ffn_gain, rel_table]), "fsdp", axis=0)
    cuts = (0, sizes[0], sizes[0] + sizes[1], sum(sizes))
    full = tuple(small[:, cuts[i] : cuts[i + 1]].reshape(-1) for i in range(3)) + tuple(
        lax.all_gather(w, "fsdp", axis=0, tiled=True) for w in (w_qkv, w_attn_out, w_in, w_down, w_prefix)
    )
    outs = []
    total = None
    for r in range(hidden.shape[0]):
        *own, small_grad, grads = plain_row_pass(
            hidden[r], segment_ids[r], memory[r], memory_row[r], buckets, cotangent[r], full
        )
        outs.append(own)
        fresh = (small_grad,) + grads
        total = fresh if total is None else jax.tree.map(jnp.add, total, fresh)
    output, hidden_grad, memory_grad = (jnp.stack(x) for x in zip(*outs))
    small_grad = lax.psum(total[0], ("fsdp", "dp"))
    me = lax.axis_index("fsdp")
    bases = (0, full[0].shape[0], full[0].shape[0] + full[1].shape[0])
    shares = [
        lax.dynamic_slice_in_dim(small_grad, base + me * size, size) for base, size in zip(bases, sizes)
    ]
    for gradient in total[1:]:
        share = lax.psum_scatter(gradient.astype(bf16), "fsdp", scatter_dimension=0, tiled=True)
        shares.append(lax.psum(share, "dp").astype(f32))
    return (output, hidden_grad, memory_grad) + tuple(shares)


def solution(mesh):
    rows = ("fsdp", "dp")
    placed = (
        P(rows, None, None), P(rows, None), P(rows, None, None, None), P(rows, None), P(),
        P("fsdp"), P("fsdp"), P("fsdp"),
        P("fsdp", None), P("fsdp", None), P("fsdp", None), P("fsdp", None), P("fsdp", None),
        P(rows, None, None),
    )
    near = mesh.shape["fsdp"] == 8 and mesh.shape["dp"] == 4
    return jax.shard_map(
        near_local if near else plain_local,
        mesh=mesh,
        in_specs=placed,
        out_specs=(
            P(rows, None, None), P(rows, None, None), P(rows, None, None, None),
            P("fsdp"), P("fsdp"), P("fsdp"),
            P("fsdp", None), P("fsdp", None), P("fsdp", None), P("fsdp", None), P("fsdp", None),
        ),
        check_vma=False,
    )
```

```python
import functools
import jax
import jax.numpy as jnp
from jax import lax
from jax.experimental import pallas as pl
from jax.experimental.pallas import tpu as pltpu
from jax.sharding import PartitionSpec as P

H = 12
DH = 64
NB = 32
QLEN = 64
QPR = 20
PAIRS = 10

WIN = 96
SLOT = 16
KEYS = WIN + 2 * SLOT
GROUP = 4
GW = GROUP * DH
STACK = GROUP * WIN
TILE = 256
BLOCK = 16
SPAN = 5
OVERLAP = 6

epsilon = 1e-06
masked_out = -1e30
f32 = jnp.float32
bf16 = jnp.bfloat16
NT = (((1,), (1,)), ((), ()))
TN = (((0,), (0,)), ((), ()))
MESH = pl.DeviceIdType.MESH
ANY = pl.BlockSpec(memory_space=pl.ANY)
SMEM = pl.BlockSpec(memory_space=pltpu.SMEM)
VMEM = pl.BlockSpec(memory_space=pltpu.VMEM)


def mm(a, b, dims=(((1,), (0,)), ((), ()))):
    return lax.dot_general(a, b, dims, preferred_element_type=f32)


def row_starts(segments):
    ids = jnp.arange(QPR + 1, dtype=jnp.int32)
    return jnp.sum((segments[None, :] < ids[:, None]).astype(jnp.int32), axis=1)


def near_buckets(buckets, length):
    return lax.slice_in_dim(buckets, length - QLEN, length - QLEN + KEYS).reshape(1, KEYS)


def lines_of(vectors, width):
    return jnp.concatenate(
        [jnp.pad(v.astype(f32), (0, width - v.shape[0]))[None] for v in vectors] + [jnp.zeros((8 - len(vectors), width), f32)]
    )


def loop(n, body, unroll=1):
    def step(i, carry):
        body(i)
        return carry

    lax.fori_loop(0, n, step, 0, unroll=unroll)


def each(items, name):
    for item in items:
        getattr(item, name)()


def rows_of(i):
    return pl.ds(pl.multiple_of(i * TILE, TILE), TILE)


class Place:
    def __init__(self):
        me = lax.axis_index("fsdp")
        self.me, self.c, self.x, self.y = me, me % 2, (me // 2) % 2, me // 4
        self.z = lax.axis_index("dp")

    def at(self, dy, dx, dc):
        return 4 * ((self.y + dy) % 2) + 2 * ((self.x + dx) % 2) + (self.c + dc) % 2


OTHERS = [(dy, dx, dc) for dy in (0, 1) for dx in (0, 1) for dc in (0, 1)][1:]


def greet(peers):
    barrier = pltpu.get_barrier_semaphore()
    for peer in peers:
        pl.semaphore_signal(barrier, inc=1, device_id=peer, device_id_type=MESH)
    pl.semaphore_wait(barrier, len(peers))


class Gather:
    COPIES = 8

    def __init__(self, place, shard, full, down, k, send, recv, own_sem, share=(0, 1)):
        self.p, self.shard, self.full, self.down = place, shard, full, down
        self.send, self.recv, self.own_sem = send.at[k], recv.at[k], own_sem.at[k]
        self.all_rows = shard.shape[0]
        self.rows = self.all_rows // share[1]
        self.skip = share[0] * self.rows
        self.half = self.rows // 2

    def piece(self, dy, dx, dc, part=None):
        f = self.p.at(dy, dx, dc)
        begin = (f % 2 if self.down else f) * self.all_rows + self.skip
        size = self.rows
        if part is not None:
            begin, size = begin + part * self.half, self.half
        if len(self.full.shape) == 5:
            rows = slice(None) if part is None else pl.ds(part * self.half, self.half)
            return self.full.at[:, f // 2, f % 2, rows, :]
        rows = pl.ds(pl.multiple_of(begin, 16), size)
        return self.full.at[f // 2, rows, :] if self.down else self.full.at[:, rows, :]

    def copy(self, k, src, dst, dy, dx, dc):
        return pltpu.make_async_remote_copy(
            src_ref=src, dst_ref=dst, send_sem=self.send.at[k], recv_sem=self.recv.at[k],
            device_id={"fsdp": self.p.at(dy, dx, dc)}, device_id_type=MESH,
        )

    def own(self):
        if self.down:
            return [
                pltpu.make_async_copy(
                    self.shard.at[pl.ds(self.skip, self.rows), :], self.piece(0, 0, 0), self.own_sem.at[0]
                )
            ]
        width = self.full.shape[-1]
        return [
            pltpu.make_async_copy(
                self.shard.at[:, s * width : (s + 1) * width], self.piece(0, 0, 0).at[s], self.own_sem.at[s]
            )
            for s in range(self.full.shape[0])
        ]

    def load(self):
        for copy in self.own():
            copy.start()

    def first(self):
        for copy in self.own():
            copy.wait()
        mine = self.piece(0, 0, 0)
        self.copy(0, mine, mine, 0, 1, 0).start()
        self.copy(1, mine, mine, 1, 0, 0).start()
        self.copy(2, mine, mine, 0, 0, 1).start()

    def landed(self, k, piece):
        self.copy(k, piece, piece, 0, 0, 1).wait_recv()

    def relay(self):
        from_x, from_y = self.piece(0, 1, 0), self.piece(1, 0, 0)
        self.landed(0, from_x)
        top = self.piece(0, 1, 0, 0)
        self.copy(3, top, top, 1, 0, 0).start()
        self.copy(4, from_x, from_x, 0, 0, 1).start()
        self.landed(1, from_y)
        low = self.piece(1, 0, 0, 1)
        self.copy(5, low, low, 0, 1, 0).start()
        self.copy(6, from_y, from_y, 0, 0, 1).start()

    def last(self):
        self.landed(3, self.piece(1, 1, 0, 0))
        self.landed(5, self.piece(1, 1, 0, 1))
        far = self.piece(1, 1, 0)
        self.copy(7, far, far, 0, 0, 1).start()

    def finish(self):
        self.landed(2, self.piece(0, 0, 1))
        self.landed(4, self.piece(0, 1, 1))
        self.landed(6, self.piece(1, 0, 1))
        self.landed(7, self.piece(1, 1, 1))

    def drain(self):
        whole, part = self.piece(0, 0, 0), self.piece(0, 0, 0, 0)
        for k in range(self.COPIES):
            src = part if k in (3, 5) else whole
            self.copy(k, src, src, 0, 0, 1).wait_send()


class Scatter:
    COPIES = 7

    def __init__(self, place, other, own, bufs, u, send, recv):
        self.p, self.other, self.own = place, other, own
        self.rc, self.rd, self.re, self.rx, self.ry = bufs if u is None else (b.at[u] for b in bufs)
        self.send, self.recv = send, recv
        self.half = self.rd.shape[0]

    def mine(self, dy, dx):
        return self.own.at[2 * ((self.p.y + dy) % 2) + (self.p.x + dx) % 2]

    def copy(self, k, src, dst, dy, dx, dc):
        return pltpu.make_async_remote_copy(
            src_ref=src, dst_ref=dst, send_sem=self.send.at[k], recv_sem=self.recv.at[k],
            device_id={"fsdp": self.p.at(dy, dx, dc)}, device_id_type=MESH,
        )

    def part(self, k):
        low, high = pl.ds(0, self.half), pl.ds(self.half, self.half)
        if k == 0:
            return self.copy(0, self.other, self.rc, 0, 0, 1)
        if k == 1:
            return self.copy(1, self.mine(1, 1).at[low], self.rd, 0, 1, 0)
        if k == 2:
            return self.copy(2, self.mine(1, 1).at[high], self.re, 1, 0, 0)
        if k == 3:
            return self.copy(3, self.mine(0, 1).at[low], self.rx.at[low], 0, 1, 0)
        if k == 4:
            return self.copy(4, self.mine(1, 0).at[high], self.ry.at[high], 1, 0, 0)
        if k == 5:
            return self.copy(5, self.mine(0, 1).at[high], self.rx.at[high], 0, 1, 0)
        return self.copy(6, self.mine(1, 0).at[low], self.ry.at[low], 1, 0, 0)

    def core(self):
        self.part(0).start()

    def fold(self):
        self.part(0).wait_recv()
        self.own[...] = (self.own[...].astype(f32) + self.rc[...].astype(f32)).astype(bf16)
        for k in (1, 2, 3, 4):
            self.part(k).start()

    def relay(self):
        low, high = pl.ds(0, self.half), pl.ds(self.half, self.half)
        nx, ny = self.mine(0, 1).at[high], self.mine(1, 0).at[low]
        self.part(1).wait_recv()
        ny[...] = (ny[...].astype(f32) + self.rd[...].astype(f32)).astype(bf16)
        self.part(6).start()
        self.part(2).wait_recv()
        nx[...] = (nx[...].astype(f32) + self.re[...].astype(f32)).astype(bf16)
        self.part(5).start()

    def total(self):
        for k in (3, 4, 5, 6):
            self.part(k).wait_recv()
        return self.mine(0, 0)[...].astype(f32) + (self.rx[...].astype(f32) + self.ry[...].astype(f32))

    def settle(self):
        total = self.total().astype(bf16)
        self.mine(0, 0)[...] = total

    def drain(self):
        for k in range(self.COPIES):
            self.part(k).wait_send()


GELU_A = 0.7978845608028654
GELU_B = 0.044715


def gelu_pair(v):
    square = v * v
    t = jnp.tanh(v * (GELU_A + (GELU_A * GELU_B) * square))
    half = 0.5 + 0.5 * t
    slope = half + (0.5 * v) * (1.0 - t * t) * (GELU_A + (3.0 * GELU_A * GELU_B) * square)
    return v * half, slope


def stack_heads(block):
    lane = lax.broadcasted_iota(jnp.int32, (1, GW), 1)
    parts = []
    for h in range(GROUP):
        mask = jnp.where((lane >= h * DH) & (lane < (h + 1) * DH), 1.0, 0.0).astype(bf16)
        parts.append(block * mask)
    return jnp.concatenate(parts, axis=0)


def merge_heads(stacked):
    lane = lax.broadcasted_iota(jnp.int32, (WIN, GW), 1)
    out = stacked[:WIN]
    for h in range(1, GROUP):
        out = jnp.where(lane >= h * DH, stacked[h * WIN : (h + 1) * WIN], out)
    return out


def key_tile(tokens, low, high):
    return jnp.concatenate([tokens, low, high], axis=0)


def key_cost(begin, end):
    row = lax.broadcasted_iota(jnp.int32, (KEYS, KEYS), 0)
    token = (row >= begin) & (row < end)
    first = (row >= WIN) & (row < WIN + PAIRS)
    second = (row >= WIN + SLOT) & (row < WIN + SLOT + PAIRS)
    return jnp.where(token | first | second, 0.0, masked_out).astype(f32)


def soft_columns(keys, stack, bias_block, cost):
    logits = mm(keys, stack, NT) + (bias_block + jnp.concatenate([cost] * (STACK // KEYS), axis=1))
    peak = jnp.max(logits, axis=0, keepdims=True)
    raw = jnp.exp(logits - peak)
    return raw * (1.0 / jnp.sum(raw, axis=0, keepdims=True))


def mirror():
    total = lax.broadcasted_iota(jnp.int32, (KEYS, KEYS), 0) + lax.broadcasted_iota(jnp.int32, (KEYS, KEYS), 1)
    return jnp.where((total == QLEN - 1) | (total == QLEN - 1 + KEYS), 1.0, 0.0).astype(f32)


def head_select():
    entry = lax.broadcasted_iota(jnp.int32, (16, NB * H), 1)
    return lax.rem(entry, H) == lax.broadcasted_iota(jnp.int32, (16, NB * H), 0)


def table_bias(gains, idx_ref, bias):
    wide = jnp.where(head_select(), jnp.broadcast_to(gains[2:3, : NB * H], (16, NB * H)), 0.0)
    lines = mm(mm(wide.astype(bf16), entry_hot(idx_ref)).astype(bf16), mirror().astype(bf16))
    lane = lax.broadcasted_iota(jnp.int32, (WIN, KEYS), 1)
    for g in range(H // GROUP):
        blocks = []
        for h in range(g * GROUP, (g + 1) * GROUP):
            rolled = pltpu.roll(jnp.broadcast_to(lines[h : h + 1, :], (WIN, KEYS)), 0, 1, stride=1, stride_axis=0)
            blocks.append(jnp.where(lane < WIN, rolled, 0.0))
        bias[g] = jnp.concatenate(blocks, axis=0).T


def entry_hot(idx_ref):
    off = lax.broadcasted_iota(jnp.int32, (NB * H, KEYS), 0) - H * idx_ref[...]
    return jnp.where((off >= 0) & (off < H), 1.0, 0.0).astype(bf16)


def question(window_ref, q):
    return window_ref[3 * q] * BLOCK, window_ref[3 * q + 1], window_ref[3 * q + 2]


def attend_one(q, window_ref, proj, prefix, bias, pad):
    base, begin, end = question(window_ref, q)
    cost = key_cost(begin, end)
    rows = pl.ds(base, WIN)
    width = proj.shape[2]
    for g in range(width // GW):
        cols = slice(g * GW, (g + 1) * GW)
        stack = stack_heads(proj[0, rows, cols] * bf16(DH**-0.5))
        keys = key_tile(proj[1, rows, cols], prefix[0, q, :, cols], prefix[1, q, :, cols])
        values = key_tile(proj[2, rows, cols], prefix[2, q, :, cols], prefix[3, q, :, cols])
        soft = soft_columns(keys, stack, bias[g], cost).astype(bf16)
        pad[q, :, cols] = merge_heads(mm(soft, values, TN)).astype(bf16)


def back_one(q, g, window_ref, proj, prefix, attended_grad, bias, bias_grad, pads, slots):
    base, begin, end = question(window_ref, q)
    cost = key_cost(begin, end)
    rows = pl.ds(base, WIN)
    cols = slice(g * GW, (g + 1) * GW)
    row = lax.broadcasted_iota(jnp.int32, (WIN, GW), 0)
    stack = stack_heads(proj[0, rows, cols] * bf16(DH**-0.5))
    keys = key_tile(proj[1, rows, cols], prefix[0, q, :, cols], prefix[1, q, :, cols])
    values = key_tile(proj[2, rows, cols], prefix[2, q, :, cols], prefix[3, q, :, cols])
    grad = attended_grad[rows, cols]
    grads = stack_heads(jnp.where((row >= begin) & (row < end), grad, jnp.zeros_like(grad)))
    soft = soft_columns(keys, stack, bias[g], cost)
    prob_grad = mm(values, grads, NT)
    mean = jnp.sum(soft * prob_grad, axis=0, keepdims=True)
    low = (soft * (prob_grad - mean)).astype(bf16)
    bias_grad[g] += low.astype(f32)
    key_grad = mm(low, stack).astype(bf16)
    value_grad = mm(soft.astype(bf16), grads).astype(bf16)
    pads[0, q] = (merge_heads(mm(low, keys, TN)) * DH**-0.5).astype(bf16)
    pads[1, q] = key_grad[:WIN]
    pads[2, q] = value_grad[:WIN]
    for s in range(2):
        part = slice(WIN + s * SLOT, WIN + (s + 1) * SLOT)
        slots[s, q, :, cols] = key_grad[part]
        slots[2 + s, q, :, cols] = value_grad[part]


def table_sums(bias_grad, lines, idx_ref):
    lane = lax.broadcasted_iota(jnp.int32, (H, KEYS), 1)
    for g in range(H // GROUP):
        lines[g * STACK : (g + 1) * STACK, :] = bias_grad[g].T
    sums = jnp.zeros((H, KEYS), f32)
    for i in range(WIN):
        line = jnp.where(lane < WIN, lines[pl.ds(i, H, stride=WIN), :], 0.0)
        sums += line if i == 0 else pltpu.roll(line, KEYS - i, 1)
    sums = jnp.concatenate([sums, jnp.zeros((16 - H, KEYS), f32)], axis=0)
    exact = dict(precision=lax.Precision.HIGHEST, preferred_element_type=f32)
    sums = lax.dot_general(sums, mirror(), NT, **exact)
    wide = lax.dot_general(sums, entry_hot(idx_ref).astype(f32), NT, **exact)
    return jnp.sum(jnp.where(head_select(), wide, 0.0), axis=0, keepdims=True)


def unpad(b, piece_ref, pads, outs):
    row = lax.broadcasted_iota(jnp.int32, (BLOCK, 1), 0)
    sums = [jnp.zeros((BLOCK, pad.shape[-1]), bf16) for pad in pads]
    for k in range(OVERLAP):
        at = 4 * (OVERLAP * b + k)
        q, off = piece_ref[at], piece_ref[at + 1] * BLOCK
        mine = (row >= piece_ref[at + 2]) & (row < piece_ref[at + 3])
        for s, pad in enumerate(pads):
            sums[s] = jnp.where(mine, pad[q, pl.ds(off, BLOCK), :], sums[s])
    for total, out in zip(sums, outs):
        out[pl.ds(pl.multiple_of(b * BLOCK, BLOCK), BLOCK), :] = total


def layout_tables(segments):
    length = segments.shape[0]
    starts = row_starts(segments)
    ids = jnp.arange(QPR, dtype=jnp.int32)
    low, high = starts[:-1], starts[1:]

    def pick(q, v):
        return jnp.sum(jnp.where(q[:, None] == ids[None, :], v[None, :], 0), axis=1)

    entry = jnp.arange(3 * QPR, dtype=jnp.int32)
    q, field = entry // 3, entry % 3
    begin, end = pick(q, low), pick(q, high)
    base = jnp.minimum(begin // BLOCK, (length - WIN) // BLOCK)
    windows = jnp.where(field == 0, base, jnp.where(field == 1, begin, end) - BLOCK * base)

    entry = jnp.arange(4 * OVERLAP * (length // BLOCK), dtype=jnp.int32)
    at, k, field = entry // (4 * OVERLAP) * BLOCK, entry // 4 % OVERLAP, entry % 4
    q = jnp.sum((high[None, :] <= at[:, None]).astype(jnp.int32), axis=1)
    q = jnp.minimum(q + k, QPR - 1)
    begin, end = pick(q, low), pick(q, high)
    base = jnp.minimum(begin // BLOCK, (length - WIN) // BLOCK)
    off = jnp.clip(at // BLOCK - base, 0, (WIN - BLOCK) // BLOCK)
    edge = jnp.clip(jnp.where(field == 2, begin, end) - at, 0, BLOCK)
    return windows, jnp.where(field == 0, q, jnp.where(field == 1, off, edge))


def back_order(chosen):
    ids = jnp.arange(QPR, dtype=jnp.int32)
    return jnp.sum(jnp.where(chosen[None, :] == ids[:, None], ids[None, :], 0), axis=1)


def forward_part_kernel(
    window_ref, piece_ref, chosen_ref, memory_ref, one_ref, two_ref, entry_ref, idx_ref,
    hidden_hbm, cot_hbm, qkv_w, prefix_w, out_w, in_w, down_w,
    output_hbm, normed_hbm, proj_hbm, prefix_hbm, picked_hbm, gains_ref, gain_grad_ref,
    attended_grad_hbm, after_grad_hbm, qkv_hbm, prefix_w_hbm, out_grad_hbm, sums_ref,
    w_qkv, w_prefix, w_out, w_in, w_down, hidden, cot, normed, act, slope, prefix, picked, pad, attended,
    after, down_grads, bias, small_all,
    rc, rd, re, rx, ry, send, recv, g_send, g_recv, own_sem, small_send, small_recv, io_sem,
):
    place = Place()
    length, width = hidden.shape
    steps = length // TILE
    chunks = w_in.shape[0]
    proj = slope
    weights = ((qkv_w, w_qkv), (prefix_w, w_prefix), (out_w, w_out), (in_w, w_in))
    g_qkv, g_prefix, g_out, g_in = (
        Gather(place, shard, full, False, k, g_send, g_recv, own_sem) for k, (shard, full) in enumerate(weights)
    )
    g_down, g_rest = (
        Gather(place, down_w, w_down, True, 4 + k, g_send, g_recv, own_sem, (k, 2)) for k in range(2)
    )

    def io(k, src, dst):
        return pltpu.make_async_copy(src, dst, io_sem.at[k])

    load_hidden, load_cot = io(0, hidden_hbm, hidden), io(1, cot_hbm, cot)
    for g in (g_qkv, g_prefix, g_out, g_in, g_down, g_rest):
        g.load()
    load_hidden.start()
    load_cot.start()
    small_all[0] = jnp.zeros(small_all.shape[1:], f32)
    small_all[0, 0:1, 0 : width // 8] = one_ref[...].astype(f32)
    small_all[0, 1:2, 0 : width // 8] = two_ref[...].astype(f32)
    small_all[0, 2:3, 0 : NB * H // 8] = entry_ref[...].astype(f32)
    raw = small_all[0]
    row = lax.broadcasted_iota(jnp.int32, raw.shape, 0)
    small_all[0] = jnp.where(
        row < 2,
        pltpu.roll(raw, place.me * (width // 8), 1),
        pltpu.roll(raw, place.me * (NB * H // 8), 1),
    )
    greet([{"fsdp": place.at(*o)} for o in OTHERS])

    def small_copy(k):
        return pltpu.make_async_remote_copy(
            src_ref=small_all.at[0], dst_ref=small_all.at[k + 1],
            send_sem=small_send.at[k], recv_sem=small_recv.at[k],
            device_id={"fsdp": place.at(*OTHERS[k])}, device_id_type=MESH,
        )

    for k in range(7):
        small_copy(k).start()
    g_qkv.first()
    g_prefix.first()
    load_hidden.wait()
    for q in range(QPR):
        picked[q] = memory_ref[chosen_ref[q]]
    keep_picked = io(2, picked, picked_hbm)
    keep_picked.start()
    for k in range(7):
        small_copy(k).wait_recv()
    gains_ref[...] = jnp.sum(small_all[...], axis=0)
    gain_one, gain_two = gains_ref[0:1, :], gains_ref[1:2, :]

    def norm(i):
        rows = rows_of(i)
        values = hidden[rows, :].astype(f32)
        scale = lax.rsqrt(jnp.mean(values * values, axis=1, keepdims=True) + epsilon)
        normed[rows, :] = (values * scale * gain_one).astype(bf16)

    loop(steps, norm)
    keep_normed = io(3, normed, normed_hbm)
    keep_normed.start()
    table_bias(gains_ref, idx_ref, bias)
    g_qkv.relay()
    g_out.first()
    g_prefix.relay()
    g_in.first()
    g_qkv.last()
    g_qkv.finish()
    keep_qkv = io(4, w_qkv, qkv_hbm)
    keep_qkv.start()

    def project(step):
        s, rows = step // steps, rows_of(step % steps)
        proj[s, rows, :] = mm(normed[rows, :], w_qkv[s]).astype(bf16)

    loop(3 * steps, project)
    keep_proj = io(5, proj.at[0:3], proj_hbm)
    keep_proj.start()
    g_prefix.last()
    g_prefix.finish()
    keep_prefix_w = io(6, w_prefix, prefix_w_hbm)
    keep_prefix_w.start()

    def make_prefix_slot(s):
        part = mm(picked[...].reshape(QPR * SLOT, width), w_prefix[s].reshape(width, width))
        prefix[s] = part.astype(bf16).reshape(QPR, SLOT, width)

    loop(4, make_prefix_slot)
    keep_prefix = io(7, prefix, prefix_hbm)
    keep_prefix.start()
    g_out.relay()

    def attend_some(step):
        for i in range(SPAN):
            attend_one(step * SPAN + i, window_ref, proj, prefix, bias, pad)

    loop(QPR // SPAN, attend_some)
    g_out.last()
    g_in.relay()
    g_down.first()
    g_rest.first()
    loop(length // BLOCK, lambda b: unpad(b, piece_ref, (pad,), (attended,)), 4)
    g_out.finish()
    keep_normed.wait()

    def attn_out(i):
        rows = rows_of(i)
        values = hidden[rows, :].astype(f32) + mm(attended[rows, :], w_out[0])
        after[rows, :] = values
        scale = lax.rsqrt(jnp.mean(values * values, axis=1, keepdims=True) + epsilon)
        normed[rows, :] = (values * scale * gain_two).astype(bf16)

    loop(steps, attn_out)
    g_in.last()
    g_in.finish()
    keep_proj.wait()

    def hidden_chunk(step):
        j, rows = step // steps, rows_of(step % steps)
        act_part, slope_part = gelu_pair(mm(normed[rows, :], w_in[j]))
        act[j, rows, :] = act_part.astype(bf16)
        slope[j, rows, :] = slope_part.astype(bf16)

    def hidden_some(part):
        loop(chunks * steps // 2, lambda step: hidden_chunk(step + part * chunks * steps // 2))

    hidden_some(0)
    g_down.relay()
    hidden_some(1)
    g_rest.relay()
    g_down.last()
    load_cot.wait()

    def down_chunk(step):
        j, c = step // 2, step % 2
        cols = pl.ds(pl.multiple_of(c * (width // 2), 128), width // 2)
        part = mm(act[j, :, cols], cot[...], TN)
        down_grads[j, c] = part.astype(bf16).reshape(4, width // 8, width)

    loop(chunks * 2, down_chunk)
    me, other = place.c, 1 - place.c
    downs = [
        Scatter(place, down_grads.at[:, other, u], down_grads.at[:, me, u], (rc, rd, re, rx, ry), u, send.at[u], recv.at[u])
        for u in range(4)
    ]
    each(downs, "core")
    g_rest.last()
    g_down.finish()
    g_rest.finish()

    def slope_chunk(step):
        j, rows = step // steps, rows_of(step % steps)
        act_grad = mm(cot[rows, :], w_down[j], NT)
        slope[j, rows, :] = (act_grad * slope[j, rows, :].astype(f32)).astype(bf16)

    def slope_some(part):
        loop(chunks * steps // 2, lambda step: slope_chunk(step + part * chunks * steps // 2))

    each(downs, "fold")
    slope_some(0)
    slope_some(1)
    keep_prefix_w.wait()
    keep_qkv.wait()
    g_qkv.drain()
    g_prefix.drain()
    in_grads, out_grad = w_prefix, w_qkv
    ins = [
        Scatter(
            place, in_grads.at[u, :, other], in_grads.at[u, :, me],
            (pad.at[4 * u : 4 * u + 4], rd.at[4 + u], re.at[4 + u], pad.at[16 + u], ry.at[4 + u]),
            None, send.at[4 + u], recv.at[4 + u],
        )
        for u in range(4)
    ]

    def in_chunk(step):
        j, c = step // 2, step % 2
        cols = pl.ds(pl.multiple_of(c * (width // 2), 128), width // 2)
        part = mm(normed[:, cols], slope[j], TN).astype(bf16)
        in_grads[j, pl.ds(c * 2, 2)] = part.reshape(2, 2, width // 8, width)
        for u in range(4):
            pl.when(step == 2 * u + 1)(ins[u].core)
        pl.when(step == 2 * chunks - 3)(lambda: each(downs, "relay"))

    loop(chunks * 2, in_chunk)
    each(ins[:3], "fold")

    def out_rows(i):
        rows = rows_of(i)
        total = after[rows, :]
        for j in range(chunks):
            total += mm(act[j, rows, :], w_down[j])
        hidden[rows, :] = total.astype(bf16)

    loop(steps, out_rows)
    keep_output = io(8, hidden, output_hbm)
    keep_output.start()
    ins[3].fold()
    gain_grad_ref[...] = jnp.zeros_like(gain_grad_ref)
    attended_grad = act.at[0]

    def back_rows(i):
        rows = rows_of(i)
        grad = mm(slope[0, rows, :], w_in[0], NT)
        for j in range(1, chunks):
            grad += mm(slope[j, rows, :], w_in[j], NT)
        values = after[rows, :]
        scale = lax.rsqrt(jnp.mean(values * values, axis=1, keepdims=True) + epsilon)
        unit = values * scale
        gain_grad_ref[0:1, :] += jnp.sum(grad * unit, axis=0, keepdims=True)
        pulled = grad * gain_two
        mixed = pulled - unit * jnp.mean(pulled * unit, axis=1, keepdims=True)
        result = cot[rows, :].astype(f32) + scale * mixed
        after[rows, :] = result
        low = result.astype(bf16)
        normed[rows, :] = low
        attended_grad[rows, :] = mm(low, w_out[0], NT).astype(bf16)
        pl.when(i == steps - 2)(lambda: each(ins[:2], "relay"))

    loop(steps, back_rows)
    each(ins[2:], "relay")
    keep_after = io(9, after, after_grad_hbm)
    keep_after.start()
    keep_attended = io(10, attended_grad, attended_grad_hbm)
    keep_attended.start()
    for u in range(4):
        sums_ref[u] = downs[u].total().astype(bf16)
    for c in range(2):
        cols = slice(c * (width // 2), (c + 1) * (width // 2))
        out_grad[0, cols, :] = mm(attended[:, cols], normed[...], TN).astype(bf16)
    keep_out = io(11, out_grad.at[0], out_grad_hbm)
    keep_out.start()
    for u in range(4):
        sums_ref[4 + u] = ins[u].total().astype(bf16)
    for k in range(7):
        small_copy(k).wait_send()
    each((g_out, g_in, g_down, g_rest), "drain")
    each(downs + ins, "drain")
    for copy in (keep_picked, keep_prefix, keep_output, keep_after, keep_attended, keep_out):
        copy.wait()


def forward_part(windows, pieces, chosen, memory, one, two, entries, idx, hidden, cot, w_qkv, w_prefix, w_out, w_in, w_down):
    length, width = hidden.shape
    chunks = w_in.shape[1] // width
    eighth = width // 8
    units = w_down.shape[0] // eighth
    sds = jax.ShapeDtypeStruct
    return pl.pallas_call(
        forward_part_kernel,
        out_shape=(
            sds((length, width), bf16),
            sds((length, width), bf16),
            sds((3, length, width), bf16),
            sds((4, QPR, SLOT, width), bf16),
            sds((QPR, SLOT, width), bf16),
            sds((8, width), f32),
            sds((8, width), f32),
            sds((length, width), bf16),
            sds((length, width), f32),
            sds((3, width, width), bf16),
            sds((4, 4, 2, eighth, width), bf16),
            sds((width, width), bf16),
            sds((2 * units, eighth, width), bf16),
        ),
        in_specs=[SMEM] * 3 + [VMEM] * 5 + [ANY] * 7,
        out_specs=(ANY,) * 5 + (VMEM,) * 2 + (ANY,) * 5 + (VMEM,),
        scratch_shapes=[
            pltpu.VMEM((3, width, width), bf16),
            pltpu.VMEM((4, 4, 2, eighth, width), bf16),
            pltpu.VMEM((1, width, width), bf16),
            pltpu.VMEM((chunks, width, width), bf16),
            pltpu.VMEM((chunks, width, width), bf16),
            pltpu.VMEM((length, width), bf16),
            pltpu.VMEM((length, width), bf16),
            pltpu.VMEM((length, width), bf16),
            pltpu.VMEM((chunks, length, width), bf16),
            pltpu.VMEM((chunks, length, width), bf16),
            pltpu.VMEM((4, QPR, SLOT, width), bf16),
            pltpu.VMEM((QPR, SLOT, width), bf16),
            pltpu.VMEM((QPR, WIN, width), bf16),
            pltpu.VMEM((length, width), bf16),
            pltpu.VMEM((length, width), f32),
            pltpu.VMEM((4, 2, units, eighth, width), bf16),
            pltpu.VMEM((H // GROUP, KEYS, STACK), f32),
            pltpu.VMEM((8, 8, width), f32),
            pltpu.VMEM((units, 4, eighth, width), bf16),
            pltpu.VMEM((2 * units, eighth // 2, width), bf16),
            pltpu.VMEM((2 * units, eighth // 2, width), bf16),
            pltpu.VMEM((units, eighth, width), bf16),
            pltpu.VMEM((2 * units, eighth, width), bf16),
            pltpu.SemaphoreType.DMA((2 * units, Scatter.COPIES)),
            pltpu.SemaphoreType.DMA((2 * units, Scatter.COPIES)),
            pltpu.SemaphoreType.DMA((6, Gather.COPIES)),
            pltpu.SemaphoreType.DMA((6, Gather.COPIES)),
            pltpu.SemaphoreType.DMA((6, 4)),
            pltpu.SemaphoreType.DMA((7,)),
            pltpu.SemaphoreType.DMA((7,)),
            pltpu.SemaphoreType.DMA((12,)),
        ],
        compiler_params=pltpu.CompilerParams(
            collective_id=0, has_side_effects=True, vmem_limit_bytes=62 << 20
        ),
        name="forward_part",
    )(windows, pieces, chosen, memory, one, two, entries, idx, hidden, cot, w_qkv, w_prefix, w_out, w_in, w_down)


class Line:
    def __init__(self, place, own, below, above, up, down, k, send, recv):
        self.z, self.own, self.below, self.above, self.up, self.down = place.z, own, below, above, up, down
        self.send, self.recv = send.at[k], recv.at[k]

    def rise(self, src):
        return pltpu.make_async_remote_copy(
            src_ref=src, dst_ref=self.below, send_sem=self.send.at[0], recv_sem=self.recv.at[0],
            device_id={"dp": self.z + 1}, device_id_type=MESH,
        )

    def sink(self, src):
        return pltpu.make_async_remote_copy(
            src_ref=src, dst_ref=self.above, send_sem=self.send.at[1], recv_sem=self.recv.at[1],
            device_id={"dp": self.z - 1}, device_id_type=MESH,
        )

    def start(self):
        @pl.when(self.z == 0)
        def _():
            self.below[...] = jnp.zeros_like(self.below)
            self.rise(self.own).start()

        @pl.when(self.z == 3)
        def _():
            self.above[...] = jnp.zeros_like(self.above)
            self.sink(self.own).start()

    def pass_up(self):
        self.rise(self.own).wait_recv()
        self.up[...] = (self.below[...].astype(f32) + self.own[...].astype(f32)).astype(self.up.dtype)
        self.rise(self.up).start()

    def pass_down(self):
        self.sink(self.own).wait_recv()
        self.down[...] = (self.above[...].astype(f32) + self.own[...].astype(f32)).astype(self.down.dtype)
        self.sink(self.down).start()

    def near(self):
        pl.when(self.z == 1)(self.pass_up)
        pl.when(self.z == 2)(self.pass_down)

    def far(self):
        pl.when(self.z == 1)(self.pass_down)
        pl.when(self.z == 2)(self.pass_up)

    def total(self):
        pl.when(self.z == 0)(lambda: self.sink(self.own).wait_recv())
        pl.when(self.z == 3)(lambda: self.rise(self.own).wait_recv())
        return self.own[...].astype(f32) + (self.below[...].astype(f32) + self.above[...].astype(f32))

    def drain(self):
        pl.when(self.z < 3)(lambda: self.rise(self.own).wait_send())
        pl.when(self.z > 0)(lambda: self.sink(self.own).wait_send())


CUTS = (((0, 7),), ((0, 2), (2, 4), (4, 6), (6, 7)), ((0, 2), (2, 4), (4, 6), (6, 7)))


def backward_part_kernel(
    window_ref, piece_ref, back_ref, idx_ref, gains_ref, gain_grad_ref, sums_ref,
    normed_hbm, proj_hbm, prefix_hbm, picked_hbm, attended_grad_hbm, after_grad_hbm, hidden_hbm,
    qkv_hbm, prefix_w_hbm, out_grad_hbm,
    hidden_grad_hbm, memory_grad_ref, gain_one_ref, gain_two_ref, table_ref,
    qkv_out, attn_out, in_out, down_out, prefix_out,
    normed, proj, prefix, picked, attended_grad, after, pads, tokens, slots, bias, bias_grad, lines, picked_grad,
    own, rc, rd, re, rx, ry, fat, fat_rc, fat_rd, fat_re, fat_rx, fat_ry,
    up, down, below, above, fat_below, fat_above, small, small_in, small_z,
    send, recv, z_send, z_recv, small_send, small_recv, io_sem, out_sem,
):
    place = Place()
    z = place.z
    length, width = normed.shape
    steps = length // TILE
    groups = width // GW
    eighth = width // 8
    me, other = place.c, 1 - place.c

    def io(k, src, dst):
        return pltpu.make_async_copy(src, dst, io_sem.at[k])

    load_own = io(4, out_grad_hbm.at[:, me], own)
    load_proj, load_prefix = io(5, proj_hbm, proj), io(6, prefix_hbm, prefix)
    load_grad, load_normed = io(7, attended_grad_hbm, attended_grad), io(8, normed_hbm, normed)
    load_picked, load_after = io(9, picked_hbm, picked), io(10, after_grad_hbm, after)
    for copy in (load_proj, load_prefix, load_grad, load_own, load_normed, load_picked, load_after):
        copy.start()

    barrier = pltpu.get_barrier_semaphore()
    for o in ((0, 0, 1), (0, 1, 0), (1, 0, 0)):
        pl.semaphore_signal(barrier, inc=1, device_id={"fsdp": place.at(*o)}, device_id_type=MESH)

    @pl.when(z > 0)
    def _():
        pl.semaphore_signal(barrier, inc=1, device_id={"dp": z - 1}, device_id_type=MESH)

    @pl.when(z < 3)
    def _():
        pl.semaphore_signal(barrier, inc=1, device_id={"dp": z + 1}, device_id_type=MESH)

    table_bias(gains_ref, idx_ref, bias)
    bias_grad[...] = jnp.zeros_like(bias_grad)
    pl.semaphore_wait(barrier, 5 - (z // 3) - (3 - z) // 3)

    out_unit = Scatter(place, out_grad_hbm.at[:, other], own, (rc, rd, re, rx, ry), None, send.at[0], recv.at[0])
    out_line = Line(place, out_unit.mine(0, 0), below.at[8], above.at[8], rx, ry, 8, z_send, z_recv)
    sum_lines = [
        Line(place, sums_ref.at[u], below.at[u], above.at[u], up.at[u], down.at[u], u, z_send, z_recv) for u in range(8)
    ]
    units, unit_lines, cuts = [], [], []
    for g in range(groups):
        for first, last in CUTS[g]:
            cols = slice(first * GW, last * GW)
            k = len(units)
            bufs = (
                fat_rc.at[g, :, :, cols], fat_rd.at[g, :, cols], fat_re.at[g, :, cols],
                fat_rx.at[g, :, cols], fat_ry.at[g, :, cols],
            )
            unit = Scatter(
                place, fat.at[g, :, other, :, cols], fat.at[g, :, me, :, cols], bufs, None, send.at[1 + k], recv.at[1 + k]
            )
            units.append(unit)
            cuts.append((g, first, last))
            unit_lines.append(
                Line(
                    place, unit.mine(0, 0), fat_below.at[g, :, cols], fat_above.at[g, :, cols],
                    fat_rx.at[g, :, cols], fat_ry.at[g, :, cols], 9 + k, z_send, z_recv,
                )
            )

    def settle(unit, line):
        unit.settle()
        line.start()

    def keep_block(g, s):
        out, at = (qkv_out, s) if s < 3 else (prefix_out, s - 3)
        return pltpu.make_async_copy(
            fat_rc.at[g, 0, :, s * GW : (s + 1) * GW],
            out.at[:, at * width + g * GW : at * width + (g + 1) * GW],
            out_sem.at[9 + 7 * g + s],
        )

    def store_unit(k):
        g, first, last = cuts[k]
        fat_rc[g, 0, :, first * GW : last * GW] = unit_lines[k].total().astype(bf16)
        for s in range(first, last):
            keep_block(g, s).start()

    def keep_sum(u):
        if u < 4:
            return pltpu.make_async_copy(up.at[u], down_out.at[u * eighth : (u + 1) * eighth, :], out_sem.at[u])
        return pltpu.make_async_copy(up.at[u], in_out.at[:, (u - 4) * width : (u - 3) * width], out_sem.at[u])

    def store_sum(u):
        total = sum_lines[u].total().astype(bf16)
        sum_lines[u].drain()
        up[u] = total
        keep_sum(u).start()

    keep_out = pltpu.make_async_copy(rc.at[0], attn_out, out_sem.at[8])

    def store_out():
        rc[0] = out_line.total().astype(bf16)
        keep_out.start()

    def near(*which):
        for u in which:
            sum_lines[u].near()

    def far(*which):
        for u in which:
            sum_lines[u].far()

    def store(*which):
        for u in which:
            store_sum(u)

    out_unit.core()
    each(sum_lines, "start")
    for copy in (load_proj, load_prefix, load_grad, load_own):
        copy.wait()

    def attend_back_all(g, pumps):
        def span(step):
            for i in range(SPAN):
                back_one(
                    step * SPAN + i, g, window_ref, proj, prefix, attended_grad, bias, bias_grad, pads, slots
                )
            for at, pump in enumerate(pumps):
                if pump is not None:
                    pl.when(step == at)(pump)

        loop(QPR // SPAN, span)

    def unit_grads(g):
        cols = slice(g * GW, (g + 1) * GW)
        loop(
            length // BLOCK,
            lambda b: unpad(
                b, piece_ref, [pads.at[s] for s in range(3)], [tokens.at[s, :, cols] for s in range(3)]
            ),
            4,
        )
        flat = picked[...].reshape(QPR * SLOT, width)

        def qkv_unit(s):
            part = mm(normed[...], tokens[s, :, cols], TN).astype(bf16)
            fat[g, :, :, :, pl.ds(pl.multiple_of(s * GW, GW), GW)] = part.reshape(4, 2, eighth, GW)

        def prefix_unit(s):
            part = mm(flat, slots[s, :, :, cols].reshape(QPR * SLOT, GW), TN).astype(bf16)
            fat[g, :, :, :, pl.ds(pl.multiple_of((3 + s) * GW, GW), GW)] = part.reshape(4, 2, eighth, GW)

        loop(3, qkv_unit)
        loop(4, prefix_unit)

    def both(*actions):
        def run():
            for action in actions:
                action()

        return run

    attend_back_all(0, (out_unit.fold, None, lambda: near(0), both(out_unit.relay, lambda: near(1))))
    load_normed.wait()
    load_picked.wait()
    unit_grads(0)
    units[0].core()
    near(2)
    far(0)
    settle(out_unit, out_line)
    attend_back_all(
        1,
        (
            both(lambda: near(3), lambda: far(1)),
            both(units[0].fold, lambda: near(4), lambda: far(2)),
            both(lambda: far(3), lambda: store(0)),
            both(lambda: near(5), lambda: store(1)),
        ),
    )
    unit_grads(1)
    second, third = units[1:5], units[5:9]
    second_lines, third_lines = unit_lines[1:5], unit_lines[5:9]
    each(second, "core")
    units[0].relay()
    near(6)
    far(4)
    store(2)
    attend_back_all(
        2,
        (
            both(lambda: near(7), lambda: far(5), lambda: store(3)),
            both(lambda: each(second, "fold"), lambda: settle(units[0], unit_lines[0])),
            both(out_line.near, lambda: far(6), lambda: store(4)),
            both(lambda: far(7), lambda: store(5), lambda: each(second[:2], "relay")),
        ),
    )
    load_qkv = io(5, qkv_hbm, proj.at[:, 0:width, :])
    load_qkv.start()
    unit_grads(2)
    each(third, "core")
    hidden = normed
    load_hidden = io(8, hidden_hbm, hidden)
    load_hidden.start()
    each(second[2:], "relay")
    unit_lines[0].near()
    out_line.far()
    store(6, 7)
    load_after.wait()
    load_qkv.wait()
    load_hidden.wait()
    row = lax.broadcasted_iota(jnp.int32, (8, width), 0)
    small[0] = jnp.where(row == 1, gain_grad_ref[0:1, :], 0.0)
    gain = gains_ref[0:1, :]

    def hidden_back(i):
        rows = rows_of(i)
        grad = mm(tokens[0, rows, :], proj[0, 0:width, :], NT)
        for s in range(1, 3):
            grad += mm(tokens[s, rows, :], proj[s, 0:width, :], NT)
        values = hidden[rows, :].astype(f32)
        scale = lax.rsqrt(jnp.mean(values * values, axis=1, keepdims=True) + epsilon)
        unit = values * scale
        small[0, 0:1, :] += jnp.sum(grad * unit, axis=0, keepdims=True)
        pulled = grad * gain
        after[rows, :] += scale * (pulled - unit * jnp.mean(pulled * unit, axis=1, keepdims=True))

    def settle_all(scatters, lines):
        for unit, line in zip(scatters, lines):
            settle(unit, line)

    tail_pumps = (
        both(lambda: each(third, "fold"), lambda: settle_all(second[:2], second_lines[:2])),
        both(lambda: settle_all(second[2:], second_lines[2:]), unit_lines[0].far),
        both(lambda: each(third[:2], "relay"), lambda: each(second_lines[:2], "near")),
        both(lambda: each(third[2:], "relay"), lambda: each(second_lines[2:], "near")),
    )

    def hidden_step(i):
        hidden_back(i)
        for at, pump in enumerate(tail_pumps):
            pl.when(i == at)(pump)

    loop(steps, hidden_step)
    keep_hidden = io(10, after, hidden_grad_hbm)
    keep_hidden.start()
    load_prefix_w = [io(5 + s, prefix_w_hbm.at[s], proj.at[s, 0:width, :]) for s in range(3)]
    load_prefix_w.append(io(9, prefix_w_hbm.at[3], attended_grad.at[0:width, :]))
    for copy in load_prefix_w:
        copy.start()
    small[0, 2:3, 0 : NB * H] = table_sums(bias_grad, lines, idx_ref)

    def swap(k, o):
        return pltpu.make_async_remote_copy(
            src_ref=small.at[k], dst_ref=small_in.at[k], send_sem=small_send.at[k], recv_sem=small_recv.at[k],
            device_id={"fsdp": place.at(*o)}, device_id_type=MESH,
        )

    swaps = [swap(0, (0, 0, 1)), swap(1, (0, 1, 0)), swap(2, (1, 0, 0))]
    swaps[0].start()
    each(second_lines[:2], "far")
    settle_all(third[:2], third_lines[:2])
    swaps[0].wait_recv()
    small[1] = small[0] + small_in[0]
    swaps[1].start()
    each(second_lines[2:], "far")
    settle_all(third[2:], third_lines[2:])
    store_out()
    swaps[1].wait_recv()
    small[2] = small[1] + small_in[1]
    swaps[2].start()
    each(third_lines[:2], "near")
    for copy in load_prefix_w:
        copy.wait()
    total = mm(slots[3].reshape(QPR * SLOT, width), attended_grad[0:width, :], NT)
    for s in range(3):
        total += mm(slots[s].reshape(QPR * SLOT, width), proj[s, 0:width, :], NT)
    picked_grad[...] = total.reshape(QPR, SLOT, width)
    swaps[2].wait_recv()
    small[3] = small[2] + small_in[2]
    small_line = Line(
        place, small.at[3], small_z.at[0], small_z.at[1], small_z.at[2], small_z.at[3], 18, z_send, z_recv
    )
    small_line.start()
    each(third_lines[2:], "near")
    small_line.near()
    for m in range(QPR):
        memory_grad_ref[m] = picked_grad[back_ref[m], 0:PAIRS, :]
    store_unit(0)
    each(third_lines, "far")
    small_line.far()
    for k in range(1, 7):
        store_unit(k)
    sums = small_line.total()
    shift = lax.rem(8 - place.me, 8)
    wide_roll = pltpu.roll(sums, shift * eighth, 1)
    gain_one_ref[...] = wide_roll[0:1, 0:eighth]
    gain_two_ref[...] = wide_roll[1:2, 0:eighth]
    entries = NB * H // 8
    table_roll = pltpu.roll(sums, lax.rem(width - place.me * entries, width), 1)
    table_ref[...] = table_roll[2:3, 0:entries]
    store_unit(7)
    store_unit(8)
    keep_hidden.wait()
    out_unit.drain()
    each(units, "drain")
    each([out_line, small_line] + unit_lines, "drain")
    for copy in [keep_out] + [keep_sum(u) for u in range(8)] + [keep_block(g, s) for g in range(groups) for s in range(7)]:
        copy.wait()
    for copy in swaps:
        copy.wait_send()


def backward_part(
    windows, pieces, back, idx, gains, gain_grad, sums,
    normed, proj, prefix, picked, attended_grad, after_grad, hidden, qkv, prefix_w, out_grad,
):
    length, width = hidden.shape
    eighth = width // 8
    groups = width // GW
    thick = 7 * GW
    sds = jax.ShapeDtypeStruct
    vm = lambda shape, dtype=bf16: pltpu.VMEM(shape, dtype)
    return pl.pallas_call(
        backward_part_kernel,
        out_shape=(
            sds((length, width), f32),
            sds((QPR, PAIRS, width), f32),
            sds((1, eighth), f32),
            sds((1, eighth), f32),
            sds((1, NB * H // 8), f32),
            sds((eighth, 3 * width), bf16),
            sds((eighth, width), bf16),
            sds((eighth, 4 * width), bf16),
            sds((4 * eighth, width), bf16),
            sds((eighth, 4 * width), bf16),
        ),
        in_specs=[SMEM] * 3 + [VMEM] * 4 + [ANY] * 10,
        out_specs=(ANY,) + (VMEM,) * 4 + (ANY,) * 5,
        scratch_shapes=[
            vm((length, width)),
            vm((3, length, width)),
            vm((4, QPR, SLOT, width)),
            vm((QPR, SLOT, width)),
            vm((length, width)),
            vm((length, width), f32),
            vm((3, QPR, WIN, GW)),
            vm((3, length, width)),
            vm((4, QPR, SLOT, width)),
            vm((groups, KEYS, STACK), f32),
            vm((groups, KEYS, STACK), f32),
            vm((H * WIN, KEYS), f32),
            vm((QPR, SLOT, width), f32),
            vm((4, eighth, width)),
            vm((4, eighth, width)),
            vm((eighth // 2, width)),
            vm((eighth // 2, width)),
            vm((eighth, width)),
            vm((eighth, width)),
            vm((groups, 4, 2, eighth, thick)),
            vm((groups, 4, eighth, thick)),
            vm((groups, eighth // 2, thick)),
            vm((groups, eighth // 2, thick)),
            vm((groups, eighth, thick)),
            vm((groups, eighth, thick)),
            vm((8, eighth, width)),
            vm((8, eighth, width)),
            vm((9, eighth, width)),
            vm((9, eighth, width)),
            vm((groups, eighth, thick)),
            vm((groups, eighth, thick)),
            vm((4, 8, width), f32),
            vm((3, 8, width), f32),
            vm((4, 8, width), f32),
            pltpu.SemaphoreType.DMA((10, Scatter.COPIES)),
            pltpu.SemaphoreType.DMA((10, Scatter.COPIES)),
            pltpu.SemaphoreType.DMA((19, 2)),
            pltpu.SemaphoreType.DMA((19, 2)),
            pltpu.SemaphoreType.DMA((3,)),
            pltpu.SemaphoreType.DMA((3,)),
            pltpu.SemaphoreType.DMA((11,)),
            pltpu.SemaphoreType.DMA((9 + 7 * groups,)),
        ],
        compiler_params=pltpu.CompilerParams(
            collective_id=1, has_side_effects=True, vmem_limit_bytes=62 << 20
        ),
        name="backward_part",
    )(
        windows, pieces, back, idx, gains, gain_grad, sums,
        normed, proj, prefix, picked, attended_grad, after_grad, hidden, qkv, prefix_w,
        out_grad.reshape(4, 2, eighth, width),
    )


def finish_kernel(*refs):
    count = (len(refs) - 2) // 4
    sources, results, held, wide = (refs[i * count : (i + 1) * count] for i in range(4))
    in_sem, out_sem = refs[-2:]
    loads = [pltpu.make_async_copy(src, dst, in_sem.at[k]) for k, (src, dst) in enumerate(zip(sources, held))]
    stores = [
        pltpu.make_async_copy(src if src.dtype != low.dtype else low, dst, out_sem.at[k])
        for k, (src, low, dst) in enumerate(zip(wide, held, results))
    ]
    for copy in loads:
        copy.start()
    for k, copy in enumerate(loads):
        copy.wait()
        if wide[k].dtype != held[k].dtype:
            wide[k][...] = held[k][...].astype(f32)
        stores[k].start()
    for copy in stores:
        copy.wait()


def finish(arrays, kinds):
    sds = jax.ShapeDtypeStruct
    return pl.pallas_call(
        finish_kernel,
        out_shape=tuple(sds(a.shape, kind) for a, kind in zip(arrays, kinds)),
        in_specs=[ANY] * len(arrays),
        out_specs=(ANY,) * len(arrays),
        scratch_shapes=[pltpu.VMEM(a.shape, a.dtype) for a in arrays]
        + [
            pltpu.VMEM(a.shape if kind != a.dtype else (8, 128), kind) for a, kind in zip(arrays, kinds)
        ]
        + [pltpu.SemaphoreType.DMA((len(arrays),)), pltpu.SemaphoreType.DMA((len(arrays),))],
        compiler_params=pltpu.CompilerParams(vmem_limit_bytes=62 << 20),
        name="finish",
    )(*arrays)


def near_local(
    hidden, segment_ids, memory, memory_row, buckets, attn_gain, ffn_gain, rel_table,
    w_qkv, w_attn_out, w_in, w_down, w_prefix, cotangent,
):
    length, width = hidden.shape[1:]
    windows, pieces = layout_tables(segment_ids[0])
    idx = near_buckets(buckets, length)
    padded = jnp.pad(memory[0], ((0, 0), (0, SLOT - PAIRS), (0, 0)))
    (
        output, normed, proj, prefix, picked, gains, ffn_gain_grad, attended_grad, after_grad,
        full_qkv, full_prefix, attn_out_grad, sums,
    ) = forward_part(
        windows, pieces, memory_row[0], padded, attn_gain[None], ffn_gain[None], rel_table[None], idx,
        hidden[0], cotangent[0], w_qkv, w_prefix, w_attn_out, w_in, w_down,
    )
    hidden_grad, memory_grad, *rest = backward_part(
        windows, pieces, back_order(memory_row[0]), idx, gains, ffn_gain_grad, sums, normed, proj, prefix,
        picked, attended_grad, after_grad, hidden[0], full_qkv, full_prefix.reshape(4, width, width), attn_out_grad,
    )
    output, hidden_grad, memory_grad, *grads = finish(
        (output, hidden_grad, memory_grad, *rest[3:]), (bf16,) + (f32,) * 7
    )
    return (output[None], hidden_grad[None], memory_grad[None]) + tuple(x[0] for x in rest[:3]) + tuple(grads)


def rms_scale(values, norm_gain):
    return (
        values * lax.rsqrt(jnp.mean(values * values, axis=-1, keepdims=True) + epsilon) * norm_gain
    )


def plain_forward_kernel(window_ref, piece_ref, idx_ref, gains_ref, proj, prefix, out, bias, pad):
    table_bias(gains_ref, idx_ref, bias)
    loop(QPR, lambda q: attend_one(q, window_ref, proj, prefix, bias, pad), SPAN)
    loop(out.shape[0] // BLOCK, lambda b: unpad(b, piece_ref, (pad,), (out,)))


def plain_attend(tables, proj, prefix):
    _, length, width = proj.shape
    return pl.pallas_call(
        plain_forward_kernel,
        out_shape=jax.ShapeDtypeStruct((length, width), bf16),
        in_specs=[SMEM] * 2 + [VMEM] * 4,
        out_specs=VMEM,
        scratch_shapes=[pltpu.VMEM((H // GROUP, KEYS, STACK), f32), pltpu.VMEM((QPR, WIN, width), bf16)],
        compiler_params=pltpu.CompilerParams(vmem_limit_bytes=40 << 20),
        name="attend",
    )(*tables, proj, prefix)


def plain_backward_kernel(
    window_ref, piece_ref, idx_ref, gains_ref, proj, prefix, grad,
    tokens, slots, table_ref, bias, bias_grad, pads, lines,
):
    table_bias(gains_ref, idx_ref, bias)
    bias_grad[...] = jnp.zeros_like(bias_grad)
    for g in range(grad.shape[1] // GW):
        loop(QPR, lambda q: back_one(q, g, window_ref, proj, prefix, grad, bias, bias_grad, pads, slots), SPAN)
        cols = slice(g * GW, (g + 1) * GW)
        loop(
            grad.shape[0] // BLOCK,
            lambda b: unpad(
                b, piece_ref, [pads.at[s] for s in range(3)], [tokens.at[s, :, cols] for s in range(3)]
            ),
        )
    table_ref[...] = table_sums(bias_grad, lines, idx_ref)


def plain_attend_back(tables, proj, prefix, grad):
    sds = jax.ShapeDtypeStruct
    return pl.pallas_call(
        plain_backward_kernel,
        out_shape=(sds(proj.shape, bf16), sds(prefix.shape, bf16), sds((1, NB * H), f32)),
        in_specs=[SMEM] * 2 + [VMEM] * 5,
        out_specs=(VMEM,) * 3,
        scratch_shapes=[
            pltpu.VMEM((H // GROUP, KEYS, STACK), f32),
            pltpu.VMEM((H // GROUP, KEYS, STACK), f32),
            pltpu.VMEM((3, QPR, WIN, GW), bf16),
            pltpu.VMEM((H * WIN, KEYS), f32),
        ],
        compiler_params=pltpu.CompilerParams(vmem_limit_bytes=48 << 20),
        name="attend_back",
    )(*tables, proj, prefix, grad)


def plain_row_pass(hidden, segments, memory, chosen, buckets, cotangent, full):
    attn_gain, ffn_gain, rel_table, w_qkv, w_attn_out, w_in, w_down, w_prefix = full
    length, width = hidden.shape
    tokens = hidden.astype(f32)
    gain_one = attn_gain.astype(f32)
    gain_two = ffn_gain.astype(f32)
    tables = layout_tables(segments) + (
        near_buckets(buckets, length), lines_of((attn_gain, ffn_gain, rel_table), width),
    )

    normed = rms_scale(tokens, gain_one).astype(bf16)
    projected = mm(normed, w_qkv).astype(bf16)
    picked = jnp.take(jnp.pad(memory, ((0, 0), (0, SLOT - PAIRS), (0, 0))), chosen, axis=0).reshape(QPR * SLOT, width)
    prefix = mm(picked, w_prefix).astype(bf16)
    proj = jnp.transpose(projected.reshape(length, 3, width), (1, 0, 2))
    prefix = jnp.transpose(prefix.reshape(QPR, SLOT, 4, width), (2, 0, 1, 3))
    attended = plain_attend(tables, proj, prefix)
    after_attn = tokens + mm(attended, w_attn_out)
    normed_ffn = rms_scale(after_attn, gain_two).astype(bf16)
    hidden_pre = mm(normed_ffn, w_in)
    activation = jax.nn.gelu(hidden_pre).astype(bf16)
    output = (after_attn + mm(activation, w_down)).astype(bf16)

    grad_out = cotangent.astype(f32)
    down_grad = mm(activation, cotangent, TN)
    act_grad = mm(cotangent, w_down, NT)
    pre_grad = jax.vjp(jax.nn.gelu, hidden_pre)[1](act_grad)[0].astype(bf16)
    in_grad = mm(normed_ffn, pre_grad, TN)
    normed_ffn_grad = mm(pre_grad, w_in, NT)
    residual_part, ffn_gain_grad = jax.vjp(rms_scale, after_attn, gain_two)[1](normed_ffn_grad)
    after_grad = grad_out + residual_part
    attn_branch = after_grad.astype(bf16)
    attn_out_grad = mm(attended, attn_branch, TN)
    attended_grad = mm(attn_branch, w_attn_out, NT).astype(bf16)
    token_grad, slot_grad, table_grad = plain_attend_back(tables, proj, prefix, attended_grad)
    token_grad = jnp.transpose(token_grad, (1, 0, 2)).reshape(length, 3 * width)
    slot_grad = jnp.transpose(slot_grad, (1, 2, 0, 3)).reshape(QPR * SLOT, 4 * width)
    qkv_grad = mm(normed, token_grad, TN)
    normed_grad = mm(token_grad, w_qkv, NT)
    prefix_grad = mm(picked, slot_grad, TN)
    picked_grad = mm(slot_grad, w_prefix, NT).reshape(QPR, SLOT, width)[:, :PAIRS]
    memory_grad = jnp.take(picked_grad, back_order(chosen), axis=0)
    norm_part, attn_gain_grad = jax.vjp(rms_scale, tokens, gain_one)[1](normed_grad)
    hidden_grad = after_grad + norm_part
    small = jnp.concatenate([attn_gain_grad, ffn_gain_grad, table_grad[0]])
    return output, hidden_grad, memory_grad, small, (qkv_grad, attn_out_grad, in_grad, down_grad, prefix_grad)


def plain_local(
    hidden, segment_ids, memory, memory_row, buckets, attn_gain, ffn_gain, rel_table,
    w_qkv, w_attn_out, w_in, w_down, w_prefix, cotangent,
):
    sizes = (attn_gain.shape[0], ffn_gain.shape[0], rel_table.shape[0])
    small = lax.all_gather(jnp.concatenate([attn_gain, ffn_gain, rel_table]), "fsdp", axis=0)
    cuts = (0, sizes[0], sizes[0] + sizes[1], sum(sizes))
    full = tuple(small[:, cuts[i] : cuts[i + 1]].reshape(-1) for i in range(3)) + tuple(
        lax.all_gather(w, "fsdp", axis=0, tiled=True) for w in (w_qkv, w_attn_out, w_in, w_down, w_prefix)
    )
    outs = []
    total = None
    for r in range(hidden.shape[0]):
        *own, small_grad, grads = plain_row_pass(
            hidden[r], segment_ids[r], memory[r], memory_row[r], buckets, cotangent[r], full
        )
        outs.append(own)
        fresh = (small_grad,) + grads
        total = fresh if total is None else jax.tree.map(jnp.add, total, fresh)
    output, hidden_grad, memory_grad = (jnp.stack(x) for x in zip(*outs))
    small_grad = lax.psum(total[0], ("fsdp", "dp"))
    me = lax.axis_index("fsdp")
    bases = (0, full[0].shape[0], full[0].shape[0] + full[1].shape[0])
    shares = [
        lax.dynamic_slice_in_dim(small_grad, base + me * size, size) for base, size in zip(bases, sizes)
    ]
    for gradient in total[1:]:
        share = lax.psum_scatter(gradient.astype(bf16), "fsdp", scatter_dimension=0, tiled=True)
        shares.append(lax.psum(share, "dp").astype(f32))
    return (output, hidden_grad, memory_grad) + tuple(shares)


def solution(mesh):
    rows = ("fsdp", "dp")
    placed = (
        P(rows, None, None), P(rows, None), P(rows, None, None, None), P(rows, None), P(),
        P("fsdp"), P("fsdp"), P("fsdp"),
        P("fsdp", None), P("fsdp", None), P("fsdp", None), P("fsdp", None), P("fsdp", None),
        P(rows, None, None),
    )
    near = mesh.shape["fsdp"] == 8 and mesh.shape["dp"] == 4
    return jax.shard_map(
        near_local if near else plain_local,
        mesh=mesh,
        in_specs=placed,
        out_specs=(
            P(rows, None, None), P(rows, None, None), P(rows, None, None, None),
            P("fsdp"), P("fsdp"), P("fsdp"),
            P("fsdp", None), P("fsdp", None), P("fsdp", None), P("fsdp", None), P("fsdp", None),
        ),
        check_vma=False,
    )
```
